128 devices in a mesh: ctx: 16 (over x, z_lo, core), fsdp: 8 (over z_hi, y).
Axes of the slice: x: 4, y: 4, z: 4 (z_hi: 2, z_lo: 2; z = z_hi * 2 + z_lo), core: 2. Of those that a mesh axis runs over, the one named last changes fastest.
Arguments:
- tokens: bfloat16 [8, 4096, 1024], P('fsdp', 'ctx'), may hold values from -6 to 6
- positions: int32 [8, 4096], P('fsdp', 'ctx'), may hold values from 0 to 16380, as said below
- cotangent: bfloat16 [8, 4096, 1024], P('fsdp', 'ctx'), may hold values from -6 to 6
- weight_qkv: float32 [1, 1024, 3072], P(None, 'fsdp'), may hold values from -0.1875 to 0.1875
- weight_attn: float32 [1, 1024, 1024], P(None, 'fsdp'), may hold values from -6 to 6
- weight_in: float32 [1, 1024, 5248], P(None, 'fsdp'), may hold values from -0.1875 to 0.1875
- weight_out: float32 [1, 2624, 1024], P(None, None, 'fsdp'), may hold values from -0.125 to 0.125
- norm_gains: float32 [1, 2, 1024], P(None, None, 'fsdp'), may hold values from 0.5 to 1.5
- first_qkv: float32 [1, 1024, 3072], P(None, 'fsdp'), may hold values from -1024 to 1024
- first_attn: float32 [1, 1024, 1024], P(None, 'fsdp'), may hold values from -28 to 28
- first_in: float32 [1, 1024, 5248], P(None, 'fsdp'), may hold values from -448 to 448
- first_out: float32 [1, 2624, 1024], P(None, None, 'fsdp'), may hold values from -640 to 640
- first_gains: float32 [1, 2, 1024], P(None, None, 'fsdp'), may hold values from -1280 to 1280
- second_qkv: float32 [1, 1024, 3072], P(None, 'fsdp'), may hold values from 16384 to 262144
- second_attn: float32 [1, 1024, 1024], P(None, 'fsdp'), may hold values from 12 to 192
- second_in: float32 [1, 1024, 5248], P(None, 'fsdp'), may hold values from 2621.44 to 42598.4
- second_out: float32 [1, 2624, 1024], P(None, None, 'fsdp'), may hold values from 6553.6 to 111411.2
- second_gains: float32 [1, 2, 1024], P(None, None, 'fsdp'), may hold values from 22937.6 to 393216
Outputs:
- layer_out: bfloat16 [8, 4096, 1024], P('fsdp', 'ctx')
- tokens_grad: float32 [8, 4096, 1024], P('fsdp', 'ctx')
- new_qkv: float32 [1, 1024, 3072], P(None, 'fsdp')
- new_attn: float32 [1, 1024, 1024], P(None, 'fsdp')
- new_in: float32 [1, 1024, 5248], P(None, 'fsdp')
- new_out: float32 [1, 2624, 1024], P(None, None, 'fsdp')
- new_gains: float32 [1, 2, 1024], P(None, None, 'fsdp')
- new_first_qkv: float32 [1, 1024, 3072], P(None, 'fsdp')
- new_first_attn: float32 [1, 1024, 1024], P(None, 'fsdp')
- new_first_in: float32 [1, 1024, 5248], P(None, 'fsdp')
- new_first_out: float32 [1, 2624, 1024], P(None, None, 'fsdp')
- new_first_gains: float32 [1, 2, 1024], P(None, None, 'fsdp')
- new_second_qkv: float32 [1, 1024, 3072], P(None, 'fsdp')
- new_second_attn: float32 [1, 1024, 1024], P(None, 'fsdp')
- new_second_in: float32 [1, 1024, 5248], P(None, 'fsdp')
- new_second_out: float32 [1, 2624, 1024], P(None, None, 'fsdp')
- new_second_gains: float32 [1, 2, 1024], P(None, None, 'fsdp')
The draws below stay inside these ranges and needn't reach their ends.
Inputs may be any that keep to these rules, and one draw needn't show every extreme that they name: Along each sequence the positions start at 0 and rise by 1 to 4 from one token to the next; in one sequence, drawn from the seed, they rise by 4 at every token.
All inputs are finite; a program needn't handle non-finite values.
Results may differ from the reference program's by a relative error of at most 0.035.
Values may be sent and summed in bfloat16 or wider, within the bound.
No kernel may reach another device: no remote copies, remote signals or barrier semaphores. Data moves between devices by JAX's collectives and lax.ppermute only.
A program may use at most 256 MiB of HBM per device.

```python
import math
import jax
import jax.numpy as jnp
from jax import lax

D = 1024
HEADS = 16
HDIM = 64
FF = 2624
LAYERS = 1
STEP = 10
LENGTH = 4096
SEQS = 8
TOKENS = 32768
ATTN_SCALE = 1
N_FSDP = 8


def draw_positions(key, part):
    key = jax.random.fold_in(key, 7)
    stride_key, pick_key = jax.random.split(key)
    strides = jax.random.randint(stride_key, (SEQS, LENGTH), 1, 5)
    chosen = jax.random.randint(pick_key, (), 0, SEQS)
    rows = jnp.arange(SEQS) == chosen
    strides = jnp.where(rows[:, None], 4, strides)
    return (jnp.cumsum(strides, axis=1) - strides[:, :1]).astype(jnp.int32)


def shard_levels(key, shape, shards, least, largest):
    level = 1.0
    for axis_at, shards_of in shards:
        steps = jax.random.uniform(jax.random.fold_in(jax.random.fold_in(key, 6), axis_at), (shards_of,), jnp.float32, least / len(shards), largest / len(shards))
        level = level * jnp.repeat(jnp.exp(steps), shape[axis_at] // shards_of).reshape((-1,) + (1,) * (len(shape) - 1 - axis_at))
    return level


def gaussian(stream_key, dims, deviation, reach, shards=(), kind=jnp.bfloat16):
    values = jax.random.normal(stream_key, dims, jnp.float32) * deviation
    if len(shards) > 0:
        values = shard_levels(stream_key, dims, shards, -0.22, 0.18) * values
    return jnp.clip(values, min=-reach, max=reach).astype(kind)


def setup_inputs(seed: int = 0) -> dict:
    key_list = jax.random.split(jax.random.key(seed), 19)
    tokens = gaussian(key_list[0], (SEQS, LENGTH, D), 1.0, 6.0, ((0, 8), (1, 16)))
    positions = draw_positions(jax.random.fold_in(key_list[18], 71), 0)
    cotangent = gaussian(key_list[2], (SEQS, LENGTH, D), 1.0, 6.0, ((0, 8), (1, 16)))
    weight_qkv = gaussian(key_list[3], (LAYERS, D, 3 * D), D ** -0.5, 0.1875, ((1, 8),), jnp.float32)
    weight_attn = gaussian(key_list[4], (LAYERS, D, D), ATTN_SCALE ** -0.5, 6.0, ((1, 8),), jnp.float32)
    weight_in = gaussian(key_list[5], (LAYERS, D, 2 * FF), D ** -0.5, 0.1875, ((1, 8),), jnp.float32)
    weight_out = gaussian(key_list[6], (LAYERS, FF, D), FF ** -0.5, 0.125, ((2, 8),), jnp.float32)
    norm_gains = jnp.clip(1.0 + 0.1 * jax.random.normal(key_list[7], (LAYERS, 2, D), jnp.float32), 0.5, 1.5)
    first_qkv = gaussian(key_list[8], (LAYERS, D, 3 * D), (TOKENS ** 0.5), 1024.0, ((1, 8),), jnp.float32)
    first_attn = gaussian(key_list[9], (LAYERS, D, D), ((3 * N_FSDP) ** 0.5), 28.0, ((1, 8),), jnp.float32)
    first_in = gaussian(key_list[10], (LAYERS, D, 2 * FF), (0.4 * TOKENS ** 0.5), 448.0, ((1, 8),), jnp.float32)
    first_out = gaussian(key_list[11], (LAYERS, FF, D), (0.65 * TOKENS ** 0.5), 640.0, ((2, 8),), jnp.float32)
    first_gains = gaussian(key_list[12], (LAYERS, 2, D), (1.2 * TOKENS ** 0.5), 1280.0, ((2, 8),), jnp.float32)
    second_qkv = jnp.clip(jnp.exp(math.log(262144.0) - 2.7725887 * jax.random.uniform(key_list[13], (LAYERS, D, 3 * D), jnp.float32) ** shard_levels(key_list[13], (LAYERS, D, 3 * D), ((1, 8),), -0.2, 0.2)), 16384.0, 262144.0)
    second_attn = jnp.clip(jnp.exp(math.log(192.0) - 2.7725887 * jax.random.uniform(key_list[14], (LAYERS, D, D), jnp.float32) ** shard_levels(key_list[14], (LAYERS, D, D), ((1, 8),), -0.2, 0.2)), 12.0, 192.0)
    second_in = jnp.clip(jnp.exp(math.log(42598.4) - 2.7880929 * jax.random.uniform(key_list[15], (LAYERS, D, 2 * FF), jnp.float32) ** shard_levels(key_list[15], (LAYERS, D, 2 * FF), ((1, 8),), -0.2, 0.2)), 2621.44, 42598.4)
    second_out = jnp.clip(jnp.exp(math.log(111411.2) - 2.8332134 * jax.random.uniform(key_list[16], (LAYERS, FF, D), jnp.float32) ** shard_levels(key_list[16], (LAYERS, FF, D), ((2, 8),), -0.2, 0.2)), 6553.6, 111411.2)
    second_gains = jnp.clip(jnp.exp(math.log(393216.0) - 2.8415816 * jax.random.uniform(key_list[17], (LAYERS, 2, D), jnp.float32) ** shard_levels(key_list[17], (LAYERS, 2, D), ((2, 8),), -0.2, 0.2)), 22937.6, 393216.0)
    return dict(tokens=tokens, positions=positions, cotangent=cotangent, weight_qkv=weight_qkv, weight_attn=weight_attn, weight_in=weight_in, weight_out=weight_out, norm_gains=norm_gains, first_qkv=first_qkv, first_attn=first_attn, first_in=first_in, first_out=first_out, first_gains=first_gains, second_qkv=second_qkv, second_attn=second_attn, second_in=second_in, second_out=second_out, second_gains=second_gains)


BETA_FIRST = 0.5
BETA_SECOND = 0.5
EPSILON = 1e-08
DECAY = 0.01
NORM_EPS = 1e-05
ROPE_BASE = 160000.0
GAIN_RATE = 0.6
HIGH = lax.Precision.HIGHEST

@jax.custom_vjp
def low(v):
    return lax.optimization_barrier(v.astype(jnp.bfloat16)).astype(jnp.float32)

@jax.custom_vjp
def low_back(v):
    return v

def low_keep(v):
    return (low(v), None)

def low_pass(kept, grad):
    return (grad,)

def back_keep(v):
    return (v, None)

def back_low(kept, grad):
    return (low(grad),)
low.defvjp(low_keep, low_pass)
low_back.defvjp(back_keep, back_low)

def norm_rows(values, gain):
    average = lax.optimization_barrier(jnp.mean(values, axis=-1, keepdims=True))
    centered = values - average
    spread = lax.optimization_barrier(jnp.mean(centered * centered, axis=-1, keepdims=True))
    return centered * lax.rsqrt(spread + NORM_EPS) * gain

def rope_tables(places):
    half_size = HDIM // 2
    freqs = jnp.exp(jnp.arange(half_size, dtype=jnp.float32) * (-2.0 * math.log(ROPE_BASE) / HDIM))
    angles = places.astype(jnp.float32)[:, None] * freqs[None, :]
    cosine = jnp.cos(angles)
    sine = jnp.sin(angles)
    return (jnp.concatenate([cosine, cosine], axis=-1), jnp.concatenate([sine, sine], axis=-1))

def rotate(values, cosine, sine):
    half_size = values.shape[-1] // 2
    turned = jnp.concatenate([-values[..., half_size:], values[..., :half_size]], axis=-1)
    return values * cosine[:, None, :] + turned * sine[:, None, :]

def head_attention(element):
    queries, all_keys, all_values = element
    scores = low_back(jnp.dot(queries, all_keys.T, precision=HIGH) * HDIM ** (-0.5))
    highest = lax.optimization_barrier(jnp.max(scores, axis=-1, keepdims=True))
    raised = jnp.exp(scores - highest)
    soft_rows = low(raised / lax.optimization_barrier(jnp.sum(raised, axis=-1, keepdims=True)))
    return jnp.dot(soft_rows, all_values, precision=HIGH)

def layer_sequence(values, cosine, sine, mat_qkv, mat_attn, mat_in, mat_out, gains):
    seq_len = values.shape[0]
    hidden = low(norm_rows(values, gains[0]))
    mixed = low_back(jnp.dot(hidden, mat_qkv, precision=HIGH))
    queries = low(low_back(rotate(mixed[:, :D].reshape(seq_len, HEADS, HDIM), cosine, sine)))
    all_keys = low(low_back(rotate(mixed[:, D:2 * D].reshape(seq_len, HEADS, HDIM), cosine, sine)))
    all_values = low(low_back(mixed[:, 2 * D:].reshape(seq_len, HEADS, HDIM)))
    per_head = lax.map(jax.checkpoint(head_attention), (queries.transpose(1, 0, 2), all_keys.transpose(1, 0, 2), all_values.transpose(1, 0, 2)))
    attended = low(low_back(per_head.transpose(1, 0, 2).reshape(seq_len, D)))
    residual = values + low_back(jnp.dot(attended, mat_attn, precision=HIGH))
    middle = low(norm_rows(residual, gains[1]))
    both = low_back(jnp.dot(middle, mat_in, precision=HIGH))
    active = low(jax.nn.gelu(both[:, :FF], approximate=False) * both[:, FF:])
    return residual + low_back(jnp.dot(active, mat_out, precision=HIGH))

def forward(weight_qkv, weight_attn, weight_in, weight_out, norm_gains, inputs, positions):
    lowered = [(low(weight_qkv[member]), low(weight_attn[member]), low(weight_in[member]), low(weight_out[member]), low(norm_gains[member])) for member in range(LAYERS)]

    def one_sequence(carry, element):
        values, places = element
        cosine, sine = rope_tables(places)
        for weights in lowered:
            values = layer_sequence(values, cosine, sine, *weights)
        return (carry, values)
    _, result = lax.scan(jax.checkpoint(one_sequence), jnp.zeros((), jnp.float32), (inputs, positions))
    return result

def adam(weight, gradient, first, second, rate):
    first = BETA_FIRST * first + (1.0 - BETA_FIRST) * gradient
    second = BETA_SECOND * second + (1.0 - BETA_SECOND) * gradient * gradient
    first_hat = first / (1.0 - BETA_FIRST ** STEP)
    second_hat = second / (1.0 - BETA_SECOND ** STEP)
    weight = weight - rate * (first_hat / (jnp.sqrt(second_hat) + EPSILON) + DECAY * weight)
    return (weight, first, second)

def reference(tokens, positions, cotangent, weight_qkv, weight_attn, weight_in, weight_out, norm_gains, first_qkv, first_attn, first_in, first_out, first_gains, second_qkv, second_attn, second_in, second_out, second_gains):

    def wrapped(mat_qkv, mat_attn, mat_in, mat_out, gains, inputs):
        return forward(mat_qkv, mat_attn, mat_in, mat_out, gains, inputs, positions)
    result, pull = jax.vjp(wrapped, weight_qkv, weight_attn, weight_in, weight_out, norm_gains, tokens.astype(jnp.float32))
    grads = pull(cotangent.astype(jnp.float32))
    rates = (D ** (-0.5), ATTN_SCALE ** (-0.5), D ** (-0.5), FF ** (-0.5), GAIN_RATE)
    masters = (weight_qkv, weight_attn, weight_in, weight_out, norm_gains)
    firsts = (first_qkv, first_attn, first_in, first_out, first_gains)
    seconds = (second_qkv, second_attn, second_in, second_out, second_gains)
    updated = [adam(masters[member], grads[member], firsts[member], seconds[member], rates[member]) for member in range(5)]
    return (result.astype(jnp.bfloat16), grads[5], updated[0][0], updated[1][0], updated[2][0], updated[3][0], updated[4][0], updated[0][1], updated[1][1], updated[2][1], updated[3][1], updated[4][1], updated[0][2], updated[1][2], updated[2][2], updated[3][2], updated[4][2])
```

```python
import functools
import math

import jax
import jax.numpy as jnp
from jax import lax
from jax.experimental import pallas as pl
from jax.experimental.pallas import tpu as pltpu
from jax.sharding import Mesh, PartitionSpec as P

HDIM = 64
STEP = 10
BETA_FIRST = 0.5
BETA_SECOND = 0.5
EPSILON = 1e-08
DECAY = 0.01
NORM_EPS = 1e-05
ROPE_BASE = 160000.0
GAIN_RATE = 0.6
LOG2E = math.log2(math.e)
f32 = jnp.float32
bf16 = jnp.bfloat16

CHIPS = ("x", "zl")
CTX = ("x", "zl", "c")
FSDP = ("zh", "y")
SWAP = [(0, 1), (1, 0)]
VMEM = 60 << 20


def dot(left, right, left_dim=1, right_dim=0):
    return lax.dot_general(
        left, right, (((left_dim,), (right_dim,)), ((), ())), preferred_element_type=f32
    )


def unit_rows(values):
    average = jnp.mean(values, axis=-1, keepdims=True)
    centered = values - average
    spread = jnp.mean(centered * centered, axis=-1, keepdims=True)
    inverse = lax.rsqrt(spread + NORM_EPS)
    return centered * inverse, inverse


def unit_back(scaled, unit, inverse):
    first_mean = jnp.mean(scaled, axis=-1, keepdims=True)
    second_mean = jnp.mean(scaled * unit, axis=-1, keepdims=True)
    return inverse * (scaled - first_mean - unit * second_mean)


def project_kernel(x_ref, w_ref, cos_ref, sin_ref, unit_ref, qkv_ref, keys_ref, values_ref, w_all):
    half = HDIM // 2
    rows = x_ref.shape[0]

    @pl.when(pl.program_id(0) == 0)
    def _():
        for part in range(w_ref.shape[0]):
            w_all[:, part * 128 : (part + 1) * 128] = w_ref[part]

    unit = unit_rows(x_ref[...].astype(f32))[0].astype(bf16)
    unit_ref[...] = unit
    mixed = dot(w_all[...], unit, 1, 1)
    cosine = cos_ref[...]
    sine = sin_ref[...]

    def turn(one, two):
        return jnp.concatenate([one * cosine - two * sine, two * cosine + one * sine], axis=0)

    queries = turn(mixed[:half], mixed[half:HDIM])
    keys = turn(mixed[HDIM : HDIM + half], mixed[HDIM + half : 2 * HDIM])
    values = mixed[2 * HDIM :]
    qkv_ref[...] = jnp.concatenate([queries, keys, values], axis=0).astype(bf16)
    key_rows = keys.T.astype(bf16)
    value_rows = values.T.astype(bf16)
    ones = jnp.where(lax.broadcasted_iota(jnp.int32, (rows, 128), 1) < 3, 1.0, 0.0).astype(bf16)
    keys_ref[...] = jnp.concatenate([key_rows, key_rows, ones], axis=1)
    values_ref[...] = jnp.concatenate([value_rows, ones[:, :HDIM]], axis=1)


def project(tokens, weights, cosine, sine, block=512):
    length, width = tokens.shape
    return pl.pallas_call(
        project_kernel,
        name="project",
        grid=(length // block,),
        in_specs=[
            pl.BlockSpec((block, width), lambda i: (i, 0)),
            pl.BlockSpec(weights.shape, lambda i: (0, 0, 0)),
            pl.BlockSpec((HDIM // 2, block), lambda i: (0, i)),
            pl.BlockSpec((HDIM // 2, block), lambda i: (0, i)),
        ],
        out_specs=[
            pl.BlockSpec((block, width), lambda i: (i, 0)),
            pl.BlockSpec((3 * HDIM, block), lambda i: (0, i)),
            pl.BlockSpec((block, 256), lambda i: (i, 0)),
            pl.BlockSpec((block, 128), lambda i: (i, 0)),
        ],
        out_shape=[
            jax.ShapeDtypeStruct((length, width), bf16),
            jax.ShapeDtypeStruct((3 * HDIM, length), bf16),
            jax.ShapeDtypeStruct((length, 256), bf16),
            jax.ShapeDtypeStruct((length, 128), bf16),
        ],
        scratch_shapes=[pltpu.VMEM((3 * HDIM, width), bf16)],
        compiler_params=pltpu.CompilerParams(vmem_limit_bytes=VMEM),
    )(tokens, weights, cosine, sine)


def scaled_queries(queries):
    scaled = queries.astype(f32) * (LOG2E / math.sqrt(HDIM))
    high = scaled.astype(bf16)
    low = (scaled - high.astype(f32)).astype(bf16)
    return high, low


def attend_kernel(keys_ref, q_ref, v_ref, low_ref, out_ref, lse_ref, v_ones, *, part):
    length = keys_ref.shape[0]
    count = length // part

    @pl.when(pl.program_id(0) == 0)
    def _():
        v_ones[:HDIM] = v_ref[...]
        v_ones[HDIM:] = jnp.where(
            lax.broadcasted_iota(jnp.int32, (16, length), 0) < 1, 1.0, 0.0
        ).astype(bf16)

    queries = jnp.concatenate(scaled_queries(q_ref[...]), axis=0)

    def score(at):
        return dot(keys_ref[at * part : (at + 1) * part, : 2 * HDIM], queries)

    scores = score(0)
    highest = total = None
    for at in range(count):
        following = score(at + 1) if at + 1 < count else None
        peak = jnp.max(scores, axis=0, keepdims=True)
        raised = peak if highest is None else jnp.maximum(highest, peak)
        soft = jnp.exp2(scores - raised).astype(bf16)
        added = dot(v_ones[:, at * part : (at + 1) * part], soft)
        total = added if total is None else total * jnp.exp2(highest - raised) + added
        highest = raised
        scores = following
    summed = total[HDIM : HDIM + 1]
    result = total[:HDIM] / summed
    out_ref[...] = result
    lse_ref[...] = highest + jnp.log2(summed)
    step = low_ref.shape[2]
    for at in range(low_ref.shape[0]):
        low_ref[at] = result[:, at * step : (at + 1) * step].astype(bf16)


def attend(keys, qkv, chips, block=1024, part=512):
    length = keys.shape[0]
    return pl.pallas_call(
        functools.partial(attend_kernel, part=part),
        name="attend",
        grid=(length // block,),
        in_specs=[
            pl.BlockSpec(keys.shape, lambda i: (0, 0)),
            pl.BlockSpec((HDIM, block), lambda i: (0, i)),
            pl.BlockSpec((HDIM, length), lambda i: (2, 0)),
        ],
        out_specs=[
            pl.BlockSpec((block * chips // length, HDIM, length // chips), lambda i: (i, 0, 0)),
            pl.BlockSpec((HDIM, block), lambda i: (0, i)),
            pl.BlockSpec((1, block), lambda i: (0, i)),
        ],
        out_shape=[
            jax.ShapeDtypeStruct((chips, HDIM, length // chips), bf16),
            jax.ShapeDtypeStruct((HDIM, length), f32),
            jax.ShapeDtypeStruct((1, length), f32),
        ],
        scratch_shapes=[pltpu.VMEM((HDIM + 16, length), bf16)],
        compiler_params=pltpu.CompilerParams(vmem_limit_bytes=VMEM),
    )(keys, qkv, qkv)


def minus_in_three(values):
    rows = values.shape[1]
    at = lax.broadcasted_iota(jnp.int32, (16, rows), 0)
    high = (-values).astype(bf16).astype(f32)
    rest = -values - high
    middle = rest.astype(bf16).astype(f32)
    low = rest - middle
    stacked = jnp.where(at == 0, high, jnp.where(at == 1, middle, jnp.where(at == 2, low, 0.0)))
    return stacked.astype(bf16)


def attend_back_kernel(
    keys_ref,
    values_ref,
    q_ref,
    k_ref,
    dout_ref,
    out_ref,
    lse_ref,
    cos_ref,
    sin_ref,
    dp_ref,
    sums,
    *,
    part,
):
    half = HDIM // 2
    here = pl.program_id(0)
    length = keys_ref.shape[0]
    block = q_ref.shape[1]
    count = length // part
    factor = HDIM ** (-0.5)

    def turn_back(grads, cosine, sine):
        low = grads.astype(bf16).astype(f32)
        one, two = low[:half], low[half:]
        return jnp.concatenate([one * cosine + two * sine, two * cosine - one * sine], axis=0)

    @pl.when(here == 0)
    def _():
        sums[...] = jnp.zeros_like(sums)

    low_queries = q_ref[...]
    high, low = scaled_queries(low_queries)
    queries = jnp.concatenate([high, low, minus_in_three(lse_ref[...])], axis=0)
    low_dout = dout_ref[0]
    dout = low_dout.astype(f32)
    centre = jnp.sum(dout * out_ref[...], axis=0, keepdims=True)
    douts = jnp.concatenate([low_dout, minus_in_three(centre)], axis=0)
    blank = jnp.zeros((block, HDIM), bf16)
    right = jnp.concatenate(
        [
            jnp.concatenate([low_queries.astype(f32).T.astype(bf16), blank], axis=1),
            jnp.concatenate([blank, dout.T.astype(bf16)], axis=1),
        ],
        axis=0,
    )

    def score(at):
        rows = slice(at * part, (at + 1) * part)
        return (
            dot(keys_ref[rows, : 2 * HDIM + 16], queries),
            dot(values_ref[rows, : HDIM + 16], douts),
        )

    now = score(0)
    grad_queries = None
    for at in range(count):
        following = score(at + 1) if at + 1 < count else None
        rows = slice(at * part, (at + 1) * part)
        soft = jnp.exp2(now[0])
        grads = (soft * now[1]).astype(bf16)
        added = dot(k_ref[:, rows], grads)
        grad_queries = added if grad_queries is None else grad_queries + added
        sums[rows] += dot(jnp.concatenate([grads, soft.astype(bf16)], axis=1), right)
        now = following
    here_columns = pl.ds(pl.multiple_of(here * block, block), block)
    dp_ref[here, :HDIM] = turn_back(
        grad_queries * factor, cos_ref[:, here_columns], sin_ref[:, here_columns]
    ).astype(bf16)

    @pl.when(here == length // block - 1)
    def _():
        for at in range(length // block):
            columns = slice(at * block, (at + 1) * block)
            both = sums[columns].T
            dp_ref[at, HDIM : 2 * HDIM] = turn_back(
                both[:HDIM] * factor, cos_ref[:, columns], sin_ref[:, columns]
            ).astype(bf16)
            dp_ref[at, 2 * HDIM :] = both[HDIM:].astype(bf16)


def attend_back(keys, values, qkv, douts, out, lse, cosine, sine, part=256):
    length = keys.shape[0]
    chips, _, block = douts.shape

    def whole(array):
        return pl.BlockSpec(array.shape, lambda i: (0, 0))

    return pl.pallas_call(
        functools.partial(attend_back_kernel, part=part),
        name="attend_back",
        grid=(length // block,),
        in_specs=[
            whole(keys),
            whole(values),
            pl.BlockSpec((HDIM, block), lambda i: (0, i)),
            pl.BlockSpec((HDIM, length), lambda i: (1, 0)),
            pl.BlockSpec((1, HDIM, block), lambda i: (i, 0, 0)),
            pl.BlockSpec((HDIM, block), lambda i: (0, i)),
            pl.BlockSpec((1, block), lambda i: (0, i)),
            whole(cosine),
            whole(sine),
        ],
        out_specs=pl.BlockSpec((chips, 3 * HDIM, block), lambda i: (0, 0, 0)),
        out_shape=jax.ShapeDtypeStruct((chips, 3 * HDIM, block), bf16),
        scratch_shapes=[pltpu.VMEM((length, 2 * HDIM), f32)],
        compiler_params=pltpu.CompilerParams(vmem_limit_bytes=VMEM),
    )(keys, values, qkv, qkv, douts, out, lse, cosine, sine)


def adam(weight, gradient, first, second, rate):
    first = BETA_FIRST * first + (1.0 - BETA_FIRST) * gradient
    second = BETA_SECOND * second + (1.0 - BETA_SECOND) * gradient * gradient
    first_hat = first / (1.0 - BETA_FIRST**STEP)
    second_hat = second / (1.0 - BETA_SECOND**STEP)
    weight = weight - rate * (first_hat / (jnp.sqrt(second_hat) + EPSILON) + DECAY * weight)
    return (weight, first, second)


def shards(
    tokens,
    positions,
    cotangent,
    weight_qkv,
    weight_attn,
    weight_in,
    weight_out,
    norm_gains,
    first_qkv,
    first_attn,
    first_in,
    first_out,
    first_gains,
    second_qkv,
    second_attn,
    second_in,
    second_out,
    second_gains,
):
    rows, width = tokens.shape[1:]
    shard_rows = weight_qkv.shape[1]
    heads = width // HDIM
    hidden = weight_out.shape[1]
    core = lax.axis_index("c")
    mine = lax.axis_index(CTX)
    chips = lax.axis_size(CHIPS)
    owners = lax.axis_size(FSDP)
    length = rows * chips * 2
    part = hidden // 2
    padded = -(-part // 128) * 128

    local = tokens[0]
    gains = norm_gains[0].astype(bf16).astype(f32)
    low_qkv = (weight_qkv[0].astype(bf16).astype(f32) * gains[0][:, None]).astype(bf16)
    by_head = low_qkv.reshape(shard_rows, 3, heads // 2, 2, HDIM)
    own_head = lax.dynamic_index_in_dim(
        low_qkv.reshape(shard_rows, 3, heads, HDIM), mine, 2, keepdims=False
    )
    head_columns = own_head.reshape(shard_rows, 3 * HDIM).T
    head_weights = lax.all_gather(head_columns, FSDP, axis=0, tiled=False)
    places = lax.all_gather(positions[0], CTX, axis=0, tiled=True)
    sequence = lax.all_gather(local, CTX, axis=0, tiled=True)

    low_in = (weight_in[0].astype(bf16).astype(f32) * gains[1][:, None]).astype(bf16)
    pad = ((0, 0), (0, padded - part))
    gate_cols = jnp.pad(lax.dynamic_slice_in_dim(low_in, core * part, part, 1), pad)
    up_cols = jnp.pad(lax.dynamic_slice_in_dim(low_in, hidden + core * part, part, 1), pad)
    out_cols = jnp.pad(
        lax.dynamic_slice_in_dim(weight_out[0].astype(bf16), core * part, part, 0).T, pad
    )
    attn_rows = lax.dynamic_slice_in_dim(weight_attn[0].astype(bf16), core * HDIM, HDIM, 0)
    attn_cols = jnp.concatenate([attn_rows[:, : width // 2], attn_rows[:, width // 2 :]], axis=0)
    packed = jnp.concatenate([gate_cols, up_cols, out_cols, attn_cols], axis=1)
    gathered = lax.all_gather(packed, FSDP, axis=0, tiled=True)
    mat_gate = gathered[:, :padded]
    mat_up = gathered[:, padded : 2 * padded]
    mat_out = gathered[:, 2 * padded : 3 * padded]
    mat_attn = gathered[:, 3 * padded :].reshape(owners, 2, HDIM, width // 2)
    mat_attn = mat_attn.transpose(0, 2, 1, 3).reshape(owners * HDIM, width)
    half_heads = lax.dynamic_index_in_dim(by_head, core, 3, keepdims=False)
    half_heads = half_heads.transpose(0, 2, 1, 3).reshape(shard_rows, 3 * width // 2)
    mat_qkv = lax.all_gather(half_heads, FSDP, axis=0, tiled=True)

    gradient = cotangent[0]
    other_gradient = lax.ppermute(gradient, "c", SWAP)
    pair_gradient = jnp.concatenate([gradient, other_gradient], axis=0)

    freqs = jnp.exp(
        jnp.arange(HDIM // 2, dtype=f32) * (-2.0 * math.log(ROPE_BASE) / HDIM)
    )
    angles = freqs[:, None] * places.astype(f32)[None, :]
    cosine = jnp.cos(angles)
    sine = jnp.sin(angles)
    unit_all, qkv, keys, values = project(sequence, head_weights, cosine, sine)
    low_out, out, lse = attend(keys, qkv, chips)
    out_pair = lax.all_to_all(low_out, CHIPS, 0, 0, tiled=True).reshape(heads // 2 * HDIM, 2 * rows)

    def exchange(pair):
        theirs = lax.dynamic_slice_in_dim(pair, (1 - core) * rows, rows, 0)
        ours = lax.dynamic_slice_in_dim(pair, core * rows, rows, 0)
        return ours + lax.ppermute(theirs.astype(bf16), "c", SWAP).astype(f32)

    def in_order(ours, theirs):
        first = jnp.where(core == 0, ours, theirs)
        second = jnp.where(core == 0, theirs, ours)
        return jnp.concatenate([first, second], axis=0)

    current = local.astype(f32)
    residual = current + exchange(dot(out_pair, mat_attn, 0, 0))
    unit_mid, scale_mid = unit_rows(residual)
    middle = unit_mid.astype(bf16)
    middle_pair = jnp.concatenate([middle, lax.ppermute(middle, "c", SWAP)], axis=0)
    gate = dot(middle_pair, mat_gate)
    upward = dot(middle_pair, mat_up)
    bent = jax.nn.gelu(gate, approximate=False)
    active = (bent * upward).astype(bf16)
    partial = dot(active, mat_out, 1, 1)
    output = (
        residual
        + partial[:rows]
        + lax.ppermute(partial[rows:].astype(bf16), "c", SWAP).astype(f32)
    )
    layer_out = output.astype(bf16)[None]

    grad_active = dot(pair_gradient, mat_out)
    grad_out_w = dot(pair_gradient, active, 0, 0).astype(bf16)
    _, pull = jax.vjp(lambda g: jax.nn.gelu(g, approximate=False), gate)
    grad_gate = pull(grad_active * upward)[0].astype(bf16)
    grad_up = (grad_active * bent).astype(bf16)
    grad_gate_w = dot(middle_pair, grad_gate, 0, 0).astype(bf16)
    grad_up_w = dot(middle_pair, grad_up, 0, 0).astype(bf16)
    partial = dot(grad_gate, mat_gate, 1, 1) + dot(grad_up, mat_up, 1, 1)
    grad_middle = partial[:rows] + lax.ppermute(
        partial[rows:].astype(bf16), "c", SWAP
    ).astype(f32)
    grad_residual = gradient.astype(f32) + unit_back(grad_middle, unit_mid, scale_mid)
    grad_low = grad_residual.astype(bf16)
    grad_pair = in_order(grad_low, lax.ppermute(grad_low, "c", SWAP))
    dout_pair = dot(mat_attn, grad_pair, 1, 1).astype(bf16).reshape(chips, HDIM, 2 * rows)
    douts = lax.all_to_all(dout_pair, CHIPS, 0, 0, tiled=True)
    grad_attn_w = dot(out_pair, grad_pair).astype(bf16)

    spread = FSDP + CHIPS

    def summed(parts):
        arrived = lax.all_to_all(parts, spread, 0, 0, tiled=True)
        arrived = arrived.reshape(owners * chips, -1, parts.shape[1])
        return jnp.sum(arrived.astype(f32), axis=0).astype(bf16)

    attn_parts = grad_attn_w.reshape(owners, chips, HDIM // chips, width)
    attn_parts = jnp.concatenate(
        [attn_parts[..., : width // 2], attn_parts[..., width // 2 :]], axis=2
    ).reshape(width, width // 2)
    owned_out = summed(grad_out_w)
    owned_gate = summed(grad_gate_w)
    owned_up = summed(grad_up_w)
    owned_attn = summed(attn_parts)
    owned_packed = jnp.concatenate([owned_gate, owned_up, owned_out, owned_attn], axis=1)
    all_packed = lax.all_gather(owned_packed, CTX, axis=0, tiled=True)
    all_packed = all_packed.reshape(chips, 2, shard_rows // chips, -1)

    def both_halves(columns):
        picked = all_packed[..., columns : columns + part]
        return picked.transpose(0, 2, 1, 3).reshape(shard_rows, hidden).astype(f32)

    grad_gate_own = both_halves(0)
    grad_up_own = both_halves(padded)
    unit_in_own = jnp.concatenate([grad_gate_own, grad_up_own], axis=1)
    grad_out_own = both_halves(2 * padded).T
    grad_attn_own = all_packed[..., 3 * padded :].reshape(
        chips, 2, 2, HDIM // chips, width // 2
    )
    grad_attn_own = (
        grad_attn_own.transpose(1, 0, 3, 2, 4).reshape(shard_rows, width).astype(f32)
    )

    grad_mixed = attend_back(keys, values, qkv, douts, out, lse, cosine, sine)
    mixed_pair = lax.all_to_all(grad_mixed, CHIPS, 0, 0, tiled=True)
    mixed_pair = mixed_pair.reshape(3 * width // 2, 2 * rows)
    unit_in, scale_in = unit_rows(current)
    grad_hidden = exchange(dot(mixed_pair, mat_qkv, 0, 1))
    tokens_grad = (grad_residual + unit_back(grad_hidden, unit_in, scale_in))[None]

    head_grad = lax.dot_general(
        unit_all.reshape(chips, 2 * rows, width),
        grad_mixed,
        (((0, 1), (0, 2)), ((), ())),
        preferred_element_type=f32,
    ).astype(bf16)
    arrived = lax.all_to_all(head_grad, FSDP, 0, 0, tiled=True)
    head_own = jnp.sum(
        arrived.reshape(owners, shard_rows, 3 * HDIM).astype(f32), axis=0
    ).astype(bf16)
    unit_qkv_own = lax.all_gather(head_own, CTX, axis=0, tiled=False)
    unit_qkv_own = (
        unit_qkv_own.reshape(heads, shard_rows, 3, HDIM)
        .transpose(1, 2, 0, 3)
        .reshape(shard_rows, 3 * width)
        .astype(f32)
    )

    gain_first = jnp.sum(unit_qkv_own * weight_qkv[0].astype(bf16).astype(f32), axis=1)
    gain_second = jnp.sum(unit_in_own * weight_in[0].astype(bf16).astype(f32), axis=1)
    owned = (
        unit_qkv_own * gains[0][:, None],
        grad_attn_own,
        unit_in_own * gains[1][:, None],
        grad_out_own,
        jnp.stack([gain_first, gain_second], axis=0),
    )
    rates = (
        width ** (-0.5),
        max(1, 3 * width // length) ** (-0.5),
        width ** (-0.5),
        hidden ** (-0.5),
        GAIN_RATE,
    )
    masters = (weight_qkv, weight_attn, weight_in, weight_out, norm_gains)
    firsts = (first_qkv, first_attn, first_in, first_out, first_gains)
    seconds = (second_qkv, second_attn, second_in, second_out, second_gains)
    updated = [
        adam(masters[member][0], owned[member], firsts[member][0], seconds[member][0], rates[member])
        for member in range(5)
    ]
    return (
        layer_out,
        tokens_grad,
        *[updated[member][0][None] for member in range(5)],
        *[updated[member][1][None] for member in range(5)],
        *[updated[member][2][None] for member in range(5)],
    )


def solution(mesh):
    split = Mesh(mesh.devices.reshape(4, 2, 2, 2, 4), ("x", "zl", "c", "zh", "y"))
    by_row = P(None, FSDP, None)
    by_column = P(None, None, FSDP)
    weights = (by_row, by_row, by_row, by_column, by_column)
    by_token = P(FSDP, CTX, None)
    return jax.shard_map(
        shards,
        mesh=split,
        in_specs=(by_token, P(FSDP, CTX), by_token) + weights * 3,
        out_specs=(by_token, by_token) + weights * 3,
        check_vma=False,
    )
```

```python
import functools
import math

import jax
import jax.numpy as jnp
from jax import lax
from jax.experimental import pallas as pl
from jax.experimental.pallas import tpu as pltpu
from jax.sharding import Mesh, PartitionSpec as P

HDIM = 64
STEP = 10
BETA_FIRST = 0.5
BETA_SECOND = 0.5
EPSILON = 1e-08
DECAY = 0.01
NORM_EPS = 1e-05
ROPE_BASE = 160000.0
GAIN_RATE = 0.6
LOG2E = math.log2(math.e)
f32 = jnp.float32
bf16 = jnp.bfloat16

CHIPS = ("x", "zl")
CTX = ("x", "zl", "c")
FSDP = ("zh", "y")
SWAP = [(0, 1), (1, 0)]
VMEM = 60 << 20


def dot(left, right, left_dim=1, right_dim=0):
    return lax.dot_general(
        left, right, (((left_dim,), (right_dim,)), ((), ())), preferred_element_type=f32
    )


def cost(flops, moved):
    return pl.CostEstimate(flops=flops, bytes_accessed=moved, transcendentals=0)


def unit_rows(values):
    average = jnp.mean(values, axis=-1, keepdims=True)
    centered = values - average
    spread = jnp.mean(centered * centered, axis=-1, keepdims=True)
    inverse = lax.rsqrt(spread + NORM_EPS)
    return centered * inverse, inverse


def unit_back(scaled, unit, inverse):
    first_mean = jnp.mean(scaled, axis=-1, keepdims=True)
    second_mean = jnp.mean(scaled * unit, axis=-1, keepdims=True)
    return inverse * (scaled - first_mean - unit * second_mean)


def project_kernel(x_ref, w_ref, cos_ref, sin_ref, unit_ref, qkv_ref, keys_ref, values_ref, w_all):
    half = HDIM // 2
    rows = x_ref.shape[0]

    @pl.when(pl.program_id(0) == 0)
    def _():
        for part in range(w_ref.shape[0]):
            w_all[:, part * 128 : (part + 1) * 128] = w_ref[part]

    unit = unit_rows(x_ref[...].astype(f32))[0].astype(bf16)
    unit_ref[...] = unit
    mixed = dot(w_all[...], unit, 1, 1)
    cosine = cos_ref[...]
    sine = sin_ref[...]

    def turn(one, two):
        return jnp.concatenate([one * cosine - two * sine, two * cosine + one * sine], axis=0)

    queries = turn(mixed[:half], mixed[half:HDIM])
    keys = turn(mixed[HDIM : HDIM + half], mixed[HDIM + half : 2 * HDIM])
    values = mixed[2 * HDIM :]
    qkv_ref[...] = jnp.concatenate([queries, keys, values], axis=0).astype(bf16)
    key_rows = keys.T.astype(bf16)
    value_rows = values.T.astype(bf16)
    ones = jnp.where(lax.broadcasted_iota(jnp.int32, (rows, 128), 1) < 3, 1.0, 0.0).astype(bf16)
    keys_ref[...] = jnp.concatenate([key_rows, key_rows, ones], axis=1)
    values_ref[...] = jnp.concatenate([value_rows, ones[:, :HDIM]], axis=1)


def project(tokens, weights, cosine, sine, block=512):
    length, width = tokens.shape
    return pl.pallas_call(
        project_kernel,
        name="project",
        grid=(length // block,),
        in_specs=[
            pl.BlockSpec((block, width), lambda i: (i, 0)),
            pl.BlockSpec(weights.shape, lambda i: (0, 0, 0)),
            pl.BlockSpec((HDIM // 2, block), lambda i: (0, i)),
            pl.BlockSpec((HDIM // 2, block), lambda i: (0, i)),
        ],
        out_specs=[
            pl.BlockSpec((block, width), lambda i: (i, 0)),
            pl.BlockSpec((3 * HDIM, block), lambda i: (0, i)),
            pl.BlockSpec((block, 256), lambda i: (i, 0)),
            pl.BlockSpec((block, 128), lambda i: (i, 0)),
        ],
        out_shape=[
            jax.ShapeDtypeStruct((length, width), bf16),
            jax.ShapeDtypeStruct((3 * HDIM, length), bf16),
            jax.ShapeDtypeStruct((length, 256), bf16),
            jax.ShapeDtypeStruct((length, 128), bf16),
        ],
        scratch_shapes=[pltpu.VMEM((3 * HDIM, width), bf16)],
        compiler_params=pltpu.CompilerParams(vmem_limit_bytes=VMEM),
        cost_estimate=cost(2 * length * width * 4 * HDIM, 22 << 20),
    )(tokens, weights, cosine, sine)


def scaled_queries(queries):
    scaled = queries.astype(f32) * (LOG2E / math.sqrt(HDIM))
    high = scaled.astype(bf16)
    low = (scaled - high.astype(f32)).astype(bf16)
    return high, low


def attend_kernel(keys_ref, q_ref, v_ref, low_ref, out_ref, lse_ref, v_ones, *, part):
    length = keys_ref.shape[0]
    count = length // part

    @pl.when(pl.program_id(0) == 0)
    def _():
        v_ones[:HDIM] = v_ref[...]
        v_ones[HDIM:] = jnp.where(
            lax.broadcasted_iota(jnp.int32, (16, length), 0) < 1, 1.0, 0.0
        ).astype(bf16)

    queries = jnp.concatenate(scaled_queries(q_ref[...]), axis=0)

    def score(at):
        return dot(keys_ref[at * part : (at + 1) * part, : 2 * HDIM], queries)

    scores = score(0)
    highest = total = None
    for at in range(count):
        following = score(at + 1) if at + 1 < count else None
        peak = jnp.max(scores, axis=0, keepdims=True)
        raised = peak if highest is None else jnp.maximum(highest, peak)
        soft = jnp.exp2(scores - raised).astype(bf16)
        added = dot(v_ones[:, at * part : (at + 1) * part], soft)
        total = added if total is None else total * jnp.exp2(highest - raised) + added
        highest = raised
        scores = following
    summed = total[HDIM : HDIM + 1]
    result = total[:HDIM] / summed
    out_ref[...] = result
    lse_ref[...] = highest + jnp.log2(summed)
    step = low_ref.shape[2]
    for at in range(low_ref.shape[0]):
        low_ref[at] = result[:, at * step : (at + 1) * step].astype(bf16)


def attend(keys, qkv, chips, block=1024, part=512):
    length = keys.shape[0]
    return pl.pallas_call(
        functools.partial(attend_kernel, part=part),
        name="attend",
        grid=(length // block,),
        in_specs=[
            pl.BlockSpec(keys.shape, lambda i: (0, 0)),
            pl.BlockSpec((HDIM, block), lambda i: (0, i)),
            pl.BlockSpec((HDIM, length), lambda i: (2, 0)),
        ],
        out_specs=[
            pl.BlockSpec((block * chips // length, HDIM, length // chips), lambda i: (i, 0, 0)),
            pl.BlockSpec((HDIM, block), lambda i: (0, i)),
            pl.BlockSpec((1, block), lambda i: (0, i)),
        ],
        out_shape=[
            jax.ShapeDtypeStruct((chips, HDIM, length // chips), bf16),
            jax.ShapeDtypeStruct((HDIM, length), f32),
            jax.ShapeDtypeStruct((1, length), f32),
        ],
        scratch_shapes=[pltpu.VMEM((HDIM + 16, length), bf16)],
        compiler_params=pltpu.CompilerParams(vmem_limit_bytes=VMEM),
        cost_estimate=cost(2 * 4 * 2 * length * length * HDIM, 6 << 20),
    )(keys, qkv, qkv)


def minus_in_three(values):
    rows = values.shape[1]
    at = lax.broadcasted_iota(jnp.int32, (16, rows), 0)
    high = (-values).astype(bf16).astype(f32)
    rest = -values - high
    middle = rest.astype(bf16).astype(f32)
    low = rest - middle
    stacked = jnp.where(at == 0, high, jnp.where(at == 1, middle, jnp.where(at == 2, low, 0.0)))
    return stacked.astype(bf16)


def attend_back_kernel(
    order_ref,
    keys_ref,
    values_ref,
    q_ref,
    k_ref,
    dout_ref,
    out_ref,
    lse_ref,
    cos_ref,
    sin_ref,
    *rest,
    part,
):
    dp_refs, (sums, dq_all) = rest[:-2], rest[-2:]
    half = HDIM // 2
    here = pl.program_id(0)
    length = keys_ref.shape[0]
    block = q_ref.shape[1]
    count = length // part
    factor = HDIM ** (-0.5)

    def turn_back(grads, cosine, sine):
        low = grads.astype(bf16).astype(f32)
        one, two = low[:half], low[half:]
        return jnp.concatenate([one * cosine + two * sine, two * cosine - one * sine], axis=0)

    @pl.when(here == 0)
    def _():
        sums[...] = jnp.zeros_like(sums)

    low_queries = q_ref[...]
    high, low = scaled_queries(low_queries)
    queries = jnp.concatenate([high, low, minus_in_three(lse_ref[...])], axis=0)
    low_dout = dout_ref[0]
    dout = low_dout.astype(f32)
    centre = jnp.sum(dout * out_ref[...], axis=0, keepdims=True)
    douts = jnp.concatenate([low_dout, minus_in_three(centre)], axis=0)
    blank = jnp.zeros((block, HDIM), bf16)
    right = jnp.concatenate(
        [
            jnp.concatenate([low_queries.astype(f32).T.astype(bf16), blank], axis=1),
            jnp.concatenate([blank, dout.T.astype(bf16)], axis=1),
        ],
        axis=0,
    )

    def score(at):
        rows = slice(at * part, (at + 1) * part)
        return (
            dot(keys_ref[rows, : 2 * HDIM + 16], queries),
            dot(values_ref[rows, : HDIM + 16], douts),
        )

    now = score(0)
    grad_queries = None
    for at in range(count):
        following = score(at + 1) if at + 1 < count else None
        rows = slice(at * part, (at + 1) * part)
        soft = jnp.exp2(now[0])
        grads = (soft * now[1]).astype(bf16)
        added = dot(k_ref[:, rows], grads)
        grad_queries = added if grad_queries is None else grad_queries + added
        sums[rows] += dot(jnp.concatenate([grads, soft.astype(bf16)], axis=1), right)
        now = following

    def columns_of(place):
        return pl.ds(pl.multiple_of(order_ref[place] * block, block), block)

    columns = columns_of(here)
    dq_all[here] = turn_back(
        grad_queries * factor, cos_ref[:, columns], sin_ref[:, columns]
    ).astype(bf16)

    @pl.when(here == length // block - 1)
    def _():
        for place, dp_ref in enumerate(dp_refs):
            columns = columns_of(place)
            both = sums[columns].T
            dp_ref[:HDIM] = dq_all[place]
            dp_ref[HDIM : 2 * HDIM] = turn_back(
                both[:HDIM] * factor, cos_ref[:, columns], sin_ref[:, columns]
            ).astype(bf16)
            dp_ref[2 * HDIM :] = both[HDIM:].astype(bf16)


def attend_back(order, keys, values, qkv, douts, out, lse, cosine, sine, part=256):
    length = keys.shape[0]
    chips, _, block = douts.shape
    scores = length * length

    def whole(array):
        return pl.BlockSpec(array.shape, lambda i, order: (0, 0))

    return pl.pallas_call(
        functools.partial(attend_back_kernel, part=part),
        name="attend_back",
        grid_spec=pltpu.PrefetchScalarGridSpec(
            num_scalar_prefetch=1,
            grid=(chips,),
            in_specs=[
                whole(keys),
                whole(values),
                pl.BlockSpec((HDIM, block), lambda i, order: (0, order[i])),
                pl.BlockSpec((HDIM, length), lambda i, order: (1, 0)),
                pl.BlockSpec((1, HDIM, block), lambda i, order: (order[i], 0, 0)),
                pl.BlockSpec((HDIM, block), lambda i, order: (0, order[i])),
                pl.BlockSpec((1, block), lambda i, order: (0, order[i])),
                whole(cosine),
                whole(sine),
            ],
            out_specs=[pl.BlockSpec((3 * HDIM, block), lambda i, order: (0, 0))] * chips,
            scratch_shapes=[
                pltpu.VMEM((length, 2 * HDIM), f32),
                pltpu.VMEM((chips, HDIM, block), bf16),
            ],
        ),
        out_shape=[jax.ShapeDtypeStruct((3 * HDIM, block), bf16)] * chips,
        compiler_params=pltpu.CompilerParams(vmem_limit_bytes=VMEM),
        cost_estimate=cost(5 * 4 * 2 * scores * HDIM, 8 << 20),
    )(order, keys, values, qkv, qkv, douts, out, lse, cosine, sine)


def feed_kernel(
    x_ref, ours_ref, theirs_ref, g_ref, gate_ref, up_ref, out_ref, rest_ref,
    residual_ref, partial_ref, back_ref, grads_ref,
    unit, unit_t, g_t, sum_out, sum_back,
):
    here = pl.program_id(0)
    last = pl.num_programs(0) - 1
    width = x_ref.shape[1]
    step = gate_ref.shape[1]

    def bend(gate, upward):
        cdf = 0.5 + 0.5 * lax.erf(gate * math.sqrt(0.5))
        slope = cdf + gate * jnp.exp(gate * gate * -0.5) * (1.0 / math.sqrt(2.0 * math.pi))
        bent = gate * cdf
        return bent, slope, (bent * upward).astype(bf16)

    @pl.when(here == 0)
    def _():
        residual = (
            x_ref[...].astype(f32) + ours_ref[...].astype(f32) + theirs_ref[...].astype(f32)
        )
        residual_ref[...] = residual
        normed = unit_rows(residual)[0]
        unit[...] = normed.astype(bf16)
        unit_t[...] = normed.T.astype(bf16)
        g_t[...] = g_ref[...].astype(f32).T.astype(bf16)
        few = rest_ref.shape[1] // 4
        both = dot(unit[...], rest_ref[...])
        grad = dot(g_ref[...], rest_ref[...])[:, 2 * few : 3 * few]
        bent, slope, active = bend(both[:, :few], both[:, few : 2 * few])
        grad_gate = (grad * both[:, few : 2 * few] * slope).astype(bf16)
        grad_up = (grad * bent).astype(bf16)
        blank = jnp.zeros_like(active)
        outs = jnp.concatenate([blank, blank, active, blank], axis=1)
        ins = jnp.concatenate([grad_gate, grad_up, blank, blank], axis=1)
        sum_out[...] = dot(outs, rest_ref[...], 1, 1)
        sum_back[...] = dot(ins, rest_ref[...], 1, 1)
        grads_ref[:, grads_ref.shape[1] - 4 * few :] = (
            dot(unit_t[...], ins) + dot(g_t[...], outs)
        ).astype(bf16)

    gate = dot(unit[...], gate_ref[...])
    upward = dot(unit[...], up_ref[...])
    grad = dot(g_ref[...], out_ref[...])
    bent, slope, active = bend(gate, upward)
    grad_gate = (grad * upward * slope).astype(bf16)
    grad_up = (grad * bent).astype(bf16)
    sum_out[...] += dot(active, out_ref[...], 1, 1)
    sum_back[...] += dot(grad_gate, gate_ref[...], 1, 1) + dot(grad_up, up_ref[...], 1, 1)
    start = width // 2
    count = grads_ref.shape[1] // step // 3
    for at, grads in enumerate(
        (dot(unit_t[...], grad_gate), dot(unit_t[...], grad_up), dot(g_t[...], active))
    ):
        place = pl.multiple_of(start + at * count * step + here * step, 128)
        grads_ref[:, pl.ds(place, step)] = grads.astype(bf16)

    @pl.when(here == last)
    def _():
        partial_ref[...] = sum_out[...].astype(bf16)
        back_ref[...] = sum_back[...].astype(bf16)


def feed(x, ours, theirs, g, first, second, step=256):
    tokens, width = x.shape
    columns = first.shape[1] + second.shape[1]
    start = width // 2 // step
    count = (first.shape[1] - width // 2) // step
    rest = second.shape[1] - 2 * count * step

    def whole(array):
        return pl.BlockSpec(array.shape, lambda i: (0, 0))

    pair = jax.ShapeDtypeStruct((tokens, width), bf16)
    return pl.pallas_call(
        feed_kernel,
        name="feed",
        grid=(count,),
        in_specs=[
            whole(x),
            whole(ours),
            whole(theirs),
            whole(g),
            pl.BlockSpec((width, step), lambda i: (0, start + i)),
            pl.BlockSpec((width, step), lambda i: (0, i)),
            pl.BlockSpec((width, step), lambda i: (0, count + i)),
            pl.BlockSpec((width, rest), lambda i: (0, 2 * count * step // rest)),
        ],
        out_specs=[
            whole(x),
            whole(x),
            whole(x),
            pl.BlockSpec((width, columns), lambda i: (0, 0)),
        ],
        out_shape=[
            jax.ShapeDtypeStruct((tokens, width), f32),
            pair,
            pair,
            jax.ShapeDtypeStruct((width, columns), bf16),
        ],
        scratch_shapes=[
            pltpu.VMEM((tokens, width), bf16),
            pltpu.VMEM((width, tokens), bf16),
            pltpu.VMEM((width, tokens), bf16),
            pltpu.VMEM((tokens, width), f32),
            pltpu.VMEM((tokens, width), f32),
        ],
        compiler_params=pltpu.CompilerParams(vmem_limit_bytes=VMEM),
        cost_estimate=cost(2 * 9 * 2 * tokens * width * count * step, 24 << 20),
    )(x, ours, theirs, g, first, second, second, second)


def middle_back_kernel(
    core_ref, residual_ref, g_ref, ours_ref, theirs_ref, attn_ref, attended_ref,
    out_ours_ref, out_theirs_ref, grads_in_ref,
    layer_ref, residual_grad_ref, dout_ref, grads_ref,
):
    rows = layer_ref.shape[0]
    half = attn_ref.shape[1]
    own = pl.ds(pl.multiple_of(core_ref[0] * rows, rows), rows)
    layer_ref[...] = (
        residual_ref[own, :]
        + out_ours_ref[own, :].astype(f32)
        + out_theirs_ref[...].astype(f32)
    ).astype(bf16)
    unit, inverse = unit_rows(residual_ref[...])
    scaled = ours_ref[...].astype(f32) + theirs_ref[...].astype(f32)
    grad = g_ref[...].astype(f32) + unit_back(scaled, unit, inverse)
    dout_scratch = grad.astype(bf16)
    residual_grad_ref[...] = grad
    left = jnp.concatenate(
        [attn_ref[at * 128 : at * 128 + HDIM] for at in range(attn_ref.shape[0] // 128)], axis=0
    )
    right = jnp.concatenate(
        [attn_ref[at * 128 + HDIM : at * 128 + 128] for at in range(attn_ref.shape[0] // 128)],
        axis=0,
    )
    dout = dot(left, dout_scratch[:, :half], 1, 1) + dot(right, dout_scratch[:, half:], 1, 1)
    for at in range(dout_ref.shape[0]):
        dout_ref[at] = dout[at * HDIM : (at + 1) * HDIM].astype(bf16)
    grads = dot(attended_ref[...], dout_scratch)
    few = grads.shape[0] // 8
    stacked = jnp.stack(
        [grads[:, :half].reshape(few, 8, half), grads[:, half:].reshape(few, 8, half)], axis=1
    )
    grads_ref[...] = stacked.reshape(2 * grads.shape[0], half).astype(bf16)


def middle_back(core, residual, g, ours, theirs, attn, attended, out_ours, out_theirs, grads):
    tokens, width = residual.shape
    rows = tokens // 2
    chips = width // 2 // HDIM
    half = width // 2

    def whole(*shape):
        return pl.BlockSpec(shape, lambda i, core: (0,) * len(shape))

    return pl.pallas_call(
        middle_back_kernel,
        name="middle_back",
        grid_spec=pltpu.PrefetchScalarGridSpec(
            num_scalar_prefetch=1,
            grid=(1,),
            in_specs=[whole(tokens, width)] * 4
            + [whole(width, half), whole(half, tokens), whole(tokens, width), whole(rows, width)]
            + [pl.BlockSpec(memory_space=pl.ANY)],
            out_specs=[
                whole(rows, width),
                whole(tokens, width),
                whole(chips, HDIM, tokens),
                whole(width, half),
            ],
        ),
        out_shape=[
            jax.ShapeDtypeStruct((rows, width), bf16),
            jax.ShapeDtypeStruct((tokens, width), f32),
            jax.ShapeDtypeStruct((chips, HDIM, tokens), bf16),
            jax.ShapeDtypeStruct(grads.shape, bf16),
        ],
        input_output_aliases={9: 3},
        compiler_params=pltpu.CompilerParams(vmem_limit_bytes=VMEM),
        cost_estimate=cost(2 * 2 * 2 * tokens * width * half, 16 << 20),
    )(core, residual, g, ours, theirs, attn, attended, out_ours, out_theirs, grads)


def hidden_back_kernel(order_ref, core_ref, w_ref, *rest):
    dp_refs, (own_ref, other_ref, stacked) = rest[:-3], rest[-3:]
    for place, dp_ref in enumerate(dp_refs):
        size = dp_ref.shape[0]
        stacked[pl.ds(pl.multiple_of(order_ref[place] * size, 64), size)] = dp_ref[...]
    rows = own_ref.shape[0]
    flat = dot(w_ref[...], stacked[...])
    first = flat[:, :rows].T
    second = flat[:, rows:].T
    zero = core_ref[0] == 0
    own_ref[...] = jnp.where(zero, first, second)
    other_ref[...] = jnp.where(zero, second, first).astype(bf16)


def hidden_back(order, core, weights, pieces):
    width, columns = weights.shape
    rows = pieces[0].shape[1] // 2

    def whole(*shape):
        return pl.BlockSpec(shape, lambda i, order, core: (0,) * len(shape))

    return pl.pallas_call(
        hidden_back_kernel,
        name="hidden_back",
        grid_spec=pltpu.PrefetchScalarGridSpec(
            num_scalar_prefetch=2,
            grid=(1,),
            in_specs=[whole(width, columns)] + [whole(*pieces[0].shape)] * len(pieces),
            out_specs=[whole(rows, width)] * 2,
            scratch_shapes=[pltpu.VMEM((columns, 2 * rows), bf16)],
        ),
        out_shape=[
            jax.ShapeDtypeStruct((rows, width), f32),
            jax.ShapeDtypeStruct((rows, width), bf16),
        ],
        compiler_params=pltpu.CompilerParams(vmem_limit_bytes=VMEM),
        cost_estimate=cost(2 * 2 * 2 * rows * width * columns, 8 << 20),
    )(order, core, weights, *pieces)


def head_grad_kernel(order_ref, unit_ref, *rest):
    dp_refs, out_ref = rest[:-1], rest[-1]
    block = dp_refs[0].shape[1]
    total = None
    for place, dp_ref in enumerate(dp_refs):
        rows = pl.ds(pl.multiple_of(order_ref[place] * block, block), block)
        added = dot(dp_ref[...], unit_ref[rows])
        total = added if total is None else total + added
    for at in range(out_ref.shape[0]):
        out_ref[at] = total[:, at * 128 : (at + 1) * 128].astype(bf16)


def head_grad(order, unit_all, pieces):
    length, width = unit_all.shape
    owners = width // 128
    size = pieces[0].shape[0]

    def whole(*shape):
        return pl.BlockSpec(shape, lambda i, order: (0,) * len(shape))

    return pl.pallas_call(
        head_grad_kernel,
        name="head_grad",
        grid_spec=pltpu.PrefetchScalarGridSpec(
            num_scalar_prefetch=1,
            grid=(1,),
            in_specs=[whole(length, width)] + [whole(*pieces[0].shape)] * len(pieces),
            out_specs=whole(owners, size, 128),
        ),
        out_shape=jax.ShapeDtypeStruct((owners, size, 128), bf16),
        compiler_params=pltpu.CompilerParams(vmem_limit_bytes=VMEM),
        cost_estimate=cost(2 * 2 * length * width * size, 10 << 20),
    )(order, unit_all, *pieces)


def adam(weight, gradient, first, second, rate):
    first = BETA_FIRST * first + (1.0 - BETA_FIRST) * gradient
    second = BETA_SECOND * second + (1.0 - BETA_SECOND) * gradient * gradient
    first_hat = first / (1.0 - BETA_FIRST**STEP)
    second_hat = second / (1.0 - BETA_SECOND**STEP)
    weight = weight - rate * (first_hat / (jnp.sqrt(second_hat) + EPSILON) + DECAY * weight)
    return (weight, first, second)


def adam_into(refs, weight, gradient, first, second, rate):
    for ref, value in zip(refs, adam(weight, gradient, first, second, rate)):
        ref[...] = value


def rounded_in_kernel(values):
    return values.astype(bf16).astype(f32)


def adam_in_kernel(
    grads_ref, gain_ref, w_ref, m_ref, v_ref, new_w, new_m, new_v, gain_grad, *, rate
):
    width = m_ref.shape[1] // 2
    main = width // 256 * 128
    few = width // 2 - main
    start = grads_ref.shape[2] - 3 * main - 128
    columns = []
    for at in range(2):
        for core in range(2):
            place = start + at * main
            columns.append(grads_ref[core, :, place : place + main].astype(f32))
        for core in range(2):
            rest = grads_ref[core, :, start + 3 * main :].astype(f32)
            columns.append(rest[:, at * few : (at + 1) * few])
    grads = jnp.concatenate(columns, axis=1)
    weight = w_ref[...]
    gain_grad[...] = jnp.sum(grads * rounded_in_kernel(weight), axis=1, keepdims=True)
    adam_into(
        (new_w, new_m, new_v), weight, grads * gain_ref[...], m_ref[...], v_ref[...], rate
    )


def adam_in(grads, gain, weight, first, second, rate):
    rows, columns = weight.shape
    steps = grads.shape[0] // 2
    block = pl.BlockSpec((rows // steps, columns), lambda i: (i, 0))
    column = pl.BlockSpec((rows // steps, 1), lambda i: (i, 0))
    same = jax.ShapeDtypeStruct((rows, columns), f32)
    return pl.pallas_call(
        functools.partial(adam_in_kernel, rate=rate),
        name="adam_in",
        grid=(steps,),
        in_specs=[pl.BlockSpec((2,) + grads.shape[1:], lambda i: (i, 0, 0)), column]
        + [block] * 3,
        out_specs=[block] * 3 + [column],
        out_shape=[same] * 3 + [jax.ShapeDtypeStruct((rows, 1), f32)],
        compiler_params=pltpu.CompilerParams(vmem_limit_bytes=VMEM),
        cost_estimate=cost(rows * columns * 20, rows * columns * 26),
    )(grads, gain, weight, first, second)


def adam_rest_kernel(grads_ref, *refs, rates):
    attn, out, new_attn, new_out = refs[:3], refs[3:6], refs[6:9], refs[9:]
    chips = grads_ref.shape[0] // 2
    hidden = out[0].shape[0]
    main = hidden // 256 * 128
    few = hidden // 2 - main
    half = attn[0].shape[1] // 2
    pieces = []
    for core in range(2):
        for chip in range(chips):
            piece = grads_ref[2 * chip + core, :, :half].astype(f32)
            pieces.append(jnp.concatenate([piece[:8], piece[8:]], axis=1))
    grads = jnp.concatenate(pieces, axis=0)
    adam_into(new_attn, attn[0][...], grads, attn[1][...], attn[2][...], rates[0])
    place = grads_ref.shape[2] - main - 128
    for core in range(2):
        columns = jnp.concatenate(
            [grads_ref[2 * chip + core, :, place : place + main] for chip in range(chips)], axis=0
        )
        rest = jnp.concatenate(
            [grads_ref[2 * chip + core, :, place + main :] for chip in range(chips)], axis=0
        )
        for rows, grads in (
            (slice(core * main, (core + 1) * main), columns.astype(f32).T),
            (
                slice(2 * main + core * few, 2 * main + (core + 1) * few),
                rest.astype(f32).T[2 * few : 3 * few],
            ),
        ):
            new = adam(out[0][rows], grads, out[1][rows], out[2][rows], rates[1])
            for ref, value in zip(new_out, new):
                ref[rows] = value


def adam_rest(grads, attn, out, rates):
    def whole(array):
        return pl.BlockSpec(array.shape, lambda i: (0,) * array.ndim)

    arrays = (*attn, *out)
    return pl.pallas_call(
        functools.partial(adam_rest_kernel, rates=rates),
        name="adam_rest",
        grid=(1,),
        in_specs=[whole(array) for array in (grads, *arrays)],
        out_specs=[whole(array) for array in arrays],
        out_shape=[jax.ShapeDtypeStruct(array.shape, f32) for array in arrays],
        compiler_params=pltpu.CompilerParams(vmem_limit_bytes=VMEM),
        cost_estimate=cost(attn[0].size * 60, 14 << 20),
    )(grads, *arrays)


def adam_qkv_kernel(
    grads_ref, gain_ref, w_ref, m_ref, v_ref, new_w, new_m, new_v, gain_grad, *, rate
):
    here = pl.program_id(0)
    rows = pl.ds(pl.multiple_of(here * HDIM, HDIM), HDIM)
    grads = jnp.concatenate([grads_ref[head, rows] for head in range(grads_ref.shape[0])], axis=0)
    grads = grads.astype(f32).T
    weight = w_ref[...]
    added = jnp.sum(grads * rounded_in_kernel(weight), axis=1, keepdims=True)
    gain_grad[...] = added + jnp.where(here == 0, 0.0, gain_grad[...])
    adam_into(
        (new_w, new_m, new_v), weight, grads * gain_ref[...], m_ref[...], v_ref[...], rate
    )


def adam_qkv(grads, gain, weight, first, second, rate):
    rows, columns = weight.shape
    block = pl.BlockSpec((rows, columns // 3), lambda i: (0, i))
    column = pl.BlockSpec((rows, 1), lambda i: (0, 0))
    same = jax.ShapeDtypeStruct((rows, columns), f32)
    return pl.pallas_call(
        functools.partial(adam_qkv_kernel, rate=rate),
        name="adam_qkv",
        grid=(3,),
        in_specs=[pl.BlockSpec(grads.shape, lambda i: (0, 0, 0)), column] + [block] * 3,
        out_specs=[block] * 3 + [column],
        out_shape=[same] * 3 + [jax.ShapeDtypeStruct((rows, 1), f32)],
        compiler_params=pltpu.CompilerParams(vmem_limit_bytes=VMEM),
        cost_estimate=cost(rows * columns * 20, rows * columns * 26),
    )(grads, gain, weight, first, second)


def ring(axis, shift):
    size = lax.axis_size(axis)
    return [(at, (at + shift) % size) for at in range(size)]


def gather_rows(planes_first, lines_first):
    plane, line = lax.axis_index("zh"), lax.axis_index("y")
    lines = lax.axis_size("y")

    def join(pieces):
        rows = pieces[0][2].shape[0]
        total = jnp.zeros((2 * lines * rows, pieces[0][2].shape[1]), bf16)
        for far, shift, piece in pieces:
            place = (plane ^ far) * lines + (line - shift) % lines
            total = lax.dynamic_update_slice_in_dim(total, piece, place * rows, 0)
        return total

    swapped = lax.ppermute(planes_first, "zh", SWAP)
    others = [lax.ppermute(lines_first, "y", ring("y", shift)) for shift in range(1, lines)]
    second = [(0, 0, lines_first)] + [(0, 1 + at, piece) for at, piece in enumerate(others)]
    second += [(1, shift, lax.ppermute(piece, "zh", SWAP)) for _, shift, piece in second]
    first = [(0, 0, planes_first), (1, 0, swapped)]
    first += [
        (far, shift, lax.ppermute(piece, "y", ring("y", shift)))
        for shift in range(1, lines)
        for far, piece in ((1, swapped), (0, planes_first))
    ]
    return join(first), join(second)


def shards(
    tokens,
    positions,
    cotangent,
    weight_qkv,
    weight_attn,
    weight_in,
    weight_out,
    norm_gains,
    first_qkv,
    first_attn,
    first_in,
    first_out,
    first_gains,
    second_qkv,
    second_attn,
    second_in,
    second_out,
    second_gains,
):
    rows, width = tokens.shape[1:]
    shard_rows = weight_qkv.shape[1]
    heads = width // HDIM
    hidden = weight_out.shape[1]
    core = lax.axis_index("c")
    mine = lax.axis_index(CTX)
    chip = lax.axis_index(CHIPS)
    chips = lax.axis_size(CHIPS)
    owners = lax.axis_size(FSDP)
    length = rows * chips * 2
    main = hidden // 256 * 128
    few = hidden // 2 - main
    core_at = core.reshape(1).astype(jnp.int32)
    offsets = [(far, near) for far in range(lax.axis_size("x")) for near in range(2)]
    across, beside = lax.axis_index("x"), lax.axis_index("zl")
    wide = lax.axis_size("x")

    def chips_at(sign):
        places = [(across + sign * far) % wide * 2 + (beside ^ near) for far, near in offsets]
        return jnp.stack(places).astype(jnp.int32)

    local = tokens[0]
    sequence = lax.all_gather(local, CTX, axis=0, tiled=True)
    gains = norm_gains[0].astype(bf16).astype(f32)

    low_in = (weight_in[0].astype(bf16).astype(f32) * gains[1][:, None]).astype(bf16)
    low_out_w = weight_out[0].astype(bf16)
    attn_rows = lax.dynamic_slice_in_dim(weight_attn[0].astype(bf16), core * HDIM, HDIM, 0)

    def columns(array, start, size, dim=1):
        return lax.dynamic_slice_in_dim(array, start + core * size, size, dim)

    first_part = jnp.concatenate(
        [
            jnp.concatenate([attn_rows[:, : width // 2], attn_rows[:, width // 2 :]], axis=0),
            columns(low_in, 0, main),
        ],
        axis=1,
    )
    second_part = jnp.concatenate(
        [
            columns(low_in, hidden, main),
            columns(low_out_w, 0, main, 0).T,
            columns(low_in, 2 * main, few),
            columns(low_in, hidden + 2 * main, few),
            columns(low_out_w, 2 * main, few, 0).T,
            jnp.zeros((shard_rows, few), bf16),
        ],
        axis=1,
    )
    mat_first, mat_second = gather_rows(first_part, second_part)
    mat_attn = mat_first[:, : width // 2].reshape(owners, 2, HDIM, width // 2)
    mat_attn = mat_attn.transpose(0, 2, 1, 3).reshape(owners * HDIM, width)

    low_qkv = (weight_qkv[0].astype(bf16).astype(f32) * gains[0][:, None]).astype(bf16)
    own_head = lax.dynamic_index_in_dim(
        low_qkv.reshape(shard_rows, 3, heads, HDIM), mine, 2, keepdims=False
    )
    head_columns = own_head.reshape(shard_rows, 3 * HDIM).T
    head_weights = lax.all_to_all(
        jnp.broadcast_to(head_columns, (owners, *head_columns.shape)), FSDP, 0, 0, tiled=True
    )
    places = lax.all_gather(positions[0], CTX, axis=0, tiled=True)

    by_head = low_qkv.reshape(shard_rows, 3, heads // 2, 2, HDIM)
    half_heads = lax.dynamic_index_in_dim(by_head, core, 3, keepdims=False)
    half_heads = half_heads.transpose(0, 2, 1, 3).reshape(shard_rows, 3 * width // 2)
    half_heads, sequence = lax.optimization_barrier((half_heads, sequence))
    mat_qkv = lax.all_gather(half_heads, FSDP, axis=0, tiled=True)

    def in_order(ours, theirs):
        first = jnp.where(core == 0, ours, theirs)
        second = jnp.where(core == 0, theirs, ours)
        return jnp.concatenate([first, second], axis=0)

    def swap(array):
        return lax.ppermute(array, "c", SWAP)

    gradient = in_order(cotangent[0], swap(cotangent[0]))

    freqs = jnp.exp(jnp.arange(HDIM // 2, dtype=f32) * (-2.0 * math.log(ROPE_BASE) / HDIM))
    angles = freqs[:, None] * places.astype(f32)[None, :]
    cosine = jnp.cos(angles)
    sine = jnp.sin(angles)
    unit_all, qkv, keys, values = project(sequence, head_weights, cosine, sine)
    low_out, out, lse = attend(keys, qkv, chips)
    attended = lax.all_to_all(low_out, CHIPS, 0, 0, tiled=True)
    attended = attended.reshape(heads // 2 * HDIM, 2 * rows)
    mixed = dot(attended, mat_attn, 0, 0).astype(bf16)
    current = lax.dynamic_slice_in_dim(sequence, chip * 2 * rows, 2 * rows, 0)
    residual, partial, back, grads = feed(
        current, mixed, swap(mixed), gradient, mat_first, mat_second
    )
    theirs = swap(lax.dynamic_slice_in_dim(partial, (1 - core) * rows, rows, 0))
    layer_out, residual_grad, dout_pair, grads = middle_back(
        core_at, residual, gradient, back, swap(back), mat_first, attended, partial, theirs, grads
    )

    douts = lax.all_to_all(dout_pair, CHIPS, 0, 0, tiled=True)
    grads, douts = lax.optimization_barrier((grads, douts))
    arrived = lax.all_to_all(grads, FSDP + CHIPS, 0, 0, tiled=True)
    arrived = arrived.reshape(owners * chips, shard_rows // chips, -1)
    summed = jnp.sum(arrived.astype(f32), axis=0).astype(bf16)
    all_grads = lax.all_gather(summed, CTX, axis=0, tiled=False)

    order = chips_at(1)
    pieces = attend_back(order, keys, values, qkv, douts, out, lse, cosine, sine)
    moved = [pieces[0]]
    for (far, near), piece in list(zip(offsets, pieces))[1:]:
        pairs = [
            (at, (at // 2 + far) % wide * 2 + (at % 2 ^ near)) for at in range(chips)
        ]
        moved.append(lax.ppermute(piece, CHIPS, pairs))
    own_hidden, other_hidden = hidden_back(chips_at(-1), core_at, mat_qkv, moved)
    grad_hidden = own_hidden + swap(other_hidden).astype(f32)
    unit_in, scale_in = unit_rows(local.astype(f32))
    own_residual = lax.dynamic_slice_in_dim(residual_grad, core * rows, rows, 0)
    tokens_grad = (own_residual + unit_back(grad_hidden, unit_in, scale_in))[None]

    head_sums = lax.all_to_all(head_grad(order, unit_all, pieces), FSDP, 0, 0, tiled=True)
    head_own = jnp.sum(head_sums.astype(f32), axis=0).astype(bf16)
    head_grads = lax.all_gather(head_own, CTX, axis=0, tiled=False)

    rates = (
        width ** (-0.5),
        max(1, 3 * width // length) ** (-0.5),
        width ** (-0.5),
        hidden ** (-0.5),
    )
    columns_of_gains = gains.T
    *new_in, gain_second = adam_in(
        all_grads, columns_of_gains[:, 1:], weight_in[0], first_in[0], second_in[0], rates[2]
    )
    rest = adam_rest(
        all_grads,
        (weight_attn[0], first_attn[0], second_attn[0]),
        (weight_out[0], first_out[0], second_out[0]),
        (rates[1], rates[3]),
    )
    *new_qkv, gain_first = adam_qkv(
        head_grads, columns_of_gains[:, :1], weight_qkv[0], first_qkv[0], second_qkv[0], rates[0]
    )
    gain_grads = jnp.concatenate([gain_first, gain_second], axis=1).T
    new_gains = adam(norm_gains[0], gain_grads, first_gains[0], second_gains[0], GAIN_RATE)
    updated = (new_qkv, rest[:3], new_in, rest[3:], new_gains)
    return (
        layer_out[None],
        tokens_grad,
        *[updated[member][0][None] for member in range(5)],
        *[updated[member][1][None] for member in range(5)],
        *[updated[member][2][None] for member in range(5)],
    )


def solution(mesh):
    split = Mesh(mesh.devices.reshape(4, 2, 2, 2, 4), ("x", "zl", "c", "zh", "y"))
    by_row = P(None, FSDP, None)
    by_column = P(None, None, FSDP)
    weights = (by_row, by_row, by_row, by_column, by_column)
    by_token = P(FSDP, CTX, None)
    return jax.shard_map(
        shards,
        mesh=split,
        in_specs=(by_token, P(FSDP, CTX), by_token) + weights * 3,
        out_specs=(by_token, by_token) + weights * 3,
        check_vma=False,
    )
```

```python
import functools
import math

import jax
import jax.numpy as jnp
from jax import lax
from jax.experimental import pallas as pl
from jax.experimental.pallas import tpu as pltpu
from jax.sharding import Mesh, PartitionSpec as P

HDIM = 64
STEP = 10
BETA_FIRST = 0.5
BETA_SECOND = 0.5
EPSILON = 1e-08
DECAY = 0.01
NORM_EPS = 1e-05
ROPE_BASE = 160000.0
GAIN_RATE = 0.6
LOG2E = math.log2(math.e)
f32 = jnp.float32
bf16 = jnp.bfloat16

CHIPS = ("x", "zl")
CTX = ("x", "zl", "c")
FSDP = ("zh", "y")
SWAP = [(0, 1), (1, 0)]
VMEM = 60 << 20


def dot(left, right, left_dim=1, right_dim=0):
    return lax.dot_general(
        left, right, (((left_dim,), (right_dim,)), ((), ())), preferred_element_type=f32
    )


def cost(flops, moved):
    return pl.CostEstimate(flops=flops, bytes_accessed=moved, transcendentals=0)


def unit_rows(values):
    average = jnp.mean(values, axis=-1, keepdims=True)
    centered = values - average
    spread = jnp.mean(centered * centered, axis=-1, keepdims=True)
    inverse = lax.rsqrt(spread + NORM_EPS)
    return centered * inverse, inverse


def unit_back(scaled, unit, inverse):
    first_mean = jnp.mean(scaled, axis=-1, keepdims=True)
    second_mean = jnp.mean(scaled * unit, axis=-1, keepdims=True)
    return inverse * (scaled - first_mean - unit * second_mean)


def project_kernel(x_ref, w_ref, cos_ref, sin_ref, unit_ref, qkv_ref, keys_ref, values_ref, w_all):
    half = HDIM // 2
    rows = cos_ref.shape[1]

    @pl.when(pl.program_id(0) == 0)
    def _():
        for part in range(w_ref.shape[0]):
            w_all[:, part * 128 : (part + 1) * 128] = w_ref[part]

    each = rows // 2
    extra = x_ref.shape[0] // 2 - each
    tokens = jnp.concatenate(
        [x_ref[:each].astype(f32), x_ref[each + extra : 2 * each + extra].astype(f32)], axis=0
    )
    unit = unit_rows(tokens)[0].astype(bf16)
    unit_ref[...] = unit
    mixed = dot(w_all[...], unit, 1, 1)
    cosine = cos_ref[...]
    sine = sin_ref[...]

    def turn(one, two):
        return jnp.concatenate([one * cosine - two * sine, two * cosine + one * sine], axis=0)

    queries = turn(mixed[:half], mixed[half:HDIM])
    keys = turn(mixed[HDIM : HDIM + half], mixed[HDIM + half : 2 * HDIM])
    values = mixed[2 * HDIM :]
    qkv_ref[...] = jnp.concatenate([queries, keys, values], axis=0).astype(bf16)
    key_rows = keys.T.astype(bf16)
    value_rows = values.T.astype(bf16)
    ones = jnp.where(lax.broadcasted_iota(jnp.int32, (rows, 128), 1) < 3, 1.0, 0.0).astype(bf16)
    keys_ref[...] = jnp.concatenate([key_rows, key_rows, ones], axis=1)
    values_ref[...] = jnp.concatenate([value_rows, ones[:, :HDIM]], axis=1)


def project(tokens, weights, cosine, sine, block=512):
    width = tokens.shape[1]
    length = cosine.shape[1]
    steps = length // block
    return pl.pallas_call(
        project_kernel,
        name="project",
        grid=(steps,),
        in_specs=[
            pl.BlockSpec((tokens.shape[0] // steps, width), lambda i: (i, 0)),
            pl.BlockSpec(weights.shape, lambda i: (0, 0, 0)),
            pl.BlockSpec((HDIM // 2, block), lambda i: (0, i)),
            pl.BlockSpec((HDIM // 2, block), lambda i: (0, i)),
        ],
        out_specs=[
            pl.BlockSpec((block, width), lambda i: (i, 0)),
            pl.BlockSpec((3 * HDIM, block), lambda i: (0, i)),
            pl.BlockSpec((block, 256), lambda i: (i, 0)),
            pl.BlockSpec((block, 128), lambda i: (i, 0)),
        ],
        out_shape=[
            jax.ShapeDtypeStruct((length, width), bf16),
            jax.ShapeDtypeStruct((3 * HDIM, length), bf16),
            jax.ShapeDtypeStruct((length, 256), bf16),
            jax.ShapeDtypeStruct((length, 128), bf16),
        ],
        scratch_shapes=[pltpu.VMEM((3 * HDIM, width), bf16)],
        compiler_params=pltpu.CompilerParams(vmem_limit_bytes=VMEM),
        cost_estimate=cost(2 * length * width * 4 * HDIM, 22 << 20),
    )(tokens, weights, cosine, sine)


def scaled_queries(queries):
    scaled = queries.astype(f32) * (LOG2E / math.sqrt(HDIM))
    high = scaled.astype(bf16)
    low = (scaled - high.astype(f32)).astype(bf16)
    return high, low


def attend_kernel(keys_ref, q_ref, v_ref, low_ref, out_ref, lse_ref, v_ones, *, part):
    length = keys_ref.shape[0]
    count = length // part

    @pl.when(pl.program_id(0) == 0)
    def _():
        v_ones[:HDIM] = v_ref[...]
        v_ones[HDIM:] = jnp.where(
            lax.broadcasted_iota(jnp.int32, (16, length), 0) < 1, 1.0, 0.0
        ).astype(bf16)

    queries = jnp.concatenate(scaled_queries(q_ref[...]), axis=0)

    def score(at):
        return dot(keys_ref[at * part : (at + 1) * part, : 2 * HDIM], queries)

    scores = score(0)
    highest = total = None
    for at in range(count):
        following = score(at + 1) if at + 1 < count else None
        peak = jnp.max(scores, axis=0, keepdims=True)
        raised = peak if highest is None else jnp.maximum(highest, peak)
        soft = jnp.exp2(scores - raised).astype(bf16)
        added = dot(v_ones[:, at * part : (at + 1) * part], soft)
        total = added if total is None else total * jnp.exp2(highest - raised) + added
        highest = raised
        scores = following
    summed = total[HDIM : HDIM + 1]
    result = total[:HDIM] / summed
    out_ref[...] = result
    lse_ref[...] = highest + jnp.log2(summed)
    step = low_ref.shape[2]
    for at in range(low_ref.shape[0]):
        low_ref[at] = result[:, at * step : (at + 1) * step].astype(bf16)


def attend(keys, qkv, chips, block=1024, part=512):
    length = keys.shape[0]
    return pl.pallas_call(
        functools.partial(attend_kernel, part=part),
        name="attend",
        grid=(length // block,),
        in_specs=[
            pl.BlockSpec(keys.shape, lambda i: (0, 0)),
            pl.BlockSpec((HDIM, block), lambda i: (0, i)),
            pl.BlockSpec((HDIM, length), lambda i: (2, 0)),
        ],
        out_specs=[
            pl.BlockSpec((block * chips // length, HDIM, length // chips), lambda i: (i, 0, 0)),
            pl.BlockSpec((HDIM, block), lambda i: (0, i)),
            pl.BlockSpec((1, block), lambda i: (0, i)),
        ],
        out_shape=[
            jax.ShapeDtypeStruct((chips, HDIM, length // chips), bf16),
            jax.ShapeDtypeStruct((HDIM, length), f32),
            jax.ShapeDtypeStruct((1, length), f32),
        ],
        scratch_shapes=[pltpu.VMEM((HDIM + 16, length), bf16)],
        compiler_params=pltpu.CompilerParams(vmem_limit_bytes=VMEM),
        cost_estimate=cost(2 * 4 * 2 * length * length * HDIM, 6 << 20),
    )(keys, qkv, qkv)


def minus_in_three(values):
    rows = values.shape[1]
    at = lax.broadcasted_iota(jnp.int32, (16, rows), 0)
    high = (-values).astype(bf16).astype(f32)
    rest = -values - high
    middle = rest.astype(bf16).astype(f32)
    low = rest - middle
    stacked = jnp.where(at == 0, high, jnp.where(at == 1, middle, jnp.where(at == 2, low, 0.0)))
    return stacked.astype(bf16)


def attend_back_kernel(
    order_ref,
    keys_ref,
    values_ref,
    q_ref,
    k_ref,
    out_ref,
    lse_ref,
    cos_ref,
    sin_ref,
    *rest,
    part,
):
    count = (len(rest) - 3) // 2
    dout_refs, dp_refs, (sums, dq_all, dout_all) = rest[:count], rest[count:-3], rest[-3:]
    half = HDIM // 2
    here = pl.program_id(0)
    length = keys_ref.shape[0]
    block = q_ref.shape[1]
    count = length // part
    factor = HDIM ** (-0.5)

    def turn_back(grads, cosine, sine):
        low = grads.astype(bf16).astype(f32)
        one, two = low[:half], low[half:]
        return jnp.concatenate([one * cosine + two * sine, two * cosine - one * sine], axis=0)

    @pl.when(here == 0)
    def _():
        sums[...] = jnp.zeros_like(sums)
        for place, dout_ref in enumerate(dout_refs):
            dout_all[place] = dout_ref[...]

    low_queries = q_ref[...]
    high, low = scaled_queries(low_queries)
    queries = jnp.concatenate([high, low, minus_in_three(lse_ref[...])], axis=0)
    low_dout = dout_all[here]
    dout = low_dout.astype(f32)
    centre = jnp.sum(dout * out_ref[...], axis=0, keepdims=True)
    douts = jnp.concatenate([low_dout, minus_in_three(centre)], axis=0)
    blank = jnp.zeros((block, HDIM), bf16)
    right = jnp.concatenate(
        [
            jnp.concatenate([low_queries.astype(f32).T.astype(bf16), blank], axis=1),
            jnp.concatenate([blank, dout.T.astype(bf16)], axis=1),
        ],
        axis=0,
    )

    def score(at):
        rows = slice(at * part, (at + 1) * part)
        return (
            dot(keys_ref[rows, : 2 * HDIM + 16], queries),
            dot(values_ref[rows, : HDIM + 16], douts),
        )

    now = score(0)
    grad_queries = None
    for at in range(count):
        following = score(at + 1) if at + 1 < count else None
        rows = slice(at * part, (at + 1) * part)
        soft = jnp.exp2(now[0])
        grads = (soft * now[1]).astype(bf16)
        added = dot(k_ref[:, rows], grads)
        grad_queries = added if grad_queries is None else grad_queries + added
        sums[rows] += dot(jnp.concatenate([grads, soft.astype(bf16)], axis=1), right)
        now = following

    def columns_of(place):
        return pl.ds(pl.multiple_of(order_ref[place] * block, block), block)

    columns = columns_of(here)
    dq_all[here] = turn_back(
        grad_queries * factor, cos_ref[:, columns], sin_ref[:, columns]
    ).astype(bf16)

    @pl.when(here == length // block - 1)
    def _():
        for place, dp_ref in enumerate(dp_refs):
            columns = columns_of(place)
            both = sums[columns].T
            dp_ref[:HDIM] = dq_all[place]
            dp_ref[HDIM : 2 * HDIM] = turn_back(
                both[:HDIM] * factor, cos_ref[:, columns], sin_ref[:, columns]
            ).astype(bf16)
            dp_ref[2 * HDIM :] = both[HDIM:].astype(bf16)


def attend_back(order, keys, values, qkv, douts, out, lse, cosine, sine, part=256):
    length = keys.shape[0]
    chips = len(douts)
    block = douts[0].shape[1]
    scores = length * length

    def whole(array):
        return pl.BlockSpec(array.shape, lambda i, order: (0, 0))

    return pl.pallas_call(
        functools.partial(attend_back_kernel, part=part),
        name="attend_back",
        grid_spec=pltpu.PrefetchScalarGridSpec(
            num_scalar_prefetch=1,
            grid=(chips,),
            in_specs=[
                whole(keys),
                whole(values),
                pl.BlockSpec((HDIM, block), lambda i, order: (0, order[i])),
                pl.BlockSpec((HDIM, length), lambda i, order: (1, 0)),
                pl.BlockSpec((HDIM, block), lambda i, order: (0, order[i])),
                pl.BlockSpec((1, block), lambda i, order: (0, order[i])),
                whole(cosine),
                whole(sine),
                *[whole(piece) for piece in douts],
            ],
            out_specs=[pl.BlockSpec((3 * HDIM, block), lambda i, order: (0, 0))] * chips,
            scratch_shapes=[
                pltpu.VMEM((length, 2 * HDIM), f32),
                pltpu.VMEM((chips, HDIM, block), bf16),
                pltpu.VMEM((chips, HDIM, block), bf16),
            ],
        ),
        out_shape=[jax.ShapeDtypeStruct((3 * HDIM, block), bf16)] * chips,
        compiler_params=pltpu.CompilerParams(vmem_limit_bytes=VMEM),
        cost_estimate=cost(5 * 4 * 2 * scores * HDIM, 8 << 20),
    )(order, keys, values, qkv, qkv, out, lse, cosine, sine, *douts)


def attend_out_kernel(order_ref, attended_ref, *rest):
    piece_refs, (mixed_ref, attn_ref) = rest[:-2], rest[-2:]
    half = attn_ref.shape[1] // 2
    at = 0
    for piece_ref in piece_refs:
        for place in range(piece_ref.shape[0]):
            rows = pl.ds(pl.multiple_of(order_ref[at] * HDIM, HDIM), HDIM)
            attn_ref[rows, :half] = piece_ref[place, :HDIM]
            attn_ref[rows, half:] = piece_ref[place, HDIM:]
            at += 1
    turned = attended_ref[...].astype(f32).T.astype(bf16)
    mixed_ref[...] = dot(turned, attn_ref[...]).astype(bf16)


def attend_out(order, attended, pieces):
    size, tokens = attended.shape
    width = 2 * size

    def whole(*shape):
        return pl.BlockSpec(shape, lambda i, order: (0,) * len(shape))

    return pl.pallas_call(
        attend_out_kernel,
        name="attend_out",
        grid_spec=pltpu.PrefetchScalarGridSpec(
            num_scalar_prefetch=1,
            grid=(1,),
            in_specs=[whole(size, tokens)]
            + [whole(*piece.shape[:2], width // 2) for piece in pieces],
            out_specs=[whole(tokens, width), whole(size, width)],
        ),
        out_shape=[
            jax.ShapeDtypeStruct((tokens, width), bf16),
            jax.ShapeDtypeStruct((size, width), bf16),
        ],
        compiler_params=pltpu.CompilerParams(vmem_limit_bytes=VMEM),
        cost_estimate=cost(2 * 2 * tokens * width * size, 4 << 20),
    )(order, attended, *pieces)


def feed_kernel(
    first_order, second_order, x_ref, ours_ref, theirs_ref, g_ref, *rest, firsts, seconds
):
    weight_refs = [rest[:firsts]]
    for kind in range(3):
        weight_refs.append(rest[firsts + kind * seconds : firsts + (kind + 1) * seconds])
    residual_ref, partial_ref, back_ref, grads_ref = rest[-13:-9]
    unit, unit_t, g_t, sum_out, sum_back = rest[-9:-4]
    gate_ref, up_ref, out_ref, rest_ref = rest[-4:]
    here = pl.program_id(0)
    last = pl.num_programs(0) - 1
    width = x_ref.shape[1]
    step = gate_ref.shape[1]

    def join(total, parts, order):
        at = 0
        for part in parts:
            size = part.shape[1]
            for place in range(part.shape[0]):
                total[pl.ds(pl.multiple_of(order[at] * size, size), size)] = part[place]
                at += 1

    def bend(gate, upward):
        cdf = 0.5 + 0.5 * lax.erf(gate * math.sqrt(0.5))
        slope = cdf + gate * jnp.exp(gate * gate * -0.5) * (1.0 / math.sqrt(2.0 * math.pi))
        bent = gate * cdf
        return bent, slope, (bent * upward).astype(bf16)

    @pl.when(here == 0)
    def _():
        residual = (
            x_ref[...].astype(f32) + ours_ref[...].astype(f32) + theirs_ref[...].astype(f32)
        )
        residual_ref[...] = residual
        normed = unit_rows(residual)[0]
        unit[...] = normed.astype(bf16)
        unit_t[...] = normed.T.astype(bf16)
        g_t[...] = g_ref[...].astype(f32).T.astype(bf16)
        join(rest_ref, weight_refs[3], second_order)
        few = rest_ref.shape[1] // 4
        both = dot(unit[...], rest_ref[...])
        grad = dot(g_ref[...], rest_ref[...])[:, 2 * few : 3 * few]
        bent, slope, active = bend(both[:, :few], both[:, few : 2 * few])
        grad_gate = (grad * both[:, few : 2 * few] * slope).astype(bf16)
        grad_up = (grad * bent).astype(bf16)
        blank = jnp.zeros_like(active)
        outs = jnp.concatenate([blank, blank, active, blank], axis=1)
        ins = jnp.concatenate([grad_gate, grad_up, blank, blank], axis=1)
        sum_out[...] = dot(outs, rest_ref[...], 1, 1)
        sum_back[...] = dot(ins, rest_ref[...], 1, 1)
        grads_ref[:, grads_ref.shape[1] - 4 * few :] = (
            dot(unit_t[...], ins) + dot(g_t[...], outs)
        ).astype(bf16)

    join(gate_ref, weight_refs[0], first_order)
    join(up_ref, weight_refs[1], second_order)
    join(out_ref, weight_refs[2], second_order)
    gate = dot(unit[...], gate_ref[...])
    upward = dot(unit[...], up_ref[...])
    grad = dot(g_ref[...], out_ref[...])
    bent, slope, active = bend(gate, upward)
    grad_gate = (grad * upward * slope).astype(bf16)
    grad_up = (grad * bent).astype(bf16)
    sum_out[...] += dot(active, out_ref[...], 1, 1)
    sum_back[...] += dot(grad_gate, gate_ref[...], 1, 1) + dot(grad_up, up_ref[...], 1, 1)
    count = grads_ref.shape[1] // step // 3
    for at, grads in enumerate(
        (dot(unit_t[...], grad_gate), dot(unit_t[...], grad_up), dot(g_t[...], active))
    ):
        place = pl.multiple_of(at * count * step + here * step, 128)
        grads_ref[:, pl.ds(place, step)] = grads.astype(bf16)

    @pl.when(here == last)
    def _():
        partial_ref[...] = sum_out[...].astype(bf16)
        back_ref[...] = sum_back[...].astype(bf16)


def feed(first_order, second_order, x, ours, theirs, g, first, second, step=256):
    tokens, width = x.shape
    start = width // 2 // step
    count = (first[0].shape[2] - width // 2) // step
    rest = second[0].shape[2] - 2 * count * step
    columns = 3 * count * step + rest

    def whole(*shape):
        return pl.BlockSpec(shape, lambda i, one, two: (0, 0))

    def piece(arrays, size, at):
        return [
            pl.BlockSpec((*array.shape[:2], size), lambda i, one, two: (0, 0, at(i)))
            for array in arrays
        ]

    pair = jax.ShapeDtypeStruct((tokens, width), bf16)
    return pl.pallas_call(
        functools.partial(feed_kernel, firsts=len(first), seconds=len(second)),
        name="feed",
        grid_spec=pltpu.PrefetchScalarGridSpec(
            num_scalar_prefetch=2,
            grid=(count,),
            in_specs=[whole(tokens, width)] * 4
            + piece(first, step, lambda i: start + i)
            + piece(second, step, lambda i: i)
            + piece(second, step, lambda i: count + i)
            + piece(second, rest, lambda i: 2 * count * step // rest),
            out_specs=[whole(tokens, width)] * 3 + [whole(width, columns)],
            scratch_shapes=[
                pltpu.VMEM((tokens, width), bf16),
                pltpu.VMEM((width, tokens), bf16),
                pltpu.VMEM((width, tokens), bf16),
                pltpu.VMEM((tokens, width), f32),
                pltpu.VMEM((tokens, width), f32),
                pltpu.VMEM((width, step), bf16),
                pltpu.VMEM((width, step), bf16),
                pltpu.VMEM((width, step), bf16),
                pltpu.VMEM((width, rest), bf16),
            ],
        ),
        out_shape=[
            jax.ShapeDtypeStruct((tokens, width), f32),
            pair,
            pair,
            jax.ShapeDtypeStruct((width, columns), bf16),
        ],
        compiler_params=pltpu.CompilerParams(vmem_limit_bytes=VMEM),
        cost_estimate=cost(2 * 9 * 2 * tokens * width * count * step, 24 << 20),
    )(first_order, second_order, x, ours, theirs, g, *first, *second, *second, *second)


def middle_back_kernel(
    core_ref, order_ref, residual_ref, g_ref, ours_ref, theirs_ref, attn_ref, attended_ref,
    out_ours_ref, out_theirs_ref, layer_ref, residual_grad_ref, *rest,
):
    dout_refs, (grads_ref, dout_all) = rest[:-2], rest[-2:]
    rows = layer_ref.shape[0]
    half = attn_ref.shape[0]
    own = pl.ds(pl.multiple_of(core_ref[0] * rows, rows), rows)
    layer_ref[...] = (
        residual_ref[own, :]
        + out_ours_ref[own, :].astype(f32)
        + out_theirs_ref[...].astype(f32)
    ).astype(bf16)
    unit, inverse = unit_rows(residual_ref[...])
    scaled = ours_ref[...].astype(f32) + theirs_ref[...].astype(f32)
    grad = g_ref[...].astype(f32) + unit_back(scaled, unit, inverse)
    low = grad.astype(bf16)
    residual_grad_ref[...] = grad
    dout_all[...] = dot(attn_ref[...], low, 1, 1).astype(bf16)
    for at, dout_ref in enumerate(dout_refs):
        dout_ref[...] = dout_all[pl.ds(pl.multiple_of(order_ref[at] * HDIM, HDIM), HDIM)]
    grads = dot(attended_ref[...], low)
    few = grads.shape[0] // 8
    tiles = grads.shape[1] // 128
    grads = jnp.stack(
        [grads[:, at * 128 : (at + 1) * 128].reshape(few, 8, 128) for at in range(tiles)], axis=1
    )
    grads_ref[...] = grads.reshape(grads_ref.shape).astype(bf16)


def middle_back(
    core, order, residual, g, ours, theirs, attn, attended, out_ours, out_theirs
):
    tokens, width = residual.shape
    rows = tokens // 2
    half = width // 2
    chips = half // HDIM

    def whole(*shape):
        return pl.BlockSpec(shape, lambda i, core, order: (0,) * len(shape))

    return pl.pallas_call(
        middle_back_kernel,
        name="middle_back",
        grid_spec=pltpu.PrefetchScalarGridSpec(
            num_scalar_prefetch=2,
            grid=(1,),
            in_specs=[whole(tokens, width)] * 4
            + [whole(half, width), whole(half, tokens), whole(tokens, width), whole(rows, width)],
            out_specs=[whole(rows, width), whole(tokens, width)]
            + [whole(HDIM, tokens)] * chips
            + [whole(half * width // 128, 128)],
            scratch_shapes=[pltpu.VMEM((half, tokens), bf16)],
        ),
        out_shape=[
            jax.ShapeDtypeStruct((rows, width), bf16),
            jax.ShapeDtypeStruct((tokens, width), f32),
        ]
        + [jax.ShapeDtypeStruct((HDIM, tokens), bf16)] * chips
        + [jax.ShapeDtypeStruct((half * width // 128, 128), bf16)],
        compiler_params=pltpu.CompilerParams(vmem_limit_bytes=VMEM),
        cost_estimate=cost(2 * 2 * 2 * tokens * width * half, 16 << 20),
    )(core, order, residual, g, ours, theirs, attn, attended, out_ours, out_theirs)


def hidden_back_kernel(order_ref, core_ref, w_ref, *rest):
    dp_refs, (own_ref, other_ref, stacked) = rest[:-3], rest[-3:]
    for place, dp_ref in enumerate(dp_refs):
        size = dp_ref.shape[0]
        stacked[pl.ds(pl.multiple_of(order_ref[place] * size, 64), size)] = dp_ref[...]
    rows = own_ref.shape[0]
    flat = dot(w_ref[...], stacked[...])
    first = flat[:, :rows].T
    second = flat[:, rows:].T
    zero = core_ref[0] == 0
    own_ref[...] = jnp.where(zero, first, second)
    other_ref[...] = jnp.where(zero, second, first).astype(bf16)


def hidden_back(order, core, weights, pieces):
    width, columns = weights.shape
    rows = pieces[0].shape[1] // 2

    def whole(*shape):
        return pl.BlockSpec(shape, lambda i, order, core: (0,) * len(shape))

    return pl.pallas_call(
        hidden_back_kernel,
        name="hidden_back",
        grid_spec=pltpu.PrefetchScalarGridSpec(
            num_scalar_prefetch=2,
            grid=(1,),
            in_specs=[whole(width, columns)] + [whole(*pieces[0].shape)] * len(pieces),
            out_specs=[whole(rows, width)] * 2,
            scratch_shapes=[pltpu.VMEM((columns, 2 * rows), bf16)],
        ),
        out_shape=[
            jax.ShapeDtypeStruct((rows, width), f32),
            jax.ShapeDtypeStruct((rows, width), bf16),
        ],
        compiler_params=pltpu.CompilerParams(vmem_limit_bytes=VMEM),
        cost_estimate=cost(2 * 2 * 2 * rows * width * columns, 8 << 20),
    )(order, core, weights, *pieces)


def head_grad_kernel(order_ref, unit_ref, *rest):
    dp_refs, out_ref = rest[:-1], rest[-1]
    block = dp_refs[0].shape[1]
    total = None
    for place, dp_ref in enumerate(dp_refs):
        rows = pl.ds(pl.multiple_of(order_ref[place] * block, block), block)
        added = dot(dp_ref[...], unit_ref[rows])
        total = added if total is None else total + added
    for at in range(out_ref.shape[0]):
        out_ref[at] = total[:, at * 128 : (at + 1) * 128].astype(bf16)


def head_grad(order, unit_all, pieces):
    length, width = unit_all.shape
    owners = width // 128
    size = pieces[0].shape[0]

    def whole(*shape):
        return pl.BlockSpec(shape, lambda i, order: (0,) * len(shape))

    return pl.pallas_call(
        head_grad_kernel,
        name="head_grad",
        grid_spec=pltpu.PrefetchScalarGridSpec(
            num_scalar_prefetch=1,
            grid=(1,),
            in_specs=[whole(length, width)] + [whole(*pieces[0].shape)] * len(pieces),
            out_specs=whole(owners, size, 128),
        ),
        out_shape=jax.ShapeDtypeStruct((owners, size, 128), bf16),
        compiler_params=pltpu.CompilerParams(vmem_limit_bytes=VMEM),
        cost_estimate=cost(2 * 2 * length * width * size, 10 << 20),
    )(order, unit_all, *pieces)


def adam(weight, gradient, first, second, rate):
    first = BETA_FIRST * first + (1.0 - BETA_FIRST) * gradient
    second = BETA_SECOND * second + (1.0 - BETA_SECOND) * gradient * gradient
    first_hat = first / (1.0 - BETA_FIRST**STEP)
    second_hat = second / (1.0 - BETA_SECOND**STEP)
    weight = weight - rate * (first_hat / (jnp.sqrt(second_hat) + EPSILON) + DECAY * weight)
    return (weight, first, second)


def adam_into(refs, weight, gradient, first, second, rate):
    for ref, value in zip(refs, adam(weight, gradient, first, second, rate)):
        ref[...] = value


def rounded_in_kernel(values):
    return values.astype(bf16).astype(f32)


def adam_in_kernel(
    grads_ref, gain_ref, w_ref, m_ref, v_ref, new_w, new_m, new_v, gain_grad, *, rate
):
    width = m_ref.shape[1] // 2
    main = width // 256 * 128
    few = width // 2 - main
    start = grads_ref.shape[2] - 3 * main - 128
    columns = []
    for at in range(2):
        for core in range(2):
            place = start + at * main
            columns.append(grads_ref[core, :, place : place + main].astype(f32))
        for core in range(2):
            rest = grads_ref[core, :, start + 3 * main :].astype(f32)
            columns.append(rest[:, at * few : (at + 1) * few])
    grads = jnp.concatenate(columns, axis=1)
    weight = w_ref[...]
    gain_grad[...] = jnp.sum(grads * rounded_in_kernel(weight), axis=1, keepdims=True)
    adam_into(
        (new_w, new_m, new_v), weight, grads * gain_ref[...], m_ref[...], v_ref[...], rate
    )


def adam_in(grads, gain, weight, first, second, rate):
    rows, columns = weight.shape
    steps = grads.shape[0] // 2
    block = pl.BlockSpec((rows // steps, columns), lambda i: (i, 0))
    column = pl.BlockSpec((rows // steps, 1), lambda i: (i, 0))
    same = jax.ShapeDtypeStruct((rows, columns), f32)
    return pl.pallas_call(
        functools.partial(adam_in_kernel, rate=rate),
        name="adam_in",
        grid=(steps,),
        in_specs=[pl.BlockSpec((2,) + grads.shape[1:], lambda i: (i, 0, 0)), column]
        + [block] * 3,
        out_specs=[block] * 3 + [column],
        out_shape=[same] * 3 + [jax.ShapeDtypeStruct((rows, 1), f32)],
        compiler_params=pltpu.CompilerParams(vmem_limit_bytes=VMEM),
        cost_estimate=cost(rows * columns * 20, rows * columns * 26),
    )(grads, gain, weight, first, second)


def adam_out_kernel(grads_ref, w_ref, m_ref, v_ref, *new, rate):
    chips = grads_ref.shape[0] // 2
    hidden = w_ref.shape[0]
    main = hidden // 256 * 128
    few = hidden // 2 - main
    place = grads_ref.shape[2] - main - 128
    for core in range(2):
        columns = jnp.concatenate(
            [grads_ref[2 * chip + core, :, place : place + main] for chip in range(chips)], axis=0
        )
        rest = jnp.concatenate(
            [grads_ref[2 * chip + core, :, place + main :] for chip in range(chips)], axis=0
        )
        for rows, grads in (
            (slice(core * main, (core + 1) * main), columns.astype(f32).T),
            (
                slice(2 * main + core * few, 2 * main + (core + 1) * few),
                rest.astype(f32).T[2 * few : 3 * few],
            ),
        ):
            values = adam(w_ref[rows], grads, m_ref[rows], v_ref[rows], rate)
            for ref, value in zip(new, values):
                ref[rows] = value


def adam_out(grads, weight, first, second, rate):
    def whole(array):
        return pl.BlockSpec(array.shape, lambda i: (0,) * array.ndim)

    arrays = (weight, first, second)
    return pl.pallas_call(
        functools.partial(adam_out_kernel, rate=rate),
        name="adam_out",
        grid=(1,),
        in_specs=[whole(array) for array in (grads, *arrays)],
        out_specs=[whole(array) for array in arrays],
        out_shape=[jax.ShapeDtypeStruct(array.shape, f32) for array in arrays],
        compiler_params=pltpu.CompilerParams(vmem_limit_bytes=VMEM),
        cost_estimate=cost(weight.size * 60, 14 << 20),
    )(grads, *arrays)


def adam_attn_kernel(order_ref, *refs, rate, chips):
    grads_refs, (w_ref, m_ref, v_ref, *new, joined) = refs[:-7], refs[-7:]
    at = 0
    for grads_ref in grads_refs:
        for place in range(grads_ref.shape[0]):
            device = order_ref[at]
            row = device % 2 * HDIM + device // 2 * (HDIM // chips)
            rows = pl.ds(pl.multiple_of(row, 8), HDIM // chips)
            tiles = grads_ref[place].astype(f32)
            for tile in range(joined.shape[1] // 128):
                joined[rows, tile * 128 : (tile + 1) * 128] = tiles[tile * 8 : (tile + 1) * 8]
            at += 1
    adam_into(new, w_ref[...], joined[...], m_ref[...], v_ref[...], rate)


def adam_attn(order, grads, chips, weight, first, second, rate):
    def whole(array):
        return pl.BlockSpec(array.shape, lambda i, order: (0,) * array.ndim)

    arrays = (weight, first, second)
    size = weight.shape[1] // 128 * (HDIM // chips)
    return pl.pallas_call(
        functools.partial(adam_attn_kernel, rate=rate, chips=chips),
        name="adam_attn",
        grid_spec=pltpu.PrefetchScalarGridSpec(
            num_scalar_prefetch=1,
            grid=(1,),
            in_specs=[
                pl.BlockSpec((piece.shape[0], size, 128), lambda i, order: (0, 3 * HDIM // size, 0))
                for piece in grads
            ]
            + [whole(array) for array in arrays],
            out_specs=[whole(array) for array in arrays],
            scratch_shapes=[pltpu.VMEM(weight.shape, f32)],
        ),
        out_shape=[jax.ShapeDtypeStruct(array.shape, f32) for array in arrays],
        compiler_params=pltpu.CompilerParams(vmem_limit_bytes=VMEM),
        cost_estimate=cost(weight.size * 20, weight.size * 26),
    )(order, *grads, *arrays)


def adam_qkv_kernel(order_ref, *refs, rate):
    grads_refs, (gain_ref, w_ref, m_ref, v_ref, new_w, new_m, new_v, gain_grad, joined) = (
        refs[:-9], refs[-9:]
    )
    here = pl.program_id(0)
    rows = pl.ds(pl.multiple_of(here * HDIM, HDIM), HDIM)
    at = 0
    for grads_ref in grads_refs:
        for place in range(grads_ref.shape[0]):
            head = pl.ds(pl.multiple_of(order_ref[at] * HDIM, HDIM), HDIM)
            joined[head] = grads_ref[place, rows].astype(f32)
            at += 1
    grads = joined[...].T
    weight = w_ref[...]
    added = jnp.sum(grads * rounded_in_kernel(weight), axis=1, keepdims=True)
    gain_grad[...] = added + jnp.where(here == 0, 0.0, gain_grad[...])
    adam_into(
        (new_w, new_m, new_v), weight, grads * gain_ref[...], m_ref[...], v_ref[...], rate
    )


def adam_qkv(order, grads, gain, weight, first, second, rate):
    rows, columns = weight.shape
    block = pl.BlockSpec((rows, columns // 3), lambda i, order: (0, i))
    column = pl.BlockSpec((rows, 1), lambda i, order: (0, 0))
    same = jax.ShapeDtypeStruct((rows, columns), f32)
    return pl.pallas_call(
        functools.partial(adam_qkv_kernel, rate=rate),
        name="adam_qkv",
        grid_spec=pltpu.PrefetchScalarGridSpec(
            num_scalar_prefetch=1,
            grid=(3,),
            in_specs=[pl.BlockSpec((piece.shape[0], 3 * HDIM, 128), lambda i, order: (0, 0, 0)) for piece in grads]
            + [column]
            + [block] * 3,
            out_specs=[block] * 3 + [column],
            scratch_shapes=[pltpu.VMEM((columns // 3, rows), f32)],
        ),
        out_shape=[same] * 3 + [jax.ShapeDtypeStruct((rows, 1), f32)],
        compiler_params=pltpu.CompilerParams(vmem_limit_bytes=VMEM),
        cost_estimate=cost(rows * columns * 20, rows * columns * 26),
    )(order, *grads, gain, weight, first, second)


def ring(axis, shift):
    size = lax.axis_size(axis)
    return [(at, (at + shift) % size) for at in range(size)]


def gather_first_step(planes_first, lines_first):
    swapped = lax.ppermute(planes_first, "zh", SWAP)
    others = [
        lax.ppermute(lines_first, "y", ring("y", shift)) for shift in range(1, lax.axis_size("y"))
    ]
    return jnp.stack([planes_first, swapped]), jnp.stack([lines_first, *others])


def gather_second_step(first, second):
    firsts = [first] + [
        lax.ppermute(first, "y", ring("y", shift)) for shift in range(1, lax.axis_size("y"))
    ]
    return firsts, [second, lax.ppermute(second, "zh", SWAP)]


def shards(
    tokens,
    positions,
    cotangent,
    weight_qkv,
    weight_attn,
    weight_in,
    weight_out,
    norm_gains,
    first_qkv,
    first_attn,
    first_in,
    first_out,
    first_gains,
    second_qkv,
    second_attn,
    second_in,
    second_out,
    second_gains,
):
    rows, width = tokens.shape[1:]
    shard_rows = weight_qkv.shape[1]
    heads = width // HDIM
    hidden = weight_out.shape[1]
    core = lax.axis_index("c")
    mine = lax.axis_index(CTX)
    chip = lax.axis_index(CHIPS)
    chips = lax.axis_size(CHIPS)
    owners = lax.axis_size(FSDP)
    length = rows * chips * 2
    main = hidden // 256 * 128
    few = hidden // 2 - main
    core_at = core.reshape(1).astype(jnp.int32)
    offsets = [(far, near) for far in range(lax.axis_size("x")) for near in range(2)]
    across, beside = lax.axis_index("x"), lax.axis_index("zl")
    wide = lax.axis_size("x")

    def chips_at(sign):
        places = [(across + sign * far) % wide * 2 + (beside ^ near) for far, near in offsets]
        return jnp.stack(places).astype(jnp.int32)

    local = tokens[0]
    extra = 16
    high, low = positions[0] // 128, positions[0] % 128
    places_row = jnp.concatenate([high, low, jnp.zeros((width - 2 * rows,), jnp.int32)])
    places_rows = jnp.concatenate(
        [places_row[None], jnp.zeros((extra - 1, width), jnp.int32)], axis=0
    ).astype(bf16)
    sequence = lax.all_gather(
        jnp.concatenate([local, places_rows], axis=0), CTX, axis=0, tiled=True
    )
    gains = norm_gains[0].astype(bf16).astype(f32)

    low_in = (weight_in[0].astype(bf16).astype(f32) * gains[1][:, None]).astype(bf16)
    low_out_w = weight_out[0].astype(bf16)
    attn_rows = lax.dynamic_slice_in_dim(weight_attn[0].astype(bf16), core * HDIM, HDIM, 0)

    def columns(array, start, size, dim=1):
        return lax.dynamic_slice_in_dim(array, start + core * size, size, dim)

    first_part = jnp.concatenate(
        [
            jnp.concatenate([attn_rows[:, : width // 2], attn_rows[:, width // 2 :]], axis=0),
            columns(low_in, 0, main),
        ],
        axis=1,
    )
    second_part = jnp.concatenate(
        [
            columns(low_in, hidden, main),
            columns(low_out_w, 0, main, 0).T,
            columns(low_in, 2 * main, few),
            columns(low_in, hidden + 2 * main, few),
            columns(low_out_w, 2 * main, few, 0).T,
            jnp.zeros((shard_rows, few), bf16),
        ],
        axis=1,
    )
    first_joined, second_joined = gather_first_step(first_part, second_part)
    first_joined, second_joined, sequence = lax.optimization_barrier(
        (first_joined, second_joined, sequence)
    )
    first_pieces, second_pieces = gather_second_step(first_joined, second_joined)
    lines = lax.axis_size("y")
    plane, line = lax.axis_index("zh"), lax.axis_index("y")
    first_order = jnp.stack(
        [(plane ^ far) * lines + (line - shift) % lines for shift in range(lines) for far in range(2)]
    ).astype(jnp.int32)
    second_order = jnp.stack(
        [(plane ^ far) * lines + (line - shift) % lines for far in range(2) for shift in range(lines)]
    ).astype(jnp.int32)

    low_qkv = (weight_qkv[0].astype(bf16).astype(f32) * gains[0][:, None]).astype(bf16)
    own_head = lax.dynamic_index_in_dim(
        low_qkv.reshape(shard_rows, 3, heads, HDIM), mine, 2, keepdims=False
    )
    head_columns = own_head.reshape(shard_rows, 3 * HDIM).T
    head_weights = lax.all_to_all(
        jnp.broadcast_to(head_columns, (owners, *head_columns.shape)), FSDP, 0, 0, tiled=True
    )

    by_head = low_qkv.reshape(shard_rows, 3, heads // 2, 2, HDIM)
    half_heads = lax.dynamic_index_in_dim(by_head, core, 3, keepdims=False)
    half_heads = half_heads.transpose(0, 2, 1, 3).reshape(shard_rows, 3 * width // 2)
    half_heads, sequence = lax.optimization_barrier((half_heads, sequence))
    mat_qkv = lax.all_gather(half_heads, FSDP, axis=0, tiled=True)

    def in_order(ours, theirs):
        first = jnp.where(core == 0, ours, theirs)
        second = jnp.where(core == 0, theirs, ours)
        return jnp.concatenate([first, second], axis=0)

    def swap(array):
        return lax.ppermute(array, "c", SWAP)

    gradient = in_order(cotangent[0], swap(cotangent[0]))

    freqs = jnp.exp(jnp.arange(HDIM // 2, dtype=f32) * (-2.0 * math.log(ROPE_BASE) / HDIM))
    by_device = sequence.reshape(2 * chips, rows + extra, width)[:, rows]
    by_device = by_device.astype(f32)
    places = by_device[:, :rows] * 128.0 + by_device[:, rows : 2 * rows]
    angles = freqs[:, None] * places.reshape(1, length)
    cosine = jnp.cos(angles)
    sine = jnp.sin(angles)
    unit_all, qkv, keys, values = project(sequence, head_weights, cosine, sine)
    low_out, out, lse = attend(keys, qkv, chips)
    attended = lax.all_to_all(low_out, CHIPS, 0, 0, tiled=True)
    attended = attended.reshape(heads // 2 * HDIM, 2 * rows)
    mixed, mat_attn = attend_out(first_order, attended, first_pieces)
    current = lax.dynamic_slice_in_dim(
        sequence, chip * 2 * (rows + extra), 2 * (rows + extra), 0
    ).reshape(2, rows + extra, width)[:, :rows].reshape(2 * rows, width)
    current, mat_qkv = lax.optimization_barrier((current, mat_qkv))
    residual, partial, back, grads = feed(
        first_order, second_order, current, mixed, swap(mixed), gradient, first_pieces,
        second_pieces,
    )
    arrived = lax.all_to_all(grads, FSDP + CHIPS, 0, 0, tiled=True)

    def move(pieces, sign):
        moved = [pieces[0]]
        for (far, near), piece in list(zip(offsets, pieces))[1:]:
            pairs = [
                (at, (at // 2 + sign * far) % wide * 2 + (at % 2 ^ near)) for at in range(chips)
            ]
            moved.append(lax.ppermute(piece, CHIPS, pairs))
        return moved

    ahead, behind = chips_at(1), chips_at(-1)
    theirs = swap(lax.dynamic_slice_in_dim(partial, (1 - core) * rows, rows, 0))
    layer_out, residual_grad, *dout_pieces, attn_parts = middle_back(
        core_at, ahead, residual, gradient, back, swap(back), mat_attn, attended, partial, theirs
    )

    douts = move(dout_pieces, 1)
    pieces = attend_back(behind, keys, values, qkv, douts, out, lse, cosine, sine)
    moved = move(pieces, -1)
    own_hidden, other_hidden = hidden_back(ahead, core_at, mat_qkv, moved)
    arrived, own_hidden = lax.optimization_barrier((arrived, own_hidden))
    grad_hidden = own_hidden + swap(other_hidden).astype(f32)
    unit_in, scale_in = unit_rows(local.astype(f32))
    own_residual = lax.dynamic_slice_in_dim(residual_grad, core * rows, rows, 0)
    tokens_grad = (own_residual + unit_back(grad_hidden, unit_in, scale_in))[None]

    def sum_parts(parts, count):
        parts = parts.reshape(count, parts.shape[0] // count, parts.shape[1])
        return jnp.sum(parts.astype(f32), axis=0).astype(bf16)

    all_grads = lax.all_gather(
        sum_parts(arrived, owners * chips), CTX, axis=0, tiled=False
    )

    head_sums = lax.all_to_all(head_grad(behind, unit_all, pieces), FSDP, 0, 0, tiled=True)
    head_own = sum_parts(head_sums.reshape(width // 128 * 3 * HDIM, 128), owners)
    attn_own = sum_parts(
        lax.all_to_all(attn_parts, FSDP + CHIPS, 0, 0, tiled=True), owners * chips
    )
    head_own = jnp.concatenate([head_own, attn_own], axis=0)[None]
    head_pair = jnp.concatenate([head_own, swap(head_own)], axis=0)
    head_four = jnp.concatenate([head_pair, lax.ppermute(head_pair, "zl", SWAP)], axis=0)
    head_grads = [head_four] + [
        lax.ppermute(head_four, "x", ring("x", shift)) for shift in range(1, wide)
    ]
    head_order = jnp.stack(
        [
            (across - shift) % wide * 4 + (beside ^ near) * 2 + (core ^ other)
            for shift in range(wide)
            for near in range(2)
            for other in range(2)
        ]
    ).astype(jnp.int32)

    rates = (
        width ** (-0.5),
        max(1, 3 * width // length) ** (-0.5),
        width ** (-0.5),
        hidden ** (-0.5),
    )
    columns_of_gains = gains.T
    *new_in, gain_second = adam_in(
        all_grads, columns_of_gains[:, 1:], weight_in[0], first_in[0], second_in[0], rates[2]
    )
    new_out = adam_out(all_grads, weight_out[0], first_out[0], second_out[0], rates[3])
    new_attn = adam_attn(
        head_order, head_grads, chips, weight_attn[0], first_attn[0], second_attn[0], rates[1]
    )
    *new_qkv, gain_first = adam_qkv(
        head_order, head_grads, columns_of_gains[:, :1], weight_qkv[0], first_qkv[0], second_qkv[0], rates[0]
    )
    gain_grads = jnp.concatenate([gain_first, gain_second], axis=1).T
    new_gains = adam(norm_gains[0], gain_grads, first_gains[0], second_gains[0], GAIN_RATE)
    updated = (new_qkv, new_attn, new_in, new_out, new_gains)
    return (
        layer_out[None],
        tokens_grad,
        *[updated[member][0][None] for member in range(5)],
        *[updated[member][1][None] for member in range(5)],
        *[updated[member][2][None] for member in range(5)],
    )


def solution(mesh):
    split = Mesh(mesh.devices.reshape(4, 2, 2, 2, 4), ("x", "zl", "c", "zh", "y"))
    by_row = P(None, FSDP, None)
    by_column = P(None, None, FSDP)
    weights = (by_row, by_row, by_row, by_column, by_column)
    by_token = P(FSDP, CTX, None)
    return jax.shard_map(
        shards,
        mesh=split,
        in_specs=(by_token, P(FSDP, CTX), by_token) + weights * 3,
        out_specs=(by_token, by_token) + weights * 3,
        check_vma=False,
    )
```

```python
import functools
import math

import jax
import jax.numpy as jnp
from jax import lax
from jax.experimental import pallas as pl
from jax.experimental.pallas import tpu as pltpu
from jax.sharding import Mesh, PartitionSpec as P

HDIM = 64
STEP = 10
BETA_FIRST = 0.5
BETA_SECOND = 0.5
EPSILON = 1e-08
DECAY = 0.01
NORM_EPS = 1e-05
ROPE_BASE = 160000.0
GAIN_RATE = 0.6
LOG2E = math.log2(math.e)
f32 = jnp.float32
bf16 = jnp.bfloat16

CHIPS = ("x", "zl")
CTX = ("x", "zl", "c")
FSDP = ("zh", "y")
SWAP = [(0, 1), (1, 0)]
VMEM = 60 << 20


def dot(left, right, left_dim=1, right_dim=0):
    return lax.dot_general(
        left, right, (((left_dim,), (right_dim,)), ((), ())), preferred_element_type=f32
    )


def cost(flops, moved):
    return pl.CostEstimate(flops=flops, bytes_accessed=moved, transcendentals=0)


def unit_rows(values):
    average = jnp.mean(values, axis=-1, keepdims=True)
    centered = values - average
    spread = jnp.mean(centered * centered, axis=-1, keepdims=True)
    inverse = lax.rsqrt(spread + NORM_EPS)
    return centered * inverse, inverse


def unit_back(scaled, unit, inverse):
    first_mean = jnp.mean(scaled, axis=-1, keepdims=True)
    second_mean = jnp.mean(scaled * unit, axis=-1, keepdims=True)
    return inverse * (scaled - first_mean - unit * second_mean)


def prepare_kernel(
    place_ref, gains_ref, qkv_ref, attn_ref, in_ref, out_ref,
    first_ref, second_ref, head_ref, heads_ref,
):
    core, chip = place_ref[0], place_ref[1]
    rows = qkv_ref.shape[0]
    width = attn_ref.shape[1]
    hidden = out_ref.shape[0]
    main = hidden // 256 * 128
    few = hidden // 2 - main
    half = width // 2
    low_gains = gains_ref[...].astype(bf16).astype(f32)
    columns = jnp.concatenate([low_gains, jnp.zeros((6, rows), f32)], axis=0).T
    gain_first, gain_second = columns[:, 0:1], columns[:, 1:2]

    def pick(array):
        size = array.shape[1] // 2
        return jnp.where(core == 0, array[:, :size], array[:, size:])

    def scaled(values, gain):
        return (values.astype(bf16).astype(f32) * gain).astype(bf16)

    attn_rows = attn_ref[pl.ds(pl.multiple_of(core * HDIM, HDIM), HDIM)].astype(bf16)
    first_ref[:HDIM, :half] = attn_rows[:, :half]
    first_ref[HDIM:, :half] = attn_rows[:, half:]
    first_ref[:, half : half + main] = scaled(pick(in_ref[:, : 2 * main]), gain_second)
    first_ref[:, half + main :] = scaled(pick(in_ref[:, hidden : hidden + 2 * main]), gain_second)
    out_rows = out_ref[pl.ds(pl.multiple_of(core * main, 128), main)]
    second_ref[:, :main] = out_rows.T.astype(bf16)
    odd_out = out_ref[2 * main :].T
    odd = [
        scaled(pick(in_ref[:, 2 * main : hidden]), gain_second),
        scaled(pick(in_ref[:, hidden + 2 * main :]), gain_second),
        pick(odd_out).astype(bf16),
        jnp.zeros((rows, few), bf16),
    ]
    second_ref[:, main:] = jnp.concatenate(odd, axis=1)
    pieces = []
    for at in range(width // 128):
        for part in range(3):
            start = part * width + at * 128
            pieces.append(scaled(pick(qkv_ref[:, start : start + 128]), gain_first))
    heads_ref[...] = jnp.concatenate(pieces, axis=1)
    own = []
    for part in range(3):
        start = pl.multiple_of(part * width + chip * 128, 128)
        own.append(scaled(pick(qkv_ref[:, pl.ds(start, 128)]), gain_first).astype(f32))
    own.append(jnp.zeros((rows, HDIM), f32))
    head_ref[...] = jnp.concatenate(own, axis=1).T[: 3 * HDIM].astype(bf16)


def prepare(place, gains, qkv, attn, weight_in, weight_out):
    rows, width = attn.shape
    hidden = weight_out.shape[0]
    main = hidden // 256 * 128
    arrays = (gains, qkv, attn, weight_in, weight_out)
    shapes = [
        (rows, width // 2 + 2 * main),
        (rows, main + 4 * (hidden // 2 - main)),
        (3 * HDIM, rows),
        (rows, 3 * width // 2),
    ]

    def whole(shape):
        return pl.BlockSpec(shape, lambda i, place: (0, 0))

    return pl.pallas_call(
        prepare_kernel,
        name="prepare",
        grid_spec=pltpu.PrefetchScalarGridSpec(
            num_scalar_prefetch=1,
            grid=(1,),
            in_specs=[whole(array.shape) for array in arrays],
            out_specs=[whole(shape) for shape in shapes],
        ),
        out_shape=[jax.ShapeDtypeStruct(shape, bf16) for shape in shapes],
        compiler_params=pltpu.CompilerParams(vmem_limit_bytes=VMEM),
        cost_estimate=cost(rows * width * 60, 10 << 20),
    )(place, *arrays)


def project_kernel(x_ref, w_ref, cos_ref, sin_ref, unit_ref, qkv_ref, keys_ref, values_ref, w_all):
    half = HDIM // 2
    rows = cos_ref.shape[1]

    @pl.when(pl.program_id(0) == 0)
    def _():
        for part in range(w_ref.shape[0]):
            w_all[:, part * 128 : (part + 1) * 128] = w_ref[part]

    each = rows // 2
    extra = x_ref.shape[0] // 2 - each
    tokens = jnp.concatenate(
        [x_ref[:each].astype(f32), x_ref[each + extra : 2 * each + extra].astype(f32)], axis=0
    )
    unit = unit_rows(tokens)[0].astype(bf16)
    unit_ref[...] = unit
    mixed = dot(w_all[...], unit, 1, 1)
    cosine = cos_ref[...]
    sine = sin_ref[...]

    def turn(one, two):
        return jnp.concatenate([one * cosine - two * sine, two * cosine + one * sine], axis=0)

    queries = turn(mixed[:half], mixed[half:HDIM])
    keys = turn(mixed[HDIM : HDIM + half], mixed[HDIM + half : 2 * HDIM])
    values = mixed[2 * HDIM :]
    qkv_ref[...] = jnp.concatenate([queries, keys, values], axis=0).astype(bf16)
    key_rows = keys.T.astype(bf16)
    value_rows = values.T.astype(bf16)
    ones = jnp.where(lax.broadcasted_iota(jnp.int32, (rows, 128), 1) < 3, 1.0, 0.0).astype(bf16)
    keys_ref[...] = jnp.concatenate([key_rows, key_rows, ones], axis=1)
    values_ref[...] = jnp.concatenate([value_rows, ones[:, :HDIM]], axis=1)


def project(tokens, weights, cosine, sine, block=512):
    width = tokens.shape[1]
    length = cosine.shape[1]
    steps = length // block
    return pl.pallas_call(
        project_kernel,
        name="project",
        grid=(steps,),
        in_specs=[
            pl.BlockSpec((tokens.shape[0] // steps, width), lambda i: (i, 0)),
            pl.BlockSpec(weights.shape, lambda i: (0, 0, 0)),
            pl.BlockSpec((HDIM // 2, block), lambda i: (0, i)),
            pl.BlockSpec((HDIM // 2, block), lambda i: (0, i)),
        ],
        out_specs=[
            pl.BlockSpec((block, width), lambda i: (i, 0)),
            pl.BlockSpec((3 * HDIM, block), lambda i: (0, i)),
            pl.BlockSpec((block, 256), lambda i: (i, 0)),
            pl.BlockSpec((block, 128), lambda i: (i, 0)),
        ],
        out_shape=[
            jax.ShapeDtypeStruct((length, width), bf16),
            jax.ShapeDtypeStruct((3 * HDIM, length), bf16),
            jax.ShapeDtypeStruct((length, 256), bf16),
            jax.ShapeDtypeStruct((length, 128), bf16),
        ],
        scratch_shapes=[pltpu.VMEM((3 * HDIM, width), bf16)],
        compiler_params=pltpu.CompilerParams(vmem_limit_bytes=VMEM),
        cost_estimate=cost(2 * length * width * 4 * HDIM, 22 << 20),
    )(tokens, weights, cosine, sine)


def scaled_queries(queries):
    scaled = queries.astype(f32) * (LOG2E / math.sqrt(HDIM))
    high = scaled.astype(bf16)
    low = (scaled - high.astype(f32)).astype(bf16)
    return high, low


def attend_kernel(keys_ref, q_ref, v_ref, low_ref, out_ref, lse_ref, v_ones, *, part):
    length = keys_ref.shape[0]
    count = length // part

    @pl.when(pl.program_id(0) == 0)
    def _():
        v_ones[:HDIM] = v_ref[...]
        v_ones[HDIM:] = jnp.where(
            lax.broadcasted_iota(jnp.int32, (16, length), 0) < 1, 1.0, 0.0
        ).astype(bf16)

    queries = jnp.concatenate(scaled_queries(q_ref[...]), axis=0)

    def score(at):
        return dot(keys_ref[at * part : (at + 1) * part, : 2 * HDIM], queries)

    scores = score(0)
    highest = total = None
    for at in range(count):
        following = score(at + 1) if at + 1 < count else None
        peak = jnp.max(scores, axis=0, keepdims=True)
        raised = peak if highest is None else jnp.maximum(highest, peak)
        soft = jnp.exp2(scores - raised).astype(bf16)
        added = dot(v_ones[:, at * part : (at + 1) * part], soft)
        total = added if total is None else total * jnp.exp2(highest - raised) + added
        highest = raised
        scores = following
    summed = total[HDIM : HDIM + 1]
    result = total[:HDIM] / summed
    out_ref[...] = result
    lse_ref[...] = highest + jnp.log2(summed)
    step = low_ref.shape[2]
    for at in range(low_ref.shape[0]):
        low_ref[at] = result[:, at * step : (at + 1) * step].astype(bf16)


def attend(keys, qkv, chips, block=1024, part=512):
    length = keys.shape[0]
    return pl.pallas_call(
        functools.partial(attend_kernel, part=part),
        name="attend",
        grid=(length // block,),
        in_specs=[
            pl.BlockSpec(keys.shape, lambda i: (0, 0)),
            pl.BlockSpec((HDIM, block), lambda i: (0, i)),
            pl.BlockSpec((HDIM, length), lambda i: (2, 0)),
        ],
        out_specs=[
            pl.BlockSpec((block * chips // length, HDIM, length // chips), lambda i: (i, 0, 0)),
            pl.BlockSpec((HDIM, block), lambda i: (0, i)),
            pl.BlockSpec((1, block), lambda i: (0, i)),
        ],
        out_shape=[
            jax.ShapeDtypeStruct((chips, HDIM, length // chips), bf16),
            jax.ShapeDtypeStruct((HDIM, length), f32),
            jax.ShapeDtypeStruct((1, length), f32),
        ],
        scratch_shapes=[pltpu.VMEM((HDIM + 16, length), bf16)],
        compiler_params=pltpu.CompilerParams(vmem_limit_bytes=VMEM),
        cost_estimate=cost(2 * 4 * 2 * length * length * HDIM, 6 << 20),
    )(keys, qkv, qkv)


def minus_in_three(values):
    rows = values.shape[1]
    at = lax.broadcasted_iota(jnp.int32, (16, rows), 0)
    high = (-values).astype(bf16).astype(f32)
    rest = -values - high
    middle = rest.astype(bf16).astype(f32)
    low = rest - middle
    stacked = jnp.where(at == 0, high, jnp.where(at == 1, middle, jnp.where(at == 2, low, 0.0)))
    return stacked.astype(bf16)


def attend_back_kernel(
    order_ref,
    keys_ref,
    values_ref,
    q_ref,
    k_ref,
    out_ref,
    lse_ref,
    cos_ref,
    sin_ref,
    *rest,
    part,
):
    count = (len(rest) - 3) // 2
    dout_refs, dp_refs, (sums, dq_all, dout_all) = rest[:count], rest[count:-3], rest[-3:]
    half = HDIM // 2
    here = pl.program_id(0)
    length = keys_ref.shape[0]
    block = q_ref.shape[1]
    count = length // part
    factor = HDIM ** (-0.5)

    def turn_back(grads, cosine, sine):
        low = grads.astype(bf16).astype(f32)
        one, two = low[:half], low[half:]
        return jnp.concatenate([one * cosine + two * sine, two * cosine - one * sine], axis=0)

    @pl.when(here == 0)
    def _():
        sums[...] = jnp.zeros_like(sums)
        for place, dout_ref in enumerate(dout_refs):
            dout_all[place] = dout_ref[...]

    low_queries = q_ref[...]
    high, low = scaled_queries(low_queries)
    queries = jnp.concatenate([high, low, minus_in_three(lse_ref[...])], axis=0)
    low_dout = dout_all[here]
    dout = low_dout.astype(f32)
    centre = jnp.sum(dout * out_ref[...], axis=0, keepdims=True)
    douts = jnp.concatenate([low_dout, minus_in_three(centre)], axis=0)
    blank = jnp.zeros((block, HDIM), bf16)
    right = jnp.concatenate(
        [
            jnp.concatenate([low_queries.astype(f32).T.astype(bf16), blank], axis=1),
            jnp.concatenate([blank, dout.T.astype(bf16)], axis=1),
        ],
        axis=0,
    )

    def score(at):
        rows = slice(at * part, (at + 1) * part)
        return (
            dot(keys_ref[rows, : 2 * HDIM + 16], queries),
            dot(values_ref[rows, : HDIM + 16], douts),
        )

    now = score(0)
    grad_queries = None
    for at in range(count):
        following = score(at + 1) if at + 1 < count else None
        rows = slice(at * part, (at + 1) * part)
        soft = jnp.exp2(now[0])
        grads = (soft * now[1]).astype(bf16)
        added = dot(k_ref[:, rows], grads)
        grad_queries = added if grad_queries is None else grad_queries + added
        sums[rows] += dot(jnp.concatenate([grads, soft.astype(bf16)], axis=1), right)
        now = following

    def columns_of(place):
        return pl.ds(pl.multiple_of(order_ref[place] * block, block), block)

    columns = columns_of(here)
    dq_all[here] = turn_back(
        grad_queries * factor, cos_ref[:, columns], sin_ref[:, columns]
    ).astype(bf16)

    @pl.when(here == length // block - 1)
    def _():
        for place, dp_ref in enumerate(dp_refs):
            columns = columns_of(place)
            both = sums[columns].T
            dp_ref[:HDIM] = dq_all[place]
            dp_ref[HDIM : 2 * HDIM] = turn_back(
                both[:HDIM] * factor, cos_ref[:, columns], sin_ref[:, columns]
            ).astype(bf16)
            dp_ref[2 * HDIM :] = both[HDIM:].astype(bf16)


def attend_back(order, keys, values, qkv, douts, out, lse, cosine, sine, part=256):
    length = keys.shape[0]
    chips = len(douts)
    block = douts[0].shape[1]
    scores = length * length

    def whole(array):
        return pl.BlockSpec(array.shape, lambda i, order: (0, 0))

    return pl.pallas_call(
        functools.partial(attend_back_kernel, part=part),
        name="attend_back",
        grid_spec=pltpu.PrefetchScalarGridSpec(
            num_scalar_prefetch=1,
            grid=(chips,),
            in_specs=[
                whole(keys),
                whole(values),
                pl.BlockSpec((HDIM, block), lambda i, order: (0, order[i])),
                pl.BlockSpec((HDIM, length), lambda i, order: (1, 0)),
                pl.BlockSpec((HDIM, block), lambda i, order: (0, order[i])),
                pl.BlockSpec((1, block), lambda i, order: (0, order[i])),
                whole(cosine),
                whole(sine),
                *[whole(piece) for piece in douts],
            ],
            out_specs=[pl.BlockSpec((3 * HDIM, block), lambda i, order: (0, 0))] * chips,
            scratch_shapes=[
                pltpu.VMEM((length, 2 * HDIM), f32),
                pltpu.VMEM((chips, HDIM, block), bf16),
                pltpu.VMEM((chips, HDIM, block), bf16),
            ],
        ),
        out_shape=[jax.ShapeDtypeStruct((3 * HDIM, block), bf16)] * chips,
        compiler_params=pltpu.CompilerParams(vmem_limit_bytes=VMEM),
        cost_estimate=cost(5 * 4 * 2 * scores * HDIM, 8 << 20),
    )(order, keys, values, qkv, qkv, out, lse, cosine, sine, *douts)


def attend_out_kernel(order_ref, attended_ref, *rest):
    piece_refs, (mixed_ref, attn_ref) = rest[:-2], rest[-2:]
    half = attn_ref.shape[1] // 2
    at = 0
    for piece_ref in piece_refs:
        for place in range(piece_ref.shape[0]):
            rows = pl.ds(pl.multiple_of(order_ref[at] * HDIM, HDIM), HDIM)
            attn_ref[rows, :half] = piece_ref[place, :HDIM]
            attn_ref[rows, half:] = piece_ref[place, HDIM:]
            at += 1
    turned = attended_ref[...].astype(f32).T.astype(bf16)
    mixed_ref[...] = dot(turned, attn_ref[...]).astype(bf16)


def attend_out(order, attended, pieces):
    size, tokens = attended.shape
    width = 2 * size

    def whole(*shape):
        return pl.BlockSpec(shape, lambda i, order: (0,) * len(shape))

    return pl.pallas_call(
        attend_out_kernel,
        name="attend_out",
        grid_spec=pltpu.PrefetchScalarGridSpec(
            num_scalar_prefetch=1,
            grid=(1,),
            in_specs=[whole(size, tokens)]
            + [whole(*piece.shape[:2], width // 2) for piece in pieces],
            out_specs=[whole(tokens, width), whole(size, width)],
        ),
        out_shape=[
            jax.ShapeDtypeStruct((tokens, width), bf16),
            jax.ShapeDtypeStruct((size, width), bf16),
        ],
        compiler_params=pltpu.CompilerParams(vmem_limit_bytes=VMEM),
        cost_estimate=cost(2 * 2 * tokens * width * size, 4 << 20),
    )(order, attended, *pieces)


def feed_kernel(
    first_order, second_order, x_ref, ours_ref, theirs_ref, g_ref, *rest, firsts, seconds, axes
):
    weight_refs = []
    start = 0
    for size in (firsts, firsts, seconds, seconds):
        weight_refs.append(rest[start : start + size])
        start += size
    planes, lines, wide, beside = axes

    def put(grads, columns):
        size = grads.shape[0] // (planes * lines * wide)
        low = grads.astype(bf16)
        for plane in range(planes):
            for line in range(lines):
                for far in range(wide):
                    source = ((plane * lines + line) * wide + far) * size
                    target = ((line * wide + far) * planes + plane) * size
                    grads_ref[target : target + size, columns] = low[source : source + size]
    residual_ref, partial_ref, back_ref, grads_ref = rest[-13:-9]
    unit, unit_t, g_t, sum_out, sum_back = rest[-9:-4]
    gate_ref, up_ref, out_ref, rest_ref = rest[-4:]
    here = pl.program_id(0)
    last = pl.num_programs(0) - 1
    width = x_ref.shape[1]
    step = gate_ref.shape[1]

    def join(total, parts, order):
        at = 0
        for part in parts:
            size = part.shape[1]
            for place in range(part.shape[0]):
                total[pl.ds(pl.multiple_of(order[at] * size, size), size)] = part[place]
                at += 1

    def bend(gate, upward):
        cdf = 0.5 + 0.5 * lax.erf(gate * math.sqrt(0.5))
        slope = cdf + gate * jnp.exp(gate * gate * -0.5) * (1.0 / math.sqrt(2.0 * math.pi))
        bent = gate * cdf
        return bent, slope, (bent * upward).astype(bf16)

    @pl.when(here == 0)
    def _():
        residual = (
            x_ref[...].astype(f32) + ours_ref[...].astype(f32) + theirs_ref[...].astype(f32)
        )
        residual_ref[...] = residual
        normed = unit_rows(residual)[0]
        unit[...] = normed.astype(bf16)
        unit_t[...] = normed.T.astype(bf16)
        g_t[...] = g_ref[...].astype(f32).T.astype(bf16)
        join(rest_ref, weight_refs[3], second_order)
        few = rest_ref.shape[1] // 4
        both = dot(unit[...], rest_ref[...])
        grad = dot(g_ref[...], rest_ref[...])[:, 2 * few : 3 * few]
        bent, slope, active = bend(both[:, :few], both[:, few : 2 * few])
        grad_gate = (grad * both[:, few : 2 * few] * slope).astype(bf16)
        grad_up = (grad * bent).astype(bf16)
        blank = jnp.zeros_like(active)
        outs = jnp.concatenate([blank, blank, active, blank], axis=1)
        ins = jnp.concatenate([grad_gate, grad_up, blank, blank], axis=1)
        sum_out[...] = dot(outs, rest_ref[...], 1, 1)
        sum_back[...] = dot(ins, rest_ref[...], 1, 1)
        put(
            dot(unit_t[...], ins) + dot(g_t[...], outs),
            slice(grads_ref.shape[1] - 4 * few, grads_ref.shape[1]),
        )

    join(gate_ref, weight_refs[0], first_order)
    join(up_ref, weight_refs[1], first_order)
    join(out_ref, weight_refs[2], second_order)
    gate = dot(unit[...], gate_ref[...])
    upward = dot(unit[...], up_ref[...])
    grad = dot(g_ref[...], out_ref[...])
    bent, slope, active = bend(gate, upward)
    grad_gate = (grad * upward * slope).astype(bf16)
    grad_up = (grad * bent).astype(bf16)
    sum_out[...] += dot(active, out_ref[...], 1, 1)
    sum_back[...] += dot(grad_gate, gate_ref[...], 1, 1) + dot(grad_up, up_ref[...], 1, 1)
    count = grads_ref.shape[1] // step // 3
    for at, grads in enumerate(
        (dot(unit_t[...], grad_gate), dot(unit_t[...], grad_up), dot(g_t[...], active))
    ):
        place = pl.multiple_of(at * count * step + here * step, 128)
        put(grads, pl.ds(place, step))

    @pl.when(here == last)
    def _():
        partial_ref[...] = sum_out[...].astype(bf16)
        back_ref[...] = sum_back[...].astype(bf16)


def feed(first_order, second_order, x, ours, theirs, g, first, second, axes, step=256):
    tokens, width = x.shape
    start = width // 2 // step
    count = (first[0].shape[2] - width // 2) // step // 2
    rest = second[0].shape[2] - count * step
    columns = 3 * count * step + rest

    def whole(*shape):
        return pl.BlockSpec(shape, lambda i, one, two: (0, 0))

    def piece(arrays, size, at):
        return [
            pl.BlockSpec((*array.shape[:2], size), lambda i, one, two: (0, 0, at(i)))
            for array in arrays
        ]

    pair = jax.ShapeDtypeStruct((tokens, width), bf16)
    return pl.pallas_call(
        functools.partial(feed_kernel, firsts=len(first), seconds=len(second), axes=axes),
        name="feed",
        grid_spec=pltpu.PrefetchScalarGridSpec(
            num_scalar_prefetch=2,
            grid=(count,),
            in_specs=[whole(tokens, width)] * 4
            + piece(first, step, lambda i: start + i)
            + piece(first, step, lambda i: start + count + i)
            + piece(second, step, lambda i: i)
            + piece(second, rest, lambda i: count * step // rest),
            out_specs=[whole(tokens, width)] * 3 + [whole(width, columns)],
            scratch_shapes=[
                pltpu.VMEM((tokens, width), bf16),
                pltpu.VMEM((width, tokens), bf16),
                pltpu.VMEM((width, tokens), bf16),
                pltpu.VMEM((tokens, width), f32),
                pltpu.VMEM((tokens, width), f32),
                pltpu.VMEM((width, step), bf16),
                pltpu.VMEM((width, step), bf16),
                pltpu.VMEM((width, step), bf16),
                pltpu.VMEM((width, rest), bf16),
            ],
        ),
        out_shape=[
            jax.ShapeDtypeStruct((tokens, width), f32),
            pair,
            pair,
            jax.ShapeDtypeStruct((width, columns), bf16),
        ],
        compiler_params=pltpu.CompilerParams(vmem_limit_bytes=VMEM),
        cost_estimate=cost(2 * 9 * 2 * tokens * width * count * step, 24 << 20),
    )(first_order, second_order, x, ours, theirs, g, *first, *first, *second, *second)


def middle_back_kernel(
    core_ref, order_ref, line_ref, residual_ref, g_ref, ours_ref, theirs_ref, attn_ref,
    attended_ref, out_ours_ref, out_theirs_ref, layer_ref, residual_grad_ref, *rest, axes,
):
    planes, lines, wide, beside = axes
    dout_refs, grads_refs, (dout_all, grads_all) = rest[: -2 - lines], rest[-2 - lines : -2], rest[-2:]
    rows = layer_ref.shape[0]
    half = attn_ref.shape[0]
    own = pl.ds(pl.multiple_of(core_ref[0] * rows, rows), rows)
    layer_ref[...] = (
        residual_ref[own, :]
        + out_ours_ref[own, :].astype(f32)
        + out_theirs_ref[...].astype(f32)
    ).astype(bf16)
    unit, inverse = unit_rows(residual_ref[...])
    scaled = ours_ref[...].astype(f32) + theirs_ref[...].astype(f32)
    grad = g_ref[...].astype(f32) + unit_back(scaled, unit, inverse)
    low = grad.astype(bf16)
    residual_grad_ref[...] = grad
    dout_all[...] = dot(attn_ref[...], low, 1, 1).astype(bf16)
    for at, dout_ref in enumerate(dout_refs):
        dout_ref[...] = dout_all[pl.ds(pl.multiple_of(order_ref[at] * HDIM, HDIM), HDIM)]
    grads_all[...] = dot(attended_ref[...], low)
    few = HDIM // wide // beside
    for shift, grads_ref in enumerate(grads_refs):
        line = (line_ref[0] + shift) % lines
        blocks = [
            grads_all[pl.ds(pl.multiple_of((plane * lines + line) * HDIM, HDIM), HDIM)]
            for plane in range(planes)
        ]
        pieces = []
        for far in range(wide):
            for plane in range(planes):
                for near in range(beside):
                    start = (far * beside + near) * few
                    piece = blocks[plane][start : start + few]
                    pieces += [piece[:, :half], piece[:, half:]]
        grads_ref[...] = jnp.concatenate(pieces, axis=0).astype(bf16)


def middle_back(
    core, order, line, residual, g, ours, theirs, attn, attended, out_ours, out_theirs, axes
):
    tokens, width = residual.shape
    rows = tokens // 2
    half = width // 2
    chips = half // HDIM
    lines = axes[1]

    def whole(*shape):
        return pl.BlockSpec(shape, lambda i, core, order, line: (0,) * len(shape))

    return pl.pallas_call(
        functools.partial(middle_back_kernel, axes=axes),
        name="middle_back",
        grid_spec=pltpu.PrefetchScalarGridSpec(
            num_scalar_prefetch=3,
            grid=(1,),
            in_specs=[whole(tokens, width)] * 4
            + [whole(half, width), whole(half, tokens), whole(tokens, width), whole(rows, width)],
            out_specs=[whole(rows, width), whole(tokens, width)]
            + [whole(HDIM, tokens)] * chips
            + [whole(width // lines, half)] * lines,
            scratch_shapes=[pltpu.VMEM((half, tokens), bf16), pltpu.VMEM((half, width), f32)],
        ),
        out_shape=[
            jax.ShapeDtypeStruct((rows, width), bf16),
            jax.ShapeDtypeStruct((tokens, width), f32),
        ]
        + [jax.ShapeDtypeStruct((HDIM, tokens), bf16)] * chips
        + [jax.ShapeDtypeStruct((width // lines, half), bf16)] * lines,
        compiler_params=pltpu.CompilerParams(vmem_limit_bytes=VMEM),
        cost_estimate=cost(2 * 2 * 2 * tokens * width * half, 16 << 20),
    )(core, order, line, residual, g, ours, theirs, attn, attended, out_ours, out_theirs)


def hidden_back_kernel(order_ref, core_ref, w_ref, *rest):
    dp_refs, (own_ref, other_ref, stacked) = rest[:-3], rest[-3:]
    for place, dp_ref in enumerate(dp_refs):
        size = dp_ref.shape[0]
        stacked[pl.ds(pl.multiple_of(order_ref[place] * size, 64), size)] = dp_ref[...]
    rows = own_ref.shape[0]
    flat = dot(w_ref[...], stacked[...])
    first = flat[:, :rows].T
    second = flat[:, rows:].T
    zero = core_ref[0] == 0
    own_ref[...] = jnp.where(zero, first, second)
    other_ref[...] = jnp.where(zero, second, first).astype(bf16)


def hidden_back(order, core, weights, pieces):
    width, columns = weights.shape
    rows = pieces[0].shape[1] // 2

    def whole(*shape):
        return pl.BlockSpec(shape, lambda i, order, core: (0,) * len(shape))

    return pl.pallas_call(
        hidden_back_kernel,
        name="hidden_back",
        grid_spec=pltpu.PrefetchScalarGridSpec(
            num_scalar_prefetch=2,
            grid=(1,),
            in_specs=[whole(width, columns)] + [whole(*pieces[0].shape)] * len(pieces),
            out_specs=[whole(rows, width)] * 2,
            scratch_shapes=[pltpu.VMEM((columns, 2 * rows), bf16)],
        ),
        out_shape=[
            jax.ShapeDtypeStruct((rows, width), f32),
            jax.ShapeDtypeStruct((rows, width), bf16),
        ],
        compiler_params=pltpu.CompilerParams(vmem_limit_bytes=VMEM),
        cost_estimate=cost(2 * 2 * 2 * rows * width * columns, 8 << 20),
    )(order, core, weights, *pieces)


def head_grad_kernel(order_ref, owner_ref, unit_ref, *rest, owners):
    dp_refs, out_refs, out_all = rest[: -1 - owners], rest[-1 - owners : -1], rest[-1]
    block = dp_refs[0].shape[1]
    total = None
    for place, dp_ref in enumerate(dp_refs):
        rows = pl.ds(pl.multiple_of(order_ref[place] * block, block), block)
        added = dot(dp_ref[...], unit_ref[rows])
        total = added if total is None else total + added
    for at in range(owners):
        out_all[at] = total[:, at * 128 : (at + 1) * 128].astype(bf16)
    for at, out_ref in enumerate(out_refs):
        out_ref[...] = out_all[owner_ref[at]]


def head_grad(order, owner_order, unit_all, pieces):
    length, width = unit_all.shape
    owners = width // 128
    size = pieces[0].shape[0]

    def whole(*shape):
        return pl.BlockSpec(shape, lambda i, order, owner: (0,) * len(shape))

    return pl.pallas_call(
        functools.partial(head_grad_kernel, owners=owners),
        name="head_grad",
        grid_spec=pltpu.PrefetchScalarGridSpec(
            num_scalar_prefetch=2,
            grid=(1,),
            in_specs=[whole(length, width)] + [whole(*pieces[0].shape)] * len(pieces),
            out_specs=[whole(size, 128)] * owners,
            scratch_shapes=[pltpu.VMEM((owners, size, 128), bf16)],
        ),
        out_shape=[jax.ShapeDtypeStruct((size, 128), bf16)] * owners,
        compiler_params=pltpu.CompilerParams(vmem_limit_bytes=VMEM),
        cost_estimate=cost(2 * 2 * length * width * size, 10 << 20),
    )(order, owner_order, unit_all, *pieces)


def adam(weight, gradient, first, second, rate):
    first = BETA_FIRST * first + (1.0 - BETA_FIRST) * gradient
    second = BETA_SECOND * second + (1.0 - BETA_SECOND) * gradient * gradient
    first_hat = first / (1.0 - BETA_FIRST**STEP)
    second_hat = second / (1.0 - BETA_SECOND**STEP)
    weight = weight - rate * (first_hat / (jnp.sqrt(second_hat) + EPSILON) + DECAY * weight)
    return (weight, first, second)


def adam_into(refs, weight, gradient, first, second, rate):
    for ref, value in zip(refs, adam(weight, gradient, first, second, rate)):
        ref[...] = value


def rounded_in_kernel(values):
    return values.astype(bf16).astype(f32)


def adam_in_kernel(
    grads_ref, gain_ref, w_ref, m_ref, v_ref, new_w, new_m, new_v, gain_grad, *, rate
):
    width = m_ref.shape[1] // 2
    main = width // 256 * 128
    few = width // 2 - main
    columns = []
    for at in range(2):
        for core in range(2):
            place = at * main
            columns.append(grads_ref[core, :, place : place + main].astype(f32))
        for core in range(2):
            rest = grads_ref[core, :, 3 * main : 3 * main + 128].astype(f32)
            columns.append(rest[:, at * few : (at + 1) * few])
    grads = jnp.concatenate(columns, axis=1)
    weight = w_ref[...]
    gain_grad[...] = jnp.sum(grads * rounded_in_kernel(weight), axis=1, keepdims=True)
    adam_into(
        (new_w, new_m, new_v), weight, grads * gain_ref[...], m_ref[...], v_ref[...], rate
    )


def adam_in(grads, gain, weight, first, second, rate):
    rows, columns = weight.shape
    steps = grads.shape[0] // 2
    block = pl.BlockSpec((rows // steps, columns), lambda i: (i, 0))
    column = pl.BlockSpec((rows // steps, 1), lambda i: (i, 0))
    same = jax.ShapeDtypeStruct((rows, columns), f32)
    return pl.pallas_call(
        functools.partial(adam_in_kernel, rate=rate),
        name="adam_in",
        grid=(steps,),
        in_specs=[pl.BlockSpec((2,) + grads.shape[1:], lambda i: (i, 0, 0)), column]
        + [block] * 3,
        out_specs=[block] * 3 + [column],
        out_shape=[same] * 3 + [jax.ShapeDtypeStruct((rows, 1), f32)],
        compiler_params=pltpu.CompilerParams(vmem_limit_bytes=VMEM),
        cost_estimate=cost(rows * columns * 20, rows * columns * 26),
    )(grads, gain, weight, first, second)


def adam_rest_kernel(grads_ref, *refs, rates):
    attn, out, new_attn, new_out = refs[:3], refs[3:6], refs[6:9], refs[9:]
    chips = grads_ref.shape[0] // 2
    hidden = out[0].shape[0]
    main = hidden // 256 * 128
    few = hidden // 2 - main
    pieces = []
    for core in range(2):
        for chip in range(chips):
            piece = grads_ref[2 * chip + core, :, 3 * main + 128 :].astype(f32)
            pieces.append(jnp.concatenate([piece[:8], piece[8:]], axis=1))
    grads = jnp.concatenate(pieces, axis=0)
    adam_into(new_attn, attn[0][...], grads, attn[1][...], attn[2][...], rates[0])
    for core in range(2):
        columns = jnp.concatenate(
            [grads_ref[2 * chip + core, :, 2 * main : 3 * main] for chip in range(chips)], axis=0
        )
        rest = jnp.concatenate(
            [grads_ref[2 * chip + core, :, 3 * main : 3 * main + 128] for chip in range(chips)],
            axis=0,
        )
        for rows, grads in (
            (slice(core * main, (core + 1) * main), columns.astype(f32).T),
            (
                slice(2 * main + core * few, 2 * main + (core + 1) * few),
                rest.astype(f32).T[2 * few : 3 * few],
            ),
        ):
            new = adam(out[0][rows], grads, out[1][rows], out[2][rows], rates[1])
            for ref, value in zip(new_out, new):
                ref[rows] = value


def adam_rest(grads, attn, out, rates):
    def whole(array):
        return pl.BlockSpec(array.shape, lambda i: (0,) * array.ndim)

    arrays = (*attn, *out)
    return pl.pallas_call(
        functools.partial(adam_rest_kernel, rates=rates),
        name="adam_rest",
        grid=(1,),
        in_specs=[whole(array) for array in (grads, *arrays)],
        out_specs=[whole(array) for array in arrays],
        out_shape=[jax.ShapeDtypeStruct(array.shape, f32) for array in arrays],
        compiler_params=pltpu.CompilerParams(vmem_limit_bytes=VMEM),
        cost_estimate=cost(attn[0].size * 60, 14 << 20),
    )(grads, *arrays)


def adam_qkv_kernel(order_ref, *refs, rate):
    grads_refs, (gain_ref, w_ref, m_ref, v_ref, new_w, new_m, new_v, gain_grad, joined) = (
        refs[:-9], refs[-9:]
    )
    here = pl.program_id(0)
    rows = pl.ds(pl.multiple_of(here * HDIM, HDIM), HDIM)
    at = 0
    for grads_ref in grads_refs:
        for place in range(grads_ref.shape[0]):
            head = pl.ds(pl.multiple_of(order_ref[at] * HDIM, HDIM), HDIM)
            joined[head] = grads_ref[place, rows].astype(f32)
            at += 1
    grads = joined[...].T
    weight = w_ref[...]
    added = jnp.sum(grads * rounded_in_kernel(weight), axis=1, keepdims=True)
    gain_grad[...] = added + jnp.where(here == 0, 0.0, gain_grad[...])
    adam_into(
        (new_w, new_m, new_v), weight, grads * gain_ref[...], m_ref[...], v_ref[...], rate
    )


def adam_qkv(order, grads, gain, weight, first, second, rate):
    rows, columns = weight.shape
    block = pl.BlockSpec((rows, columns // 3), lambda i, order: (0, i))
    column = pl.BlockSpec((rows, 1), lambda i, order: (0, 0))
    same = jax.ShapeDtypeStruct((rows, columns), f32)
    return pl.pallas_call(
        functools.partial(adam_qkv_kernel, rate=rate),
        name="adam_qkv",
        grid_spec=pltpu.PrefetchScalarGridSpec(
            num_scalar_prefetch=1,
            grid=(3,),
            in_specs=[pl.BlockSpec((piece.shape[0], 3 * HDIM, 128), lambda i, order: (0, 0, 0)) for piece in grads]
            + [column]
            + [block] * 3,
            out_specs=[block] * 3 + [column],
            scratch_shapes=[pltpu.VMEM((columns // 3, rows), f32)],
        ),
        out_shape=[same] * 3 + [jax.ShapeDtypeStruct((rows, 1), f32)],
        compiler_params=pltpu.CompilerParams(vmem_limit_bytes=VMEM),
        cost_estimate=cost(rows * columns * 20, rows * columns * 26),
    )(order, *grads, gain, weight, first, second)


def ring(axis, shift):
    size = lax.axis_size(axis)
    return [(at, (at + shift) % size) for at in range(size)]


def gather_first_step(planes_first, lines_first):
    swapped = lax.ppermute(planes_first, "zh", SWAP)
    others = [
        lax.ppermute(lines_first, "y", ring("y", shift)) for shift in range(1, lax.axis_size("y"))
    ]
    return jnp.stack([planes_first, swapped]), jnp.stack([lines_first, *others])


def gather_second_step(first, second):
    firsts = [first] + [
        lax.ppermute(first, "y", ring("y", shift)) for shift in range(1, lax.axis_size("y"))
    ]
    return firsts, [second, lax.ppermute(second, "zh", SWAP)]


def shards(
    tokens,
    positions,
    cotangent,
    weight_qkv,
    weight_attn,
    weight_in,
    weight_out,
    norm_gains,
    first_qkv,
    first_attn,
    first_in,
    first_out,
    first_gains,
    second_qkv,
    second_attn,
    second_in,
    second_out,
    second_gains,
):
    rows, width = tokens.shape[1:]
    shard_rows = weight_qkv.shape[1]
    heads = width // HDIM
    hidden = weight_out.shape[1]
    core = lax.axis_index("c")
    mine = lax.axis_index(CTX)
    chip = lax.axis_index(CHIPS)
    chips = lax.axis_size(CHIPS)
    owners = lax.axis_size(FSDP)
    length = rows * chips * 2
    main = hidden // 256 * 128
    few = hidden // 2 - main
    core_at = core.reshape(1).astype(jnp.int32)
    axes = (lax.axis_size("zh"), lax.axis_size("y"), lax.axis_size("x"), lax.axis_size("zl"))
    offsets = [(far, near) for far in range(lax.axis_size("x")) for near in range(2)]
    across, beside = lax.axis_index("x"), lax.axis_index("zl")
    wide = lax.axis_size("x")

    def chips_at(sign):
        places = [(across + sign * far) % wide * 2 + (beside ^ near) for far, near in offsets]
        return jnp.stack(places).astype(jnp.int32)

    local = tokens[0]
    extra = 16
    high, low = positions[0] // 128, positions[0] % 128
    places_row = jnp.concatenate([high, low, jnp.zeros((width - 2 * rows,), jnp.int32)])
    places_rows = jnp.concatenate(
        [places_row[None], jnp.zeros((extra - 1, width), jnp.int32)], axis=0
    ).astype(bf16)
    sequence = lax.all_gather(
        jnp.concatenate([local, places_rows], axis=0), CTX, axis=0, tiled=True
    )
    first_part, second_part, head_part, half_heads = prepare(
        jnp.stack([core, chip]).astype(jnp.int32),
        norm_gains[0],
        weight_qkv[0],
        weight_attn[0],
        weight_in[0],
        weight_out[0],
    )
    first_joined, second_joined = gather_first_step(first_part, second_part)
    head_weights = lax.all_to_all(
        jnp.broadcast_to(head_part, (owners, *head_part.shape)), FSDP, 0, 0, tiled=True
    )
    first_pieces, second_pieces = gather_second_step(first_joined, second_joined)
    sequence, *_ = lax.optimization_barrier(
        (sequence, first_joined, second_joined, head_weights)
    )
    lines = lax.axis_size("y")
    plane, line = lax.axis_index("zh"), lax.axis_index("y")
    first_order = jnp.stack(
        [(plane ^ far) * lines + (line - shift) % lines for shift in range(lines) for far in range(2)]
    ).astype(jnp.int32)
    second_order = jnp.stack(
        [(plane ^ far) * lines + (line - shift) % lines for far in range(2) for shift in range(lines)]
    ).astype(jnp.int32)

    def in_order(ours, theirs):
        first = jnp.where(core == 0, ours, theirs)
        second = jnp.where(core == 0, theirs, ours)
        return jnp.concatenate([first, second], axis=0)

    def swap(array):
        return lax.ppermute(array, "c", SWAP)

    gradient = in_order(cotangent[0], swap(cotangent[0]))

    freqs = jnp.exp(jnp.arange(HDIM // 2, dtype=f32) * (-2.0 * math.log(ROPE_BASE) / HDIM))
    by_device = sequence.reshape(2 * chips, rows + extra, width)[:, rows]
    by_device = by_device.astype(f32)
    places = by_device[:, :rows] * 128.0 + by_device[:, rows : 2 * rows]
    angles = freqs[:, None] * places.reshape(1, length)
    cosine = jnp.cos(angles)
    sine = jnp.sin(angles)
    unit_all, qkv, keys, values = project(sequence, head_weights, cosine, sine)
    keys, *second_pieces, half_heads = lax.optimization_barrier(
        (keys, *second_pieces, half_heads)
    )
    mat_qkv = lax.all_gather(half_heads, FSDP, axis=0, tiled=True)
    low_out, out, lse = attend(keys, qkv, chips)
    attended = lax.all_to_all(low_out, CHIPS, 0, 0, tiled=True)
    attended = attended.reshape(heads // 2 * HDIM, 2 * rows)
    mixed, mat_attn = attend_out(first_order, attended, first_pieces)
    current = lax.dynamic_slice_in_dim(
        sequence, chip * 2 * (rows + extra), 2 * (rows + extra), 0
    ).reshape(2, rows + extra, width)[:, :rows].reshape(2 * rows, width)
    residual, partial, back, grads = feed(
        first_order, second_order, current, mixed, swap(mixed), gradient, first_pieces,
        second_pieces, axes,
    )
    arrived = lax.all_to_all(grads, "y", 0, 0, tiled=True)

    def move(pieces, sign):
        moved = [pieces[0]]
        for (far, near), piece in list(zip(offsets, pieces))[1:]:
            pairs = [
                (at, (at // 2 + sign * far) % wide * 2 + (at % 2 ^ near)) for at in range(chips)
            ]
            moved.append(lax.ppermute(piece, CHIPS, pairs))
        return moved

    ahead, behind = chips_at(1), chips_at(-1)
    residual, mat_qkv = lax.optimization_barrier((residual, mat_qkv))
    theirs = swap(lax.dynamic_slice_in_dim(partial, (1 - core) * rows, rows, 0))
    layer_out, residual_grad, *pieces = middle_back(
        core_at, ahead, line.reshape(1).astype(jnp.int32), residual, gradient, back, swap(back),
        mat_attn, attended, partial, theirs, axes,
    )
    dout_pieces, attn_pieces = pieces[:chips], pieces[chips:]

    douts = move(dout_pieces, 1)
    attn_arrived = attn_pieces[:1] + [
        lax.ppermute(piece, "y", ring("y", shift))
        for shift, piece in list(enumerate(attn_pieces))[1:]
    ]
    pieces = attend_back(behind, keys, values, qkv, douts, out, lse, cosine, sine)
    moved = move(pieces, -1)
    owner_places = [(far, shift) for far in range(2) for shift in range(lines)]
    owner_order = jnp.stack(
        [(plane ^ far) * lines + (line + shift) % lines for far, shift in owner_places]
    ).astype(jnp.int32)
    head_parts = head_grad(behind, owner_order, unit_all, pieces)
    moved = lax.optimization_barrier((*moved, *head_parts))[:chips]
    own_hidden, other_hidden = hidden_back(ahead, core_at, mat_qkv, moved)
    arrived, own_hidden = lax.optimization_barrier((arrived, own_hidden))
    grad_hidden = own_hidden + swap(other_hidden).astype(f32)
    unit_in, scale_in = unit_rows(local.astype(f32))
    own_residual = lax.dynamic_slice_in_dim(residual_grad, core * rows, rows, 0)
    tokens_grad = (own_residual + unit_back(grad_hidden, unit_in, scale_in))[None]

    def total(arrays):
        return sum(array.astype(f32) for array in arrays).astype(bf16)

    first_sum = total([arrived[at * width // lines : (at + 1) * width // lines] for at in range(lines)])
    first_sum = jnp.concatenate([first_sum, total(attn_arrived)], axis=1)
    arrived = lax.all_to_all(first_sum, ("x", "zh", "zl"), 0, 0, tiled=True)
    head_arrived = [head_parts[0]]
    for (far, shift), piece in list(zip(owner_places, head_parts))[1:]:
        pairs = [
            (at, (at // lines ^ far) * lines + (at % lines + shift) % lines) for at in range(owners)
        ]
        head_arrived.append(lax.ppermute(piece, FSDP, pairs))
    head_own = total(head_arrived)[None]
    arrived, head_own = lax.optimization_barrier((arrived, head_own))
    arrived = arrived.reshape(2 * chips, shard_rows // chips, -1)
    second_sum = jnp.sum(arrived.astype(f32), axis=0).astype(bf16)
    all_grads = lax.all_gather(second_sum, CTX, axis=0, tiled=False)

    head_pair = jnp.concatenate([head_own, swap(head_own)], axis=0)
    head_four = jnp.concatenate([head_pair, lax.ppermute(head_pair, "zl", SWAP)], axis=0)
    head_grads = [head_four] + [
        lax.ppermute(head_four, "x", ring("x", shift)) for shift in range(1, wide)
    ]
    head_order = jnp.stack(
        [
            (across - shift) % wide * 4 + (beside ^ near) * 2 + (core ^ other)
            for shift in range(wide)
            for near in range(2)
            for other in range(2)
        ]
    ).astype(jnp.int32)

    rates = (
        width ** (-0.5),
        max(1, 3 * width // length) ** (-0.5),
        width ** (-0.5),
        hidden ** (-0.5),
    )
    columns_of_gains = norm_gains[0].astype(bf16).astype(f32).T
    *new_in, gain_second = adam_in(
        all_grads, columns_of_gains[:, 1:], weight_in[0], first_in[0], second_in[0], rates[2]
    )
    rest = adam_rest(
        all_grads,
        (weight_attn[0], first_attn[0], second_attn[0]),
        (weight_out[0], first_out[0], second_out[0]),
        (rates[1], rates[3]),
    )
    *new_qkv, gain_first = adam_qkv(
        head_order, head_grads, columns_of_gains[:, :1], weight_qkv[0], first_qkv[0], second_qkv[0], rates[0]
    )
    gain_grads = jnp.concatenate([gain_first, gain_second], axis=1).T
    new_gains = adam(norm_gains[0], gain_grads, first_gains[0], second_gains[0], GAIN_RATE)
    updated = (new_qkv, rest[:3], new_in, rest[3:], new_gains)
    return (
        layer_out[None],
        tokens_grad,
        *[updated[member][0][None] for member in range(5)],
        *[updated[member][1][None] for member in range(5)],
        *[updated[member][2][None] for member in range(5)],
    )


def solution(mesh):
    split = Mesh(mesh.devices.reshape(4, 2, 2, 2, 4), ("x", "zl", "c", "zh", "y"))
    by_row = P(None, FSDP, None)
    by_column = P(None, None, FSDP)
    weights = (by_row, by_row, by_row, by_column, by_column)
    by_token = P(FSDP, CTX, None)
    return jax.shard_map(
        shards,
        mesh=split,
        in_specs=(by_token, P(FSDP, CTX), by_token) + weights * 3,
        out_specs=(by_token, by_token) + weights * 3,
        check_vma=False,
    )
```

```python
import functools
import math

import jax
import jax.numpy as jnp
from jax import lax
from jax.experimental import pallas as pl
from jax.experimental.pallas import tpu as pltpu
from jax.sharding import Mesh, PartitionSpec as P

HDIM = 64
STEP = 10
BETA_FIRST = 0.5
BETA_SECOND = 0.5
EPSILON = 1e-08
DECAY = 0.01
NORM_EPS = 1e-05
ROPE_BASE = 160000.0
GAIN_RATE = 0.6
LOG2E = math.log2(math.e)
f32 = jnp.float32
bf16 = jnp.bfloat16

CHIPS = ("x", "zl")
CTX = ("x", "zl", "c")
FSDP = ("zh", "y")
SWAP = [(0, 1), (1, 0)]
VMEM = 60 << 20


def dot(left, right, left_dim=1, right_dim=0):
    return lax.dot_general(
        left, right, (((left_dim,), (right_dim,)), ((), ())), preferred_element_type=f32
    )


def cost(flops, moved):
    return pl.CostEstimate(flops=flops, bytes_accessed=moved, transcendentals=0)


def unit_rows(values):
    average = jnp.mean(values, axis=-1, keepdims=True)
    centered = values - average
    spread = jnp.mean(centered * centered, axis=-1, keepdims=True)
    inverse = lax.rsqrt(spread + NORM_EPS)
    return centered * inverse, inverse


def unit_back(scaled, unit, inverse):
    first_mean = jnp.mean(scaled, axis=-1, keepdims=True)
    second_mean = jnp.mean(scaled * unit, axis=-1, keepdims=True)
    return inverse * (scaled - first_mean - unit * second_mean)


def prepare_kernel(
    place_ref, gains_ref, qkv_ref, attn_ref, in_ref, out_ref,
    first_ref, second_ref, head_ref, heads_ref,
):
    core, chip = place_ref[0], place_ref[1]
    rows = qkv_ref.shape[0]
    width = attn_ref.shape[1]
    hidden = out_ref.shape[0]
    main = hidden // 256 * 128
    few = hidden // 2 - main
    half = width // 2
    low_gains = gains_ref[...].astype(bf16).astype(f32)
    columns = jnp.concatenate([low_gains, jnp.zeros((6, rows), f32)], axis=0).T
    gain_first, gain_second = columns[:, 0:1], columns[:, 1:2]

    def pick(array):
        size = array.shape[1] // 2
        return jnp.where(core == 0, array[:, :size], array[:, size:])

    def scaled(values, gain):
        return (values.astype(bf16).astype(f32) * gain).astype(bf16)

    attn_rows = attn_ref[pl.ds(pl.multiple_of(core * HDIM, HDIM), HDIM)].astype(bf16)
    first_ref[:HDIM, :half] = attn_rows[:, :half]
    first_ref[HDIM:, :half] = attn_rows[:, half:]
    first_ref[:, half : half + main] = scaled(pick(in_ref[:, : 2 * main]), gain_second)
    first_ref[:, half + main :] = scaled(pick(in_ref[:, hidden : hidden + 2 * main]), gain_second)
    out_rows = out_ref[pl.ds(pl.multiple_of(core * main, 128), main)]
    second_ref[:, :main] = out_rows.T.astype(bf16)
    odd_out = out_ref[2 * main :].T
    odd = [
        scaled(pick(in_ref[:, 2 * main : hidden]), gain_second),
        scaled(pick(in_ref[:, hidden + 2 * main :]), gain_second),
        pick(odd_out).astype(bf16),
        jnp.zeros((rows, few), bf16),
    ]
    second_ref[:, main:] = jnp.concatenate(odd, axis=1)
    pieces = []
    for at in range(width // 128):
        for part in range(3):
            start = part * width + at * 128
            pieces.append(scaled(pick(qkv_ref[:, start : start + 128]), gain_first))
    heads_ref[...] = jnp.concatenate(pieces, axis=1)
    own = []
    for part in range(3):
        start = pl.multiple_of(part * width + chip * 128, 128)
        own.append(scaled(pick(qkv_ref[:, pl.ds(start, 128)]), gain_first).astype(f32))
    own.append(jnp.zeros((rows, HDIM), f32))
    head_ref[...] = jnp.concatenate(own, axis=1).T[: 3 * HDIM].astype(bf16)


def prepare(place, gains, qkv, attn, weight_in, weight_out):
    rows, width = attn.shape
    hidden = weight_out.shape[0]
    main = hidden // 256 * 128
    arrays = (gains, qkv, attn, weight_in, weight_out)
    shapes = [
        (rows, width // 2 + 2 * main),
        (rows, main + 4 * (hidden // 2 - main)),
        (3 * HDIM, rows),
        (rows, 3 * width // 2),
    ]

    def whole(shape):
        return pl.BlockSpec(shape, lambda i, place: (0, 0))

    return pl.pallas_call(
        prepare_kernel,
        name="prepare",
        grid_spec=pltpu.PrefetchScalarGridSpec(
            num_scalar_prefetch=1,
            grid=(1,),
            in_specs=[whole(array.shape) for array in arrays],
            out_specs=[whole(shape) for shape in shapes],
        ),
        out_shape=[jax.ShapeDtypeStruct(shape, bf16) for shape in shapes],
        compiler_params=pltpu.CompilerParams(vmem_limit_bytes=VMEM),
        cost_estimate=cost(rows * width * 60, 10 << 20),
    )(place, *arrays)


def project_kernel(x_ref, w_ref, cos_ref, sin_ref, unit_ref, qkv_ref, keys_ref, values_ref, w_all):
    half = HDIM // 2
    rows = cos_ref.shape[1]

    @pl.when(pl.program_id(0) == 0)
    def _():
        for part in range(w_ref.shape[0]):
            w_all[:, part * 128 : (part + 1) * 128] = w_ref[part]

    each = rows // 2
    extra = x_ref.shape[0] // 2 - each
    tokens = jnp.concatenate(
        [x_ref[:each].astype(f32), x_ref[each + extra : 2 * each + extra].astype(f32)], axis=0
    )
    unit = unit_rows(tokens)[0].astype(bf16)
    unit_ref[...] = unit
    mixed = dot(w_all[...], unit, 1, 1)
    cosine = cos_ref[...]
    sine = sin_ref[...]

    def turn(one, two):
        return jnp.concatenate([one * cosine - two * sine, two * cosine + one * sine], axis=0)

    queries = turn(mixed[:half], mixed[half:HDIM])
    keys = turn(mixed[HDIM : HDIM + half], mixed[HDIM + half : 2 * HDIM])
    values = mixed[2 * HDIM :]
    qkv_ref[...] = jnp.concatenate([queries, keys, values], axis=0).astype(bf16)
    key_rows = keys.T.astype(bf16)
    value_rows = values.T.astype(bf16)
    ones = jnp.where(lax.broadcasted_iota(jnp.int32, (rows, 128), 1) < 3, 1.0, 0.0).astype(bf16)
    keys_ref[...] = jnp.concatenate([key_rows, key_rows, ones], axis=1)
    values_ref[...] = jnp.concatenate([value_rows, ones[:, :HDIM]], axis=1)


def project(tokens, weights, cosine, sine, block=512):
    width = tokens.shape[1]
    length = cosine.shape[1]
    steps = length // block
    return pl.pallas_call(
        project_kernel,
        name="project",
        grid=(steps,),
        in_specs=[
            pl.BlockSpec((tokens.shape[0] // steps, width), lambda i: (i, 0)),
            pl.BlockSpec(weights.shape, lambda i: (0, 0, 0)),
            pl.BlockSpec((HDIM // 2, block), lambda i: (0, i)),
            pl.BlockSpec((HDIM // 2, block), lambda i: (0, i)),
        ],
        out_specs=[
            pl.BlockSpec((block, width), lambda i: (i, 0)),
            pl.BlockSpec((3 * HDIM, block), lambda i: (0, i)),
            pl.BlockSpec((block, 256), lambda i: (i, 0)),
            pl.BlockSpec((block, 128), lambda i: (i, 0)),
        ],
        out_shape=[
            jax.ShapeDtypeStruct((length, width), bf16),
            jax.ShapeDtypeStruct((3 * HDIM, length), bf16),
            jax.ShapeDtypeStruct((length, 256), bf16),
            jax.ShapeDtypeStruct((length, 128), bf16),
        ],
        scratch_shapes=[pltpu.VMEM((3 * HDIM, width), bf16)],
        compiler_params=pltpu.CompilerParams(vmem_limit_bytes=VMEM),
        cost_estimate=cost(2 * length * width * 4 * HDIM, 22 << 20),
    )(tokens, weights, cosine, sine)


def scaled_queries(queries):
    scaled = queries.astype(f32) * (LOG2E / math.sqrt(HDIM))
    high = scaled.astype(bf16)
    low = (scaled - high.astype(f32)).astype(bf16)
    return high, low


def attend_kernel(keys_ref, q_ref, v_ref, low_ref, out_ref, lse_ref, v_ones, *, part):
    length = keys_ref.shape[0]
    count = length // part

    @pl.when(pl.program_id(0) == 0)
    def _():
        v_ones[:HDIM] = v_ref[...]
        v_ones[HDIM:] = jnp.where(
            lax.broadcasted_iota(jnp.int32, (16, length), 0) < 1, 1.0, 0.0
        ).astype(bf16)

    queries = jnp.concatenate(scaled_queries(q_ref[...]), axis=0)

    def score(at):
        return dot(keys_ref[at * part : (at + 1) * part, : 2 * HDIM], queries)

    scores = score(0)
    highest = total = None
    for at in range(count):
        following = score(at + 1) if at + 1 < count else None
        peak = jnp.max(scores, axis=0, keepdims=True)
        raised = peak if highest is None else jnp.maximum(highest, peak)
        soft = jnp.exp2(scores - raised).astype(bf16)
        added = dot(v_ones[:, at * part : (at + 1) * part], soft)
        total = added if total is None else total * jnp.exp2(highest - raised) + added
        highest = raised
        scores = following
    summed = total[HDIM : HDIM + 1]
    result = total[:HDIM] / summed
    out_ref[...] = result
    lse_ref[...] = highest + jnp.log2(summed)
    step = low_ref.shape[2]
    for at in range(low_ref.shape[0]):
        low_ref[at] = result[:, at * step : (at + 1) * step].astype(bf16)


def attend(keys, qkv, chips, block=1024, part=512):
    length = keys.shape[0]
    return pl.pallas_call(
        functools.partial(attend_kernel, part=part),
        name="attend",
        grid=(length // block,),
        in_specs=[
            pl.BlockSpec(keys.shape, lambda i: (0, 0)),
            pl.BlockSpec((HDIM, block), lambda i: (0, i)),
            pl.BlockSpec((HDIM, length), lambda i: (2, 0)),
        ],
        out_specs=[
            pl.BlockSpec((block * chips // length, HDIM, length // chips), lambda i: (i, 0, 0)),
            pl.BlockSpec((HDIM, block), lambda i: (0, i)),
            pl.BlockSpec((1, block), lambda i: (0, i)),
        ],
        out_shape=[
            jax.ShapeDtypeStruct((chips, HDIM, length // chips), bf16),
            jax.ShapeDtypeStruct((HDIM, length), f32),
            jax.ShapeDtypeStruct((1, length), f32),
        ],
        scratch_shapes=[pltpu.VMEM((HDIM + 16, length), bf16)],
        compiler_params=pltpu.CompilerParams(vmem_limit_bytes=VMEM),
        cost_estimate=cost(2 * 4 * 2 * length * length * HDIM, 6 << 20),
    )(keys, qkv, qkv)


def minus_in_three(values):
    rows = values.shape[1]
    at = lax.broadcasted_iota(jnp.int32, (16, rows), 0)
    high = (-values).astype(bf16).astype(f32)
    rest = -values - high
    middle = rest.astype(bf16).astype(f32)
    low = rest - middle
    stacked = jnp.where(at == 0, high, jnp.where(at == 1, middle, jnp.where(at == 2, low, 0.0)))
    return stacked.astype(bf16)


def attend_back_kernel(
    order_ref,
    keys_ref,
    values_ref,
    q_ref,
    k_ref,
    out_ref,
    lse_ref,
    cos_ref,
    sin_ref,
    *rest,
    part,
):
    count = (len(rest) - 3) // 2
    dout_refs, dp_refs, (sums, dq_all, dout_all) = rest[:count], rest[count:-3], rest[-3:]
    half = HDIM // 2
    here = pl.program_id(0)
    length = keys_ref.shape[0]
    block = q_ref.shape[1]
    count = length // part
    factor = HDIM ** (-0.5)

    def turn_back(grads, cosine, sine):
        low = grads.astype(bf16).astype(f32)
        one, two = low[:half], low[half:]
        return jnp.concatenate([one * cosine + two * sine, two * cosine - one * sine], axis=0)

    @pl.when(here == 0)
    def _():
        sums[...] = jnp.zeros_like(sums)
        for place, dout_ref in enumerate(dout_refs):
            dout_all[place] = dout_ref[...]

    low_queries = q_ref[...]
    high, low = scaled_queries(low_queries)
    queries = jnp.concatenate([high, low, minus_in_three(lse_ref[...])], axis=0)
    low_dout = dout_all[here]
    dout = low_dout.astype(f32)
    centre = jnp.sum(dout * out_ref[...], axis=0, keepdims=True)
    douts = jnp.concatenate([low_dout, minus_in_three(centre)], axis=0)
    blank = jnp.zeros((block, HDIM), bf16)
    right = jnp.concatenate(
        [
            jnp.concatenate([low_queries.astype(f32).T.astype(bf16), blank], axis=1),
            jnp.concatenate([blank, dout.T.astype(bf16)], axis=1),
        ],
        axis=0,
    )

    def score(at):
        rows = slice(at * part, (at + 1) * part)
        return (
            dot(keys_ref[rows, : 2 * HDIM + 16], queries),
            dot(values_ref[rows, : HDIM + 16], douts),
        )

    now = score(0)
    grad_queries = None
    for at in range(count):
        following = score(at + 1) if at + 1 < count else None
        rows = slice(at * part, (at + 1) * part)
        soft = jnp.exp2(now[0])
        grads = (soft * now[1]).astype(bf16)
        added = dot(k_ref[:, rows], grads)
        grad_queries = added if grad_queries is None else grad_queries + added
        sums[rows] += dot(jnp.concatenate([grads, soft.astype(bf16)], axis=1), right)
        now = following

    def columns_of(place):
        return pl.ds(pl.multiple_of(order_ref[place] * block, block), block)

    columns = columns_of(here)
    dq_all[here] = turn_back(
        grad_queries * factor, cos_ref[:, columns], sin_ref[:, columns]
    ).astype(bf16)

    @pl.when(here == length // block - 1)
    def _():
        for place, dp_ref in enumerate(dp_refs):
            columns = columns_of(place)
            both = sums[columns].T
            dp_ref[:HDIM] = dq_all[place]
            dp_ref[HDIM : 2 * HDIM] = turn_back(
                both[:HDIM] * factor, cos_ref[:, columns], sin_ref[:, columns]
            ).astype(bf16)
            dp_ref[2 * HDIM :] = both[HDIM:].astype(bf16)


def attend_back(order, keys, values, qkv, douts, out, lse, cosine, sine, part=256):
    length = keys.shape[0]
    chips = len(douts)
    block = douts[0].shape[1]
    scores = length * length

    def whole(array):
        return pl.BlockSpec(array.shape, lambda i, order: (0, 0))

    return pl.pallas_call(
        functools.partial(attend_back_kernel, part=part),
        name="attend_back",
        grid_spec=pltpu.PrefetchScalarGridSpec(
            num_scalar_prefetch=1,
            grid=(chips,),
            in_specs=[
                whole(keys),
                whole(values),
                pl.BlockSpec((HDIM, block), lambda i, order: (0, order[i])),
                pl.BlockSpec((HDIM, length), lambda i, order: (1, 0)),
                pl.BlockSpec((HDIM, block), lambda i, order: (0, order[i])),
                pl.BlockSpec((1, block), lambda i, order: (0, order[i])),
                whole(cosine),
                whole(sine),
                *[whole(piece) for piece in douts],
            ],
            out_specs=[pl.BlockSpec((3 * HDIM, block), lambda i, order: (0, 0))] * chips,
            scratch_shapes=[
                pltpu.VMEM((length, 2 * HDIM), f32),
                pltpu.VMEM((chips, HDIM, block), bf16),
                pltpu.VMEM((chips, HDIM, block), bf16),
            ],
        ),
        out_shape=[jax.ShapeDtypeStruct((3 * HDIM, block), bf16)] * chips,
        compiler_params=pltpu.CompilerParams(vmem_limit_bytes=VMEM),
        cost_estimate=cost(5 * 4 * 2 * scores * HDIM, 8 << 20),
    )(order, keys, values, qkv, qkv, out, lse, cosine, sine, *douts)


def attend_out_kernel(order_ref, attended_ref, *rest):
    piece_refs, (mixed_ref, attn_ref) = rest[:-2], rest[-2:]
    half = attn_ref.shape[1] // 2
    at = 0
    for piece_ref in piece_refs:
        for place in range(piece_ref.shape[0]):
            rows = pl.ds(pl.multiple_of(order_ref[at] * HDIM, HDIM), HDIM)
            attn_ref[rows, :half] = piece_ref[place, :HDIM]
            attn_ref[rows, half:] = piece_ref[place, HDIM:]
            at += 1
    turned = attended_ref[...].astype(f32).T.astype(bf16)
    mixed_ref[...] = dot(turned, attn_ref[...]).astype(bf16)


def attend_out(order, attended, pieces):
    size, tokens = attended.shape
    width = 2 * size

    def whole(*shape):
        return pl.BlockSpec(shape, lambda i, order: (0,) * len(shape))

    return pl.pallas_call(
        attend_out_kernel,
        name="attend_out",
        grid_spec=pltpu.PrefetchScalarGridSpec(
            num_scalar_prefetch=1,
            grid=(1,),
            in_specs=[whole(size, tokens)]
            + [whole(*piece.shape[:2], width // 2) for piece in pieces],
            out_specs=[whole(tokens, width), whole(size, width)],
        ),
        out_shape=[
            jax.ShapeDtypeStruct((tokens, width), bf16),
            jax.ShapeDtypeStruct((size, width), bf16),
        ],
        compiler_params=pltpu.CompilerParams(vmem_limit_bytes=VMEM),
        cost_estimate=cost(2 * 2 * tokens * width * size, 4 << 20),
    )(order, attended, *pieces)


def feed_kernel(
    first_order, second_order, x_ref, ours_ref, theirs_ref, g_ref, *rest, firsts, seconds, axes
):
    weight_refs = []
    start = 0
    for size in (firsts, firsts, seconds, seconds):
        weight_refs.append(rest[start : start + size])
        start += size
    planes, lines, wide, beside = axes

    def put(grads, columns):
        size = grads.shape[0] // (planes * lines * wide)
        low = grads.astype(bf16)
        for plane in range(planes):
            for line in range(lines):
                for far in range(wide):
                    source = ((plane * lines + line) * wide + far) * size
                    target = ((line * wide + far) * planes + plane) * size
                    grads_ref[target : target + size, columns] = low[source : source + size]
    residual_ref, partial_ref, back_ref, grads_ref = rest[-13:-9]
    unit, unit_t, g_t, sum_out, sum_back = rest[-9:-4]
    gate_ref, up_ref, out_ref, rest_ref = rest[-4:]
    here = pl.program_id(0)
    last = pl.num_programs(0) - 1
    width = x_ref.shape[1]
    step = gate_ref.shape[1]

    def join(total, parts, order):
        at = 0
        for part in parts:
            size = part.shape[1]
            for place in range(part.shape[0]):
                total[pl.ds(pl.multiple_of(order[at] * size, size), size)] = part[place]
                at += 1

    def bend(gate, upward):
        cdf = 0.5 + 0.5 * lax.erf(gate * math.sqrt(0.5))
        slope = cdf + gate * jnp.exp(gate * gate * -0.5) * (1.0 / math.sqrt(2.0 * math.pi))
        bent = gate * cdf
        return bent, slope, (bent * upward).astype(bf16)

    @pl.when(here == 0)
    def _():
        residual = (
            x_ref[...].astype(f32) + ours_ref[...].astype(f32) + theirs_ref[...].astype(f32)
        )
        residual_ref[...] = residual
        normed = unit_rows(residual)[0]
        unit[...] = normed.astype(bf16)
        unit_t[...] = normed.T.astype(bf16)
        g_t[...] = g_ref[...].astype(f32).T.astype(bf16)
        join(rest_ref, weight_refs[3], second_order)
        few = rest_ref.shape[1] // 4
        both = dot(unit[...], rest_ref[...])
        grad = dot(g_ref[...], rest_ref[...])[:, 2 * few : 3 * few]
        bent, slope, active = bend(both[:, :few], both[:, few : 2 * few])
        grad_gate = (grad * both[:, few : 2 * few] * slope).astype(bf16)
        grad_up = (grad * bent).astype(bf16)
        blank = jnp.zeros_like(active)
        outs = jnp.concatenate([blank, blank, active, blank], axis=1)
        ins = jnp.concatenate([grad_gate, grad_up, blank, blank], axis=1)
        sum_out[...] = dot(outs, rest_ref[...], 1, 1)
        sum_back[...] = dot(ins, rest_ref[...], 1, 1)
        put(
            dot(unit_t[...], ins) + dot(g_t[...], outs),
            slice(grads_ref.shape[1] - 4 * few, grads_ref.shape[1]),
        )

    join(gate_ref, weight_refs[0], first_order)
    join(up_ref, weight_refs[1], first_order)
    join(out_ref, weight_refs[2], second_order)
    gate = dot(unit[...], gate_ref[...])
    upward = dot(unit[...], up_ref[...])
    grad = dot(g_ref[...], out_ref[...])
    bent, slope, active = bend(gate, upward)
    grad_gate = (grad * upward * slope).astype(bf16)
    grad_up = (grad * bent).astype(bf16)
    sum_out[...] += dot(active, out_ref[...], 1, 1)
    sum_back[...] += dot(grad_gate, gate_ref[...], 1, 1) + dot(grad_up, up_ref[...], 1, 1)
    count = grads_ref.shape[1] // step // 3
    for at, grads in enumerate(
        (dot(unit_t[...], grad_gate), dot(unit_t[...], grad_up), dot(g_t[...], active))
    ):
        place = pl.multiple_of(at * count * step + here * step, 128)
        put(grads, pl.ds(place, step))

    @pl.when(here == last)
    def _():
        partial_ref[...] = sum_out[...].astype(bf16)
        back_ref[...] = sum_back[...].astype(bf16)


def feed(first_order, second_order, x, ours, theirs, g, first, second, axes, step=256):
    tokens, width = x.shape
    start = width // 2 // step
    count = (first[0].shape[2] - width // 2) // step // 2
    rest = second[0].shape[2] - count * step
    columns = 3 * count * step + rest

    def whole(*shape):
        return pl.BlockSpec(shape, lambda i, one, two: (0, 0))

    def piece(arrays, size, at):
        return [
            pl.BlockSpec((*array.shape[:2], size), lambda i, one, two: (0, 0, at(i)))
            for array in arrays
        ]

    pair = jax.ShapeDtypeStruct((tokens, width), bf16)
    return pl.pallas_call(
        functools.partial(feed_kernel, firsts=len(first), seconds=len(second), axes=axes),
        name="feed",
        grid_spec=pltpu.PrefetchScalarGridSpec(
            num_scalar_prefetch=2,
            grid=(count,),
            in_specs=[whole(tokens, width)] * 4
            + piece(first, step, lambda i: start + i)
            + piece(first, step, lambda i: start + count + i)
            + piece(second, step, lambda i: i)
            + piece(second, rest, lambda i: count * step // rest),
            out_specs=[whole(tokens, width)] * 3 + [whole(width, columns)],
            scratch_shapes=[
                pltpu.VMEM((tokens, width), bf16),
                pltpu.VMEM((width, tokens), bf16),
                pltpu.VMEM((width, tokens), bf16),
                pltpu.VMEM((tokens, width), f32),
                pltpu.VMEM((tokens, width), f32),
                pltpu.VMEM((width, step), bf16),
                pltpu.VMEM((width, step), bf16),
                pltpu.VMEM((width, step), bf16),
                pltpu.VMEM((width, rest), bf16),
            ],
        ),
        out_shape=[
            jax.ShapeDtypeStruct((tokens, width), f32),
            pair,
            pair,
            jax.ShapeDtypeStruct((width, columns), bf16),
        ],
        compiler_params=pltpu.CompilerParams(vmem_limit_bytes=VMEM),
        cost_estimate=cost(2 * 9 * 2 * tokens * width * count * step, 24 << 20),
    )(first_order, second_order, x, ours, theirs, g, *first, *first, *second, *second)


def middle_back_kernel(
    core_ref, order_ref, line_ref, residual_ref, g_ref, ours_ref, theirs_ref, attn_ref,
    attended_ref, out_ours_ref, out_theirs_ref, layer_ref, residual_grad_ref, *rest, axes,
):
    planes, lines, wide, beside = axes
    dout_refs, grads_refs, (dout_all, grads_all) = rest[: -2 - lines], rest[-2 - lines : -2], rest[-2:]
    rows = layer_ref.shape[0]
    half = attn_ref.shape[0]
    own = pl.ds(pl.multiple_of(core_ref[0] * rows, rows), rows)
    layer_ref[...] = (
        residual_ref[own, :]
        + out_ours_ref[own, :].astype(f32)
        + out_theirs_ref[...].astype(f32)
    ).astype(bf16)
    unit, inverse = unit_rows(residual_ref[...])
    scaled = ours_ref[...].astype(f32) + theirs_ref[...].astype(f32)
    grad = g_ref[...].astype(f32) + unit_back(scaled, unit, inverse)
    low = grad.astype(bf16)
    residual_grad_ref[...] = grad
    dout_all[...] = dot(attn_ref[...], low, 1, 1).astype(bf16)
    for at, dout_ref in enumerate(dout_refs):
        dout_ref[...] = dout_all[pl.ds(pl.multiple_of(order_ref[at] * HDIM, HDIM), HDIM)]
    grads_all[...] = dot(attended_ref[...], low)
    few = HDIM // wide // beside
    for shift, grads_ref in enumerate(grads_refs):
        line = (line_ref[0] + shift) % lines
        blocks = [
            grads_all[pl.ds(pl.multiple_of((plane * lines + line) * HDIM, HDIM), HDIM)]
            for plane in range(planes)
        ]
        pieces = []
        for far in range(wide):
            for plane in range(planes):
                for near in range(beside):
                    start = (far * beside + near) * few
                    piece = blocks[plane][start : start + few]
                    pieces += [piece[:, :half], piece[:, half:]]
        grads_ref[...] = jnp.concatenate(pieces, axis=0).astype(bf16)


def middle_back(
    core, order, line, residual, g, ours, theirs, attn, attended, out_ours, out_theirs, axes
):
    tokens, width = residual.shape
    rows = tokens // 2
    half = width // 2
    chips = half // HDIM
    lines = axes[1]

    def whole(*shape):
        return pl.BlockSpec(shape, lambda i, core, order, line: (0,) * len(shape))

    return pl.pallas_call(
        functools.partial(middle_back_kernel, axes=axes),
        name="middle_back",
        grid_spec=pltpu.PrefetchScalarGridSpec(
            num_scalar_prefetch=3,
            grid=(1,),
            in_specs=[whole(tokens, width)] * 4
            + [whole(half, width), whole(half, tokens), whole(tokens, width), whole(rows, width)],
            out_specs=[whole(rows, width), whole(tokens, width)]
            + [whole(HDIM, tokens)] * chips
            + [whole(width // lines, half)] * lines,
            scratch_shapes=[pltpu.VMEM((half, tokens), bf16), pltpu.VMEM((half, width), f32)],
        ),
        out_shape=[
            jax.ShapeDtypeStruct((rows, width), bf16),
            jax.ShapeDtypeStruct((tokens, width), f32),
        ]
        + [jax.ShapeDtypeStruct((HDIM, tokens), bf16)] * chips
        + [jax.ShapeDtypeStruct((width // lines, half), bf16)] * lines,
        compiler_params=pltpu.CompilerParams(vmem_limit_bytes=VMEM),
        cost_estimate=cost(2 * 2 * 2 * tokens * width * half, 16 << 20),
    )(core, order, line, residual, g, ours, theirs, attn, attended, out_ours, out_theirs)


def hidden_back_kernel(order_ref, core_ref, w_ref, *rest):
    dp_refs, (own_ref, other_ref, stacked) = rest[:-3], rest[-3:]
    for place, dp_ref in enumerate(dp_refs):
        size = dp_ref.shape[0]
        stacked[pl.ds(pl.multiple_of(order_ref[place] * size, 64), size)] = dp_ref[...]
    rows = own_ref.shape[0]
    flat = dot(w_ref[...], stacked[...])
    first = flat[:, :rows].T
    second = flat[:, rows:].T
    zero = core_ref[0] == 0
    own_ref[...] = jnp.where(zero, first, second)
    other_ref[...] = jnp.where(zero, second, first).astype(bf16)


def hidden_back(order, core, weights, pieces):
    width, columns = weights.shape
    rows = pieces[0].shape[1] // 2

    def whole(*shape):
        return pl.BlockSpec(shape, lambda i, order, core: (0,) * len(shape))

    return pl.pallas_call(
        hidden_back_kernel,
        name="hidden_back",
        grid_spec=pltpu.PrefetchScalarGridSpec(
            num_scalar_prefetch=2,
            grid=(1,),
            in_specs=[whole(width, columns)] + [whole(*pieces[0].shape)] * len(pieces),
            out_specs=[whole(rows, width)] * 2,
            scratch_shapes=[pltpu.VMEM((columns, 2 * rows), bf16)],
        ),
        out_shape=[
            jax.ShapeDtypeStruct((rows, width), f32),
            jax.ShapeDtypeStruct((rows, width), bf16),
        ],
        compiler_params=pltpu.CompilerParams(vmem_limit_bytes=VMEM),
        cost_estimate=cost(2 * 2 * 2 * rows * width * columns, 8 << 20),
    )(order, core, weights, *pieces)


def head_grad_kernel(order_ref, owner_ref, unit_ref, *rest, owners):
    dp_refs, out_refs, out_all = rest[: -1 - owners], rest[-1 - owners : -1], rest[-1]
    block = dp_refs[0].shape[1]
    total = None
    for place, dp_ref in enumerate(dp_refs):
        rows = pl.ds(pl.multiple_of(order_ref[place] * block, block), block)
        added = dot(dp_ref[...], unit_ref[rows])
        total = added if total is None else total + added
    for at in range(owners):
        out_all[at] = total[:, at * 128 : (at + 1) * 128].astype(bf16)
    for at, out_ref in enumerate(out_refs):
        out_ref[...] = out_all[owner_ref[at]]


def head_grad(order, owner_order, unit_all, pieces):
    length, width = unit_all.shape
    owners = width // 128
    size = pieces[0].shape[0]

    def whole(*shape):
        return pl.BlockSpec(shape, lambda i, order, owner: (0,) * len(shape))

    return pl.pallas_call(
        functools.partial(head_grad_kernel, owners=owners),
        name="head_grad",
        grid_spec=pltpu.PrefetchScalarGridSpec(
            num_scalar_prefetch=2,
            grid=(1,),
            in_specs=[whole(length, width)] + [whole(*pieces[0].shape)] * len(pieces),
            out_specs=[whole(size, 128)] * owners,
            scratch_shapes=[pltpu.VMEM((owners, size, 128), bf16)],
        ),
        out_shape=[jax.ShapeDtypeStruct((size, 128), bf16)] * owners,
        compiler_params=pltpu.CompilerParams(vmem_limit_bytes=VMEM),
        cost_estimate=cost(2 * 2 * length * width * size, 10 << 20),
    )(order, owner_order, unit_all, *pieces)


def adam(weight, gradient, first, second, rate):
    first = BETA_FIRST * first + (1.0 - BETA_FIRST) * gradient
    second = BETA_SECOND * second + (1.0 - BETA_SECOND) * gradient * gradient
    first_hat = first / (1.0 - BETA_FIRST**STEP)
    second_hat = second / (1.0 - BETA_SECOND**STEP)
    weight = weight - rate * (first_hat / (jnp.sqrt(second_hat) + EPSILON) + DECAY * weight)
    return (weight, first, second)


def adam_into(refs, weight, gradient, first, second, rate):
    for ref, value in zip(refs, adam(weight, gradient, first, second, rate)):
        ref[...] = value


def rounded_in_kernel(values):
    return values.astype(bf16).astype(f32)


def adam_in_kernel(
    grads_ref, gain_ref, w_ref, m_ref, v_ref, new_w, new_m, new_v, gain_grad, *, rate
):
    width = m_ref.shape[1] // 2
    main = width // 256 * 128
    few = width // 2 - main
    columns = []
    for at in range(2):
        for core in range(2):
            place = at * main
            columns.append(grads_ref[core, :, place : place + main].astype(f32))
        for core in range(2):
            rest = grads_ref[core, :, 3 * main : 3 * main + 128].astype(f32)
            columns.append(rest[:, at * few : (at + 1) * few])
    grads = jnp.concatenate(columns, axis=1)
    weight = w_ref[...]
    gain_grad[...] = jnp.sum(grads * rounded_in_kernel(weight), axis=1, keepdims=True)
    adam_into(
        (new_w, new_m, new_v), weight, grads * gain_ref[...], m_ref[...], v_ref[...], rate
    )


def adam_in(grads, gain, weight, first, second, rate):
    rows, columns = weight.shape
    steps = grads.shape[0] // 2
    block = pl.BlockSpec((rows // steps, columns), lambda i: (i, 0))
    column = pl.BlockSpec((rows // steps, 1), lambda i: (i, 0))
    same = jax.ShapeDtypeStruct((rows, columns), f32)
    return pl.pallas_call(
        functools.partial(adam_in_kernel, rate=rate),
        name="adam_in",
        grid=(steps,),
        in_specs=[pl.BlockSpec((2,) + grads.shape[1:], lambda i: (i, 0, 0)), column]
        + [block] * 3,
        out_specs=[block] * 3 + [column],
        out_shape=[same] * 3 + [jax.ShapeDtypeStruct((rows, 1), f32)],
        compiler_params=pltpu.CompilerParams(vmem_limit_bytes=VMEM),
        cost_estimate=cost(rows * columns * 20, rows * columns * 26),
    )(grads, gain, weight, first, second)


def adam_rest_kernel(grads_ref, *refs, rates):
    attn, out, new_attn, new_out = refs[:3], refs[3:6], refs[6:9], refs[9:]
    chips = grads_ref.shape[0] // 2
    hidden = out[0].shape[0]
    main = hidden // 256 * 128
    few = hidden // 2 - main
    pieces = []
    for core in range(2):
        for chip in range(chips):
            piece = grads_ref[2 * chip + core, :, 3 * main + 128 :].astype(f32)
            pieces.append(jnp.concatenate([piece[:8], piece[8:]], axis=1))
    grads = jnp.concatenate(pieces, axis=0)
    adam_into(new_attn, attn[0][...], grads, attn[1][...], attn[2][...], rates[0])
    for core in range(2):
        columns = jnp.concatenate(
            [grads_ref[2 * chip + core, :, 2 * main : 3 * main] for chip in range(chips)], axis=0
        )
        rest = jnp.concatenate(
            [grads_ref[2 * chip + core, :, 3 * main : 3 * main + 128] for chip in range(chips)],
            axis=0,
        )
        for rows, grads in (
            (slice(core * main, (core + 1) * main), columns.astype(f32).T),
            (
                slice(2 * main + core * few, 2 * main + (core + 1) * few),
                rest.astype(f32).T[2 * few : 3 * few],
            ),
        ):
            new = adam(out[0][rows], grads, out[1][rows], out[2][rows], rates[1])
            for ref, value in zip(new_out, new):
                ref[rows] = value


def adam_rest(grads, attn, out, rates):
    def whole(array):
        return pl.BlockSpec(array.shape, lambda i: (0,) * array.ndim)

    arrays = (*attn, *out)
    return pl.pallas_call(
        functools.partial(adam_rest_kernel, rates=rates),
        name="adam_rest",
        grid=(1,),
        in_specs=[whole(array) for array in (grads, *arrays)],
        out_specs=[whole(array) for array in arrays],
        out_shape=[jax.ShapeDtypeStruct(array.shape, f32) for array in arrays],
        compiler_params=pltpu.CompilerParams(vmem_limit_bytes=VMEM),
        cost_estimate=cost(attn[0].size * 60, 14 << 20),
    )(grads, *arrays)


def adam_qkv_kernel(order_ref, *refs, rate):
    grads_refs, (gain_ref, w_ref, m_ref, v_ref, new_w, new_m, new_v, gain_grad, joined) = (
        refs[:-9], refs[-9:]
    )
    here = pl.program_id(0)
    rows = pl.ds(pl.multiple_of(here * HDIM, HDIM), HDIM)
    at = 0
    for grads_ref in grads_refs:
        for place in range(grads_ref.shape[0]):
            head = pl.ds(pl.multiple_of(order_ref[at] * HDIM, HDIM), HDIM)
            joined[head] = grads_ref[place, rows].astype(f32)
            at += 1
    grads = joined[...].T
    weight = w_ref[...]
    added = jnp.sum(grads * rounded_in_kernel(weight), axis=1, keepdims=True)
    gain_grad[...] = added + jnp.where(here == 0, 0.0, gain_grad[...])
    adam_into(
        (new_w, new_m, new_v), weight, grads * gain_ref[...], m_ref[...], v_ref[...], rate
    )


def adam_qkv(order, grads, gain, weight, first, second, rate):
    rows, columns = weight.shape
    block = pl.BlockSpec((rows, columns // 3), lambda i, order: (0, i))
    column = pl.BlockSpec((rows, 1), lambda i, order: (0, 0))
    same = jax.ShapeDtypeStruct((rows, columns), f32)
    return pl.pallas_call(
        functools.partial(adam_qkv_kernel, rate=rate),
        name="adam_qkv",
        grid_spec=pltpu.PrefetchScalarGridSpec(
            num_scalar_prefetch=1,
            grid=(3,),
            in_specs=[pl.BlockSpec((piece.shape[0], 3 * HDIM, 128), lambda i, order: (0, 0, 0)) for piece in grads]
            + [column]
            + [block] * 3,
            out_specs=[block] * 3 + [column],
            scratch_shapes=[pltpu.VMEM((columns // 3, rows), f32)],
        ),
        out_shape=[same] * 3 + [jax.ShapeDtypeStruct((rows, 1), f32)],
        compiler_params=pltpu.CompilerParams(vmem_limit_bytes=VMEM),
        cost_estimate=cost(rows * columns * 20, rows * columns * 26),
    )(order, *grads, gain, weight, first, second)


def ring(axis, shift):
    size = lax.axis_size(axis)
    return [(at, (at + shift) % size) for at in range(size)]


def gather_first_step(planes_first, lines_first):
    swapped = lax.ppermute(planes_first, "zh", SWAP)
    others = [
        lax.ppermute(lines_first, "y", ring("y", shift)) for shift in range(1, lax.axis_size("y"))
    ]
    return jnp.stack([planes_first, swapped]), jnp.stack([lines_first, *others])


def shards(
    tokens,
    positions,
    cotangent,
    weight_qkv,
    weight_attn,
    weight_in,
    weight_out,
    norm_gains,
    first_qkv,
    first_attn,
    first_in,
    first_out,
    first_gains,
    second_qkv,
    second_attn,
    second_in,
    second_out,
    second_gains,
):
    rows, width = tokens.shape[1:]
    shard_rows = weight_qkv.shape[1]
    heads = width // HDIM
    hidden = weight_out.shape[1]
    core = lax.axis_index("c")
    mine = lax.axis_index(CTX)
    chip = lax.axis_index(CHIPS)
    chips = lax.axis_size(CHIPS)
    owners = lax.axis_size(FSDP)
    length = rows * chips * 2
    main = hidden // 256 * 128
    few = hidden // 2 - main
    core_at = core.reshape(1).astype(jnp.int32)
    axes = (lax.axis_size("zh"), lax.axis_size("y"), lax.axis_size("x"), lax.axis_size("zl"))
    offsets = [(far, near) for far in range(lax.axis_size("x")) for near in range(2)]
    across, beside = lax.axis_index("x"), lax.axis_index("zl")
    wide = lax.axis_size("x")

    def chips_at(sign):
        places = [(across + sign * far) % wide * 2 + (beside ^ near) for far, near in offsets]
        return jnp.stack(places).astype(jnp.int32)

    local = tokens[0]
    extra = 16
    high, low = positions[0] // 128, positions[0] % 128
    places_row = jnp.concatenate([high, low, jnp.zeros((width - 2 * rows,), jnp.int32)])
    places_rows = jnp.concatenate(
        [places_row[None], jnp.zeros((extra - 1, width), jnp.int32)], axis=0
    ).astype(bf16)
    sequence = lax.all_gather(
        jnp.concatenate([local, places_rows], axis=0), CTX, axis=0, tiled=True
    )
    first_part, second_part, head_part, half_heads = prepare(
        jnp.stack([core, chip]).astype(jnp.int32),
        norm_gains[0],
        weight_qkv[0],
        weight_attn[0],
        weight_in[0],
        weight_out[0],
    )
    first_joined, second_joined = gather_first_step(first_part, second_part)
    head_weights = lax.all_to_all(
        jnp.broadcast_to(head_part, (owners, *head_part.shape)), FSDP, 0, 0, tiled=True
    )
    first_pieces = [first_joined] + [
        lax.ppermute(first_joined, "y", ring("y", shift))
        for shift in range(1, lax.axis_size("y"))
    ]
    sequence, _, second_joined, _ = lax.optimization_barrier(
        (sequence, first_joined, second_joined, head_weights)
    )
    second_pieces = [second_joined, lax.ppermute(second_joined, "zh", SWAP)]
    lines = lax.axis_size("y")
    plane, line = lax.axis_index("zh"), lax.axis_index("y")
    first_order = jnp.stack(
        [(plane ^ far) * lines + (line - shift) % lines for shift in range(lines) for far in range(2)]
    ).astype(jnp.int32)
    second_order = jnp.stack(
        [(plane ^ far) * lines + (line - shift) % lines for far in range(2) for shift in range(lines)]
    ).astype(jnp.int32)

    def in_order(ours, theirs):
        first = jnp.where(core == 0, ours, theirs)
        second = jnp.where(core == 0, theirs, ours)
        return jnp.concatenate([first, second], axis=0)

    def swap(array):
        return lax.ppermute(array, "c", SWAP)

    gradient = in_order(cotangent[0], swap(cotangent[0]))

    freqs = jnp.exp(jnp.arange(HDIM // 2, dtype=f32) * (-2.0 * math.log(ROPE_BASE) / HDIM))
    by_device = sequence.reshape(2 * chips, rows + extra, width)[:, rows]
    by_device = by_device.astype(f32)
    places = by_device[:, :rows] * 128.0 + by_device[:, rows : 2 * rows]
    angles = freqs[:, None] * places.reshape(1, length)
    cosine = jnp.cos(angles)
    sine = jnp.sin(angles)
    unit_all, qkv, keys, values = project(sequence, head_weights, cosine, sine)
    keys, *second_pieces = lax.optimization_barrier((keys, *second_pieces))
    low_out, out, lse = attend(keys, qkv, chips)
    half_heads, low_out = lax.optimization_barrier((half_heads, low_out))
    mat_qkv = lax.all_gather(half_heads, FSDP, axis=0, tiled=True)
    attended = lax.all_to_all(low_out, CHIPS, 0, 0, tiled=True)
    attended = attended.reshape(heads // 2 * HDIM, 2 * rows)
    mixed, mat_attn = attend_out(first_order, attended, first_pieces)
    current = lax.dynamic_slice_in_dim(
        sequence, chip * 2 * (rows + extra), 2 * (rows + extra), 0
    ).reshape(2, rows + extra, width)[:, :rows].reshape(2 * rows, width)
    residual, partial, back, grads = feed(
        first_order, second_order, current, mixed, swap(mixed), gradient, first_pieces,
        second_pieces, axes,
    )
    arrived = lax.all_to_all(grads, "y", 0, 0, tiled=True)

    def move(pieces, sign):
        moved = [pieces[0]]
        for (far, near), piece in list(zip(offsets, pieces))[1:]:
            pairs = [
                (at, (at // 2 + sign * far) % wide * 2 + (at % 2 ^ near)) for at in range(chips)
            ]
            moved.append(lax.ppermute(piece, CHIPS, pairs))
        return moved

    ahead, behind = chips_at(1), chips_at(-1)
    residual, mat_qkv = lax.optimization_barrier((residual, mat_qkv))
    theirs = swap(lax.dynamic_slice_in_dim(partial, (1 - core) * rows, rows, 0))
    layer_out, residual_grad, *pieces = middle_back(
        core_at, ahead, line.reshape(1).astype(jnp.int32), residual, gradient, back, swap(back),
        mat_attn, attended, partial, theirs, axes,
    )
    dout_pieces, attn_pieces = pieces[:chips], pieces[chips:]

    douts = move(dout_pieces, 1)
    attn_arrived = attn_pieces[:1] + [
        lax.ppermute(piece, "y", ring("y", shift))
        for shift, piece in list(enumerate(attn_pieces))[1:]
    ]
    pieces = attend_back(behind, keys, values, qkv, douts, out, lse, cosine, sine)
    owner_places = [(far, shift) for far in range(2) for shift in range(lines)]
    owner_order = jnp.stack(
        [(plane ^ far) * lines + (line + shift) % lines for far, shift in owner_places]
    ).astype(jnp.int32)
    head_parts = head_grad(behind, owner_order, unit_all, pieces)

    def total(arrays):
        return sum(array.astype(f32) for array in arrays).astype(bf16)

    arrived, *head_parts = lax.optimization_barrier((arrived, *head_parts))
    first_sum = total([arrived[at * width // lines : (at + 1) * width // lines] for at in range(lines)])
    first_sum = jnp.concatenate([first_sum, total(attn_arrived)], axis=1)
    first_sum, *pieces = lax.optimization_barrier((first_sum, *pieces))
    arrived = lax.all_to_all(first_sum, ("x", "zh", "zl"), 0, 0, tiled=True)

    moved = move(pieces, -1)
    own_hidden, other_hidden = hidden_back(ahead, core_at, mat_qkv, moved)
    grad_hidden = own_hidden + swap(other_hidden).astype(f32)
    unit_in, scale_in = unit_rows(local.astype(f32))
    own_residual = lax.dynamic_slice_in_dim(residual_grad, core * rows, rows, 0)
    tokens_grad = (own_residual + unit_back(grad_hidden, unit_in, scale_in))[None]

    head_arrived = [head_parts[0]]
    for (far, shift), piece in list(zip(owner_places, head_parts))[1:]:
        pairs = [
            (at, (at // lines ^ far) * lines + (at % lines + shift) % lines) for at in range(owners)
        ]
        head_arrived.append(lax.ppermute(piece, FSDP, pairs))
    head_own = total(head_arrived)[None]
    arrived, head_own = lax.optimization_barrier((arrived, head_own))
    arrived = arrived.reshape(2 * chips, shard_rows // chips, -1)
    second_sum = jnp.sum(arrived.astype(f32), axis=0).astype(bf16)
    all_grads = lax.all_gather(second_sum, CTX, axis=0, tiled=False)

    head_pair = jnp.concatenate([head_own, swap(head_own)], axis=0)
    head_four = jnp.concatenate([head_pair, lax.ppermute(head_pair, "zl", SWAP)], axis=0)
    head_grads = [head_four] + [
        lax.ppermute(head_four, "x", ring("x", shift)) for shift in range(1, wide)
    ]
    head_order = jnp.stack(
        [
            (across - shift) % wide * 4 + (beside ^ near) * 2 + (core ^ other)
            for shift in range(wide)
            for near in range(2)
            for other in range(2)
        ]
    ).astype(jnp.int32)

    rates = (
        width ** (-0.5),
        max(1, 3 * width // length) ** (-0.5),
        width ** (-0.5),
        hidden ** (-0.5),
    )
    columns_of_gains = norm_gains[0].astype(bf16).astype(f32).T
    *new_in, gain_second = adam_in(
        all_grads, columns_of_gains[:, 1:], weight_in[0], first_in[0], second_in[0], rates[2]
    )
    rest = adam_rest(
        all_grads,
        (weight_attn[0], first_attn[0], second_attn[0]),
        (weight_out[0], first_out[0], second_out[0]),
        (rates[1], rates[3]),
    )
    *new_qkv, gain_first = adam_qkv(
        head_order, head_grads, columns_of_gains[:, :1], weight_qkv[0], first_qkv[0], second_qkv[0], rates[0]
    )
    gain_grads = jnp.concatenate([gain_first, gain_second], axis=1).T
    new_gains = adam(norm_gains[0], gain_grads, first_gains[0], second_gains[0], GAIN_RATE)
    updated = (new_qkv, rest[:3], new_in, rest[3:], new_gains)
    return (
        layer_out[None],
        tokens_grad,
        *[updated[member][0][None] for member in range(5)],
        *[updated[member][1][None] for member in range(5)],
        *[updated[member][2][None] for member in range(5)],
    )


def solution(mesh):
    split = Mesh(mesh.devices.reshape(4, 2, 2, 2, 4), ("x", "zl", "c", "zh", "y"))
    by_row = P(None, FSDP, None)
    by_column = P(None, None, FSDP)
    weights = (by_row, by_row, by_row, by_column, by_column)
    by_token = P(FSDP, CTX, None)
    return jax.shard_map(
        shards,
        mesh=split,
        in_specs=(by_token, P(FSDP, CTX), by_token) + weights * 3,
        out_specs=(by_token, by_token) + weights * 3,
        check_vma=False,
    )
```

```python
import functools
import math

import jax
import jax.numpy as jnp
from jax import lax
from jax.experimental import pallas as pl
from jax.experimental.pallas import tpu as pltpu
from jax.sharding import Mesh, PartitionSpec as P

HDIM = 64
STEP = 10
BETA_FIRST = 0.5
BETA_SECOND = 0.5
EPSILON = 1e-08
DECAY = 0.01
NORM_EPS = 1e-05
ROPE_BASE = 160000.0
GAIN_RATE = 0.6
LOG2E = math.log2(math.e)
f32 = jnp.float32
bf16 = jnp.bfloat16

CHIPS = ("x", "zl")
CTX = ("x", "zl", "c")
FSDP = ("zh", "y")
SWAP = [(0, 1), (1, 0)]
VMEM = 60 << 20


def dot(left, right, left_dim=1, right_dim=0):
    return lax.dot_general(
        left, right, (((left_dim,), (right_dim,)), ((), ())), preferred_element_type=f32
    )


def cost(flops, moved):
    return pl.CostEstimate(flops=flops, bytes_accessed=moved, transcendentals=0)


def unit_rows(values):
    average = jnp.mean(values, axis=-1, keepdims=True)
    centered = values - average
    spread = jnp.mean(centered * centered, axis=-1, keepdims=True)
    inverse = lax.rsqrt(spread + NORM_EPS)
    return centered * inverse, inverse


def unit_back(scaled, unit, inverse):
    first_mean = jnp.mean(scaled, axis=-1, keepdims=True)
    second_mean = jnp.mean(scaled * unit, axis=-1, keepdims=True)
    return inverse * (scaled - first_mean - unit * second_mean)


def prepare_kernel(
    place_ref, gains_ref, qkv_ref, attn_ref, in_ref, out_ref,
    first_ref, second_ref, head_ref, heads_ref,
):
    core, chip = place_ref[0], place_ref[1]
    rows = qkv_ref.shape[0]
    width = attn_ref.shape[1]
    hidden = out_ref.shape[0]
    main = hidden // 256 * 128
    few = hidden // 2 - main
    half = width // 2
    low_gains = gains_ref[...].astype(bf16).astype(f32)
    columns = jnp.concatenate([low_gains, jnp.zeros((6, rows), f32)], axis=0).T
    gain_first, gain_second = columns[:, 0:1], columns[:, 1:2]

    def pick(array):
        size = array.shape[1] // 2
        return jnp.where(core == 0, array[:, :size], array[:, size:])

    def scaled(values, gain):
        return (values.astype(bf16).astype(f32) * gain).astype(bf16)

    attn_rows = attn_ref[pl.ds(pl.multiple_of(core * HDIM, HDIM), HDIM)].astype(bf16)
    first_ref[:HDIM, :half] = attn_rows[:, :half]
    first_ref[HDIM:, :half] = attn_rows[:, half:]
    first_ref[:, half:] = scaled(pick(in_ref[:, : 2 * main]), gain_second)
    second_ref[:, :main] = scaled(pick(in_ref[:, hidden : hidden + 2 * main]), gain_second)
    out_rows = out_ref[pl.ds(pl.multiple_of(core * main, 128), main)]
    second_ref[:, main : 2 * main] = out_rows.T.astype(bf16)
    odd_out = out_ref[2 * main :].T
    odd = [
        scaled(pick(in_ref[:, 2 * main : hidden]), gain_second),
        scaled(pick(in_ref[:, hidden + 2 * main :]), gain_second),
        pick(odd_out).astype(bf16),
        jnp.zeros((rows, few), bf16),
    ]
    second_ref[:, 2 * main :] = jnp.concatenate(odd, axis=1)
    pieces = []
    for at in range(width // 128):
        for part in range(3):
            start = part * width + at * 128
            pieces.append(scaled(pick(qkv_ref[:, start : start + 128]), gain_first))
    heads_ref[...] = jnp.concatenate(pieces, axis=1)
    own = []
    for part in range(3):
        start = pl.multiple_of(part * width + chip * 128, 128)
        own.append(scaled(pick(qkv_ref[:, pl.ds(start, 128)]), gain_first).astype(f32))
    own.append(jnp.zeros((rows, HDIM), f32))
    head_ref[...] = jnp.concatenate(own, axis=1).T[: 3 * HDIM].astype(bf16)


def prepare(place, gains, qkv, attn, weight_in, weight_out):
    rows, width = attn.shape
    hidden = weight_out.shape[0]
    main = hidden // 256 * 128
    arrays = (gains, qkv, attn, weight_in, weight_out)
    shapes = [
        (rows, width // 2 + main),
        (rows, 2 * main + 4 * (hidden // 2 - main)),
        (3 * HDIM, rows),
        (rows, 3 * width // 2),
    ]

    def whole(shape):
        return pl.BlockSpec(shape, lambda i, place: (0, 0))

    return pl.pallas_call(
        prepare_kernel,
        name="prepare",
        grid_spec=pltpu.PrefetchScalarGridSpec(
            num_scalar_prefetch=1,
            grid=(1,),
            in_specs=[whole(array.shape) for array in arrays],
            out_specs=[whole(shape) for shape in shapes],
        ),
        out_shape=[jax.ShapeDtypeStruct(shape, bf16) for shape in shapes],
        compiler_params=pltpu.CompilerParams(vmem_limit_bytes=VMEM),
        cost_estimate=cost(rows * width * 60, 10 << 20),
    )(place, *arrays)


def project_kernel(x_ref, w_ref, cos_ref, sin_ref, unit_ref, qkv_ref, keys_ref, values_ref, w_all):
    half = HDIM // 2
    rows = cos_ref.shape[1]

    @pl.when(pl.program_id(0) == 0)
    def _():
        for part in range(w_ref.shape[0]):
            w_all[:, part * 128 : (part + 1) * 128] = w_ref[part]

    each = rows // 2
    extra = x_ref.shape[0] // 2 - each
    tokens = jnp.concatenate(
        [x_ref[:each].astype(f32), x_ref[each + extra : 2 * each + extra].astype(f32)], axis=0
    )
    unit = unit_rows(tokens)[0].astype(bf16)
    unit_ref[...] = unit
    mixed = dot(w_all[...], unit, 1, 1)
    cosine = cos_ref[...]
    sine = sin_ref[...]

    def turn(one, two):
        return jnp.concatenate([one * cosine - two * sine, two * cosine + one * sine], axis=0)

    queries = turn(mixed[:half], mixed[half:HDIM])
    keys = turn(mixed[HDIM : HDIM + half], mixed[HDIM + half : 2 * HDIM])
    values = mixed[2 * HDIM :]
    qkv_ref[...] = jnp.concatenate([queries, keys, values], axis=0).astype(bf16)
    key_rows = keys.T.astype(bf16)
    value_rows = values.T.astype(bf16)
    ones = jnp.where(lax.broadcasted_iota(jnp.int32, (rows, 128), 1) < 3, 1.0, 0.0).astype(bf16)
    keys_ref[...] = jnp.concatenate([key_rows, key_rows, ones], axis=1)
    values_ref[...] = jnp.concatenate([value_rows, ones[:, :HDIM]], axis=1)


def project(tokens, weights, cosine, sine, block=512):
    width = tokens.shape[1]
    length = cosine.shape[1]
    steps = length // block
    return pl.pallas_call(
        project_kernel,
        name="project",
        grid=(steps,),
        in_specs=[
            pl.BlockSpec((tokens.shape[0] // steps, width), lambda i: (i, 0)),
            pl.BlockSpec(weights.shape, lambda i: (0, 0, 0)),
            pl.BlockSpec((HDIM // 2, block), lambda i: (0, i)),
            pl.BlockSpec((HDIM // 2, block), lambda i: (0, i)),
        ],
        out_specs=[
            pl.BlockSpec((block, width), lambda i: (i, 0)),
            pl.BlockSpec((3 * HDIM, block), lambda i: (0, i)),
            pl.BlockSpec((block, 256), lambda i: (i, 0)),
            pl.BlockSpec((block, 128), lambda i: (i, 0)),
        ],
        out_shape=[
            jax.ShapeDtypeStruct((length, width), bf16),
            jax.ShapeDtypeStruct((3 * HDIM, length), bf16),
            jax.ShapeDtypeStruct((length, 256), bf16),
            jax.ShapeDtypeStruct((length, 128), bf16),
        ],
        scratch_shapes=[pltpu.VMEM((3 * HDIM, width), bf16)],
        compiler_params=pltpu.CompilerParams(vmem_limit_bytes=VMEM),
        cost_estimate=cost(length * width, 1 << 20),
    )(tokens, weights, cosine, sine)


def scaled_queries(queries):
    scaled = queries.astype(f32) * (LOG2E / math.sqrt(HDIM))
    high = scaled.astype(bf16)
    low = (scaled - high.astype(f32)).astype(bf16)
    return high, low


def attend_kernel(keys_ref, q_ref, v_ref, low_ref, out_ref, lse_ref, v_ones, *, part):
    length = keys_ref.shape[0]
    count = length // part

    @pl.when(pl.program_id(0) == 0)
    def _():
        v_ones[:HDIM] = v_ref[...]
        v_ones[HDIM:] = jnp.where(
            lax.broadcasted_iota(jnp.int32, (16, length), 0) < 1, 1.0, 0.0
        ).astype(bf16)

    queries = jnp.concatenate(scaled_queries(q_ref[...]), axis=0)

    def score(at):
        return dot(keys_ref[at * part : (at + 1) * part, : 2 * HDIM], queries)

    scores = score(0)
    highest = total = None
    for at in range(count):
        following = score(at + 1) if at + 1 < count else None
        peak = jnp.max(scores, axis=0, keepdims=True)
        raised = peak if highest is None else jnp.maximum(highest, peak)
        soft = jnp.exp2(scores - raised).astype(bf16)
        added = dot(v_ones[:, at * part : (at + 1) * part], soft)
        total = added if total is None else total * jnp.exp2(highest - raised) + added
        highest = raised
        scores = following
    summed = total[HDIM : HDIM + 1]
    result = total[:HDIM] / summed
    out_ref[...] = result
    lse_ref[...] = highest + jnp.log2(summed)
    step = low_ref.shape[2]
    for at in range(low_ref.shape[0]):
        low_ref[at] = result[:, at * step : (at + 1) * step].astype(bf16)


def attend(keys, qkv, chips, block=1024, part=512):
    length = keys.shape[0]
    return pl.pallas_call(
        functools.partial(attend_kernel, part=part),
        name="attend",
        grid=(length // block,),
        in_specs=[
            pl.BlockSpec(keys.shape, lambda i: (0, 0)),
            pl.BlockSpec((HDIM, block), lambda i: (0, i)),
            pl.BlockSpec((HDIM, length), lambda i: (2, 0)),
        ],
        out_specs=[
            pl.BlockSpec((block * chips // length, HDIM, length // chips), lambda i: (i, 0, 0)),
            pl.BlockSpec((HDIM, block), lambda i: (0, i)),
            pl.BlockSpec((1, block), lambda i: (0, i)),
        ],
        out_shape=[
            jax.ShapeDtypeStruct((chips, HDIM, length // chips), bf16),
            jax.ShapeDtypeStruct((HDIM, length), f32),
            jax.ShapeDtypeStruct((1, length), f32),
        ],
        scratch_shapes=[pltpu.VMEM((HDIM + 16, length), bf16)],
        compiler_params=pltpu.CompilerParams(vmem_limit_bytes=VMEM),
        cost_estimate=cost(length * HDIM, 1 << 20),
    )(keys, qkv, qkv)


def minus_in_three(values):
    rows = values.shape[1]
    at = lax.broadcasted_iota(jnp.int32, (16, rows), 0)
    high = (-values).astype(bf16).astype(f32)
    rest = -values - high
    middle = rest.astype(bf16).astype(f32)
    low = rest - middle
    stacked = jnp.where(at == 0, high, jnp.where(at == 1, middle, jnp.where(at == 2, low, 0.0)))
    return stacked.astype(bf16)


def attend_back_kernel(
    order_ref,
    keys_ref,
    values_ref,
    q_ref,
    k_ref,
    out_ref,
    lse_ref,
    cos_ref,
    sin_ref,
    *rest,
    part,
):
    count = (len(rest) - 3) // 2
    dout_refs, dp_refs, (sums, dq_all, dout_all) = rest[:count], rest[count:-3], rest[-3:]
    half = HDIM // 2
    here = pl.program_id(0)
    length = keys_ref.shape[0]
    block = q_ref.shape[1]
    count = length // part
    factor = HDIM ** (-0.5)

    def turn_back(grads, cosine, sine):
        low = grads.astype(bf16).astype(f32)
        one, two = low[:half], low[half:]
        return jnp.concatenate([one * cosine + two * sine, two * cosine - one * sine], axis=0)

    @pl.when(here == 0)
    def _():
        sums[...] = jnp.zeros_like(sums)
        for place, dout_ref in enumerate(dout_refs):
            dout_all[place] = dout_ref[...]

    low_queries = q_ref[...]
    high, low = scaled_queries(low_queries)
    queries = jnp.concatenate([high, low, minus_in_three(lse_ref[...])], axis=0)
    low_dout = dout_all[here]
    dout = low_dout.astype(f32)
    centre = jnp.sum(dout * out_ref[...], axis=0, keepdims=True)
    douts = jnp.concatenate([low_dout, minus_in_three(centre)], axis=0)
    blank = jnp.zeros((block, HDIM), bf16)
    right = jnp.concatenate(
        [
            jnp.concatenate([low_queries.astype(f32).T.astype(bf16), blank], axis=1),
            jnp.concatenate([blank, dout.T.astype(bf16)], axis=1),
        ],
        axis=0,
    )

    def score(at):
        rows = slice(at * part, (at + 1) * part)
        return (
            dot(keys_ref[rows, : 2 * HDIM + 16], queries),
            dot(values_ref[rows, : HDIM + 16], douts),
        )

    now = score(0)
    grad_queries = None
    for at in range(count):
        following = score(at + 1) if at + 1 < count else None
        rows = slice(at * part, (at + 1) * part)
        soft = jnp.exp2(now[0])
        grads = (soft * now[1]).astype(bf16)
        added = dot(k_ref[:, rows], grads)
        grad_queries = added if grad_queries is None else grad_queries + added
        sums[rows] += dot(jnp.concatenate([grads, soft.astype(bf16)], axis=1), right)
        now = following

    def columns_of(place):
        return pl.ds(pl.multiple_of(order_ref[place] * block, block), block)

    columns = columns_of(here)
    dq_all[here] = turn_back(
        grad_queries * factor, cos_ref[:, columns], sin_ref[:, columns]
    ).astype(bf16)

    @pl.when(here == length // block - 1)
    def _():
        for place, dp_ref in enumerate(dp_refs):
            columns = columns_of(place)
            both = sums[columns].T
            dp_ref[:HDIM] = dq_all[place]
            dp_ref[HDIM : 2 * HDIM] = turn_back(
                both[:HDIM] * factor, cos_ref[:, columns], sin_ref[:, columns]
            ).astype(bf16)
            dp_ref[2 * HDIM :] = both[HDIM:].astype(bf16)


def attend_back(order, keys, values, qkv, douts, out, lse, cosine, sine, part=256):
    length = keys.shape[0]
    chips = len(douts)
    block = douts[0].shape[1]
    scores = length * length

    def whole(array):
        return pl.BlockSpec(array.shape, lambda i, order: (0, 0))

    return pl.pallas_call(
        functools.partial(attend_back_kernel, part=part),
        name="attend_back",
        grid_spec=pltpu.PrefetchScalarGridSpec(
            num_scalar_prefetch=1,
            grid=(chips,),
            in_specs=[
                whole(keys),
                whole(values),
                pl.BlockSpec((HDIM, block), lambda i, order: (0, order[i])),
                pl.BlockSpec((HDIM, length), lambda i, order: (1, 0)),
                pl.BlockSpec((HDIM, block), lambda i, order: (0, order[i])),
                pl.BlockSpec((1, block), lambda i, order: (0, order[i])),
                whole(cosine),
                whole(sine),
                *[whole(piece) for piece in douts],
            ],
            out_specs=[pl.BlockSpec((3 * HDIM, block), lambda i, order: (0, 0))] * chips,
            scratch_shapes=[
                pltpu.VMEM((length, 2 * HDIM), f32),
                pltpu.VMEM((chips, HDIM, block), bf16),
                pltpu.VMEM((chips, HDIM, block), bf16),
            ],
        ),
        out_shape=[jax.ShapeDtypeStruct((3 * HDIM, block), bf16)] * chips,
        compiler_params=pltpu.CompilerParams(vmem_limit_bytes=VMEM),
        cost_estimate=cost(5 * 4 * 2 * scores * HDIM, 8 << 20),
    )(order, keys, values, qkv, qkv, out, lse, cosine, sine, *douts)


def attend_out_kernel(order_ref, attended_ref, *rest):
    piece_refs, (mixed_ref, attn_ref) = rest[:-2], rest[-2:]
    half = attn_ref.shape[1] // 2
    at = 0
    for piece_ref in piece_refs:
        for place in range(piece_ref.shape[0]):
            rows = pl.ds(pl.multiple_of(order_ref[at] * HDIM, HDIM), HDIM)
            attn_ref[rows, :half] = piece_ref[place, :HDIM]
            attn_ref[rows, half:] = piece_ref[place, HDIM:]
            at += 1
    turned = attended_ref[...].astype(f32).T.astype(bf16)
    mixed_ref[...] = dot(turned, attn_ref[...]).astype(bf16)


def attend_out(order, attended, pieces):
    size, tokens = attended.shape
    width = 2 * size

    def whole(*shape):
        return pl.BlockSpec(shape, lambda i, order: (0,) * len(shape))

    return pl.pallas_call(
        attend_out_kernel,
        name="attend_out",
        grid_spec=pltpu.PrefetchScalarGridSpec(
            num_scalar_prefetch=1,
            grid=(1,),
            in_specs=[whole(size, tokens)]
            + [whole(*piece.shape[:2], width // 2) for piece in pieces],
            out_specs=[whole(tokens, width), whole(size, width)],
        ),
        out_shape=[
            jax.ShapeDtypeStruct((tokens, width), bf16),
            jax.ShapeDtypeStruct((size, width), bf16),
        ],
        compiler_params=pltpu.CompilerParams(vmem_limit_bytes=VMEM),
        cost_estimate=cost(2 * 2 * tokens * width * size, 4 << 20),
    )(order, attended, *pieces)


def feed_kernel(
    first_order, second_order, x_ref, ours_ref, theirs_ref, g_ref, *rest, firsts, seconds, axes
):
    weight_refs = []
    start = 0
    for size in (firsts, seconds, seconds, seconds):
        weight_refs.append(rest[start : start + size])
        start += size
    planes, lines, wide, beside = axes

    def put(grads, columns):
        size = grads.shape[0] // (planes * lines * wide)
        low = grads.astype(bf16)
        for plane in range(planes):
            for line in range(lines):
                for far in range(wide):
                    source = ((plane * lines + line) * wide + far) * size
                    target = ((line * wide + far) * planes + plane) * size
                    grads_ref[target : target + size, columns] = low[source : source + size]
    residual_ref, partial_ref, back_ref, grads_ref = rest[-13:-9]
    unit, unit_t, g_t, sum_out, sum_back = rest[-9:-4]
    gate_ref, up_ref, out_ref, rest_ref = rest[-4:]
    here = pl.program_id(0)
    last = pl.num_programs(0) - 1
    width = x_ref.shape[1]
    step = gate_ref.shape[1]

    def join(total, parts, order):
        at = 0
        for part in parts:
            size = part.shape[1]
            for place in range(part.shape[0]):
                total[pl.ds(pl.multiple_of(order[at] * size, size), size)] = part[place]
                at += 1

    def bend(gate, upward):
        cdf = 0.5 + 0.5 * lax.erf(gate * math.sqrt(0.5))
        slope = cdf + gate * jnp.exp(gate * gate * -0.5) * (1.0 / math.sqrt(2.0 * math.pi))
        bent = gate * cdf
        return bent, slope, (bent * upward).astype(bf16)

    @pl.when(here == 0)
    def _():
        residual = (
            x_ref[...].astype(f32) + ours_ref[...].astype(f32) + theirs_ref[...].astype(f32)
        )
        residual_ref[...] = residual
        normed = unit_rows(residual)[0]
        unit[...] = normed.astype(bf16)
        unit_t[...] = normed.T.astype(bf16)
        g_t[...] = g_ref[...].astype(f32).T.astype(bf16)
        join(rest_ref, weight_refs[3], second_order)
        few = rest_ref.shape[1] // 4
        both = dot(unit[...], rest_ref[...])
        grad = dot(g_ref[...], rest_ref[...])[:, 2 * few : 3 * few]
        bent, slope, active = bend(both[:, :few], both[:, few : 2 * few])
        grad_gate = (grad * both[:, few : 2 * few] * slope).astype(bf16)
        grad_up = (grad * bent).astype(bf16)
        blank = jnp.zeros_like(active)
        outs = jnp.concatenate([blank, blank, active, blank], axis=1)
        ins = jnp.concatenate([grad_gate, grad_up, blank, blank], axis=1)
        sum_out[...] = dot(outs, rest_ref[...], 1, 1)
        sum_back[...] = dot(ins, rest_ref[...], 1, 1)
        put(
            dot(unit_t[...], ins) + dot(g_t[...], outs),
            slice(grads_ref.shape[1] - 4 * few, grads_ref.shape[1]),
        )

    join(gate_ref, weight_refs[0], first_order)
    join(up_ref, weight_refs[1], second_order)
    join(out_ref, weight_refs[2], second_order)
    gate = dot(unit[...], gate_ref[...])
    upward = dot(unit[...], up_ref[...])
    grad = dot(g_ref[...], out_ref[...])
    bent, slope, active = bend(gate, upward)
    grad_gate = (grad * upward * slope).astype(bf16)
    grad_up = (grad * bent).astype(bf16)
    sum_out[...] += dot(active, out_ref[...], 1, 1)
    sum_back[...] += dot(grad_gate, gate_ref[...], 1, 1) + dot(grad_up, up_ref[...], 1, 1)
    count = grads_ref.shape[1] // step // 3
    for at, grads in enumerate(
        (dot(unit_t[...], grad_gate), dot(unit_t[...], grad_up), dot(g_t[...], active))
    ):
        place = pl.multiple_of(at * count * step + here * step, 128)
        put(grads, pl.ds(place, step))

    @pl.when(here == last)
    def _():
        partial_ref[...] = sum_out[...].astype(bf16)
        back_ref[...] = sum_back[...].astype(bf16)


def feed(first_order, second_order, x, ours, theirs, g, first, second, axes, step=256):
    tokens, width = x.shape
    start = width // 2 // step
    count = (first[0].shape[2] - width // 2) // step
    rest = second[0].shape[2] - 2 * count * step
    columns = 3 * count * step + rest

    def whole(*shape):
        return pl.BlockSpec(shape, lambda i, one, two: (0, 0))

    def piece(arrays, size, at):
        return [
            pl.BlockSpec((*array.shape[:2], size), lambda i, one, two: (0, 0, at(i)))
            for array in arrays
        ]

    pair = jax.ShapeDtypeStruct((tokens, width), bf16)
    return pl.pallas_call(
        functools.partial(feed_kernel, firsts=len(first), seconds=len(second), axes=axes),
        name="feed",
        grid_spec=pltpu.PrefetchScalarGridSpec(
            num_scalar_prefetch=2,
            grid=(count,),
            in_specs=[whole(tokens, width)] * 4
            + piece(first, step, lambda i: start + i)
            + piece(second, step, lambda i: i)
            + piece(second, step, lambda i: count + i)
            + piece(second, rest, lambda i: 2 * count * step // rest),
            out_specs=[whole(tokens, width)] * 3 + [whole(width, columns)],
            scratch_shapes=[
                pltpu.VMEM((tokens, width), bf16),
                pltpu.VMEM((width, tokens), bf16),
                pltpu.VMEM((width, tokens), bf16),
                pltpu.VMEM((tokens, width), f32),
                pltpu.VMEM((tokens, width), f32),
                pltpu.VMEM((width, step), bf16),
                pltpu.VMEM((width, step), bf16),
                pltpu.VMEM((width, step), bf16),
                pltpu.VMEM((width, rest), bf16),
            ],
        ),
        out_shape=[
            jax.ShapeDtypeStruct((tokens, width), f32),
            pair,
            pair,
            jax.ShapeDtypeStruct((width, columns), bf16),
        ],
        compiler_params=pltpu.CompilerParams(vmem_limit_bytes=VMEM),
        cost_estimate=cost(2 * 9 * 2 * tokens * width * count * step, 24 << 20),
    )(first_order, second_order, x, ours, theirs, g, *first, *second, *second, *second)


def middle_back_kernel(
    core_ref, order_ref, line_ref, residual_ref, g_ref, ours_ref, theirs_ref, attn_ref,
    attended_ref, out_ours_ref, out_theirs_ref, layer_ref, residual_grad_ref, *rest, axes,
):
    planes, lines, wide, beside = axes
    dout_refs, grads_refs, (dout_all, grads_all) = rest[: -2 - lines], rest[-2 - lines : -2], rest[-2:]
    rows = layer_ref.shape[0]
    half = attn_ref.shape[0]
    own = pl.ds(pl.multiple_of(core_ref[0] * rows, rows), rows)
    layer_ref[...] = (
        residual_ref[own, :]
        + out_ours_ref[own, :].astype(f32)
        + out_theirs_ref[...].astype(f32)
    ).astype(bf16)
    unit, inverse = unit_rows(residual_ref[...])
    scaled = ours_ref[...].astype(f32) + theirs_ref[...].astype(f32)
    grad = g_ref[...].astype(f32) + unit_back(scaled, unit, inverse)
    low = grad.astype(bf16)
    residual_grad_ref[...] = grad
    dout_all[...] = dot(attn_ref[...], low, 1, 1).astype(bf16)
    for at, dout_ref in enumerate(dout_refs):
        dout_ref[...] = dout_all[pl.ds(pl.multiple_of(order_ref[at] * HDIM, HDIM), HDIM)]
    grads_all[...] = dot(attended_ref[...], low)
    few = HDIM // wide // beside
    for shift, grads_ref in enumerate(grads_refs):
        line = (line_ref[0] + shift) % lines
        blocks = [
            grads_all[pl.ds(pl.multiple_of((plane * lines + line) * HDIM, HDIM), HDIM)]
            for plane in range(planes)
        ]
        pieces = []
        for far in range(wide):
            for plane in range(planes):
                for near in range(beside):
                    start = (far * beside + near) * few
                    piece = blocks[plane][start : start + few]
                    pieces += [piece[:, :half], piece[:, half:]]
        grads_ref[...] = jnp.concatenate(pieces, axis=0).astype(bf16)


def middle_back(
    core, order, line, residual, g, ours, theirs, attn, attended, out_ours, out_theirs, axes
):
    tokens, width = residual.shape
    rows = tokens // 2
    half = width // 2
    chips = half // HDIM
    lines = axes[1]

    def whole(*shape):
        return pl.BlockSpec(shape, lambda i, core, order, line: (0,) * len(shape))

    return pl.pallas_call(
        functools.partial(middle_back_kernel, axes=axes),
        name="middle_back",
        grid_spec=pltpu.PrefetchScalarGridSpec(
            num_scalar_prefetch=3,
            grid=(1,),
            in_specs=[whole(tokens, width)] * 4
            + [whole(half, width), whole(half, tokens), whole(tokens, width), whole(rows, width)],
            out_specs=[whole(rows, width), whole(tokens, width)]
            + [whole(HDIM, tokens)] * chips
            + [whole(width // lines, half)] * lines,
            scratch_shapes=[pltpu.VMEM((half, tokens), bf16), pltpu.VMEM((half, width), f32)],
        ),
        out_shape=[
            jax.ShapeDtypeStruct((rows, width), bf16),
            jax.ShapeDtypeStruct((tokens, width), f32),
        ]
        + [jax.ShapeDtypeStruct((HDIM, tokens), bf16)] * chips
        + [jax.ShapeDtypeStruct((width // lines, half), bf16)] * lines,
        compiler_params=pltpu.CompilerParams(vmem_limit_bytes=VMEM),
        cost_estimate=cost(2 * 2 * 2 * tokens * width * half, 16 << 20),
    )(core, order, line, residual, g, ours, theirs, attn, attended, out_ours, out_theirs)


def hidden_back_kernel(order_ref, core_ref, w_ref, *rest):
    dp_refs, (own_ref, other_ref, stacked) = rest[:-3], rest[-3:]
    for place, dp_ref in enumerate(dp_refs):
        size = dp_ref.shape[0]
        stacked[pl.ds(pl.multiple_of(order_ref[place] * size, 64), size)] = dp_ref[...]
    rows = own_ref.shape[0]
    flat = dot(w_ref[...], stacked[...])
    first = flat[:, :rows].T
    second = flat[:, rows:].T
    zero = core_ref[0] == 0
    own_ref[...] = jnp.where(zero, first, second)
    other_ref[...] = jnp.where(zero, second, first).astype(bf16)


def hidden_back(order, core, weights, pieces):
    width, columns = weights.shape
    rows = pieces[0].shape[1] // 2

    def whole(*shape):
        return pl.BlockSpec(shape, lambda i, order, core: (0,) * len(shape))

    return pl.pallas_call(
        hidden_back_kernel,
        name="hidden_back",
        grid_spec=pltpu.PrefetchScalarGridSpec(
            num_scalar_prefetch=2,
            grid=(1,),
            in_specs=[whole(width, columns)] + [whole(*pieces[0].shape)] * len(pieces),
            out_specs=[whole(rows, width)] * 2,
            scratch_shapes=[pltpu.VMEM((columns, 2 * rows), bf16)],
        ),
        out_shape=[
            jax.ShapeDtypeStruct((rows, width), f32),
            jax.ShapeDtypeStruct((rows, width), bf16),
        ],
        compiler_params=pltpu.CompilerParams(vmem_limit_bytes=VMEM),
        cost_estimate=cost(2 * 2 * 2 * rows * width * columns, 8 << 20),
    )(order, core, weights, *pieces)


def head_grad_kernel(order_ref, owner_ref, unit_ref, *rest, owners):
    dp_refs, out_refs, out_all = rest[: -1 - owners], rest[-1 - owners : -1], rest[-1]
    block = dp_refs[0].shape[1]
    total = None
    for place, dp_ref in enumerate(dp_refs):
        rows = pl.ds(pl.multiple_of(order_ref[place] * block, block), block)
        added = dot(dp_ref[...], unit_ref[rows])
        total = added if total is None else total + added
    for at in range(owners):
        out_all[at] = total[:, at * 128 : (at + 1) * 128].astype(bf16)
    for at, out_ref in enumerate(out_refs):
        out_ref[...] = out_all[owner_ref[at]]


def head_grad(order, owner_order, unit_all, pieces):
    length, width = unit_all.shape
    owners = width // 128
    size = pieces[0].shape[0]

    def whole(*shape):
        return pl.BlockSpec(shape, lambda i, order, owner: (0,) * len(shape))

    return pl.pallas_call(
        functools.partial(head_grad_kernel, owners=owners),
        name="head_grad",
        grid_spec=pltpu.PrefetchScalarGridSpec(
            num_scalar_prefetch=2,
            grid=(1,),
            in_specs=[whole(length, width)] + [whole(*pieces[0].shape)] * len(pieces),
            out_specs=[whole(size, 128)] * owners,
            scratch_shapes=[pltpu.VMEM((owners, size, 128), bf16)],
        ),
        out_shape=[jax.ShapeDtypeStruct((size, 128), bf16)] * owners,
        compiler_params=pltpu.CompilerParams(vmem_limit_bytes=VMEM),
        cost_estimate=cost(2 * 2 * length * width * size, 10 << 20),
    )(order, owner_order, unit_all, *pieces)


def adam(weight, gradient, first, second, rate):
    first = BETA_FIRST * first + (1.0 - BETA_FIRST) * gradient
    second = BETA_SECOND * second + (1.0 - BETA_SECOND) * gradient * gradient
    first_hat = first / (1.0 - BETA_FIRST**STEP)
    second_hat = second / (1.0 - BETA_SECOND**STEP)
    weight = weight - rate * (first_hat / (jnp.sqrt(second_hat) + EPSILON) + DECAY * weight)
    return (weight, first, second)


def adam_into(refs, weight, gradient, first, second, rate):
    for ref, value in zip(refs, adam(weight, gradient, first, second, rate)):
        ref[...] = value


def rounded_in_kernel(values):
    return values.astype(bf16).astype(f32)


def adam_in_kernel(
    grads_ref, gain_ref, w_ref, m_ref, v_ref, new_w, new_m, new_v, gain_grad, *, rate
):
    width = m_ref.shape[1] // 2
    main = width // 256 * 128
    few = width // 2 - main
    columns = []
    for at in range(2):
        for core in range(2):
            place = at * main
            columns.append(grads_ref[core, :, place : place + main].astype(f32))
        for core in range(2):
            rest = grads_ref[core, :, 3 * main : 3 * main + 128].astype(f32)
            columns.append(rest[:, at * few : (at + 1) * few])
    grads = jnp.concatenate(columns, axis=1)
    weight = w_ref[...]
    gain_grad[...] = jnp.sum(grads * rounded_in_kernel(weight), axis=1, keepdims=True)
    adam_into(
        (new_w, new_m, new_v), weight, grads * gain_ref[...], m_ref[...], v_ref[...], rate
    )


def adam_in(grads, gain, weight, first, second, rate):
    rows, columns = weight.shape
    steps = grads.shape[0] // 2
    block = pl.BlockSpec((rows // steps, columns), lambda i: (i, 0))
    column = pl.BlockSpec((rows // steps, 1), lambda i: (i, 0))
    same = jax.ShapeDtypeStruct((rows, columns), f32)
    return pl.pallas_call(
        functools.partial(adam_in_kernel, rate=rate),
        name="adam_in",
        grid=(steps,),
        in_specs=[pl.BlockSpec((2,) + grads.shape[1:], lambda i: (i, 0, 0)), column]
        + [block] * 3,
        out_specs=[block] * 3 + [column],
        out_shape=[same] * 3 + [jax.ShapeDtypeStruct((rows, 1), f32)],
        compiler_params=pltpu.CompilerParams(vmem_limit_bytes=VMEM),
        cost_estimate=cost(rows * columns * 20, rows * columns * 26),
    )(grads, gain, weight, first, second)


def adam_rest_kernel(grads_ref, *refs, rates):
    attn, out, new_attn, new_out = refs[:3], refs[3:6], refs[6:9], refs[9:]
    chips = grads_ref.shape[0] // 2
    hidden = out[0].shape[0]
    main = hidden // 256 * 128
    few = hidden // 2 - main
    pieces = []
    for core in range(2):
        for chip in range(chips):
            piece = grads_ref[2 * chip + core, :, 3 * main + 128 :].astype(f32)
            pieces.append(jnp.concatenate([piece[:8], piece[8:]], axis=1))
    grads = jnp.concatenate(pieces, axis=0)
    adam_into(new_attn, attn[0][...], grads, attn[1][...], attn[2][...], rates[0])
    for core in range(2):
        columns = jnp.concatenate(
            [grads_ref[2 * chip + core, :, 2 * main : 3 * main] for chip in range(chips)], axis=0
        )
        rest = jnp.concatenate(
            [grads_ref[2 * chip + core, :, 3 * main : 3 * main + 128] for chip in range(chips)],
            axis=0,
        )
        for rows, grads in (
            (slice(core * main, (core + 1) * main), columns.astype(f32).T),
            (
                slice(2 * main + core * few, 2 * main + (core + 1) * few),
                rest.astype(f32).T[2 * few : 3 * few],
            ),
        ):
            new = adam(out[0][rows], grads, out[1][rows], out[2][rows], rates[1])
            for ref, value in zip(new_out, new):
                ref[rows] = value


def adam_rest(grads, attn, out, rates):
    def whole(array):
        return pl.BlockSpec(array.shape, lambda i: (0,) * array.ndim)

    arrays = (*attn, *out)
    return pl.pallas_call(
        functools.partial(adam_rest_kernel, rates=rates),
        name="adam_rest",
        grid=(1,),
        in_specs=[whole(array) for array in (grads, *arrays)],
        out_specs=[whole(array) for array in arrays],
        out_shape=[jax.ShapeDtypeStruct(array.shape, f32) for array in arrays],
        compiler_params=pltpu.CompilerParams(vmem_limit_bytes=VMEM),
        cost_estimate=cost(attn[0].size * 60, 14 << 20),
    )(grads, *arrays)


def adam_qkv_kernel(order_ref, *refs, rate):
    grads_refs, (gain_ref, w_ref, m_ref, v_ref, new_w, new_m, new_v, gain_grad, joined) = (
        refs[:-9], refs[-9:]
    )
    here = pl.program_id(0)
    rows = pl.ds(pl.multiple_of(here * HDIM, HDIM), HDIM)
    at = 0
    for grads_ref in grads_refs:
        for place in range(grads_ref.shape[0]):
            head = pl.ds(pl.multiple_of(order_ref[at] * HDIM, HDIM), HDIM)
            joined[head] = grads_ref[place, rows].astype(f32)
            at += 1
    grads = joined[...].T
    weight = w_ref[...]
    added = jnp.sum(grads * rounded_in_kernel(weight), axis=1, keepdims=True)
    gain_grad[...] = added + jnp.where(here == 0, 0.0, gain_grad[...])
    adam_into(
        (new_w, new_m, new_v), weight, grads * gain_ref[...], m_ref[...], v_ref[...], rate
    )


def adam_qkv(order, grads, gain, weight, first, second, rate):
    rows, columns = weight.shape
    block = pl.BlockSpec((rows, columns // 3), lambda i, order: (0, i))
    column = pl.BlockSpec((rows, 1), lambda i, order: (0, 0))
    same = jax.ShapeDtypeStruct((rows, columns), f32)
    return pl.pallas_call(
        functools.partial(adam_qkv_kernel, rate=rate),
        name="adam_qkv",
        grid_spec=pltpu.PrefetchScalarGridSpec(
            num_scalar_prefetch=1,
            grid=(3,),
            in_specs=[pl.BlockSpec((piece.shape[0], 3 * HDIM, 128), lambda i, order: (0, 0, 0)) for piece in grads]
            + [column]
            + [block] * 3,
            out_specs=[block] * 3 + [column],
            scratch_shapes=[pltpu.VMEM((columns // 3, rows), f32)],
        ),
        out_shape=[same] * 3 + [jax.ShapeDtypeStruct((rows, 1), f32)],
        compiler_params=pltpu.CompilerParams(vmem_limit_bytes=VMEM),
        cost_estimate=cost(rows * columns * 20, rows * columns * 26),
    )(order, *grads, gain, weight, first, second)


def ring(axis, shift):
    size = lax.axis_size(axis)
    return [(at, (at + shift) % size) for at in range(size)]


def gather_first_step(planes_first, lines_first):
    swapped = lax.ppermute(planes_first, "zh", SWAP)
    others = [
        lax.ppermute(lines_first, "y", ring("y", shift)) for shift in range(1, lax.axis_size("y"))
    ]
    return jnp.stack([planes_first, swapped]), jnp.stack([lines_first, *others])


def shards(
    tokens,
    positions,
    cotangent,
    weight_qkv,
    weight_attn,
    weight_in,
    weight_out,
    norm_gains,
    first_qkv,
    first_attn,
    first_in,
    first_out,
    first_gains,
    second_qkv,
    second_attn,
    second_in,
    second_out,
    second_gains,
):
    rows, width = tokens.shape[1:]
    shard_rows = weight_qkv.shape[1]
    heads = width // HDIM
    hidden = weight_out.shape[1]
    core = lax.axis_index("c")
    mine = lax.axis_index(CTX)
    chip = lax.axis_index(CHIPS)
    chips = lax.axis_size(CHIPS)
    owners = lax.axis_size(FSDP)
    length = rows * chips * 2
    main = hidden // 256 * 128
    few = hidden // 2 - main
    core_at = core.reshape(1).astype(jnp.int32)
    axes = (lax.axis_size("zh"), lax.axis_size("y"), lax.axis_size("x"), lax.axis_size("zl"))
    offsets = [(far, near) for far in range(lax.axis_size("x")) for near in range(2)]
    across, beside = lax.axis_index("x"), lax.axis_index("zl")
    wide = lax.axis_size("x")

    def chips_at(sign):
        places = [(across + sign * far) % wide * 2 + (beside ^ near) for far, near in offsets]
        return jnp.stack(places).astype(jnp.int32)

    local = tokens[0]
    extra = 16
    high, low = positions[0] // 128, positions[0] % 128
    places_row = jnp.concatenate([high, low, jnp.zeros((width - 2 * rows,), jnp.int32)])
    places_rows = jnp.concatenate(
        [places_row[None], jnp.zeros((extra - 1, width), jnp.int32)], axis=0
    ).astype(bf16)
    sequence = lax.all_gather(
        jnp.concatenate([local, places_rows], axis=0), CTX, axis=0, tiled=True
    )
    first_part, second_part, head_part, half_heads = prepare(
        jnp.stack([core, chip]).astype(jnp.int32),
        norm_gains[0],
        weight_qkv[0],
        weight_attn[0],
        weight_in[0],
        weight_out[0],
    )
    first_joined, second_joined = gather_first_step(first_part, second_part)
    head_weights = lax.all_to_all(
        jnp.broadcast_to(head_part, (owners, *head_part.shape)), FSDP, 0, 0, tiled=True
    )
    first_pieces = [first_joined] + [
        lax.ppermute(first_joined, "y", ring("y", shift))
        for shift in range(1, lax.axis_size("y"))
    ]
    sequence, _, second_joined, _ = lax.optimization_barrier(
        (sequence, first_joined, second_joined, head_weights)
    )
    second_pieces = [second_joined, lax.ppermute(second_joined, "zh", SWAP)]
    lines = lax.axis_size("y")
    plane, line = lax.axis_index("zh"), lax.axis_index("y")
    first_order = jnp.stack(
        [(plane ^ far) * lines + (line - shift) % lines for shift in range(lines) for far in range(2)]
    ).astype(jnp.int32)
    second_order = jnp.stack(
        [(plane ^ far) * lines + (line - shift) % lines for far in range(2) for shift in range(lines)]
    ).astype(jnp.int32)

    def in_order(ours, theirs):
        first = jnp.where(core == 0, ours, theirs)
        second = jnp.where(core == 0, theirs, ours)
        return jnp.concatenate([first, second], axis=0)

    def swap(array):
        return lax.ppermute(array, "c", SWAP)

    gradient = in_order(cotangent[0], swap(cotangent[0]))

    freqs = jnp.exp(jnp.arange(HDIM // 2, dtype=f32) * (-2.0 * math.log(ROPE_BASE) / HDIM))
    by_device = sequence.reshape(2 * chips, rows + extra, width)[:, rows]
    by_device = by_device.astype(f32)
    places = by_device[:, :rows] * 128.0 + by_device[:, rows : 2 * rows]
    angles = freqs[:, None] * places.reshape(1, length)
    cosine = jnp.cos(angles)
    sine = jnp.sin(angles)
    unit_all, qkv, keys, values = project(sequence, head_weights, cosine, sine)
    low_out, out, lse = attend(keys, qkv, chips)
    half_heads, low_out = lax.optimization_barrier((half_heads, low_out))
    mat_qkv = lax.all_gather(half_heads, FSDP, axis=0, tiled=True)
    attended = lax.all_to_all(low_out, CHIPS, 0, 0, tiled=True)
    attended = attended.reshape(heads // 2 * HDIM, 2 * rows)
    mixed, mat_attn = attend_out(first_order, attended, first_pieces)
    current = lax.dynamic_slice_in_dim(
        sequence, chip * 2 * (rows + extra), 2 * (rows + extra), 0
    ).reshape(2, rows + extra, width)[:, :rows].reshape(2 * rows, width)
    residual, partial, back, grads = feed(
        first_order, second_order, current, mixed, swap(mixed), gradient, first_pieces,
        second_pieces, axes,
    )
    first_sum = lax.psum_scatter(grads, "y", scatter_dimension=0, tiled=True)

    def move(pieces, sign):
        moved = [pieces[0]]
        for (far, near), piece in list(zip(offsets, pieces))[1:]:
            pairs = [
                (at, (at // 2 + sign * far) % wide * 2 + (at % 2 ^ near)) for at in range(chips)
            ]
            moved.append(lax.ppermute(piece, CHIPS, pairs))
        return moved

    ahead, behind = chips_at(1), chips_at(-1)
    theirs = swap(lax.dynamic_slice_in_dim(partial, (1 - core) * rows, rows, 0))
    layer_out, residual_grad, *pieces = middle_back(
        core_at, ahead, line.reshape(1).astype(jnp.int32), residual, gradient, back, swap(back),
        mat_attn, attended, partial, theirs, axes,
    )
    dout_pieces, attn_pieces = pieces[:chips], pieces[chips:]

    douts = move(dout_pieces, 1)
    attn_arrived = attn_pieces[:1] + [
        lax.ppermute(piece, "y", ring("y", shift))
        for shift, piece in list(enumerate(attn_pieces))[1:]
    ]
    pieces = attend_back(behind, keys, values, qkv, douts, out, lse, cosine, sine)
    owner_places = [(far, shift) for far in range(2) for shift in range(lines)]
    owner_order = jnp.stack(
        [(plane ^ far) * lines + (line + shift) % lines for far, shift in owner_places]
    ).astype(jnp.int32)
    head_parts = head_grad(behind, owner_order, unit_all, pieces)

    def total(arrays):
        return sum(array.astype(f32) for array in arrays).astype(bf16)

    first_sum, *head_parts = lax.optimization_barrier((first_sum, *head_parts))
    first_sum = jnp.concatenate([first_sum, total(attn_arrived)], axis=1)
    first_sum, *pieces = lax.optimization_barrier((first_sum, *pieces))
    arrived = lax.all_to_all(first_sum, ("x", "zh", "zl"), 0, 0, tiled=True)

    moved = move(pieces, -1)
    own_hidden, other_hidden = hidden_back(ahead, core_at, mat_qkv, moved)
    grad_hidden = own_hidden + swap(other_hidden).astype(f32)
    unit_in, scale_in = unit_rows(local.astype(f32))
    own_residual = lax.dynamic_slice_in_dim(residual_grad, core * rows, rows, 0)
    tokens_grad = (own_residual + unit_back(grad_hidden, unit_in, scale_in))[None]

    head_arrived = [head_parts[0]]
    for (far, shift), piece in list(zip(owner_places, head_parts))[1:]:
        pairs = [
            (at, (at // lines ^ far) * lines + (at % lines + shift) % lines) for at in range(owners)
        ]
        head_arrived.append(lax.ppermute(piece, FSDP, pairs))
    head_own = total(head_arrived)[None]
    arrived, head_own = lax.optimization_barrier((arrived, head_own))
    arrived = arrived.reshape(2 * chips, shard_rows // chips, -1)
    second_sum = jnp.sum(arrived.astype(f32), axis=0).astype(bf16)
    all_grads = lax.all_gather(second_sum, CTX, axis=0, tiled=False)

    head_pair = jnp.concatenate([head_own, swap(head_own)], axis=0)
    head_four = jnp.concatenate([head_pair, lax.ppermute(head_pair, "zl", SWAP)], axis=0)
    head_grads = [head_four] + [
        lax.ppermute(head_four, "x", ring("x", shift)) for shift in range(1, wide)
    ]
    head_order = jnp.stack(
        [
            (across - shift) % wide * 4 + (beside ^ near) * 2 + (core ^ other)
            for shift in range(wide)
            for near in range(2)
            for other in range(2)
        ]
    ).astype(jnp.int32)

    rates = (
        width ** (-0.5),
        max(1, 3 * width // length) ** (-0.5),
        width ** (-0.5),
        hidden ** (-0.5),
    )
    columns_of_gains = norm_gains[0].astype(bf16).astype(f32).T
    *new_in, gain_second = adam_in(
        all_grads, columns_of_gains[:, 1:], weight_in[0], first_in[0], second_in[0], rates[2]
    )
    rest = adam_rest(
        all_grads,
        (weight_attn[0], first_attn[0], second_attn[0]),
        (weight_out[0], first_out[0], second_out[0]),
        (rates[1], rates[3]),
    )
    *new_qkv, gain_first = adam_qkv(
        head_order, head_grads, columns_of_gains[:, :1], weight_qkv[0], first_qkv[0], second_qkv[0], rates[0]
    )
    gain_grads = jnp.concatenate([gain_first, gain_second], axis=1).T
    new_gains = adam(norm_gains[0], gain_grads, first_gains[0], second_gains[0], GAIN_RATE)
    updated = (new_qkv, rest[:3], new_in, rest[3:], new_gains)
    return (
        layer_out[None],
        tokens_grad,
        *[updated[member][0][None] for member in range(5)],
        *[updated[member][1][None] for member in range(5)],
        *[updated[member][2][None] for member in range(5)],
    )


def solution(mesh):
    split = Mesh(mesh.devices.reshape(4, 2, 2, 2, 4), ("x", "zl", "c", "zh", "y"))
    by_row = P(None, FSDP, None)
    by_column = P(None, None, FSDP)
    weights = (by_row, by_row, by_row, by_column, by_column)
    by_token = P(FSDP, CTX, None)
    return jax.shard_map(
        shards,
        mesh=split,
        in_specs=(by_token, P(FSDP, CTX), by_token) + weights * 3,
        out_specs=(by_token, by_token) + weights * 3,
        check_vma=False,
    )
```

```python
import functools
import math

import jax
import jax.numpy as jnp
from jax import lax
from jax.experimental import pallas as pl
from jax.experimental.pallas import tpu as pltpu
from jax.sharding import Mesh, PartitionSpec as P

HDIM = 64
STEP = 10
BETA_FIRST = 0.5
BETA_SECOND = 0.5
EPSILON = 1e-08
DECAY = 0.01
NORM_EPS = 1e-05
ROPE_BASE = 160000.0
GAIN_RATE = 0.6
LOG2E = math.log2(math.e)
f32 = jnp.float32
bf16 = jnp.bfloat16

CHIPS = ("x", "zl")
CTX = ("x", "zl", "c")
FSDP = ("zh", "y")
SWAP = [(0, 1), (1, 0)]
VMEM = 60 << 20


def dot(left, right, left_dim=1, right_dim=0):
    return lax.dot_general(
        left, right, (((left_dim,), (right_dim,)), ((), ())), preferred_element_type=f32
    )


def cost(flops, moved):
    return pl.CostEstimate(flops=flops, bytes_accessed=moved, transcendentals=0)


def unit_rows(values):
    average = jnp.mean(values, axis=-1, keepdims=True)
    centered = values - average
    spread = jnp.mean(centered * centered, axis=-1, keepdims=True)
    inverse = lax.rsqrt(spread + NORM_EPS)
    return centered * inverse, inverse


def unit_back(scaled, unit, inverse):
    first_mean = jnp.mean(scaled, axis=-1, keepdims=True)
    second_mean = jnp.mean(scaled * unit, axis=-1, keepdims=True)
    return inverse * (scaled - first_mean - unit * second_mean)


def prepare_kernel(
    place_ref, gains_ref, qkv_ref, attn_ref, in_ref, out_ref,
    first_ref, second_ref, head_ref, heads_ref,
):
    core, chip = place_ref[0], place_ref[1]
    rows = qkv_ref.shape[0]
    width = attn_ref.shape[1]
    hidden = out_ref.shape[0]
    main = hidden // 256 * 128
    few = hidden // 2 - main
    half = width // 2
    low_gains = gains_ref[...].astype(bf16).astype(f32)
    columns = jnp.concatenate([low_gains, jnp.zeros((6, rows), f32)], axis=0).T
    gain_first, gain_second = columns[:, 0:1], columns[:, 1:2]

    def pick(array):
        size = array.shape[1] // 2
        return jnp.where(core == 0, array[:, :size], array[:, size:])

    def scaled(values, gain):
        return (values.astype(bf16).astype(f32) * gain).astype(bf16)

    attn_rows = attn_ref[pl.ds(pl.multiple_of(core * HDIM, HDIM), HDIM)].astype(bf16)
    first_ref[:HDIM, :half] = attn_rows[:, :half]
    first_ref[HDIM:, :half] = attn_rows[:, half:]
    first_ref[:, half : half + main] = scaled(pick(in_ref[:, : 2 * main]), gain_second)
    first_ref[:, half + main :] = scaled(pick(in_ref[:, hidden : hidden + 2 * main]), gain_second)
    out_rows = out_ref[pl.ds(pl.multiple_of(core * main, 128), main)]
    second_ref[:, :main] = out_rows.T.astype(bf16)
    odd_out = out_ref[2 * main :].T
    odd = [
        scaled(pick(in_ref[:, 2 * main : hidden]), gain_second),
        scaled(pick(in_ref[:, hidden + 2 * main :]), gain_second),
        pick(odd_out).astype(bf16),
        jnp.zeros((rows, few), bf16),
    ]
    second_ref[:, main:] = jnp.concatenate(odd, axis=1)
    pieces = []
    for at in range(width // 128):
        for part in range(3):
            start = part * width + at * 128
            pieces.append(scaled(pick(qkv_ref[:, start : start + 128]), gain_first))
    heads_ref[...] = jnp.concatenate(pieces, axis=1)
    own = []
    for part in range(3):
        start = pl.multiple_of(part * width + chip * 128, 128)
        own.append(scaled(pick(qkv_ref[:, pl.ds(start, 128)]), gain_first).astype(f32))
    own.append(jnp.zeros((rows, HDIM), f32))
    head_ref[...] = jnp.concatenate(own, axis=1).T[: 3 * HDIM].astype(bf16)


def prepare(place, gains, qkv, attn, weight_in, weight_out):
    rows, width = attn.shape
    hidden = weight_out.shape[0]
    main = hidden // 256 * 128
    arrays = (gains, qkv, attn, weight_in, weight_out)
    shapes = [
        (rows, width // 2 + 2 * main),
        (rows, main + 4 * (hidden // 2 - main)),
        (3 * HDIM, rows),
        (rows, 3 * width // 2),
    ]

    def whole(shape):
        return pl.BlockSpec(shape, lambda i, place: (0, 0))

    return pl.pallas_call(
        prepare_kernel,
        name="prepare",
        grid_spec=pltpu.PrefetchScalarGridSpec(
            num_scalar_prefetch=1,
            grid=(1,),
            in_specs=[whole(array.shape) for array in arrays],
            out_specs=[whole(shape) for shape in shapes],
        ),
        out_shape=[jax.ShapeDtypeStruct(shape, bf16) for shape in shapes],
        compiler_params=pltpu.CompilerParams(vmem_limit_bytes=VMEM),
        cost_estimate=cost(rows * width * 60, 10 << 20),
    )(place, *arrays)


def project_kernel(
    x_ref, w_ref, cos_ref, sin_ref, unit_ref, qkv_ref, keys_ref, values_ref, w_all, *, extra
):
    half = HDIM // 2
    rows = cos_ref.shape[1]

    @pl.when(pl.program_id(0) == 0)
    def _():
        for part in range(w_ref.shape[0]):
            w_all[part * 128 : (part + 1) * 128] = w_ref[part].astype(f32).T.astype(bf16)

    count = (x_ref.shape[0] - rows) // extra
    each = rows // count
    for at in range(count):
        tokens = x_ref[at * (each + extra) : at * (each + extra) + each].astype(f32)
        unit_ref[at * each : (at + 1) * each] = unit_rows(tokens)[0].astype(bf16)
    unit = unit_ref[...]
    mixed = dot(unit, w_all[...]).T
    cosine = cos_ref[...]
    sine = sin_ref[...]

    def turn(one, two):
        return jnp.concatenate([one * cosine - two * sine, two * cosine + one * sine], axis=0)

    queries = turn(mixed[:half], mixed[half:HDIM])
    keys = turn(mixed[HDIM : HDIM + half], mixed[HDIM + half : 2 * HDIM])
    values = mixed[2 * HDIM :]
    qkv_ref[...] = jnp.concatenate([queries, keys, values], axis=0).astype(bf16)
    key_rows = keys.T.astype(bf16)
    value_rows = values.T.astype(bf16)
    ones = jnp.where(lax.broadcasted_iota(jnp.int32, (rows, 128), 1) < 3, 1.0, 0.0).astype(bf16)
    keys_ref[...] = jnp.concatenate([key_rows, key_rows, ones], axis=1)
    values_ref[...] = jnp.concatenate([value_rows, ones[:, :HDIM]], axis=1)


def project(tokens, weights, cosine, sine, extra, block=1024):
    width = tokens.shape[1]
    length = cosine.shape[1]
    steps = length // block
    return pl.pallas_call(
        functools.partial(project_kernel, extra=extra),
        name="project",
        grid=(steps,),
        in_specs=[
            pl.BlockSpec((tokens.shape[0] // steps, width), lambda i: (i, 0)),
            pl.BlockSpec(weights.shape, lambda i: (0, 0, 0)),
            pl.BlockSpec((HDIM // 2, block), lambda i: (0, i)),
            pl.BlockSpec((HDIM // 2, block), lambda i: (0, i)),
        ],
        out_specs=[
            pl.BlockSpec((block, width), lambda i: (i, 0)),
            pl.BlockSpec((3 * HDIM, block), lambda i: (0, i)),
            pl.BlockSpec((block, 256), lambda i: (i, 0)),
            pl.BlockSpec((block, 128), lambda i: (i, 0)),
        ],
        out_shape=[
            jax.ShapeDtypeStruct((length, width), bf16),
            jax.ShapeDtypeStruct((3 * HDIM, length), bf16),
            jax.ShapeDtypeStruct((length, 256), bf16),
            jax.ShapeDtypeStruct((length, 128), bf16),
        ],
        scratch_shapes=[pltpu.VMEM((width, 3 * HDIM), bf16)],
        compiler_params=pltpu.CompilerParams(vmem_limit_bytes=VMEM),
        cost_estimate=cost(length * width, 1 << 20),
    )(tokens, weights, cosine, sine)


def scaled_queries(queries):
    scaled = queries.astype(f32) * (LOG2E / math.sqrt(HDIM))
    high = scaled.astype(bf16)
    low = (scaled - high.astype(f32)).astype(bf16)
    return high, low


def attend_kernel(keys_ref, q_ref, v_ref, low_ref, out_ref, lse_ref, v_ones, *, part):
    length = keys_ref.shape[0]
    count = length // part

    @pl.when(pl.program_id(0) == 0)
    def _():
        v_ones[:HDIM] = v_ref[...]
        v_ones[HDIM:] = jnp.where(
            lax.broadcasted_iota(jnp.int32, (16, length), 0) < 1, 1.0, 0.0
        ).astype(bf16)

    queries = jnp.concatenate(scaled_queries(q_ref[...]), axis=0)

    def score(at):
        return dot(keys_ref[at * part : (at + 1) * part, : 2 * HDIM], queries)

    scores = score(0)
    highest = total = None
    for at in range(count):
        following = score(at + 1) if at + 1 < count else None
        peak = jnp.max(scores, axis=0, keepdims=True)
        raised = peak if highest is None else jnp.maximum(highest, peak)
        soft = jnp.exp2(scores - raised).astype(bf16)
        added = dot(v_ones[:, at * part : (at + 1) * part], soft)
        total = added if total is None else total * jnp.exp2(highest - raised) + added
        highest = raised
        scores = following
    summed = total[HDIM : HDIM + 1]
    result = total[:HDIM] / summed
    out_ref[...] = result
    lse_ref[...] = highest + jnp.log2(summed)
    step = low_ref.shape[2]
    for at in range(low_ref.shape[0]):
        low_ref[at] = result[:, at * step : (at + 1) * step].astype(bf16)


def attend(keys, qkv, chips, block=1024, part=512):
    length = keys.shape[0]
    return pl.pallas_call(
        functools.partial(attend_kernel, part=part),
        name="attend",
        grid=(length // block,),
        in_specs=[
            pl.BlockSpec(keys.shape, lambda i: (0, 0)),
            pl.BlockSpec((HDIM, block), lambda i: (0, i)),
            pl.BlockSpec((HDIM, length), lambda i: (2, 0)),
        ],
        out_specs=[
            pl.BlockSpec((block * chips // length, HDIM, length // chips), lambda i: (i, 0, 0)),
            pl.BlockSpec((HDIM, block), lambda i: (0, i)),
            pl.BlockSpec((1, block), lambda i: (0, i)),
        ],
        out_shape=[
            jax.ShapeDtypeStruct((chips, HDIM, length // chips), bf16),
            jax.ShapeDtypeStruct((HDIM, length), f32),
            jax.ShapeDtypeStruct((1, length), f32),
        ],
        scratch_shapes=[pltpu.VMEM((HDIM + 16, length), bf16)],
        compiler_params=pltpu.CompilerParams(vmem_limit_bytes=VMEM),
        cost_estimate=cost(length * HDIM, 1 << 20),
    )(keys, qkv, qkv)


def minus_in_three(values):
    rows = values.shape[1]
    at = lax.broadcasted_iota(jnp.int32, (16, rows), 0)
    high = (-values).astype(bf16).astype(f32)
    rest = -values - high
    middle = rest.astype(bf16).astype(f32)
    low = rest - middle
    stacked = jnp.where(at == 0, high, jnp.where(at == 1, middle, jnp.where(at == 2, low, 0.0)))
    return stacked.astype(bf16)


def attend_back_kernel(
    order_ref,
    keys_ref,
    values_ref,
    q_ref,
    k_ref,
    out_ref,
    lse_ref,
    cos_ref,
    sin_ref,
    *rest,
    part,
):
    count = (len(rest) - 3) // 2
    dout_refs, dp_refs, (sums, dq_all, dout_all) = rest[:count], rest[count:-3], rest[-3:]
    half = HDIM // 2
    here = pl.program_id(0)
    length = keys_ref.shape[0]
    block = q_ref.shape[1]
    count = length // part
    factor = HDIM ** (-0.5)

    def turn_back(grads, cosine, sine):
        low = grads.astype(bf16).astype(f32)
        one, two = low[:half], low[half:]
        return jnp.concatenate([one * cosine + two * sine, two * cosine - one * sine], axis=0)

    @pl.when(here == 0)
    def _():
        sums[...] = jnp.zeros_like(sums)
        for place, dout_ref in enumerate(dout_refs):
            dout_all[place] = dout_ref[...]

    low_queries = q_ref[...]
    high, low = scaled_queries(low_queries)
    queries = jnp.concatenate([high, low, minus_in_three(lse_ref[...])], axis=0)
    low_dout = dout_all[here]
    dout = low_dout.astype(f32)
    centre = jnp.sum(dout * out_ref[...], axis=0, keepdims=True)
    douts = jnp.concatenate([low_dout, minus_in_three(centre)], axis=0)
    blank = jnp.zeros((block, HDIM), bf16)
    right = jnp.concatenate(
        [
            jnp.concatenate([low_queries.astype(f32).T.astype(bf16), blank], axis=1),
            jnp.concatenate([blank, dout.T.astype(bf16)], axis=1),
        ],
        axis=0,
    )

    def score(at):
        rows = slice(at * part, (at + 1) * part)
        return (
            dot(keys_ref[rows, : 2 * HDIM + 16], queries),
            dot(values_ref[rows, : HDIM + 16], douts),
        )

    now = score(0)
    grad_queries = None
    for at in range(count):
        following = score(at + 1) if at + 1 < count else None
        rows = slice(at * part, (at + 1) * part)
        soft = jnp.exp2(now[0])
        grads = (soft * now[1]).astype(bf16)
        added = dot(k_ref[:, rows], grads)
        grad_queries = added if grad_queries is None else grad_queries + added
        sums[rows] += dot(jnp.concatenate([grads, soft.astype(bf16)], axis=1), right)
        now = following

    def columns_of(place):
        return pl.ds(pl.multiple_of(order_ref[place] * block, block), block)

    columns = columns_of(here)
    dq_all[here] = turn_back(
        grad_queries * factor, cos_ref[:, columns], sin_ref[:, columns]
    ).astype(bf16)

    @pl.when(here == length // block - 1)
    def _():
        for place, dp_ref in enumerate(dp_refs):
            columns = columns_of(place)
            both = sums[columns].T
            dp_ref[:HDIM] = dq_all[place]
            dp_ref[HDIM : 2 * HDIM] = turn_back(
                both[:HDIM] * factor, cos_ref[:, columns], sin_ref[:, columns]
            ).astype(bf16)
            dp_ref[2 * HDIM :] = both[HDIM:].astype(bf16)


def attend_back(order, keys, values, qkv, douts, out, lse, cosine, sine, part=256):
    length = keys.shape[0]
    chips = len(douts)
    block = douts[0].shape[1]
    scores = length * length

    def whole(array):
        return pl.BlockSpec(array.shape, lambda i, order: (0, 0))

    return pl.pallas_call(
        functools.partial(attend_back_kernel, part=part),
        name="attend_back",
        grid_spec=pltpu.PrefetchScalarGridSpec(
            num_scalar_prefetch=1,
            grid=(chips,),
            in_specs=[
                whole(keys),
                whole(values),
                pl.BlockSpec((HDIM, block), lambda i, order: (0, order[i])),
                pl.BlockSpec((HDIM, length), lambda i, order: (1, 0)),
                pl.BlockSpec((HDIM, block), lambda i, order: (0, order[i])),
                pl.BlockSpec((1, block), lambda i, order: (0, order[i])),
                whole(cosine),
                whole(sine),
                *[whole(piece) for piece in douts],
            ],
            out_specs=[pl.BlockSpec((3 * HDIM, block), lambda i, order: (0, 0))] * chips,
            scratch_shapes=[
                pltpu.VMEM((length, 2 * HDIM), f32),
                pltpu.VMEM((chips, HDIM, block), bf16),
                pltpu.VMEM((chips, HDIM, block), bf16),
            ],
        ),
        out_shape=[jax.ShapeDtypeStruct((3 * HDIM, block), bf16)] * chips,
        compiler_params=pltpu.CompilerParams(vmem_limit_bytes=VMEM),
        cost_estimate=cost(5 * 4 * 2 * scores * HDIM, 8 << 20),
    )(order, keys, values, qkv, qkv, out, lse, cosine, sine, *douts)


def attend_out_kernel(order_ref, attended_ref, *rest):
    piece_refs, (mixed_ref, attn_ref) = rest[:-2], rest[-2:]
    half = attn_ref.shape[1] // 2
    at = 0
    for piece_ref in piece_refs:
        for place in range(piece_ref.shape[0]):
            rows = pl.ds(pl.multiple_of(order_ref[at] * HDIM, HDIM), HDIM)
            attn_ref[rows, :half] = piece_ref[place, :HDIM]
            attn_ref[rows, half:] = piece_ref[place, HDIM:]
            at += 1
    turned = attended_ref[...].astype(f32).T.astype(bf16)
    mixed_ref[...] = dot(turned, attn_ref[...]).astype(bf16)


def attend_out(order, attended, pieces):
    size, tokens = attended.shape
    width = 2 * size

    def whole(*shape):
        return pl.BlockSpec(shape, lambda i, order: (0,) * len(shape))

    return pl.pallas_call(
        attend_out_kernel,
        name="attend_out",
        grid_spec=pltpu.PrefetchScalarGridSpec(
            num_scalar_prefetch=1,
            grid=(1,),
            in_specs=[whole(size, tokens)]
            + [whole(*piece.shape[:2], width // 2) for piece in pieces],
            out_specs=[whole(tokens, width), whole(size, width)],
        ),
        out_shape=[
            jax.ShapeDtypeStruct((tokens, width), bf16),
            jax.ShapeDtypeStruct((size, width), bf16),
        ],
        compiler_params=pltpu.CompilerParams(vmem_limit_bytes=VMEM),
        cost_estimate=cost(2 * 2 * tokens * width * size, 4 << 20),
    )(order, attended, *pieces)


def feed_kernel(
    first_order, second_order, x_ref, ours_ref, theirs_ref, g_ref, *rest, firsts, seconds, axes
):
    weight_refs = []
    start = 0
    for size in (firsts, firsts, seconds, seconds):
        weight_refs.append(rest[start : start + size])
        start += size
    planes, lines, wide, beside = axes

    def put(grads, columns):
        size = grads.shape[0] // (planes * lines * wide)
        low = grads.astype(bf16)
        for plane in range(planes):
            for line in range(lines):
                for far in range(wide):
                    source = ((plane * lines + line) * wide + far) * size
                    target = ((line * wide + far) * planes + plane) * size
                    grads_ref[target : target + size, columns] = low[source : source + size]
    residual_ref, partial_ref, back_ref, grads_ref = rest[-13:-9]
    unit, unit_t, g_t, sum_out, sum_back = rest[-9:-4]
    gate_ref, up_ref, out_ref, rest_ref = rest[-4:]
    here = pl.program_id(0)
    last = pl.num_programs(0) - 1
    width = x_ref.shape[1]
    step = gate_ref.shape[1]

    def join(total, parts, order):
        at = 0
        for part in parts:
            size = part.shape[1]
            for place in range(part.shape[0]):
                total[pl.ds(pl.multiple_of(order[at] * size, size), size)] = part[place]
                at += 1

    def bend(gate, upward):
        cdf = 0.5 + 0.5 * lax.erf(gate * math.sqrt(0.5))
        slope = cdf + gate * jnp.exp(gate * gate * -0.5) * (1.0 / math.sqrt(2.0 * math.pi))
        bent = gate * cdf
        return bent, slope, (bent * upward).astype(bf16)

    @pl.when(here == 0)
    def _():
        residual = (
            x_ref[...].astype(f32) + ours_ref[...].astype(f32) + theirs_ref[...].astype(f32)
        )
        residual_ref[...] = residual
        normed = unit_rows(residual)[0]
        unit[...] = normed.astype(bf16)
        unit_t[...] = normed.T.astype(bf16)
        g_t[...] = g_ref[...].astype(f32).T.astype(bf16)
        join(rest_ref, weight_refs[3], second_order)
        few = rest_ref.shape[1] // 4
        both = dot(unit[...], rest_ref[...])
        grad = dot(g_ref[...], rest_ref[...])[:, 2 * few : 3 * few]
        bent, slope, active = bend(both[:, :few], both[:, few : 2 * few])
        grad_gate = (grad * both[:, few : 2 * few] * slope).astype(bf16)
        grad_up = (grad * bent).astype(bf16)
        blank = jnp.zeros_like(active)
        outs = jnp.concatenate([blank, blank, active, blank], axis=1)
        ins = jnp.concatenate([grad_gate, grad_up, blank, blank], axis=1)
        sum_out[...] = dot(outs, rest_ref[...], 1, 1)
        sum_back[...] = dot(ins, rest_ref[...], 1, 1)
        put(
            dot(unit_t[...], ins) + dot(g_t[...], outs),
            slice(grads_ref.shape[1] - 4 * few, grads_ref.shape[1]),
        )

    join(gate_ref, weight_refs[0], first_order)
    join(up_ref, weight_refs[1], first_order)
    join(out_ref, weight_refs[2], second_order)
    gate = dot(unit[...], gate_ref[...])
    upward = dot(unit[...], up_ref[...])
    grad = dot(g_ref[...], out_ref[...])
    bent, slope, active = bend(gate, upward)
    grad_gate = (grad * upward * slope).astype(bf16)
    grad_up = (grad * bent).astype(bf16)
    sum_out[...] += dot(active, out_ref[...], 1, 1)
    sum_back[...] += dot(grad_gate, gate_ref[...], 1, 1) + dot(grad_up, up_ref[...], 1, 1)
    count = grads_ref.shape[1] // step // 3
    for at, grads in enumerate(
        (dot(unit_t[...], grad_gate), dot(unit_t[...], grad_up), dot(g_t[...], active))
    ):
        place = pl.multiple_of(at * count * step + here * step, 128)
        put(grads, pl.ds(place, step))

    @pl.when(here == last)
    def _():
        partial_ref[...] = sum_out[...].astype(bf16)
        back_ref[...] = sum_back[...].astype(bf16)


def feed(first_order, second_order, x, ours, theirs, g, first, second, axes, step=256):
    tokens, width = x.shape
    start = width // 2 // step
    count = (first[0].shape[2] - width // 2) // step // 2
    rest = second[0].shape[2] - count * step
    columns = 3 * count * step + rest

    def whole(*shape):
        return pl.BlockSpec(shape, lambda i, one, two: (0, 0))

    def piece(arrays, size, at):
        return [
            pl.BlockSpec((*array.shape[:2], size), lambda i, one, two: (0, 0, at(i)))
            for array in arrays
        ]

    pair = jax.ShapeDtypeStruct((tokens, width), bf16)
    return pl.pallas_call(
        functools.partial(feed_kernel, firsts=len(first), seconds=len(second), axes=axes),
        name="feed",
        grid_spec=pltpu.PrefetchScalarGridSpec(
            num_scalar_prefetch=2,
            grid=(count,),
            in_specs=[whole(tokens, width)] * 4
            + piece(first, step, lambda i: start + i)
            + piece(first, step, lambda i: start + count + i)
            + piece(second, step, lambda i: i)
            + piece(second, rest, lambda i: count * step // rest),
            out_specs=[whole(tokens, width)] * 3 + [whole(width, columns)],
            scratch_shapes=[
                pltpu.VMEM((tokens, width), bf16),
                pltpu.VMEM((width, tokens), bf16),
                pltpu.VMEM((width, tokens), bf16),
                pltpu.VMEM((tokens, width), f32),
                pltpu.VMEM((tokens, width), f32),
                pltpu.VMEM((width, step), bf16),
                pltpu.VMEM((width, step), bf16),
                pltpu.VMEM((width, step), bf16),
                pltpu.VMEM((width, rest), bf16),
            ],
        ),
        out_shape=[
            jax.ShapeDtypeStruct((tokens, width), f32),
            pair,
            pair,
            jax.ShapeDtypeStruct((width, columns), bf16),
        ],
        compiler_params=pltpu.CompilerParams(vmem_limit_bytes=VMEM),
        cost_estimate=cost(2 * 9 * 2 * tokens * width * count * step, 24 << 20),
    )(first_order, second_order, x, ours, theirs, g, *first, *first, *second, *second)


def middle_back_kernel(
    core_ref, order_ref, line_ref, residual_ref, g_ref, ours_ref, theirs_ref, attn_ref,
    attended_ref, out_ours_ref, out_theirs_ref, layer_ref, residual_grad_ref, *rest, axes,
):
    planes, lines, wide, beside = axes
    dout_refs, grads_refs, (dout_all, grads_all) = rest[: -2 - lines], rest[-2 - lines : -2], rest[-2:]
    rows = layer_ref.shape[0]
    half = attn_ref.shape[0]
    own = pl.ds(pl.multiple_of(core_ref[0] * rows, rows), rows)
    layer_ref[...] = (
        residual_ref[own, :]
        + out_ours_ref[own, :].astype(f32)
        + out_theirs_ref[...].astype(f32)
    ).astype(bf16)
    unit, inverse = unit_rows(residual_ref[...])
    scaled = ours_ref[...].astype(f32) + theirs_ref[...].astype(f32)
    grad = g_ref[...].astype(f32) + unit_back(scaled, unit, inverse)
    low = grad.astype(bf16)
    residual_grad_ref[...] = grad
    dout_all[...] = dot(attn_ref[...], low, 1, 1).astype(bf16)
    for at, dout_ref in enumerate(dout_refs):
        dout_ref[...] = dout_all[pl.ds(pl.multiple_of(order_ref[at] * HDIM, HDIM), HDIM)]
    grads_all[...] = dot(attended_ref[...], low)
    few = HDIM // wide // beside
    for shift, grads_ref in enumerate(grads_refs):
        line = (line_ref[0] + shift) % lines
        blocks = [
            grads_all[pl.ds(pl.multiple_of((plane * lines + line) * HDIM, HDIM), HDIM)]
            for plane in range(planes)
        ]
        pieces = []
        for far in range(wide):
            for plane in range(planes):
                for near in range(beside):
                    start = (far * beside + near) * few
                    piece = blocks[plane][start : start + few]
                    pieces += [piece[:, :half], piece[:, half:]]
        grads_ref[...] = jnp.concatenate(pieces, axis=0).astype(bf16)


def middle_back(
    core, order, line, residual, g, ours, theirs, attn, attended, out_ours, out_theirs, axes
):
    tokens, width = residual.shape
    rows = tokens // 2
    half = width // 2
    chips = half // HDIM
    lines = axes[1]

    def whole(*shape):
        return pl.BlockSpec(shape, lambda i, core, order, line: (0,) * len(shape))

    return pl.pallas_call(
        functools.partial(middle_back_kernel, axes=axes),
        name="middle_back",
        grid_spec=pltpu.PrefetchScalarGridSpec(
            num_scalar_prefetch=3,
            grid=(1,),
            in_specs=[whole(tokens, width)] * 4
            + [whole(half, width), whole(half, tokens), whole(tokens, width), whole(rows, width)],
            out_specs=[whole(rows, width), whole(tokens, width)]
            + [whole(HDIM, tokens)] * chips
            + [whole(width // lines, half)] * lines,
            scratch_shapes=[pltpu.VMEM((half, tokens), bf16), pltpu.VMEM((half, width), f32)],
        ),
        out_shape=[
            jax.ShapeDtypeStruct((rows, width), bf16),
            jax.ShapeDtypeStruct((tokens, width), f32),
        ]
        + [jax.ShapeDtypeStruct((HDIM, tokens), bf16)] * chips
        + [jax.ShapeDtypeStruct((width // lines, half), bf16)] * lines,
        compiler_params=pltpu.CompilerParams(vmem_limit_bytes=VMEM),
        cost_estimate=cost(2 * 2 * 2 * tokens * width * half, 16 << 20),
    )(core, order, line, residual, g, ours, theirs, attn, attended, out_ours, out_theirs)


def hidden_back_kernel(order_ref, core_ref, w_ref, *rest):
    dp_refs, (own_ref, other_ref, stacked) = rest[:-3], rest[-3:]
    for place, dp_ref in enumerate(dp_refs):
        size = dp_ref.shape[0]
        stacked[pl.ds(pl.multiple_of(order_ref[place] * size, 64), size)] = dp_ref[...]
    rows = own_ref.shape[0]
    flat = dot(w_ref[...], stacked[...])
    first = flat[:, :rows].T
    second = flat[:, rows:].T
    zero = core_ref[0] == 0
    own_ref[...] = jnp.where(zero, first, second)
    other_ref[...] = jnp.where(zero, second, first).astype(bf16)


def hidden_back(order, core, weights, pieces):
    width, columns = weights.shape
    rows = pieces[0].shape[1] // 2

    def whole(*shape):
        return pl.BlockSpec(shape, lambda i, order, core: (0,) * len(shape))

    return pl.pallas_call(
        hidden_back_kernel,
        name="hidden_back",
        grid_spec=pltpu.PrefetchScalarGridSpec(
            num_scalar_prefetch=2,
            grid=(1,),
            in_specs=[whole(width, columns)] + [whole(*pieces[0].shape)] * len(pieces),
            out_specs=[whole(rows, width)] * 2,
            scratch_shapes=[pltpu.VMEM((columns, 2 * rows), bf16)],
        ),
        out_shape=[
            jax.ShapeDtypeStruct((rows, width), f32),
            jax.ShapeDtypeStruct((rows, width), bf16),
        ],
        compiler_params=pltpu.CompilerParams(vmem_limit_bytes=VMEM),
        cost_estimate=cost(2 * 2 * 2 * rows * width * columns, 8 << 20),
    )(order, core, weights, *pieces)


def head_grad_kernel(order_ref, owner_ref, unit_ref, *rest, owners):
    dp_refs, out_refs, out_all = rest[: -1 - owners], rest[-1 - owners : -1], rest[-1]
    block = dp_refs[0].shape[1]
    total = None
    for place, dp_ref in enumerate(dp_refs):
        rows = pl.ds(pl.multiple_of(order_ref[place] * block, block), block)
        added = dot(dp_ref[...], unit_ref[rows])
        total = added if total is None else total + added
    for at in range(owners):
        out_all[at] = total[:, at * 128 : (at + 1) * 128].astype(bf16)
    for at, out_ref in enumerate(out_refs):
        out_ref[...] = out_all[owner_ref[at]]


def head_grad(order, owner_order, unit_all, pieces):
    length, width = unit_all.shape
    owners = width // 128
    size = pieces[0].shape[0]

    def whole(*shape):
        return pl.BlockSpec(shape, lambda i, order, owner: (0,) * len(shape))

    return pl.pallas_call(
        functools.partial(head_grad_kernel, owners=owners),
        name="head_grad",
        grid_spec=pltpu.PrefetchScalarGridSpec(
            num_scalar_prefetch=2,
            grid=(1,),
            in_specs=[whole(length, width)] + [whole(*pieces[0].shape)] * len(pieces),
            out_specs=[whole(size, 128)] * owners,
            scratch_shapes=[pltpu.VMEM((owners, size, 128), bf16)],
        ),
        out_shape=[jax.ShapeDtypeStruct((size, 128), bf16)] * owners,
        compiler_params=pltpu.CompilerParams(vmem_limit_bytes=VMEM),
        cost_estimate=cost(2 * 2 * length * width * size, 10 << 20),
    )(order, owner_order, unit_all, *pieces)


def adam(weight, gradient, first, second, rate):
    first = BETA_FIRST * first + (1.0 - BETA_FIRST) * gradient
    second = BETA_SECOND * second + (1.0 - BETA_SECOND) * gradient * gradient
    first_hat = first / (1.0 - BETA_FIRST**STEP)
    second_hat = second / (1.0 - BETA_SECOND**STEP)
    weight = weight - rate * (first_hat / (jnp.sqrt(second_hat) + EPSILON) + DECAY * weight)
    return (weight, first, second)


def adam_in_kernels(weight, gradient, first, second, rate):
    first = BETA_FIRST * first + (1.0 - BETA_FIRST) * gradient
    second = BETA_SECOND * second + (1.0 - BETA_SECOND) * gradient * gradient
    second_hat = second * (1.0 / (1.0 - BETA_SECOND**STEP))
    bottom = second_hat * lax.rsqrt(second_hat) + EPSILON
    guess = pl.reciprocal(bottom, approx=True)
    guess = guess * (2.0 - bottom * guess)
    scale = rate / (1.0 - BETA_FIRST**STEP)
    weight = weight * (1.0 - rate * DECAY) - (scale * first) * guess
    return (weight, first, second)


def adam_into(refs, weight, gradient, first, second, rate):
    for ref, value in zip(refs, adam_in_kernels(weight, gradient, first, second, rate)):
        ref[...] = value


def rounded_in_kernel(values):
    return values.astype(bf16).astype(f32)


def adam_most_kernel(grads_ref, gain_ref, *refs, rates):
    (w_in, m_in, v_in), attn, out = refs[:3], refs[3:6], refs[6:9]
    new_in, new_attn, new_out = refs[9:12], refs[12:15], refs[15:18]
    gain_grad, turned = refs[18:]
    here = pl.program_id(0)
    chips = grads_ref.shape[0] // 2
    width = w_in.shape[1] // 2
    main = width // 256 * 128
    few = width // 2 - main

    @pl.when(here == 0)
    def _():
        for core in range(2):
            columns = jnp.concatenate(
                [grads_ref[2 * chip + core, :, 2 * main : 3 * main] for chip in range(chips)],
                axis=0,
            )
            turned[core * main : (core + 1) * main] = columns.astype(f32).T
            rest = jnp.concatenate(
                [
                    grads_ref[2 * chip + core, :, 3 * main : 3 * main + 128]
                    for chip in range(chips)
                ],
                axis=0,
            )
            start = 2 * main + core * few
            turned[start : start + few] = rest.astype(f32).T[2 * few : 3 * few]

    each = grads_ref.shape[1]
    some = w_in.shape[0] // each
    for at_chip in range(some):
        source = 2 * (here * some + at_chip)
        columns = []
        for at in range(2):
            for core in range(2):
                place = at * main
                columns.append(grads_ref[source + core, :, place : place + main].astype(f32))
            for core in range(2):
                rest = grads_ref[source + core, :, 3 * main : 3 * main + 128].astype(f32)
                columns.append(rest[:, at * few : (at + 1) * few])
        grads = jnp.concatenate(columns, axis=1)
        rows = slice(at_chip * each, (at_chip + 1) * each)
        weight = w_in[rows]
        gain_grad[rows] = jnp.sum(grads * rounded_in_kernel(weight), axis=1, keepdims=True)
        values = adam_in_kernels(
            weight, grads * gain_ref[rows], m_in[rows], v_in[rows], rates[0]
        )
        for ref, value in zip(new_in, values):
            ref[rows] = value
        rows = slice(at_chip * each // 2, (at_chip + 1) * each // 2)
        for core in range(2):
            piece = grads_ref[source + core, :, 3 * main + 128 :].astype(f32)
            grads = jnp.concatenate([piece[: each // 2], piece[each // 2 :]], axis=1)
            values = adam_in_kernels(
                attn[0][core, rows], grads, attn[1][core, rows], attn[2][core, rows], rates[1]
            )
            for ref, value in zip(new_attn, values):
                ref[core, rows] = value

    size = out[0].shape[0]
    grads = turned[pl.ds(pl.multiple_of(here * size, 8), size)]
    adam_into(new_out, out[0][...], grads, out[1][...], out[2][...], rates[2])


def adam_most(grads, gain, weights_in, weights_attn, weights_out, rates, steps=2):
    rows, columns = weights_in[0].shape
    width = weights_attn[0].shape[1]
    hidden = weights_out[0].shape[0]
    weights_attn = [array.reshape(2, rows // 2, width) for array in weights_attn]
    block_in = pl.BlockSpec((rows // steps, columns), lambda i: (i, 0))
    block_attn = pl.BlockSpec((2, rows // 2 // steps, width), lambda i: (0, i, 0))
    block_out = pl.BlockSpec((hidden // steps, rows), lambda i: (i, 0))
    column = pl.BlockSpec((rows // steps, 1), lambda i: (i, 0))
    blocks = [block_in] * 3 + [block_attn] * 3 + [block_out] * 3
    arrays = (*weights_in, *weights_attn, *weights_out)
    *results, gain_grad = pl.pallas_call(
        functools.partial(adam_most_kernel, rates=rates),
        name="adam_most",
        grid=(steps,),
        in_specs=[pl.BlockSpec(grads.shape, lambda i: (0, 0, 0)), column] + blocks,
        out_specs=blocks + [column],
        out_shape=[jax.ShapeDtypeStruct(array.shape, f32) for array in arrays]
        + [jax.ShapeDtypeStruct((rows, 1), f32)],
        scratch_shapes=[pltpu.VMEM((hidden, rows), f32)],
        compiler_params=pltpu.CompilerParams(vmem_limit_bytes=VMEM),
        cost_estimate=cost(rows * columns * 20, rows * columns * 26),
    )(grads, gain, *arrays)
    new_attn = [array.reshape(rows, width) for array in results[3:6]]
    return results[:3], new_attn, results[6:], gain_grad


def adam_qkv_kernel(order_ref, *refs, rate):
    grads_refs, (gain_ref, w_ref, m_ref, v_ref, new_w, new_m, new_v, gain_grad, joined) = (
        refs[:-9], refs[-9:]
    )
    here = pl.program_id(0)
    heads = sum(grads_ref.shape[0] for grads_ref in grads_refs)

    @pl.when(here == 0)
    def _():
        at = 0
        for grads_ref in grads_refs:
            for place in range(grads_ref.shape[0]):
                for part in range(3):
                    row = (part * heads + order_ref[at]) * HDIM
                    joined[pl.ds(pl.multiple_of(row, HDIM), HDIM)] = grads_ref[
                        place, part * HDIM : (part + 1) * HDIM
                    ].astype(f32)
                at += 1

    size = w_ref.shape[1]
    grads = joined[pl.ds(pl.multiple_of(here * size, size), size)].T
    weight = w_ref[...]
    added = jnp.sum(grads * rounded_in_kernel(weight), axis=1, keepdims=True)
    gain_grad[...] = added + jnp.where(here == 0, 0.0, gain_grad[...])
    adam_into(
        (new_w, new_m, new_v), weight, grads * gain_ref[...], m_ref[...], v_ref[...], rate
    )


def adam_qkv(order, grads, gain, weight, first, second, rate, step=1536):
    rows, columns = weight.shape
    block = pl.BlockSpec((rows, step), lambda i, order: (0, i))
    column = pl.BlockSpec((rows, 1), lambda i, order: (0, 0))
    same = jax.ShapeDtypeStruct((rows, columns), f32)
    return pl.pallas_call(
        functools.partial(adam_qkv_kernel, rate=rate),
        name="adam_qkv",
        grid_spec=pltpu.PrefetchScalarGridSpec(
            num_scalar_prefetch=1,
            grid=(columns // step,),
            in_specs=[pl.BlockSpec(piece.shape, lambda i, order: (0, 0, 0)) for piece in grads]
            + [column]
            + [block] * 3,
            out_specs=[block] * 3 + [column],
            scratch_shapes=[pltpu.VMEM((columns, rows), f32)],
        ),
        out_shape=[same] * 3 + [jax.ShapeDtypeStruct((rows, 1), f32)],
        compiler_params=pltpu.CompilerParams(vmem_limit_bytes=VMEM),
        cost_estimate=cost(rows * columns * 20, rows * columns * 26),
    )(order, *grads, gain, weight, first, second)


def ring(axis, shift):
    size = lax.axis_size(axis)
    return [(at, (at + shift) % size) for at in range(size)]


def gather_first_step(planes_first, lines_first):
    swapped = lax.ppermute(planes_first, "zh", SWAP)
    others = [
        lax.ppermute(lines_first, "y", ring("y", shift)) for shift in range(1, lax.axis_size("y"))
    ]
    return jnp.stack([planes_first, swapped]), jnp.stack([lines_first, *others])


def shards(
    tokens,
    positions,
    cotangent,
    weight_qkv,
    weight_attn,
    weight_in,
    weight_out,
    norm_gains,
    first_qkv,
    first_attn,
    first_in,
    first_out,
    first_gains,
    second_qkv,
    second_attn,
    second_in,
    second_out,
    second_gains,
):
    rows, width = tokens.shape[1:]
    shard_rows = weight_qkv.shape[1]
    heads = width // HDIM
    hidden = weight_out.shape[1]
    core = lax.axis_index("c")
    mine = lax.axis_index(CTX)
    chip = lax.axis_index(CHIPS)
    chips = lax.axis_size(CHIPS)
    owners = lax.axis_size(FSDP)
    length = rows * chips * 2
    main = hidden // 256 * 128
    few = hidden // 2 - main
    core_at = core.reshape(1).astype(jnp.int32)
    axes = (lax.axis_size("zh"), lax.axis_size("y"), lax.axis_size("x"), lax.axis_size("zl"))
    offsets = [(far, near) for far in range(lax.axis_size("x")) for near in range(2)]
    across, beside = lax.axis_index("x"), lax.axis_index("zl")
    wide = lax.axis_size("x")

    def chips_at(sign):
        places = [(across + sign * far) % wide * 2 + (beside ^ near) for far, near in offsets]
        return jnp.stack(places).astype(jnp.int32)

    local = tokens[0]
    extra = 16
    high, low = positions[0] // 128, positions[0] % 128
    places_row = jnp.concatenate([high, low, jnp.zeros((width - 2 * rows,), jnp.int32)])
    places_rows = jnp.concatenate(
        [places_row[None], jnp.zeros((extra - 1, width), jnp.int32)], axis=0
    ).astype(bf16)
    sequence = lax.all_gather(
        jnp.concatenate([local, places_rows], axis=0), CTX, axis=0, tiled=True
    )
    first_part, second_part, head_part, half_heads = prepare(
        jnp.stack([core, chip]).astype(jnp.int32),
        norm_gains[0],
        weight_qkv[0],
        weight_attn[0],
        weight_in[0],
        weight_out[0],
    )
    first_joined, second_joined = gather_first_step(first_part, second_part)
    head_weights = lax.all_to_all(
        jnp.broadcast_to(head_part, (owners, *head_part.shape)), FSDP, 0, 0, tiled=True
    )
    first_pieces = [first_joined] + [
        lax.ppermute(first_joined, "y", ring("y", shift))
        for shift in range(1, lax.axis_size("y"))
    ]
    sequence, _, second_joined, _ = lax.optimization_barrier(
        (sequence, first_joined, second_joined, head_weights)
    )
    second_pieces = [second_joined, lax.ppermute(second_joined, "zh", SWAP)]
    lines = lax.axis_size("y")
    plane, line = lax.axis_index("zh"), lax.axis_index("y")
    first_order = jnp.stack(
        [(plane ^ far) * lines + (line - shift) % lines for shift in range(lines) for far in range(2)]
    ).astype(jnp.int32)
    second_order = jnp.stack(
        [(plane ^ far) * lines + (line - shift) % lines for far in range(2) for shift in range(lines)]
    ).astype(jnp.int32)

    def in_order(ours, theirs):
        first = jnp.where(core == 0, ours, theirs)
        second = jnp.where(core == 0, theirs, ours)
        return jnp.concatenate([first, second], axis=0)

    def swap(array):
        return lax.ppermute(array, "c", SWAP)

    gradient = in_order(cotangent[0], swap(cotangent[0]))

    freqs = jnp.exp(jnp.arange(HDIM // 2, dtype=f32) * (-2.0 * math.log(ROPE_BASE) / HDIM))
    by_device = sequence.reshape(2 * chips, rows + extra, width)[:, rows]
    by_device = by_device.astype(f32)
    places = by_device[:, :rows] * 128.0 + by_device[:, rows : 2 * rows]
    angles = freqs[:, None] * places.reshape(1, length)
    cosine = jnp.cos(angles)
    sine = jnp.sin(angles)
    unit_all, qkv, keys, values = project(sequence, head_weights, cosine, sine, extra)
    low_out, out, lse = attend(keys, qkv, chips)
    firsts = len(first_pieces)
    low_out, *arrived = lax.optimization_barrier((low_out, *first_pieces, *second_pieces))
    first_pieces, second_pieces = arrived[:firsts], arrived[firsts:]
    attended = lax.all_to_all(low_out, CHIPS, 0, 0, tiled=True)
    half_heads, attended = lax.optimization_barrier((half_heads, attended))
    mat_qkv = lax.all_gather(half_heads, FSDP, axis=0, tiled=True)
    attended = attended.reshape(heads // 2 * HDIM, 2 * rows)
    mixed, mat_attn = attend_out(first_order, attended, first_pieces)
    current = lax.dynamic_slice_in_dim(
        sequence, chip * 2 * (rows + extra), 2 * (rows + extra), 0
    ).reshape(2, rows + extra, width)[:, :rows].reshape(2 * rows, width)
    residual, partial, back, grads = feed(
        first_order, second_order, current, mixed, swap(mixed), gradient, first_pieces,
        second_pieces, axes,
    )
    grads, mat_qkv = lax.optimization_barrier((grads, mat_qkv))
    first_sum = lax.psum_scatter(grads, "y", scatter_dimension=0, tiled=True)

    def move(pieces, sign):
        moved = [pieces[0]]
        for (far, near), piece in list(zip(offsets, pieces))[1:]:
            pairs = [
                (at, (at // 2 + sign * far) % wide * 2 + (at % 2 ^ near)) for at in range(chips)
            ]
            moved.append(lax.ppermute(piece, CHIPS, pairs))
        return moved

    ahead, behind = chips_at(1), chips_at(-1)
    theirs = swap(lax.dynamic_slice_in_dim(partial, (1 - core) * rows, rows, 0))
    layer_out, residual_grad, *pieces = middle_back(
        core_at, ahead, line.reshape(1).astype(jnp.int32), residual, gradient, back, swap(back),
        mat_attn, attended, partial, theirs, axes,
    )
    dout_pieces, attn_pieces = pieces[:chips], pieces[chips:]

    douts = move(dout_pieces, 1)
    attn_arrived = attn_pieces[:1] + [
        lax.ppermute(piece, "y", ring("y", shift))
        for shift, piece in list(enumerate(attn_pieces))[1:]
    ]
    pieces = attend_back(behind, keys, values, qkv, douts, out, lse, cosine, sine)
    rest = lax.optimization_barrier((*pieces, *attn_arrived))
    pieces, attn_arrived = rest[:chips], rest[chips:]
    owner_places = [(far, shift) for far in range(2) for shift in range(lines)]
    owner_order = jnp.stack(
        [(plane ^ far) * lines + (line + shift) % lines for far, shift in owner_places]
    ).astype(jnp.int32)
    head_parts = head_grad(behind, owner_order, unit_all, pieces)

    def total(arrays):
        return sum(array.astype(f32) for array in arrays).astype(bf16)

    moved = move(pieces, -1)
    first_sum, *rest = lax.optimization_barrier((first_sum, *moved, *head_parts))
    moved, head_parts = rest[:chips], rest[chips:]
    first_sum = jnp.concatenate([first_sum, total(attn_arrived)], axis=1)
    arrived = lax.all_to_all(first_sum, ("x", "zh", "zl"), 0, 0, tiled=True)
    own_hidden, other_hidden = hidden_back(ahead, core_at, mat_qkv, moved)
    arrived, own_hidden, *head_parts = lax.optimization_barrier(
        (arrived, own_hidden, *head_parts)
    )
    grad_hidden = own_hidden + swap(other_hidden).astype(f32)
    unit_in, scale_in = unit_rows(local.astype(f32))
    own_residual = lax.dynamic_slice_in_dim(residual_grad, core * rows, rows, 0)
    tokens_grad = (own_residual + unit_back(grad_hidden, unit_in, scale_in))[None]

    head_arrived = [head_parts[0]]
    for (far, shift), piece in list(zip(owner_places, head_parts))[1:]:
        pairs = [
            (at, (at // lines ^ far) * lines + (at % lines + shift) % lines) for at in range(owners)
        ]
        head_arrived.append(lax.ppermute(piece, FSDP, pairs))
    head_own = total(head_arrived)[None]
    arrived = arrived.reshape(2 * chips, shard_rows // chips, -1)
    second_sum = jnp.sum(arrived.astype(f32), axis=0).astype(bf16)
    all_grads = lax.all_gather(second_sum, CTX, axis=0, tiled=False)

    head_pair = jnp.concatenate([head_own, swap(head_own)], axis=0)
    head_four = jnp.concatenate([head_pair, lax.ppermute(head_pair, "zl", SWAP)], axis=0)
    head_grads = [head_four] + [
        lax.ppermute(head_four, "x", ring("x", shift)) for shift in range(1, wide)
    ]
    head_order = jnp.stack(
        [
            (across - shift) % wide * 4 + (beside ^ near) * 2 + (core ^ other)
            for shift in range(wide)
            for near in range(2)
            for other in range(2)
        ]
    ).astype(jnp.int32)

    rates = (
        width ** (-0.5),
        max(1, 3 * width // length) ** (-0.5),
        width ** (-0.5),
        hidden ** (-0.5),
    )
    columns_of_gains = norm_gains[0].astype(bf16).astype(f32).T
    new_in, new_attn, new_out, gain_second = adam_most(
        all_grads,
        columns_of_gains[:, 1:],
        (weight_in[0], first_in[0], second_in[0]),
        (weight_attn[0], first_attn[0], second_attn[0]),
        (weight_out[0], first_out[0], second_out[0]),
        (rates[2], rates[1], rates[3]),
    )
    *new_qkv, gain_first = adam_qkv(
        head_order, head_grads, columns_of_gains[:, :1], weight_qkv[0], first_qkv[0], second_qkv[0], rates[0]
    )
    gain_grads = jnp.concatenate([gain_first, gain_second], axis=1).T
    new_gains = adam(norm_gains[0], gain_grads, first_gains[0], second_gains[0], GAIN_RATE)
    updated = (new_qkv, new_attn, new_in, new_out, new_gains)
    return (
        layer_out[None],
        tokens_grad,
        *[updated[member][0][None] for member in range(5)],
        *[updated[member][1][None] for member in range(5)],
        *[updated[member][2][None] for member in range(5)],
    )


def solution(mesh):
    split = Mesh(mesh.devices.reshape(4, 2, 2, 2, 4), ("x", "zl", "c", "zh", "y"))
    by_row = P(None, FSDP, None)
    by_column = P(None, None, FSDP)
    weights = (by_row, by_row, by_row, by_column, by_column)
    by_token = P(FSDP, CTX, None)
    return jax.shard_map(
        shards,
        mesh=split,
        in_specs=(by_token, P(FSDP, CTX), by_token) + weights * 3,
        out_specs=(by_token, by_token) + weights * 3,
        check_vma=False,
    )
```

```python
import functools
import math

import jax
import jax.numpy as jnp
from jax import lax
from jax.experimental import pallas as pl
from jax.experimental.pallas import tpu as pltpu
from jax.sharding import Mesh, PartitionSpec as P

HDIM = 64
STEP = 10
BETA_FIRST = 0.5
BETA_SECOND = 0.5
EPSILON = 1e-08
DECAY = 0.01
NORM_EPS = 1e-05
ROPE_BASE = 160000.0
GAIN_RATE = 0.6
LOG2E = math.log2(math.e)
f32 = jnp.float32
bf16 = jnp.bfloat16

CHIPS = ("x", "zl")
CTX = ("x", "zl", "c")
FSDP = ("zh", "y")
SWAP = [(0, 1), (1, 0)]
VMEM = 60 << 20


def dot(left, right, left_dim=1, right_dim=0):
    return lax.dot_general(
        left, right, (((left_dim,), (right_dim,)), ((), ())), preferred_element_type=f32
    )


def cost(flops, moved):
    return pl.CostEstimate(flops=flops, bytes_accessed=moved, transcendentals=0)


def unit_rows(values):
    average = jnp.mean(values, axis=-1, keepdims=True)
    centered = values - average
    spread = jnp.mean(centered * centered, axis=-1, keepdims=True)
    inverse = lax.rsqrt(spread + NORM_EPS)
    return centered * inverse, inverse


def unit_back(scaled, unit, inverse):
    first_mean = jnp.mean(scaled, axis=-1, keepdims=True)
    second_mean = jnp.mean(scaled * unit, axis=-1, keepdims=True)
    return inverse * (scaled - first_mean - unit * second_mean)


def prepare_kernel(
    place_ref, gains_ref, qkv_ref, attn_ref, in_ref, out_ref,
    first_ref, second_ref, head_ref, heads_ref,
):
    core, chip = place_ref[0], place_ref[1]
    rows = qkv_ref.shape[0]
    width = attn_ref.shape[1]
    hidden = out_ref.shape[0]
    main = hidden // 256 * 128
    few = hidden // 2 - main
    half = width // 2
    low_gains = gains_ref[...].astype(bf16).astype(f32)
    columns = jnp.concatenate([low_gains, jnp.zeros((6, rows), f32)], axis=0).T
    gain_first, gain_second = columns[:, 0:1], columns[:, 1:2]

    def pick(array):
        size = array.shape[1] // 2
        return jnp.where(core == 0, array[:, :size], array[:, size:])

    def scaled(values, gain):
        return (values.astype(bf16).astype(f32) * gain).astype(bf16)

    attn_rows = attn_ref[pl.ds(pl.multiple_of(core * HDIM, HDIM), HDIM)].astype(bf16)
    first_ref[:HDIM, :half] = attn_rows[:, :half]
    first_ref[HDIM:, :half] = attn_rows[:, half:]
    out_rows = out_ref[pl.ds(pl.multiple_of(core * main, 128), main)]
    first_ref[:, half:] = out_rows.T.astype(bf16)
    second_ref[:, :main] = scaled(pick(in_ref[:, : 2 * main]), gain_second)
    second_ref[:, main : 2 * main] = scaled(
        pick(in_ref[:, hidden : hidden + 2 * main]), gain_second
    )
    odd_out = out_ref[2 * main :].T
    odd = [
        scaled(pick(in_ref[:, 2 * main : hidden]), gain_second),
        scaled(pick(in_ref[:, hidden + 2 * main :]), gain_second),
        pick(odd_out).astype(bf16),
        jnp.zeros((rows, few), bf16),
    ]
    second_ref[:, 2 * main :] = jnp.concatenate(odd, axis=1)
    pieces = []
    for at in range(width // 128):
        for part in range(3):
            start = part * width + at * 128
            pieces.append(scaled(pick(qkv_ref[:, start : start + 128]), gain_first))
    heads_ref[...] = jnp.concatenate(pieces, axis=1)
    own = []
    for part in range(3):
        start = pl.multiple_of(part * width + chip * 128, 128)
        own.append(scaled(pick(qkv_ref[:, pl.ds(start, 128)]), gain_first).astype(f32))
    own.append(jnp.zeros((rows, HDIM), f32))
    head_ref[...] = jnp.concatenate(own, axis=1).T[: 3 * HDIM].astype(bf16)


def prepare(place, gains, qkv, attn, weight_in, weight_out):
    rows, width = attn.shape
    hidden = weight_out.shape[0]
    main = hidden // 256 * 128
    arrays = (gains, qkv, attn, weight_in, weight_out)
    shapes = [
        (rows, width // 2 + main),
        (rows, 2 * main + 4 * (hidden // 2 - main)),
        (3 * HDIM, rows),
        (rows, 3 * width // 2),
    ]

    def whole(shape):
        return pl.BlockSpec(shape, lambda i, place: (0, 0))

    return pl.pallas_call(
        prepare_kernel,
        name="prepare",
        grid_spec=pltpu.PrefetchScalarGridSpec(
            num_scalar_prefetch=1,
            grid=(1,),
            in_specs=[whole(array.shape) for array in arrays],
            out_specs=[whole(shape) for shape in shapes],
        ),
        out_shape=[jax.ShapeDtypeStruct(shape, bf16) for shape in shapes],
        compiler_params=pltpu.CompilerParams(vmem_limit_bytes=VMEM),
        cost_estimate=cost(rows * width * 60, 10 << 20),
    )(place, *arrays)


def project_kernel(
    x_ref, w_ref, cos_ref, sin_ref, unit_ref, qkv_ref, keys_ref, values_ref, w_all, *, extra
):
    half = HDIM // 2
    rows = cos_ref.shape[1]

    @pl.when(pl.program_id(0) == 0)
    def _():
        for part in range(w_ref.shape[0]):
            w_all[part * 128 : (part + 1) * 128] = w_ref[part].astype(f32).T.astype(bf16)

    count = (x_ref.shape[0] - rows) // extra
    each = rows // count
    for at in range(count):
        tokens = x_ref[at * (each + extra) : at * (each + extra) + each].astype(f32)
        unit_ref[at * each : (at + 1) * each] = unit_rows(tokens)[0].astype(bf16)
    unit = unit_ref[...]
    mixed = dot(unit, w_all[...]).T
    cosine = cos_ref[...]
    sine = sin_ref[...]

    def turn(one, two):
        return jnp.concatenate([one * cosine - two * sine, two * cosine + one * sine], axis=0)

    queries = turn(mixed[:half], mixed[half:HDIM])
    keys = turn(mixed[HDIM : HDIM + half], mixed[HDIM + half : 2 * HDIM])
    values = mixed[2 * HDIM :]
    qkv_ref[...] = jnp.concatenate([queries, keys, values], axis=0).astype(bf16)
    key_rows = keys.T.astype(bf16)
    value_rows = values.T.astype(bf16)
    ones = jnp.where(lax.broadcasted_iota(jnp.int32, (rows, 128), 1) < 3, 1.0, 0.0).astype(bf16)
    keys_ref[...] = jnp.concatenate([key_rows, key_rows, ones], axis=1)
    values_ref[...] = jnp.concatenate([value_rows, ones[:, :HDIM]], axis=1)


def project(tokens, weights, cosine, sine, extra, block=1024):
    width = tokens.shape[1]
    length = cosine.shape[1]
    steps = length // block
    return pl.pallas_call(
        functools.partial(project_kernel, extra=extra),
        name="project",
        grid=(steps,),
        in_specs=[
            pl.BlockSpec((tokens.shape[0] // steps, width), lambda i: (i, 0)),
            pl.BlockSpec(weights.shape, lambda i: (0, 0, 0)),
            pl.BlockSpec((HDIM // 2, block), lambda i: (0, i)),
            pl.BlockSpec((HDIM // 2, block), lambda i: (0, i)),
        ],
        out_specs=[
            pl.BlockSpec((block, width), lambda i: (i, 0)),
            pl.BlockSpec((3 * HDIM, block), lambda i: (0, i)),
            pl.BlockSpec((block, 256), lambda i: (i, 0)),
            pl.BlockSpec((block, 128), lambda i: (i, 0)),
        ],
        out_shape=[
            jax.ShapeDtypeStruct((length, width), bf16),
            jax.ShapeDtypeStruct((3 * HDIM, length), bf16),
            jax.ShapeDtypeStruct((length, 256), bf16),
            jax.ShapeDtypeStruct((length, 128), bf16),
        ],
        scratch_shapes=[pltpu.VMEM((width, 3 * HDIM), bf16)],
        compiler_params=pltpu.CompilerParams(vmem_limit_bytes=VMEM),
        cost_estimate=cost(length * width, 1 << 20),
    )(tokens, weights, cosine, sine)


def scaled_queries(queries):
    scaled = queries.astype(f32) * (LOG2E / math.sqrt(HDIM))
    high = scaled.astype(bf16)
    low = (scaled - high.astype(f32)).astype(bf16)
    return high, low


def attend_kernel(keys_ref, q_ref, v_ref, low_ref, out_ref, lse_ref, v_ones, *, part):
    length = keys_ref.shape[0]
    count = length // part

    @pl.when(pl.program_id(0) == 0)
    def _():
        v_ones[:HDIM] = v_ref[...]
        v_ones[HDIM:] = jnp.where(
            lax.broadcasted_iota(jnp.int32, (16, length), 0) < 1, 1.0, 0.0
        ).astype(bf16)

    queries = jnp.concatenate(scaled_queries(q_ref[...]), axis=0)

    def score(at):
        return dot(keys_ref[at * part : (at + 1) * part, : 2 * HDIM], queries)

    scores = score(0)
    highest = total = None
    for at in range(count):
        following = score(at + 1) if at + 1 < count else None
        peak = jnp.max(scores, axis=0, keepdims=True)
        raised = peak if highest is None else jnp.maximum(highest, peak)
        soft = jnp.exp2(scores - raised).astype(bf16)
        added = dot(v_ones[:, at * part : (at + 1) * part], soft)
        total = added if total is None else total * jnp.exp2(highest - raised) + added
        highest = raised
        scores = following
    summed = total[HDIM : HDIM + 1]
    result = total[:HDIM] / summed
    out_ref[...] = result
    lse_ref[...] = highest + jnp.log2(summed)
    step = low_ref.shape[2]
    for at in range(low_ref.shape[0]):
        low_ref[at] = result[:, at * step : (at + 1) * step].astype(bf16)


def attend(keys, qkv, chips, block=1024, part=512):
    length = keys.shape[0]
    return pl.pallas_call(
        functools.partial(attend_kernel, part=part),
        name="attend",
        grid=(length // block,),
        in_specs=[
            pl.BlockSpec(keys.shape, lambda i: (0, 0)),
            pl.BlockSpec((HDIM, block), lambda i: (0, i)),
            pl.BlockSpec((HDIM, length), lambda i: (2, 0)),
        ],
        out_specs=[
            pl.BlockSpec((block * chips // length, HDIM, length // chips), lambda i: (i, 0, 0)),
            pl.BlockSpec((HDIM, block), lambda i: (0, i)),
            pl.BlockSpec((1, block), lambda i: (0, i)),
        ],
        out_shape=[
            jax.ShapeDtypeStruct((chips, HDIM, length // chips), bf16),
            jax.ShapeDtypeStruct((HDIM, length), f32),
            jax.ShapeDtypeStruct((1, length), f32),
        ],
        scratch_shapes=[pltpu.VMEM((HDIM + 16, length), bf16)],
        compiler_params=pltpu.CompilerParams(vmem_limit_bytes=VMEM),
        cost_estimate=cost(length * HDIM, 1 << 20),
    )(keys, qkv, qkv)


def minus_in_three(values):
    rows = values.shape[1]
    at = lax.broadcasted_iota(jnp.int32, (16, rows), 0)
    high = (-values).astype(bf16).astype(f32)
    rest = -values - high
    middle = rest.astype(bf16).astype(f32)
    low = rest - middle
    stacked = jnp.where(at == 0, high, jnp.where(at == 1, middle, jnp.where(at == 2, low, 0.0)))
    return stacked.astype(bf16)


def attend_back_kernel(
    order_ref,
    keys_ref,
    values_ref,
    q_ref,
    k_ref,
    out_ref,
    lse_ref,
    cos_ref,
    sin_ref,
    *rest,
    part,
):
    count = (len(rest) - 3) // 2
    dout_refs, dp_refs, (sums, dq_all, dout_all) = rest[:count], rest[count:-3], rest[-3:]
    half = HDIM // 2
    here = pl.program_id(0)
    length = keys_ref.shape[0]
    block = q_ref.shape[1]
    count = length // part
    factor = HDIM ** (-0.5)

    def turn_back(grads, cosine, sine):
        low = grads.astype(bf16).astype(f32)
        one, two = low[:half], low[half:]
        return jnp.concatenate([one * cosine + two * sine, two * cosine - one * sine], axis=0)

    @pl.when(here == 0)
    def _():
        sums[...] = jnp.zeros_like(sums)
        for place, dout_ref in enumerate(dout_refs):
            dout_all[place] = dout_ref[...]

    low_queries = q_ref[...]
    high, low = scaled_queries(low_queries)
    queries = jnp.concatenate([high, low, minus_in_three(lse_ref[...])], axis=0)
    low_dout = dout_all[here]
    dout = low_dout.astype(f32)
    centre = jnp.sum(dout * out_ref[...], axis=0, keepdims=True)
    douts = jnp.concatenate([low_dout, minus_in_three(centre)], axis=0)
    blank = jnp.zeros((block, HDIM), bf16)
    right = jnp.concatenate(
        [
            jnp.concatenate([low_queries.astype(f32).T.astype(bf16), blank], axis=1),
            jnp.concatenate([blank, dout.T.astype(bf16)], axis=1),
        ],
        axis=0,
    )

    def score(at):
        rows = slice(at * part, (at + 1) * part)
        return (
            dot(keys_ref[rows, : 2 * HDIM + 16], queries),
            dot(values_ref[rows, : HDIM + 16], douts),
        )

    now = score(0)
    grad_queries = None
    for at in range(count):
        following = score(at + 1) if at + 1 < count else None
        rows = slice(at * part, (at + 1) * part)
        soft = jnp.exp2(now[0])
        grads = (soft * now[1]).astype(bf16)
        added = dot(k_ref[:, rows], grads)
        grad_queries = added if grad_queries is None else grad_queries + added
        sums[rows] += dot(jnp.concatenate([grads, soft.astype(bf16)], axis=1), right)
        now = following

    def columns_of(place):
        return pl.ds(pl.multiple_of(order_ref[place] * block, block), block)

    columns = columns_of(here)
    dq_all[here] = turn_back(
        grad_queries * factor, cos_ref[:, columns], sin_ref[:, columns]
    ).astype(bf16)

    @pl.when(here == length // block - 1)
    def _():
        for place, dp_ref in enumerate(dp_refs):
            columns = columns_of(place)
            both = sums[columns].T
            dp_ref[:HDIM] = dq_all[place]
            dp_ref[HDIM : 2 * HDIM] = turn_back(
                both[:HDIM] * factor, cos_ref[:, columns], sin_ref[:, columns]
            ).astype(bf16)
            dp_ref[2 * HDIM :] = both[HDIM:].astype(bf16)


def attend_back(order, keys, values, qkv, douts, out, lse, cosine, sine, part=256):
    length = keys.shape[0]
    chips = len(douts)
    block = douts[0].shape[1]
    scores = length * length

    def whole(array):
        return pl.BlockSpec(array.shape, lambda i, order: (0, 0))

    return pl.pallas_call(
        functools.partial(attend_back_kernel, part=part),
        name="attend_back",
        grid_spec=pltpu.PrefetchScalarGridSpec(
            num_scalar_prefetch=1,
            grid=(chips,),
            in_specs=[
                whole(keys),
                whole(values),
                pl.BlockSpec((HDIM, block), lambda i, order: (0, order[i])),
                pl.BlockSpec((HDIM, length), lambda i, order: (1, 0)),
                pl.BlockSpec((HDIM, block), lambda i, order: (0, order[i])),
                pl.BlockSpec((1, block), lambda i, order: (0, order[i])),
                whole(cosine),
                whole(sine),
                *[whole(piece) for piece in douts],
            ],
            out_specs=[pl.BlockSpec((3 * HDIM, block), lambda i, order: (0, 0))] * chips,
            scratch_shapes=[
                pltpu.VMEM((length, 2 * HDIM), f32),
                pltpu.VMEM((chips, HDIM, block), bf16),
                pltpu.VMEM((chips, HDIM, block), bf16),
            ],
        ),
        out_shape=[jax.ShapeDtypeStruct((3 * HDIM, block), bf16)] * chips,
        compiler_params=pltpu.CompilerParams(vmem_limit_bytes=VMEM),
        cost_estimate=cost(5 * 4 * 2 * scores * HDIM, 8 << 20),
    )(order, keys, values, qkv, qkv, out, lse, cosine, sine, *douts)


def attend_out_kernel(order_ref, attended_ref, *rest):
    piece_refs, (mixed_ref, attn_ref) = rest[:-2], rest[-2:]
    half = attn_ref.shape[1] // 2
    at = 0
    for piece_ref in piece_refs:
        for place in range(piece_ref.shape[0]):
            rows = pl.ds(pl.multiple_of(order_ref[at] * HDIM, HDIM), HDIM)
            attn_ref[rows, :half] = piece_ref[place, :HDIM]
            attn_ref[rows, half:] = piece_ref[place, HDIM:]
            at += 1
    turned = attended_ref[...].astype(f32).T.astype(bf16)
    mixed_ref[...] = dot(turned, attn_ref[...]).astype(bf16)


def attend_out(order, attended, pieces):
    size, tokens = attended.shape
    width = 2 * size

    def whole(*shape):
        return pl.BlockSpec(shape, lambda i, order: (0,) * len(shape))

    return pl.pallas_call(
        attend_out_kernel,
        name="attend_out",
        grid_spec=pltpu.PrefetchScalarGridSpec(
            num_scalar_prefetch=1,
            grid=(1,),
            in_specs=[whole(size, tokens)]
            + [whole(*piece.shape[:2], width // 2) for piece in pieces],
            out_specs=[whole(tokens, width), whole(size, width)],
        ),
        out_shape=[
            jax.ShapeDtypeStruct((tokens, width), bf16),
            jax.ShapeDtypeStruct((size, width), bf16),
        ],
        compiler_params=pltpu.CompilerParams(vmem_limit_bytes=VMEM),
        cost_estimate=cost(2 * 2 * tokens * width * size, 4 << 20),
    )(order, attended, *pieces)


def feed_kernel(
    first_order, second_order, x_ref, ours_ref, theirs_ref, g_ref, *rest, firsts, seconds, axes
):
    weight_refs = []
    start = 0
    for size in (seconds, seconds, firsts, seconds):
        weight_refs.append(rest[start : start + size])
        start += size
    planes, lines, wide, beside = axes

    def put(grads, columns):
        size = grads.shape[0] // (planes * lines * wide)
        low = grads.astype(bf16)
        for plane in range(planes):
            for line in range(lines):
                for far in range(wide):
                    source = ((plane * lines + line) * wide + far) * size
                    target = ((line * wide + far) * planes + plane) * size
                    grads_ref[target : target + size, columns] = low[source : source + size]
    residual_ref, partial_ref, back_ref, grads_ref = rest[-13:-9]
    unit, unit_t, g_t, sum_out, sum_back = rest[-9:-4]
    gate_ref, up_ref, out_ref, rest_ref = rest[-4:]
    here = pl.program_id(0)
    last = pl.num_programs(0) - 1
    width = x_ref.shape[1]
    step = gate_ref.shape[1]

    def join(total, parts, order):
        at = 0
        for part in parts:
            size = part.shape[1]
            for place in range(part.shape[0]):
                total[pl.ds(pl.multiple_of(order[at] * size, size), size)] = part[place]
                at += 1

    def bend(gate, upward):
        cdf = 0.5 + 0.5 * lax.erf(gate * math.sqrt(0.5))
        slope = cdf + gate * jnp.exp(gate * gate * -0.5) * (1.0 / math.sqrt(2.0 * math.pi))
        bent = gate * cdf
        return bent, slope, (bent * upward).astype(bf16)

    @pl.when(here == 0)
    def _():
        residual = (
            x_ref[...].astype(f32) + ours_ref[...].astype(f32) + theirs_ref[...].astype(f32)
        )
        residual_ref[...] = residual
        normed = unit_rows(residual)[0]
        unit[...] = normed.astype(bf16)
        unit_t[...] = normed.T.astype(bf16)
        g_t[...] = g_ref[...].astype(f32).T.astype(bf16)
        join(rest_ref, weight_refs[3], second_order)
        few = rest_ref.shape[1] // 4
        both = dot(unit[...], rest_ref[...])
        grad = dot(g_ref[...], rest_ref[...])[:, 2 * few : 3 * few]
        bent, slope, active = bend(both[:, :few], both[:, few : 2 * few])
        grad_gate = (grad * both[:, few : 2 * few] * slope).astype(bf16)
        grad_up = (grad * bent).astype(bf16)
        blank = jnp.zeros_like(active)
        outs = jnp.concatenate([blank, blank, active, blank], axis=1)
        ins = jnp.concatenate([grad_gate, grad_up, blank, blank], axis=1)
        sum_out[...] = dot(outs, rest_ref[...], 1, 1)
        sum_back[...] = dot(ins, rest_ref[...], 1, 1)
        put(
            dot(unit_t[...], ins) + dot(g_t[...], outs),
            slice(grads_ref.shape[1] - 4 * few, grads_ref.shape[1]),
        )

    join(gate_ref, weight_refs[0], second_order)
    join(up_ref, weight_refs[1], second_order)
    join(out_ref, weight_refs[2], first_order)
    gate = dot(unit[...], gate_ref[...])
    upward = dot(unit[...], up_ref[...])
    grad = dot(g_ref[...], out_ref[...])
    bent, slope, active = bend(gate, upward)
    grad_gate = (grad * upward * slope).astype(bf16)
    grad_up = (grad * bent).astype(bf16)
    sum_out[...] += dot(active, out_ref[...], 1, 1)
    sum_back[...] += dot(grad_gate, gate_ref[...], 1, 1) + dot(grad_up, up_ref[...], 1, 1)
    count = grads_ref.shape[1] // step // 3
    for at, grads in enumerate(
        (dot(unit_t[...], grad_gate), dot(unit_t[...], grad_up), dot(g_t[...], active))
    ):
        place = pl.multiple_of(at * count * step + here * step, 128)
        put(grads, pl.ds(place, step))

    @pl.when(here == last)
    def _():
        partial_ref[...] = sum_out[...].astype(bf16)
        back_ref[...] = sum_back[...].astype(bf16)


def feed(first_order, second_order, x, ours, theirs, g, first, second, axes, step=256):
    tokens, width = x.shape
    start = width // 2 // step
    count = (first[0].shape[2] - width // 2) // step
    rest = second[0].shape[2] - 2 * count * step
    columns = 3 * count * step + rest

    def whole(*shape):
        return pl.BlockSpec(shape, lambda i, one, two: (0, 0))

    def piece(arrays, size, at):
        return [
            pl.BlockSpec((*array.shape[:2], size), lambda i, one, two: (0, 0, at(i)))
            for array in arrays
        ]

    pair = jax.ShapeDtypeStruct((tokens, width), bf16)
    return pl.pallas_call(
        functools.partial(feed_kernel, firsts=len(first), seconds=len(second), axes=axes),
        name="feed",
        grid_spec=pltpu.PrefetchScalarGridSpec(
            num_scalar_prefetch=2,
            grid=(count,),
            in_specs=[whole(tokens, width)] * 4
            + piece(second, step, lambda i: i)
            + piece(second, step, lambda i: count + i)
            + piece(first, step, lambda i: start + i)
            + piece(second, rest, lambda i: 2 * count * step // rest),
            out_specs=[whole(tokens, width)] * 3 + [whole(width, columns)],
            scratch_shapes=[
                pltpu.VMEM((tokens, width), bf16),
                pltpu.VMEM((width, tokens), bf16),
                pltpu.VMEM((width, tokens), bf16),
                pltpu.VMEM((tokens, width), f32),
                pltpu.VMEM((tokens, width), f32),
                pltpu.VMEM((width, step), bf16),
                pltpu.VMEM((width, step), bf16),
                pltpu.VMEM((width, step), bf16),
                pltpu.VMEM((width, rest), bf16),
            ],
        ),
        out_shape=[
            jax.ShapeDtypeStruct((tokens, width), f32),
            pair,
            pair,
            jax.ShapeDtypeStruct((width, columns), bf16),
        ],
        compiler_params=pltpu.CompilerParams(vmem_limit_bytes=VMEM),
        cost_estimate=cost(2 * 9 * 2 * tokens * width * count * step, 24 << 20),
    )(first_order, second_order, x, ours, theirs, g, *second, *second, *first, *second)


def middle_back_kernel(
    core_ref, order_ref, line_ref, residual_ref, g_ref, ours_ref, theirs_ref, attn_ref,
    attended_ref, out_ours_ref, out_theirs_ref, layer_ref, residual_grad_ref, *rest, axes,
):
    planes, lines, wide, beside = axes
    dout_refs, grads_refs, (dout_all, grads_all) = rest[: -2 - lines], rest[-2 - lines : -2], rest[-2:]
    rows = layer_ref.shape[0]
    half = attn_ref.shape[0]
    own = pl.ds(pl.multiple_of(core_ref[0] * rows, rows), rows)
    layer_ref[...] = (
        residual_ref[own, :]
        + out_ours_ref[own, :].astype(f32)
        + out_theirs_ref[...].astype(f32)
    ).astype(bf16)
    unit, inverse = unit_rows(residual_ref[...])
    scaled = ours_ref[...].astype(f32) + theirs_ref[...].astype(f32)
    grad = g_ref[...].astype(f32) + unit_back(scaled, unit, inverse)
    low = grad.astype(bf16)
    residual_grad_ref[...] = grad
    dout_all[...] = dot(attn_ref[...], low, 1, 1).astype(bf16)
    for at, dout_ref in enumerate(dout_refs):
        dout_ref[...] = dout_all[pl.ds(pl.multiple_of(order_ref[at] * HDIM, HDIM), HDIM)]
    grads_all[...] = dot(attended_ref[...], low)
    few = HDIM // wide // beside
    for shift, grads_ref in enumerate(grads_refs):
        line = (line_ref[0] + shift) % lines
        blocks = [
            grads_all[pl.ds(pl.multiple_of((plane * lines + line) * HDIM, HDIM), HDIM)]
            for plane in range(planes)
        ]
        pieces = []
        for far in range(wide):
            for plane in range(planes):
                for near in range(beside):
                    start = (far * beside + near) * few
                    piece = blocks[plane][start : start + few]
                    pieces += [piece[:, :half], piece[:, half:]]
        grads_ref[...] = jnp.concatenate(pieces, axis=0).astype(bf16)


def middle_back(
    core, order, line, residual, g, ours, theirs, attn, attended, out_ours, out_theirs, axes
):
    tokens, width = residual.shape
    rows = tokens // 2
    half = width // 2
    chips = half // HDIM
    lines = axes[1]

    def whole(*shape):
        return pl.BlockSpec(shape, lambda i, core, order, line: (0,) * len(shape))

    return pl.pallas_call(
        functools.partial(middle_back_kernel, axes=axes),
        name="middle_back",
        grid_spec=pltpu.PrefetchScalarGridSpec(
            num_scalar_prefetch=3,
            grid=(1,),
            in_specs=[whole(tokens, width)] * 4
            + [whole(half, width), whole(half, tokens), whole(tokens, width), whole(rows, width)],
            out_specs=[whole(rows, width), whole(tokens, width)]
            + [whole(HDIM, tokens)] * chips
            + [whole(width // lines, half)] * lines,
            scratch_shapes=[pltpu.VMEM((half, tokens), bf16), pltpu.VMEM((half, width), f32)],
        ),
        out_shape=[
            jax.ShapeDtypeStruct((rows, width), bf16),
            jax.ShapeDtypeStruct((tokens, width), f32),
        ]
        + [jax.ShapeDtypeStruct((HDIM, tokens), bf16)] * chips
        + [jax.ShapeDtypeStruct((width // lines, half), bf16)] * lines,
        compiler_params=pltpu.CompilerParams(vmem_limit_bytes=VMEM),
        cost_estimate=cost(2 * 2 * 2 * tokens * width * half, 16 << 20),
    )(core, order, line, residual, g, ours, theirs, attn, attended, out_ours, out_theirs)


def hidden_back_kernel(order_ref, core_ref, w_ref, *rest):
    dp_refs, (own_ref, other_ref, stacked) = rest[:-3], rest[-3:]
    for place, dp_ref in enumerate(dp_refs):
        size = dp_ref.shape[0]
        stacked[pl.ds(pl.multiple_of(order_ref[place] * size, 64), size)] = dp_ref[...]
    rows = own_ref.shape[0]
    flat = dot(w_ref[...], stacked[...])
    first = flat[:, :rows].T
    second = flat[:, rows:].T
    zero = core_ref[0] == 0
    own_ref[...] = jnp.where(zero, first, second)
    other_ref[...] = jnp.where(zero, second, first).astype(bf16)


def hidden_back(order, core, weights, pieces):
    width, columns = weights.shape
    rows = pieces[0].shape[1] // 2

    def whole(*shape):
        return pl.BlockSpec(shape, lambda i, order, core: (0,) * len(shape))

    return pl.pallas_call(
        hidden_back_kernel,
        name="hidden_back",
        grid_spec=pltpu.PrefetchScalarGridSpec(
            num_scalar_prefetch=2,
            grid=(1,),
            in_specs=[whole(width, columns)] + [whole(*pieces[0].shape)] * len(pieces),
            out_specs=[whole(rows, width)] * 2,
            scratch_shapes=[pltpu.VMEM((columns, 2 * rows), bf16)],
        ),
        out_shape=[
            jax.ShapeDtypeStruct((rows, width), f32),
            jax.ShapeDtypeStruct((rows, width), bf16),
        ],
        compiler_params=pltpu.CompilerParams(vmem_limit_bytes=VMEM),
        cost_estimate=cost(2 * 2 * 2 * rows * width * columns, 8 << 20),
    )(order, core, weights, *pieces)


def head_grad_kernel(order_ref, owner_ref, unit_ref, *rest, owners):
    dp_refs, out_refs, out_all = rest[: -1 - owners], rest[-1 - owners : -1], rest[-1]
    block = dp_refs[0].shape[1]
    total = None
    for place, dp_ref in enumerate(dp_refs):
        rows = pl.ds(pl.multiple_of(order_ref[place] * block, block), block)
        added = dot(dp_ref[...], unit_ref[rows])
        total = added if total is None else total + added
    for at in range(owners):
        out_all[at] = total[:, at * 128 : (at + 1) * 128].astype(bf16)
    for at, out_ref in enumerate(out_refs):
        out_ref[...] = out_all[owner_ref[at]]


def head_grad(order, owner_order, unit_all, pieces):
    length, width = unit_all.shape
    owners = width // 128
    size = pieces[0].shape[0]

    def whole(*shape):
        return pl.BlockSpec(shape, lambda i, order, owner: (0,) * len(shape))

    return pl.pallas_call(
        functools.partial(head_grad_kernel, owners=owners),
        name="head_grad",
        grid_spec=pltpu.PrefetchScalarGridSpec(
            num_scalar_prefetch=2,
            grid=(1,),
            in_specs=[whole(length, width)] + [whole(*pieces[0].shape)] * len(pieces),
            out_specs=[whole(size, 128)] * owners,
            scratch_shapes=[pltpu.VMEM((owners, size, 128), bf16)],
        ),
        out_shape=[jax.ShapeDtypeStruct((size, 128), bf16)] * owners,
        compiler_params=pltpu.CompilerParams(vmem_limit_bytes=VMEM),
        cost_estimate=cost(2 * 2 * length * width * size, 10 << 20),
    )(order, owner_order, unit_all, *pieces)


def adam(weight, gradient, first, second, rate):
    first = BETA_FIRST * first + (1.0 - BETA_FIRST) * gradient
    second = BETA_SECOND * second + (1.0 - BETA_SECOND) * gradient * gradient
    first_hat = first / (1.0 - BETA_FIRST**STEP)
    second_hat = second / (1.0 - BETA_SECOND**STEP)
    weight = weight - rate * (first_hat / (jnp.sqrt(second_hat) + EPSILON) + DECAY * weight)
    return (weight, first, second)


def adam_in_kernels(weight, gradient, first, second, rate):
    first = BETA_FIRST * first + (1.0 - BETA_FIRST) * gradient
    second = BETA_SECOND * second + (1.0 - BETA_SECOND) * gradient * gradient
    second_hat = second * (1.0 / (1.0 - BETA_SECOND**STEP))
    bottom = second_hat * lax.rsqrt(second_hat) + EPSILON
    guess = pl.reciprocal(bottom, approx=True)
    guess = guess * (2.0 - bottom * guess)
    scale = rate / (1.0 - BETA_FIRST**STEP)
    weight = weight * (1.0 - rate * DECAY) - (scale * first) * guess
    return (weight, first, second)


def adam_into(refs, weight, gradient, first, second, rate):
    for ref, value in zip(refs, adam_in_kernels(weight, gradient, first, second, rate)):
        ref[...] = value


def rounded_in_kernel(values):
    return values.astype(bf16).astype(f32)


def adam_most_kernel(grads_ref, gain_ref, *refs, rates):
    (w_in, m_in, v_in), attn, out = refs[:3], refs[3:6], refs[6:9]
    new_in, new_attn, new_out = refs[9:12], refs[12:15], refs[15:18]
    gain_grad, turned = refs[18:]
    here = pl.program_id(0)
    chips = grads_ref.shape[0] // 2
    width = w_in.shape[1] // 2
    main = width // 256 * 128
    few = width // 2 - main

    @pl.when(here == 0)
    def _():
        for core in range(2):
            columns = jnp.concatenate(
                [grads_ref[2 * chip + core, :, 2 * main : 3 * main] for chip in range(chips)],
                axis=0,
            )
            turned[core * main : (core + 1) * main] = columns.astype(f32).T
            rest = jnp.concatenate(
                [
                    grads_ref[2 * chip + core, :, 3 * main : 3 * main + 128]
                    for chip in range(chips)
                ],
                axis=0,
            )
            start = 2 * main + core * few
            turned[start : start + few] = rest.astype(f32).T[2 * few : 3 * few]

    each = grads_ref.shape[1]
    some = w_in.shape[0] // each
    for at_chip in range(some):
        source = 2 * (here * some + at_chip)
        columns = []
        for at in range(2):
            for core in range(2):
                place = at * main
                columns.append(grads_ref[source + core, :, place : place + main].astype(f32))
            for core in range(2):
                rest = grads_ref[source + core, :, 3 * main : 3 * main + 128].astype(f32)
                columns.append(rest[:, at * few : (at + 1) * few])
        grads = jnp.concatenate(columns, axis=1)
        rows = slice(at_chip * each, (at_chip + 1) * each)
        weight = w_in[rows]
        gain_grad[rows] = jnp.sum(grads * rounded_in_kernel(weight), axis=1, keepdims=True)
        values = adam_in_kernels(
            weight, grads * gain_ref[rows], m_in[rows], v_in[rows], rates[0]
        )
        for ref, value in zip(new_in, values):
            ref[rows] = value
        rows = slice(at_chip * each // 2, (at_chip + 1) * each // 2)
        for core in range(2):
            piece = grads_ref[source + core, :, 3 * main + 128 :].astype(f32)
            grads = jnp.concatenate([piece[: each // 2], piece[each // 2 :]], axis=1)
            values = adam_in_kernels(
                attn[0][core, rows], grads, attn[1][core, rows], attn[2][core, rows], rates[1]
            )
            for ref, value in zip(new_attn, values):
                ref[core, rows] = value

    size = out[0].shape[0]
    grads = turned[pl.ds(pl.multiple_of(here * size, 8), size)]
    adam_into(new_out, out[0][...], grads, out[1][...], out[2][...], rates[2])


def adam_most(grads, gain, weights_in, weights_attn, weights_out, rates, steps=2):
    rows, columns = weights_in[0].shape
    width = weights_attn[0].shape[1]
    hidden = weights_out[0].shape[0]
    weights_attn = [array.reshape(2, rows // 2, width) for array in weights_attn]
    block_in = pl.BlockSpec((rows // steps, columns), lambda i: (i, 0))
    block_attn = pl.BlockSpec((2, rows // 2 // steps, width), lambda i: (0, i, 0))
    block_out = pl.BlockSpec((hidden // steps, rows), lambda i: (i, 0))
    column = pl.BlockSpec((rows // steps, 1), lambda i: (i, 0))
    blocks = [block_in] * 3 + [block_attn] * 3 + [block_out] * 3
    arrays = (*weights_in, *weights_attn, *weights_out)
    *results, gain_grad = pl.pallas_call(
        functools.partial(adam_most_kernel, rates=rates),
        name="adam_most",
        grid=(steps,),
        in_specs=[pl.BlockSpec(grads.shape, lambda i: (0, 0, 0)), column] + blocks,
        out_specs=blocks + [column],
        out_shape=[jax.ShapeDtypeStruct(array.shape, f32) for array in arrays]
        + [jax.ShapeDtypeStruct((rows, 1), f32)],
        scratch_shapes=[pltpu.VMEM((hidden, rows), f32)],
        compiler_params=pltpu.CompilerParams(vmem_limit_bytes=VMEM),
        cost_estimate=cost(rows * columns * 20, rows * columns * 26),
    )(grads, gain, *arrays)
    new_attn = [array.reshape(rows, width) for array in results[3:6]]
    return results[:3], new_attn, results[6:], gain_grad


def adam_qkv_kernel(order_ref, *refs, rate):
    grads_refs, (gain_ref, w_ref, m_ref, v_ref, new_w, new_m, new_v, gain_grad, joined) = (
        refs[:-9], refs[-9:]
    )
    here = pl.program_id(0)
    heads = sum(grads_ref.shape[0] for grads_ref in grads_refs)

    @pl.when(here == 0)
    def _():
        at = 0
        for grads_ref in grads_refs:
            for place in range(grads_ref.shape[0]):
                for part in range(3):
                    row = (part * heads + order_ref[at]) * HDIM
                    joined[pl.ds(pl.multiple_of(row, HDIM), HDIM)] = grads_ref[
                        place, part * HDIM : (part + 1) * HDIM
                    ].astype(f32)
                at += 1

    size = w_ref.shape[1]
    grads = joined[pl.ds(pl.multiple_of(here * size, size), size)].T
    weight = w_ref[...]
    added = jnp.sum(grads * rounded_in_kernel(weight), axis=1, keepdims=True)
    gain_grad[...] = added + jnp.where(here == 0, 0.0, gain_grad[...])
    adam_into(
        (new_w, new_m, new_v), weight, grads * gain_ref[...], m_ref[...], v_ref[...], rate
    )


def adam_qkv(order, grads, gain, weight, first, second, rate, step=1536):
    rows, columns = weight.shape
    block = pl.BlockSpec((rows, step), lambda i, order: (0, i))
    column = pl.BlockSpec((rows, 1), lambda i, order: (0, 0))
    same = jax.ShapeDtypeStruct((rows, columns), f32)
    return pl.pallas_call(
        functools.partial(adam_qkv_kernel, rate=rate),
        name="adam_qkv",
        grid_spec=pltpu.PrefetchScalarGridSpec(
            num_scalar_prefetch=1,
            grid=(columns // step,),
            in_specs=[pl.BlockSpec(piece.shape, lambda i, order: (0, 0, 0)) for piece in grads]
            + [column]
            + [block] * 3,
            out_specs=[block] * 3 + [column],
            scratch_shapes=[pltpu.VMEM((columns, rows), f32)],
        ),
        out_shape=[same] * 3 + [jax.ShapeDtypeStruct((rows, 1), f32)],
        compiler_params=pltpu.CompilerParams(vmem_limit_bytes=VMEM),
        cost_estimate=cost(rows * columns * 20, rows * columns * 26),
    )(order, *grads, gain, weight, first, second)


def ring(axis, shift):
    size = lax.axis_size(axis)
    return [(at, (at + shift) % size) for at in range(size)]


def along(axis, array):
    return [array] + [
        lax.ppermute(array, axis, ring(axis, shift)) for shift in range(1, lax.axis_size(axis))
    ]


def shards(
    tokens,
    positions,
    cotangent,
    weight_qkv,
    weight_attn,
    weight_in,
    weight_out,
    norm_gains,
    first_qkv,
    first_attn,
    first_in,
    first_out,
    first_gains,
    second_qkv,
    second_attn,
    second_in,
    second_out,
    second_gains,
):
    rows, width = tokens.shape[1:]
    shard_rows = weight_qkv.shape[1]
    heads = width // HDIM
    hidden = weight_out.shape[1]
    core = lax.axis_index("c")
    mine = lax.axis_index(CTX)
    chip = lax.axis_index(CHIPS)
    chips = lax.axis_size(CHIPS)
    owners = lax.axis_size(FSDP)
    length = rows * chips * 2
    main = hidden // 256 * 128
    few = hidden // 2 - main
    core_at = core.reshape(1).astype(jnp.int32)
    axes = (lax.axis_size("zh"), lax.axis_size("y"), lax.axis_size("x"), lax.axis_size("zl"))
    offsets = [(far, near) for far in range(lax.axis_size("x")) for near in range(2)]
    across, beside = lax.axis_index("x"), lax.axis_index("zl")
    wide = lax.axis_size("x")

    def chips_at(sign):
        places = [(across + sign * far) % wide * 2 + (beside ^ near) for far, near in offsets]
        return jnp.stack(places).astype(jnp.int32)

    local = tokens[0]
    extra = 16
    high, low = positions[0] // 128, positions[0] % 128
    places_row = jnp.concatenate([high, low, jnp.zeros((width - 2 * rows,), jnp.int32)])
    places_rows = jnp.concatenate(
        [places_row[None], jnp.zeros((extra - 1, width), jnp.int32)], axis=0
    ).astype(bf16)
    sequence = lax.all_gather(
        jnp.concatenate([local, places_rows], axis=0), CTX, axis=0, tiled=True
    )
    first_part, second_part, head_part, half_heads = prepare(
        jnp.stack([core, chip]).astype(jnp.int32),
        norm_gains[0],
        weight_qkv[0],
        weight_attn[0],
        weight_in[0],
        weight_out[0],
    )
    first_joined = jnp.stack(along("y", first_part))
    second_joined = jnp.stack(along("y", second_part))
    head_weights = lax.all_to_all(
        jnp.broadcast_to(head_part, (owners, *head_part.shape)), FSDP, 0, 0, tiled=True
    )
    sequence, first_joined, second_joined, _ = lax.optimization_barrier(
        (sequence, first_joined, second_joined, head_weights)
    )
    one_shard = lax.dynamic_slice_in_dim(second_joined, across, 1, 0)
    one_shard = lax.ppermute(one_shard, "zh", SWAP)
    lines = lax.axis_size("y")
    plane, line = lax.axis_index("zh"), lax.axis_index("y")

    def owner(far, shift):
        return (plane ^ far) * lines + (line - shift) % lines

    own_shards = [owner(0, shift) for shift in range(lines)]
    first_order = jnp.stack(own_shards + [owner(1, shift) for shift in range(lines)])
    second_order = jnp.stack(
        own_shards + [owner(1, (across - shift) % wide) for shift in range(wide)]
    )
    first_order, second_order = first_order.astype(jnp.int32), second_order.astype(jnp.int32)

    def in_order(ours, theirs):
        first = jnp.where(core == 0, ours, theirs)
        second = jnp.where(core == 0, theirs, ours)
        return jnp.concatenate([first, second], axis=0)

    def swap(array):
        return lax.ppermute(array, "c", SWAP)

    gradient = in_order(cotangent[0], swap(cotangent[0]))

    freqs = jnp.exp(jnp.arange(HDIM // 2, dtype=f32) * (-2.0 * math.log(ROPE_BASE) / HDIM))
    by_device = sequence.reshape(2 * chips, rows + extra, width)[:, rows]
    by_device = by_device.astype(f32)
    places = by_device[:, :rows] * 128.0 + by_device[:, rows : 2 * rows]
    angles = freqs[:, None] * places.reshape(1, length)
    cosine = jnp.cos(angles)
    sine = jnp.sin(angles)
    unit_all, qkv, keys, values = project(sequence, head_weights, cosine, sine, extra)
    keys, half_heads, one_shard, first_joined = lax.optimization_barrier(
        (keys, half_heads, one_shard, first_joined)
    )
    second_pieces = [second_joined, *along("x", one_shard)]
    first_pieces = [first_joined, lax.ppermute(first_joined, "zh", SWAP)]
    mat_qkv = lax.all_gather(half_heads, FSDP, axis=0, tiled=True)
    low_out, out, lse = attend(keys, qkv, chips)
    firsts = len(first_pieces)
    low_out, *arrived = lax.optimization_barrier((low_out, *first_pieces, *second_pieces))
    first_pieces, second_pieces = arrived[:firsts], arrived[firsts:]
    attended = lax.all_to_all(low_out, CHIPS, 0, 0, tiled=True)
    attended = attended.reshape(heads // 2 * HDIM, 2 * rows)
    mixed, mat_attn = attend_out(first_order, attended, first_pieces)
    current = lax.dynamic_slice_in_dim(
        sequence, chip * 2 * (rows + extra), 2 * (rows + extra), 0
    ).reshape(2, rows + extra, width)[:, :rows].reshape(2 * rows, width)
    residual, partial, back, grads = feed(
        first_order, second_order, current, mixed, swap(mixed), gradient, first_pieces,
        second_pieces, axes,
    )
    grads, mat_qkv = lax.optimization_barrier((grads, mat_qkv))
    first_sum = lax.psum_scatter(grads, "y", scatter_dimension=0, tiled=True)

    def move(pieces, sign):
        moved = [pieces[0]]
        for (far, near), piece in list(zip(offsets, pieces))[1:]:
            pairs = [
                (at, (at // 2 + sign * far) % wide * 2 + (at % 2 ^ near)) for at in range(chips)
            ]
            moved.append(lax.ppermute(piece, CHIPS, pairs))
        return moved

    ahead, behind = chips_at(1), chips_at(-1)
    theirs = swap(lax.dynamic_slice_in_dim(partial, (1 - core) * rows, rows, 0))
    layer_out, residual_grad, *pieces = middle_back(
        core_at, ahead, line.reshape(1).astype(jnp.int32), residual, gradient, back, swap(back),
        mat_attn, attended, partial, theirs, axes,
    )
    dout_pieces, attn_pieces = pieces[:chips], pieces[chips:]

    douts = move(dout_pieces, 1)
    attn_arrived = attn_pieces[:1] + [
        lax.ppermute(piece, "y", ring("y", shift))
        for shift, piece in list(enumerate(attn_pieces))[1:]
    ]
    pieces = attend_back(behind, keys, values, qkv, douts, out, lse, cosine, sine)
    rest = lax.optimization_barrier((*pieces, *attn_arrived))
    pieces, attn_arrived = rest[:chips], rest[chips:]
    owner_places = [(far, shift) for far in range(2) for shift in range(lines)]
    owner_order = jnp.stack(
        [(plane ^ far) * lines + (line + shift) % lines for far, shift in owner_places]
    ).astype(jnp.int32)
    head_parts = head_grad(behind, owner_order, unit_all, pieces)

    def total(arrays):
        return sum(array.astype(f32) for array in arrays).astype(bf16)

    moved = move(pieces, -1)
    first_sum, *rest = lax.optimization_barrier((first_sum, *moved, *head_parts))
    moved, head_parts = rest[:chips], rest[chips:]
    first_sum = jnp.concatenate([first_sum, total(attn_arrived)], axis=1)
    arrived = lax.all_to_all(first_sum, ("x", "zh", "zl"), 0, 0, tiled=True)
    own_hidden, other_hidden = hidden_back(ahead, core_at, mat_qkv, moved)
    arrived, own_hidden, *head_parts = lax.optimization_barrier(
        (arrived, own_hidden, *head_parts)
    )
    grad_hidden = own_hidden + swap(other_hidden).astype(f32)
    unit_in, scale_in = unit_rows(local.astype(f32))
    own_residual = lax.dynamic_slice_in_dim(residual_grad, core * rows, rows, 0)
    tokens_grad = (own_residual + unit_back(grad_hidden, unit_in, scale_in))[None]

    head_arrived = [head_parts[0]]
    for (far, shift), piece in list(zip(owner_places, head_parts))[1:]:
        pairs = [
            (at, (at // lines ^ far) * lines + (at % lines + shift) % lines) for at in range(owners)
        ]
        head_arrived.append(lax.ppermute(piece, FSDP, pairs))
    head_own = total(head_arrived)[None]
    arrived = arrived.reshape(2 * chips, shard_rows // chips, -1)
    second_sum = jnp.sum(arrived.astype(f32), axis=0).astype(bf16)
    all_grads = lax.all_gather(second_sum, CTX, axis=0, tiled=False)

    head_pair = jnp.concatenate([head_own, swap(head_own)], axis=0)
    head_four = jnp.concatenate([head_pair, lax.ppermute(head_pair, "zl", SWAP)], axis=0)
    head_grads = [head_four] + [
        lax.ppermute(head_four, "x", ring("x", shift)) for shift in range(1, wide)
    ]
    head_order = jnp.stack(
        [
            (across - shift) % wide * 4 + (beside ^ near) * 2 + (core ^ other)
            for shift in range(wide)
            for near in range(2)
            for other in range(2)
        ]
    ).astype(jnp.int32)

    rates = (
        width ** (-0.5),
        max(1, 3 * width // length) ** (-0.5),
        width ** (-0.5),
        hidden ** (-0.5),
    )
    columns_of_gains = norm_gains[0].astype(bf16).astype(f32).T
    new_in, new_attn, new_out, gain_second = adam_most(
        all_grads,
        columns_of_gains[:, 1:],
        (weight_in[0], first_in[0], second_in[0]),
        (weight_attn[0], first_attn[0], second_attn[0]),
        (weight_out[0], first_out[0], second_out[0]),
        (rates[2], rates[1], rates[3]),
    )
    *new_qkv, gain_first = adam_qkv(
        head_order, head_grads, columns_of_gains[:, :1], weight_qkv[0], first_qkv[0], second_qkv[0], rates[0]
    )
    gain_grads = jnp.concatenate([gain_first, gain_second], axis=1).T
    new_gains = adam(norm_gains[0], gain_grads, first_gains[0], second_gains[0], GAIN_RATE)
    updated = (new_qkv, new_attn, new_in, new_out, new_gains)
    return (
        layer_out[None],
        tokens_grad,
        *[updated[member][0][None] for member in range(5)],
        *[updated[member][1][None] for member in range(5)],
        *[updated[member][2][None] for member in range(5)],
    )


def solution(mesh):
    split = Mesh(mesh.devices.reshape(4, 2, 2, 2, 4), ("x", "zl", "c", "zh", "y"))
    by_row = P(None, FSDP, None)
    by_column = P(None, None, FSDP)
    weights = (by_row, by_row, by_row, by_column, by_column)
    by_token = P(FSDP, CTX, None)
    return jax.shard_map(
        shards,
        mesh=split,
        in_specs=(by_token, P(FSDP, CTX), by_token) + weights * 3,
        out_specs=(by_token, by_token) + weights * 3,
        check_vma=False,
    )
```

```python
import functools
import math

import jax
import jax.numpy as jnp
from jax import lax
from jax.experimental import pallas as pl
from jax.experimental.pallas import tpu as pltpu
from jax.sharding import Mesh, PartitionSpec as P

HDIM = 64
STEP = 10
BETA_FIRST = 0.5
BETA_SECOND = 0.5
EPSILON = 1e-08
DECAY = 0.01
NORM_EPS = 1e-05
ROPE_BASE = 160000.0
GAIN_RATE = 0.6
LOG2E = math.log2(math.e)
f32 = jnp.float32
bf16 = jnp.bfloat16

CHIPS = ("x", "zl")
CTX = ("x", "zl", "c")
FSDP = ("zh", "y")
SWAP = [(0, 1), (1, 0)]
VMEM = 60 << 20


def dot(left, right, left_dim=1, right_dim=0):
    return lax.dot_general(
        left, right, (((left_dim,), (right_dim,)), ((), ())), preferred_element_type=f32
    )


def cost(flops, moved):
    return pl.CostEstimate(flops=flops, bytes_accessed=moved, transcendentals=0)


def unit_rows(values):
    average = jnp.mean(values, axis=-1, keepdims=True)
    centered = values - average
    spread = jnp.mean(centered * centered, axis=-1, keepdims=True)
    inverse = lax.rsqrt(spread + NORM_EPS)
    return centered * inverse, inverse


def unit_back(scaled, unit, inverse):
    first_mean = jnp.mean(scaled, axis=-1, keepdims=True)
    second_mean = jnp.mean(scaled * unit, axis=-1, keepdims=True)
    return inverse * (scaled - first_mean - unit * second_mean)


def prepare_kernel(
    place_ref, gains_ref, qkv_ref, attn_ref, in_ref, out_ref,
    first_ref, second_ref, head_ref, heads_ref,
):
    core, chip = place_ref[0], place_ref[1]
    rows = qkv_ref.shape[0]
    width = attn_ref.shape[1]
    hidden = out_ref.shape[0]
    main = hidden // 256 * 128
    few = hidden // 2 - main
    half = width // 2
    low_gains = gains_ref[...].astype(bf16).astype(f32)
    columns = jnp.concatenate([low_gains, jnp.zeros((6, rows), f32)], axis=0).T
    gain_first, gain_second = columns[:, 0:1], columns[:, 1:2]

    def pick(array):
        size = array.shape[1] // 2
        return jnp.where(core == 0, array[:, :size], array[:, size:])

    def scaled(values, gain):
        return (values.astype(bf16).astype(f32) * gain).astype(bf16)

    attn_rows = attn_ref[pl.ds(pl.multiple_of(core * HDIM, HDIM), HDIM)].astype(bf16)
    first_ref[:HDIM, :half] = attn_rows[:, :half]
    first_ref[HDIM:, :half] = attn_rows[:, half:]
    out_rows = out_ref[pl.ds(pl.multiple_of(core * main, 128), main)]
    first_ref[:, half:] = out_rows.T.astype(bf16)
    second_ref[:, :main] = scaled(pick(in_ref[:, : 2 * main]), gain_second)
    second_ref[:, main : 2 * main] = scaled(
        pick(in_ref[:, hidden : hidden + 2 * main]), gain_second
    )
    odd_out = out_ref[2 * main :].T
    odd = [
        scaled(pick(in_ref[:, 2 * main : hidden]), gain_second),
        scaled(pick(in_ref[:, hidden + 2 * main :]), gain_second),
        pick(odd_out).astype(bf16),
        jnp.zeros((rows, few), bf16),
    ]
    second_ref[:, 2 * main :] = jnp.concatenate(odd, axis=1)
    pieces = []
    for at in range(width // 128):
        for part in range(3):
            start = part * width + at * 128
            pieces.append(scaled(pick(qkv_ref[:, start : start + 128]), gain_first))
    heads_ref[...] = jnp.concatenate(pieces, axis=1)
    own = []
    for part in range(3):
        start = pl.multiple_of(part * width + chip * 128, 128)
        own.append(scaled(pick(qkv_ref[:, pl.ds(start, 128)]), gain_first).astype(f32))
    own.append(jnp.zeros((rows, HDIM), f32))
    head_ref[...] = jnp.concatenate(own, axis=1).T[: 3 * HDIM].astype(bf16)


def prepare(place, gains, qkv, attn, weight_in, weight_out):
    rows, width = attn.shape
    hidden = weight_out.shape[0]
    main = hidden // 256 * 128
    arrays = (gains, qkv, attn, weight_in, weight_out)
    shapes = [
        (rows, width // 2 + main),
        (rows, 2 * main + 4 * (hidden // 2 - main)),
        (3 * HDIM, rows),
        (rows, 3 * width // 2),
    ]

    def whole(shape):
        return pl.BlockSpec(shape, lambda i, place: (0, 0))

    return pl.pallas_call(
        prepare_kernel,
        name="prepare",
        grid_spec=pltpu.PrefetchScalarGridSpec(
            num_scalar_prefetch=1,
            grid=(1,),
            in_specs=[whole(array.shape) for array in arrays],
            out_specs=[whole(shape) for shape in shapes],
        ),
        out_shape=[jax.ShapeDtypeStruct(shape, bf16) for shape in shapes],
        compiler_params=pltpu.CompilerParams(vmem_limit_bytes=VMEM),
        cost_estimate=cost(rows * width * 60, 10 << 20),
    )(place, *arrays)


def project_kernel(
    x_ref, w_ref, cos_ref, sin_ref, unit_ref, qkv_ref, keys_ref, values_ref, w_all, *, extra
):
    half = HDIM // 2
    rows = cos_ref.shape[1]

    @pl.when(pl.program_id(0) == 0)
    def _():
        for part in range(w_ref.shape[0]):
            w_all[part * 128 : (part + 1) * 128] = w_ref[part].astype(f32).T.astype(bf16)

    count = (x_ref.shape[0] - rows) // extra
    each = rows // count
    for at in range(count):
        tokens = x_ref[at * (each + extra) : at * (each + extra) + each].astype(f32)
        unit_ref[at * each : (at + 1) * each] = unit_rows(tokens)[0].astype(bf16)
    unit = unit_ref[...]
    mixed = dot(unit, w_all[...]).T
    cosine = cos_ref[...]
    sine = sin_ref[...]

    def turn(one, two):
        return jnp.concatenate([one * cosine - two * sine, two * cosine + one * sine], axis=0)

    queries = turn(mixed[:half], mixed[half:HDIM])
    keys = turn(mixed[HDIM : HDIM + half], mixed[HDIM + half : 2 * HDIM])
    values = mixed[2 * HDIM :]
    qkv_ref[...] = jnp.concatenate([queries, keys, values], axis=0).astype(bf16)
    key_rows = keys.T.astype(bf16)
    value_rows = values.T.astype(bf16)
    ones = jnp.where(lax.broadcasted_iota(jnp.int32, (rows, HDIM), 1) < 3, 1.0, 0.0).astype(bf16)
    keys_ref[...] = jnp.concatenate([key_rows, key_rows, key_rows, ones], axis=1)
    values_ref[...] = jnp.concatenate([value_rows, ones], axis=1)


def project(tokens, weights, cosine, sine, extra, block=1024):
    width = tokens.shape[1]
    length = cosine.shape[1]
    steps = length // block
    return pl.pallas_call(
        functools.partial(project_kernel, extra=extra),
        name="project",
        grid=(steps,),
        in_specs=[
            pl.BlockSpec((tokens.shape[0] // steps, width), lambda i: (i, 0)),
            pl.BlockSpec(weights.shape, lambda i: (0, 0, 0)),
            pl.BlockSpec((HDIM // 2, block), lambda i: (0, i)),
            pl.BlockSpec((HDIM // 2, block), lambda i: (0, i)),
        ],
        out_specs=[
            pl.BlockSpec((block, width), lambda i: (i, 0)),
            pl.BlockSpec((3 * HDIM, block), lambda i: (0, i)),
            pl.BlockSpec((block, 256), lambda i: (i, 0)),
            pl.BlockSpec((block, 128), lambda i: (i, 0)),
        ],
        out_shape=[
            jax.ShapeDtypeStruct((length, width), bf16),
            jax.ShapeDtypeStruct((3 * HDIM, length), bf16),
            jax.ShapeDtypeStruct((length, 256), bf16),
            jax.ShapeDtypeStruct((length, 128), bf16),
        ],
        scratch_shapes=[pltpu.VMEM((width, 3 * HDIM), bf16)],
        compiler_params=pltpu.CompilerParams(vmem_limit_bytes=VMEM),
        cost_estimate=cost(length * width, 1 << 20),
    )(tokens, weights, cosine, sine)


def scaled_queries(queries):
    scaled = queries.astype(f32) * (LOG2E / math.sqrt(HDIM))
    high = scaled.astype(bf16)
    rest = scaled - high.astype(f32)
    middle = rest.astype(bf16)
    low = (rest - middle.astype(f32)).astype(bf16)
    return high, middle, low


def minus_in_three(values):
    rows = values.shape[1]
    at = lax.broadcasted_iota(jnp.int32, (16, rows), 0)
    high = (-values).astype(bf16).astype(f32)
    rest = -values - high
    middle = rest.astype(bf16).astype(f32)
    low = rest - middle
    stacked = jnp.where(at == 0, high, jnp.where(at == 1, middle, jnp.where(at == 2, low, 0.0)))
    return stacked.astype(bf16)


def attend_kernel(
    keys_ref, q_ref, k_ref, v_ref, low_ref, out_ref, lse_ref, v_ones, longest, *, part
):
    length = keys_ref.shape[0]
    count = length // part

    @pl.when(pl.program_id(0) == 0)
    def _():
        v_ones[:HDIM] = v_ref[...]
        v_ones[HDIM:] = jnp.where(
            lax.broadcasted_iota(jnp.int32, (16, length), 0) < 1, 1.0, 0.0
        ).astype(bf16)
        squares = jnp.sum(k_ref[...].astype(f32) ** 2, axis=0, keepdims=True)
        longest[...] = jnp.broadcast_to(jnp.max(squares, axis=1, keepdims=True), longest.shape)

    queries = jnp.concatenate(scaled_queries(q_ref[...]), axis=0)

    def finish(total, shift):
        summed = total[HDIM : HDIM + 1]
        result = total[:HDIM] / summed
        out_ref[...] = result
        lse_ref[...] = shift + jnp.log2(summed)
        step = low_ref.shape[2]
        for at in range(low_ref.shape[0]):
            low_ref[at] = result[:, at * step : (at + 1) * step].astype(bf16)
        return summed

    squares = jnp.sum((q_ref[...].astype(f32) * (LOG2E / math.sqrt(HDIM))) ** 2, axis=0, keepdims=True)
    shift = jnp.sqrt(squares * longest[0:1, 0:1])
    shifted = jnp.concatenate([queries, minus_in_three(shift)], axis=0)

    def score(at):
        return dot(keys_ref[at * part : (at + 1) * part, : 3 * HDIM + 16], shifted)

    scores = score(0)
    total = None
    for at in range(count):
        following = score(at + 1) if at + 1 < count else None
        soft = jnp.exp2(scores).astype(bf16)
        added = dot(v_ones[:, at * part : (at + 1) * part], soft)
        total = added if total is None else total + added
        scores = following
    summed = finish(total, shift)

    @pl.when(jnp.min(summed) < 2.0**-60)
    def _():
        def exact(at, carry):
            highest, total = carry
            rows = pl.ds(pl.multiple_of(at * part, part), part)
            scores = dot(keys_ref[rows, : 3 * HDIM], queries)
            raised = jnp.maximum(highest, jnp.max(scores, axis=0, keepdims=True))
            soft = jnp.exp2(scores - raised).astype(bf16)
            added = dot(v_ones[:, rows], soft)
            return raised, total * jnp.exp2(highest - raised) + added

        start = (
            jnp.full((1, q_ref.shape[1]), -1e30, f32),
            jnp.zeros((HDIM + 16, q_ref.shape[1]), f32),
        )
        highest, total = lax.fori_loop(0, count, exact, start)
        finish(total, highest)


def attend(keys, qkv, chips, block=1024, part=512):
    length = keys.shape[0]
    return pl.pallas_call(
        functools.partial(attend_kernel, part=part),
        name="attend",
        grid=(length // block,),
        in_specs=[
            pl.BlockSpec(keys.shape, lambda i: (0, 0)),
            pl.BlockSpec((HDIM, block), lambda i: (0, i)),
            pl.BlockSpec((HDIM, length), lambda i: (1, 0)),
            pl.BlockSpec((HDIM, length), lambda i: (2, 0)),
        ],
        out_specs=[
            pl.BlockSpec((block * chips // length, HDIM, length // chips), lambda i: (i, 0, 0)),
            pl.BlockSpec((HDIM, block), lambda i: (0, i)),
            pl.BlockSpec((1, block), lambda i: (0, i)),
        ],
        out_shape=[
            jax.ShapeDtypeStruct((chips, HDIM, length // chips), bf16),
            jax.ShapeDtypeStruct((HDIM, length), f32),
            jax.ShapeDtypeStruct((1, length), f32),
        ],
        scratch_shapes=[pltpu.VMEM((HDIM + 16, length), bf16), pltpu.VMEM((8, 128), f32)],
        compiler_params=pltpu.CompilerParams(vmem_limit_bytes=VMEM),
        cost_estimate=cost(length * HDIM, 1 << 20),
    )(keys, qkv, qkv, qkv)


def attend_back_kernel(
    order_ref,
    keys_ref,
    values_ref,
    q_ref,
    k_ref,
    out_ref,
    lse_ref,
    cos_ref,
    sin_ref,
    *rest,
    part,
):
    count = (len(rest) - 3) // 2
    dout_refs, dp_refs, (sums, dq_all, dout_all) = rest[:count], rest[count:-3], rest[-3:]
    half = HDIM // 2
    here = pl.program_id(0)
    length = keys_ref.shape[0]
    block = q_ref.shape[1]
    count = length // part
    factor = HDIM ** (-0.5)

    def turn_back(grads, cosine, sine):
        low = grads.astype(bf16).astype(f32)
        one, two = low[:half], low[half:]
        return jnp.concatenate([one * cosine + two * sine, two * cosine - one * sine], axis=0)

    @pl.when(here == 0)
    def _():
        sums[...] = jnp.zeros_like(sums)
        for place, dout_ref in enumerate(dout_refs):
            dout_all[place] = dout_ref[...]

    low_queries = q_ref[...]
    queries = jnp.concatenate(
        [*scaled_queries(low_queries), minus_in_three(lse_ref[...])], axis=0
    )
    low_dout = dout_all[here]
    dout = low_dout.astype(f32)
    centre = jnp.sum(dout * out_ref[...], axis=0, keepdims=True)
    douts = jnp.concatenate([low_dout, minus_in_three(centre)], axis=0)
    blank = jnp.zeros((block, HDIM), bf16)
    right = jnp.concatenate(
        [
            jnp.concatenate([low_queries.astype(f32).T.astype(bf16), blank], axis=1),
            jnp.concatenate([blank, dout.T.astype(bf16)], axis=1),
        ],
        axis=0,
    )

    def score(at):
        rows = slice(at * part, (at + 1) * part)
        return (
            dot(keys_ref[rows, : 3 * HDIM + 16], queries),
            dot(values_ref[rows, : HDIM + 16], douts),
        )

    now = score(0)
    grad_queries = None
    for at in range(count):
        following = score(at + 1) if at + 1 < count else None
        rows = slice(at * part, (at + 1) * part)
        soft = jnp.exp2(now[0])
        grads = (soft * now[1]).astype(bf16)
        added = dot(k_ref[:, rows], grads)
        grad_queries = added if grad_queries is None else grad_queries + added
        sums[rows] += dot(jnp.concatenate([grads, soft.astype(bf16)], axis=1), right)
        now = following

    def columns_of(place):
        return pl.ds(pl.multiple_of(order_ref[place] * block, block), block)

    columns = columns_of(here)
    dq_all[here] = turn_back(
        grad_queries * factor, cos_ref[:, columns], sin_ref[:, columns]
    ).astype(bf16)

    @pl.when(here == length // block - 1)
    def _():
        for place, dp_ref in enumerate(dp_refs):
            columns = columns_of(place)
            both = sums[columns].T
            dp_ref[:HDIM] = dq_all[place]
            dp_ref[HDIM : 2 * HDIM] = turn_back(
                both[:HDIM] * factor, cos_ref[:, columns], sin_ref[:, columns]
            ).astype(bf16)
            dp_ref[2 * HDIM :] = both[HDIM:].astype(bf16)


def attend_back(order, keys, values, qkv, douts, out, lse, cosine, sine, part=256):
    length = keys.shape[0]
    chips = len(douts)
    block = douts[0].shape[1]
    scores = length * length

    def whole(array):
        return pl.BlockSpec(array.shape, lambda i, order: (0, 0))

    return pl.pallas_call(
        functools.partial(attend_back_kernel, part=part),
        name="attend_back",
        grid_spec=pltpu.PrefetchScalarGridSpec(
            num_scalar_prefetch=1,
            grid=(chips,),
            in_specs=[
                whole(keys),
                whole(values),
                pl.BlockSpec((HDIM, block), lambda i, order: (0, order[i])),
                pl.BlockSpec((HDIM, length), lambda i, order: (1, 0)),
                pl.BlockSpec((HDIM, block), lambda i, order: (0, order[i])),
                pl.BlockSpec((1, block), lambda i, order: (0, order[i])),
                whole(cosine),
                whole(sine),
                *[whole(piece) for piece in douts],
            ],
            out_specs=[pl.BlockSpec((3 * HDIM, block), lambda i, order: (0, 0))] * chips,
            scratch_shapes=[
                pltpu.VMEM((length, 2 * HDIM), f32),
                pltpu.VMEM((chips, HDIM, block), bf16),
                pltpu.VMEM((chips, HDIM, block), bf16),
            ],
        ),
        out_shape=[jax.ShapeDtypeStruct((3 * HDIM, block), bf16)] * chips,
        compiler_params=pltpu.CompilerParams(vmem_limit_bytes=VMEM),
        cost_estimate=cost(5 * 4 * 2 * scores * HDIM, 8 << 20),
    )(order, keys, values, qkv, qkv, out, lse, cosine, sine, *douts)


def attend_out_kernel(order_ref, attended_ref, *rest):
    piece_refs, (mixed_ref, attn_ref) = rest[:-2], rest[-2:]
    half = attn_ref.shape[1] // 2
    at = 0
    for piece_ref in piece_refs:
        for place in range(piece_ref.shape[0]):
            rows = pl.ds(pl.multiple_of(order_ref[at] * HDIM, HDIM), HDIM)
            attn_ref[rows, :half] = piece_ref[place, :HDIM]
            attn_ref[rows, half:] = piece_ref[place, HDIM:]
            at += 1
    turned = attended_ref[...].astype(f32).T.astype(bf16)
    mixed_ref[...] = dot(turned, attn_ref[...]).astype(bf16)


def attend_out(order, attended, pieces):
    size, tokens = attended.shape
    width = 2 * size

    def whole(*shape):
        return pl.BlockSpec(shape, lambda i, order: (0,) * len(shape))

    return pl.pallas_call(
        attend_out_kernel,
        name="attend_out",
        grid_spec=pltpu.PrefetchScalarGridSpec(
            num_scalar_prefetch=1,
            grid=(1,),
            in_specs=[whole(size, tokens)]
            + [whole(*piece.shape[:2], width // 2) for piece in pieces],
            out_specs=[whole(tokens, width), whole(size, width)],
        ),
        out_shape=[
            jax.ShapeDtypeStruct((tokens, width), bf16),
            jax.ShapeDtypeStruct((size, width), bf16),
        ],
        compiler_params=pltpu.CompilerParams(vmem_limit_bytes=VMEM),
        cost_estimate=cost(2 * 2 * tokens * width * size, 4 << 20),
    )(order, attended, *pieces)


def feed_kernel(
    first_order, second_order, x_ref, ours_ref, theirs_ref, g_ref, *rest, firsts, seconds, axes
):
    weight_refs = []
    start = 0
    for size in (seconds, seconds, firsts, seconds):
        weight_refs.append(rest[start : start + size])
        start += size
    planes, lines, wide, beside = axes

    def put(grads, columns):
        size = grads.shape[0] // (planes * lines * wide)
        low = grads.astype(bf16)
        for plane in range(planes):
            for line in range(lines):
                for far in range(wide):
                    source = ((plane * lines + line) * wide + far) * size
                    target = ((line * wide + far) * planes + plane) * size
                    grads_ref[target : target + size, columns] = low[source : source + size]
    residual_ref, partial_ref, back_ref, grads_ref = rest[-13:-9]
    unit, unit_t, g_t, sum_out, sum_back = rest[-9:-4]
    gate_ref, up_ref, out_ref, rest_ref = rest[-4:]
    here = pl.program_id(0)
    last = pl.num_programs(0) - 1
    width = x_ref.shape[1]
    step = gate_ref.shape[1]

    def join(total, parts, order):
        at = 0
        for part in parts:
            size = part.shape[1]
            for place in range(part.shape[0]):
                total[pl.ds(pl.multiple_of(order[at] * size, size), size)] = part[place]
                at += 1

    def bend(gate, upward):
        cdf = 0.5 + 0.5 * lax.erf(gate * math.sqrt(0.5))
        slope = cdf + gate * jnp.exp(gate * gate * -0.5) * (1.0 / math.sqrt(2.0 * math.pi))
        bent = gate * cdf
        return bent, slope, (bent * upward).astype(bf16)

    @pl.when(here == 0)
    def _():
        residual = (
            x_ref[...].astype(f32) + ours_ref[...].astype(f32) + theirs_ref[...].astype(f32)
        )
        residual_ref[...] = residual
        normed = unit_rows(residual)[0]
        unit[...] = normed.astype(bf16)
        unit_t[...] = normed.T.astype(bf16)
        g_t[...] = g_ref[...].astype(f32).T.astype(bf16)
        join(rest_ref, weight_refs[3], second_order)
        few = rest_ref.shape[1] // 4
        both = dot(unit[...], rest_ref[...])
        grad = dot(g_ref[...], rest_ref[...])[:, 2 * few : 3 * few]
        bent, slope, active = bend(both[:, :few], both[:, few : 2 * few])
        grad_gate = (grad * both[:, few : 2 * few] * slope).astype(bf16)
        grad_up = (grad * bent).astype(bf16)
        blank = jnp.zeros_like(active)
        outs = jnp.concatenate([blank, blank, active, blank], axis=1)
        ins = jnp.concatenate([grad_gate, grad_up, blank, blank], axis=1)
        sum_out[...] = dot(outs, rest_ref[...], 1, 1)
        sum_back[...] = dot(ins, rest_ref[...], 1, 1)
        put(
            dot(unit_t[...], ins) + dot(g_t[...], outs),
            slice(grads_ref.shape[1] - 4 * few, grads_ref.shape[1]),
        )

    join(gate_ref, weight_refs[0], second_order)
    join(up_ref, weight_refs[1], second_order)
    join(out_ref, weight_refs[2], first_order)
    gate = dot(unit[...], gate_ref[...])
    upward = dot(unit[...], up_ref[...])
    grad = dot(g_ref[...], out_ref[...])
    bent, slope, active = bend(gate, upward)
    grad_gate = (grad * upward * slope).astype(bf16)
    grad_up = (grad * bent).astype(bf16)
    sum_out[...] += dot(active, out_ref[...], 1, 1)
    sum_back[...] += dot(grad_gate, gate_ref[...], 1, 1) + dot(grad_up, up_ref[...], 1, 1)
    count = grads_ref.shape[1] // step // 3
    for at, grads in enumerate(
        (dot(unit_t[...], grad_gate), dot(unit_t[...], grad_up), dot(g_t[...], active))
    ):
        place = pl.multiple_of(at * count * step + here * step, 128)
        put(grads, pl.ds(place, step))

    @pl.when(here == last)
    def _():
        partial_ref[...] = sum_out[...].astype(bf16)
        back_ref[...] = sum_back[...].astype(bf16)


def feed(first_order, second_order, x, ours, theirs, g, first, second, axes, step=256):
    tokens, width = x.shape
    start = width // 2 // step
    count = (first[0].shape[2] - width // 2) // step
    rest = second[0].shape[2] - 2 * count * step
    columns = 3 * count * step + rest

    def whole(*shape):
        return pl.BlockSpec(shape, lambda i, one, two: (0, 0))

    def piece(arrays, size, at):
        return [
            pl.BlockSpec((*array.shape[:2], size), lambda i, one, two: (0, 0, at(i)))
            for array in arrays
        ]

    pair = jax.ShapeDtypeStruct((tokens, width), bf16)
    return pl.pallas_call(
        functools.partial(feed_kernel, firsts=len(first), seconds=len(second), axes=axes),
        name="feed",
        grid_spec=pltpu.PrefetchScalarGridSpec(
            num_scalar_prefetch=2,
            grid=(count,),
            in_specs=[whole(tokens, width)] * 4
            + piece(second, step, lambda i: i)
            + piece(second, step, lambda i: count + i)
            + piece(first, step, lambda i: start + i)
            + piece(second, rest, lambda i: 2 * count * step // rest),
            out_specs=[whole(tokens, width)] * 3 + [whole(width, columns)],
            scratch_shapes=[
                pltpu.VMEM((tokens, width), bf16),
                pltpu.VMEM((width, tokens), bf16),
                pltpu.VMEM((width, tokens), bf16),
                pltpu.VMEM((tokens, width), f32),
                pltpu.VMEM((tokens, width), f32),
                pltpu.VMEM((width, step), bf16),
                pltpu.VMEM((width, step), bf16),
                pltpu.VMEM((width, step), bf16),
                pltpu.VMEM((width, rest), bf16),
            ],
        ),
        out_shape=[
            jax.ShapeDtypeStruct((tokens, width), f32),
            pair,
            pair,
            jax.ShapeDtypeStruct((width, columns), bf16),
        ],
        compiler_params=pltpu.CompilerParams(vmem_limit_bytes=VMEM),
        cost_estimate=cost(2 * 9 * 2 * tokens * width * count * step, 24 << 20),
    )(first_order, second_order, x, ours, theirs, g, *second, *second, *first, *second)


def middle_back_kernel(
    core_ref, order_ref, line_ref, residual_ref, g_ref, ours_ref, theirs_ref, attn_ref,
    attended_ref, out_ours_ref, out_theirs_ref, layer_ref, residual_grad_ref, *rest, axes,
):
    planes, lines, wide, beside = axes
    dout_refs, grads_refs, (dout_all, grads_all) = rest[: -2 - lines], rest[-2 - lines : -2], rest[-2:]
    rows = layer_ref.shape[0]
    half = attn_ref.shape[0]
    own = pl.ds(pl.multiple_of(core_ref[0] * rows, rows), rows)
    layer_ref[...] = (
        residual_ref[own, :]
        + out_ours_ref[own, :].astype(f32)
        + out_theirs_ref[...].astype(f32)
    ).astype(bf16)
    unit, inverse = unit_rows(residual_ref[...])
    scaled = ours_ref[...].astype(f32) + theirs_ref[...].astype(f32)
    grad = g_ref[...].astype(f32) + unit_back(scaled, unit, inverse)
    low = grad.astype(bf16)
    residual_grad_ref[...] = grad
    dout_all[...] = dot(attn_ref[...], low, 1, 1).astype(bf16)
    for at, dout_ref in enumerate(dout_refs):
        dout_ref[...] = dout_all[pl.ds(pl.multiple_of(order_ref[at] * HDIM, HDIM), HDIM)]
    grads_all[...] = dot(attended_ref[...], low)
    few = HDIM // wide // beside
    for shift, grads_ref in enumerate(grads_refs):
        line = (line_ref[0] + shift) % lines
        blocks = [
            grads_all[pl.ds(pl.multiple_of((plane * lines + line) * HDIM, HDIM), HDIM)]
            for plane in range(planes)
        ]
        pieces = []
        for far in range(wide):
            for plane in range(planes):
                for near in range(beside):
                    start = (far * beside + near) * few
                    piece = blocks[plane][start : start + few]
                    pieces += [piece[:, :half], piece[:, half:]]
        grads_ref[...] = jnp.concatenate(pieces, axis=0).astype(bf16)


def middle_back(
    core, order, line, residual, g, ours, theirs, attn, attended, out_ours, out_theirs, axes
):
    tokens, width = residual.shape
    rows = tokens // 2
    half = width // 2
    chips = half // HDIM
    lines = axes[1]

    def whole(*shape):
        return pl.BlockSpec(shape, lambda i, core, order, line: (0,) * len(shape))

    return pl.pallas_call(
        functools.partial(middle_back_kernel, axes=axes),
        name="middle_back",
        grid_spec=pltpu.PrefetchScalarGridSpec(
            num_scalar_prefetch=3,
            grid=(1,),
            in_specs=[whole(tokens, width)] * 4
            + [whole(half, width), whole(half, tokens), whole(tokens, width), whole(rows, width)],
            out_specs=[whole(rows, width), whole(tokens, width)]
            + [whole(HDIM, tokens)] * chips
            + [whole(width // lines, half)] * lines,
            scratch_shapes=[pltpu.VMEM((half, tokens), bf16), pltpu.VMEM((half, width), f32)],
        ),
        out_shape=[
            jax.ShapeDtypeStruct((rows, width), bf16),
            jax.ShapeDtypeStruct((tokens, width), f32),
        ]
        + [jax.ShapeDtypeStruct((HDIM, tokens), bf16)] * chips
        + [jax.ShapeDtypeStruct((width // lines, half), bf16)] * lines,
        compiler_params=pltpu.CompilerParams(vmem_limit_bytes=VMEM),
        cost_estimate=cost(2 * 2 * 2 * tokens * width * half, 16 << 20),
    )(core, order, line, residual, g, ours, theirs, attn, attended, out_ours, out_theirs)


def hidden_back_kernel(order_ref, core_ref, shard_ref, w_ref, *rest):
    dp_refs, (own_ref, other_ref, stacked) = rest[:-3], rest[-3:]
    for place, dp_ref in enumerate(dp_refs):
        size = dp_ref.shape[0]
        stacked[pl.ds(pl.multiple_of(order_ref[place] * size, 64), size)] = dp_ref[...]
    rows = own_ref.shape[0]
    zero = core_ref[0] == 0
    size = w_ref.shape[1]
    for at in range(w_ref.shape[0]):
        flat = dot(w_ref[at], stacked[...])
        first = flat[:, :rows].T
        second = flat[:, rows:].T
        columns = pl.ds(pl.multiple_of(shard_ref[at] * size, size), size)
        own_ref[:, columns] = jnp.where(zero, first, second)
        other_ref[:, columns] = jnp.where(zero, second, first).astype(bf16)


def hidden_back(order, core, shard_order, weights, pieces):
    shards, size, columns = weights.shape
    width = shards * size
    rows = pieces[0].shape[1] // 2

    def whole(*shape):
        return pl.BlockSpec(shape, lambda i, order, core, shard: (0,) * len(shape))

    return pl.pallas_call(
        hidden_back_kernel,
        name="hidden_back",
        grid_spec=pltpu.PrefetchScalarGridSpec(
            num_scalar_prefetch=3,
            grid=(1,),
            in_specs=[whole(shards, size, columns)] + [whole(*pieces[0].shape)] * len(pieces),
            out_specs=[whole(rows, width)] * 2,
            scratch_shapes=[pltpu.VMEM((columns, 2 * rows), bf16)],
        ),
        out_shape=[
            jax.ShapeDtypeStruct((rows, width), f32),
            jax.ShapeDtypeStruct((rows, width), bf16),
        ],
        compiler_params=pltpu.CompilerParams(vmem_limit_bytes=VMEM),
        cost_estimate=cost(2 * 2 * 2 * rows * width * columns, 8 << 20),
    )(order, core, shard_order, weights, *pieces)


def head_grad_kernel(order_ref, owner_ref, unit_ref, *rest, owners):
    dp_refs, out_refs, out_all = rest[: -1 - owners], rest[-1 - owners : -1], rest[-1]
    block = dp_refs[0].shape[1]
    total = None
    for place, dp_ref in enumerate(dp_refs):
        rows = pl.ds(pl.multiple_of(order_ref[place] * block, block), block)
        added = dot(dp_ref[...], unit_ref[rows])
        total = added if total is None else total + added
    for at in range(owners):
        out_all[at] = total[:, at * 128 : (at + 1) * 128].astype(bf16)
    for at, out_ref in enumerate(out_refs):
        out_ref[...] = out_all[owner_ref[at]]


def head_grad(order, owner_order, unit_all, pieces):
    length, width = unit_all.shape
    owners = width // 128
    size = pieces[0].shape[0]

    def whole(*shape):
        return pl.BlockSpec(shape, lambda i, order, owner: (0,) * len(shape))

    return pl.pallas_call(
        functools.partial(head_grad_kernel, owners=owners),
        name="head_grad",
        grid_spec=pltpu.PrefetchScalarGridSpec(
            num_scalar_prefetch=2,
            grid=(1,),
            in_specs=[whole(length, width)] + [whole(*pieces[0].shape)] * len(pieces),
            out_specs=[whole(size, 128)] * owners,
            scratch_shapes=[pltpu.VMEM((owners, size, 128), bf16)],
        ),
        out_shape=[jax.ShapeDtypeStruct((size, 128), bf16)] * owners,
        compiler_params=pltpu.CompilerParams(vmem_limit_bytes=VMEM),
        cost_estimate=cost(2 * 2 * length * width * size, 10 << 20),
    )(order, owner_order, unit_all, *pieces)


def adam_in_kernels(weight, gradient, first, second, rate):
    first = BETA_FIRST * first + (1.0 - BETA_FIRST) * gradient
    second = BETA_SECOND * second + (1.0 - BETA_SECOND) * gradient * gradient
    second_hat = second * (1.0 / (1.0 - BETA_SECOND**STEP))
    bottom = second_hat * lax.rsqrt(second_hat) + EPSILON
    guess = pl.reciprocal(bottom, approx=True)
    guess = guess * (2.0 - bottom * guess)
    scale = rate / (1.0 - BETA_FIRST**STEP)
    weight = weight * (1.0 - rate * DECAY) - (scale * first) * guess
    return (weight, first, second)


def adam_into(refs, weight, gradient, first, second, rate):
    for ref, value in zip(refs, adam_in_kernels(weight, gradient, first, second, rate)):
        ref[...] = value


def rounded_in_kernel(values):
    return values.astype(bf16).astype(f32)


def adam_most_kernel(grads_ref, gain_ref, other_gain_ref, *refs, rates):
    (w_in, m_in, v_in), attn, out, gains = refs[:3], refs[3:6], refs[6:9], refs[9:12]
    new_in, new_attn, new_out, new_gains = refs[12:15], refs[15:18], refs[18:21], refs[21:24]
    gain_grad, turned = refs[24:]
    here = pl.program_id(0)
    chips = grads_ref.shape[0] // 2
    width = w_in.shape[1] // 2
    main = width // 256 * 128
    few = width // 2 - main

    @pl.when(here == 0)
    def _():
        for core in range(2):
            columns = jnp.concatenate(
                [grads_ref[2 * chip + core, :, 2 * main : 3 * main] for chip in range(chips)],
                axis=0,
            )
            turned[core * main : (core + 1) * main] = columns.astype(f32).T
            rest = jnp.concatenate(
                [
                    grads_ref[2 * chip + core, :, 3 * main : 3 * main + 128]
                    for chip in range(chips)
                ],
                axis=0,
            )
            start = 2 * main + core * few
            turned[start : start + few] = rest.astype(f32).T[2 * few : 3 * few]

    each = grads_ref.shape[1]
    some = w_in.shape[0] // each
    for at_chip in range(some):
        source = 2 * (here * some + at_chip)
        columns = []
        for at in range(2):
            for core in range(2):
                place = at * main
                columns.append(grads_ref[source + core, :, place : place + main].astype(f32))
            for core in range(2):
                rest = grads_ref[source + core, :, 3 * main : 3 * main + 128].astype(f32)
                columns.append(rest[:, at * few : (at + 1) * few])
        grads = jnp.concatenate(columns, axis=1)
        rows = slice(at_chip * each, (at_chip + 1) * each)
        weight = w_in[rows]
        gain_rows = pl.ds(pl.multiple_of((here * some + at_chip) * each, each), each)
        gain_grad[gain_rows] = jnp.sum(
            grads * rounded_in_kernel(weight), axis=1, keepdims=True
        )
        values = adam_in_kernels(
            weight, grads * gain_ref[rows], m_in[rows], v_in[rows], rates[0]
        )
        for ref, value in zip(new_in, values):
            ref[rows] = value
        rows = slice(at_chip * each // 2, (at_chip + 1) * each // 2)
        for core in range(2):
            piece = grads_ref[source + core, :, 3 * main + 128 :].astype(f32)
            grads = jnp.concatenate([piece[: each // 2], piece[each // 2 :]], axis=1)
            values = adam_in_kernels(
                attn[0][core, rows], grads, attn[1][core, rows], attn[2][core, rows], rates[1]
            )
            for ref, value in zip(new_attn, values):
                ref[core, rows] = value

    size = out[0].shape[0]
    grads = turned[pl.ds(pl.multiple_of(here * size, 8), size)]
    adam_into(new_out, out[0][...], grads, out[1][...], out[2][...], rates[2])

    @pl.when(here == pl.num_programs(0) - 1)
    def _():
        both = jnp.concatenate(
            [other_gain_ref[...], gain_grad[...], jnp.zeros((gain_grad.shape[0], 6), f32)], axis=1
        )
        adam_into(
            new_gains, gains[0][...], both.T[:2], gains[1][...], gains[2][...], GAIN_RATE
        )


def adam_most(
    grads, gain, other_gain, weights_in, weights_attn, weights_out, gains, rates, steps=2
):
    rows, columns = weights_in[0].shape
    width = weights_attn[0].shape[1]
    hidden = weights_out[0].shape[0]
    weights_attn = [array.reshape(2, rows // 2, width) for array in weights_attn]
    block_in = pl.BlockSpec((rows // steps, columns), lambda i: (i, 0))
    block_attn = pl.BlockSpec((2, rows // 2 // steps, width), lambda i: (0, i, 0))
    block_out = pl.BlockSpec((hidden // steps, rows), lambda i: (i, 0))
    column = pl.BlockSpec((rows // steps, 1), lambda i: (i, 0))
    whole_column = pl.BlockSpec((rows, 1), lambda i: (0, 0))
    block_gains = pl.BlockSpec(gains[0].shape, lambda i: (0, 0))
    blocks = [block_in] * 3 + [block_attn] * 3 + [block_out] * 3 + [block_gains] * 3
    arrays = (*weights_in, *weights_attn, *weights_out, *gains)
    results = pl.pallas_call(
        functools.partial(adam_most_kernel, rates=rates),
        name="adam_most",
        grid=(steps,),
        in_specs=[pl.BlockSpec(grads.shape, lambda i: (0, 0, 0)), column, whole_column] + blocks,
        out_specs=blocks,
        out_shape=[jax.ShapeDtypeStruct(array.shape, f32) for array in arrays],
        scratch_shapes=[pltpu.VMEM((rows, 1), f32), pltpu.VMEM((hidden, rows), f32)],
        compiler_params=pltpu.CompilerParams(vmem_limit_bytes=VMEM),
        cost_estimate=cost(rows * columns * 20, rows * columns * 26),
    )(grads, gain, other_gain, *arrays)
    new_attn = [array.reshape(rows, width) for array in results[3:6]]
    return results[:3], new_attn, results[6:9], results[9:]


def adam_qkv_kernel(order_ref, *refs, rate):
    grads_refs, (gain_ref, w_ref, m_ref, v_ref, new_w, new_m, new_v, gain_grad, joined) = (
        refs[:-9], refs[-9:]
    )
    here = pl.program_id(0)
    heads = sum(grads_ref.shape[0] for grads_ref in grads_refs)

    @pl.when(here == 0)
    def _():
        at = 0
        for grads_ref in grads_refs:
            for place in range(grads_ref.shape[0]):
                for part in range(3):
                    row = (part * heads + order_ref[at]) * HDIM
                    joined[pl.ds(pl.multiple_of(row, HDIM), HDIM)] = grads_ref[
                        place, part * HDIM : (part + 1) * HDIM
                    ].astype(f32)
                at += 1

    size = w_ref.shape[1]
    grads = joined[pl.ds(pl.multiple_of(here * size, size), size)].T
    weight = w_ref[...]
    added = jnp.sum(grads * rounded_in_kernel(weight), axis=1, keepdims=True)
    gain_grad[...] = added + jnp.where(here == 0, 0.0, gain_grad[...])
    adam_into(
        (new_w, new_m, new_v), weight, grads * gain_ref[...], m_ref[...], v_ref[...], rate
    )


def adam_qkv(order, grads, gain, weight, first, second, rate, step=1536):
    rows, columns = weight.shape
    block = pl.BlockSpec((rows, step), lambda i, order: (0, i))
    column = pl.BlockSpec((rows, 1), lambda i, order: (0, 0))
    same = jax.ShapeDtypeStruct((rows, columns), f32)
    return pl.pallas_call(
        functools.partial(adam_qkv_kernel, rate=rate),
        name="adam_qkv",
        grid_spec=pltpu.PrefetchScalarGridSpec(
            num_scalar_prefetch=1,
            grid=(columns // step,),
            in_specs=[pl.BlockSpec(piece.shape, lambda i, order: (0, 0, 0)) for piece in grads]
            + [column]
            + [block] * 3,
            out_specs=[block] * 3 + [column],
            scratch_shapes=[pltpu.VMEM((columns, rows), f32)],
        ),
        out_shape=[same] * 3 + [jax.ShapeDtypeStruct((rows, 1), f32)],
        compiler_params=pltpu.CompilerParams(vmem_limit_bytes=VMEM),
        cost_estimate=cost(rows * columns * 20, rows * columns * 26),
    )(order, *grads, gain, weight, first, second)


def ring(axis, shift):
    size = lax.axis_size(axis)
    return [(at, (at + shift) % size) for at in range(size)]


def along(axis, array):
    return [array] + [
        lax.ppermute(array, axis, ring(axis, shift)) for shift in range(1, lax.axis_size(axis))
    ]


def shards(
    tokens,
    positions,
    cotangent,
    weight_qkv,
    weight_attn,
    weight_in,
    weight_out,
    norm_gains,
    first_qkv,
    first_attn,
    first_in,
    first_out,
    first_gains,
    second_qkv,
    second_attn,
    second_in,
    second_out,
    second_gains,
):
    rows, width = tokens.shape[1:]
    shard_rows = weight_qkv.shape[1]
    heads = width // HDIM
    hidden = weight_out.shape[1]
    core = lax.axis_index("c")
    mine = lax.axis_index(CTX)
    chip = lax.axis_index(CHIPS)
    chips = lax.axis_size(CHIPS)
    owners = lax.axis_size(FSDP)
    length = rows * chips * 2
    main = hidden // 256 * 128
    few = hidden // 2 - main
    core_at = core.reshape(1).astype(jnp.int32)
    axes = (lax.axis_size("zh"), lax.axis_size("y"), lax.axis_size("x"), lax.axis_size("zl"))
    offsets = [(far, near) for far in range(lax.axis_size("x")) for near in range(2)]
    across, beside = lax.axis_index("x"), lax.axis_index("zl")
    wide = lax.axis_size("x")

    def chips_at(sign):
        places = [(across + sign * far) % wide * 2 + (beside ^ near) for far, near in offsets]
        return jnp.stack(places).astype(jnp.int32)

    local = tokens[0]
    extra = 16
    high, low = positions[0] // 128, positions[0] % 128
    places_row = jnp.concatenate([high, low, jnp.zeros((width - 2 * rows,), jnp.int32)])
    places_rows = jnp.concatenate(
        [places_row[None], jnp.zeros((extra - 1, width), jnp.int32)], axis=0
    ).astype(bf16)
    sequence = lax.all_gather(
        jnp.concatenate([local, places_rows], axis=0), CTX, axis=0, tiled=True
    )
    first_part, second_part, head_part, half_heads = prepare(
        jnp.stack([core, chip]).astype(jnp.int32),
        norm_gains[0],
        weight_qkv[0],
        weight_attn[0],
        weight_in[0],
        weight_out[0],
    )
    second_joined = jnp.stack(along("y", second_part))
    head_weights = lax.all_to_all(
        jnp.broadcast_to(head_part, (owners, *head_part.shape)), FSDP, 0, 0, tiled=True
    )
    sequence, first_part, second_joined, half_heads, _ = lax.optimization_barrier(
        (sequence, first_part, second_joined, half_heads, head_weights)
    )
    one_shard = lax.dynamic_slice_in_dim(second_joined, across, 1, 0)
    one_shard = lax.ppermute(one_shard, "zh", SWAP)
    first_other = lax.ppermute(first_part, "zh", SWAP)
    half_heads_other = lax.ppermute(half_heads, "zh", SWAP)
    lines = lax.axis_size("y")
    plane, line = lax.axis_index("zh"), lax.axis_index("y")

    def owner(far, shift):
        return (plane ^ far) * lines + (line - shift) % lines

    first_order = jnp.stack([(plane ^ far) * lines + at for at in range(lines) for far in range(2)])
    second_order = jnp.stack(
        [owner(0, shift) for shift in range(lines)]
        + [owner(1, (across - shift) % wide) for shift in range(wide)]
    )
    first_order, second_order = first_order.astype(jnp.int32), second_order.astype(jnp.int32)

    def in_order(ours, theirs):
        first = jnp.where(core == 0, ours, theirs)
        second = jnp.where(core == 0, theirs, ours)
        return jnp.concatenate([first, second], axis=0)

    def swap(array):
        return lax.ppermute(array, "c", SWAP)

    gradient = in_order(cotangent[0], swap(cotangent[0]))

    freqs = jnp.exp(jnp.arange(HDIM // 2, dtype=f32) * (-2.0 * math.log(ROPE_BASE) / HDIM))
    by_device = sequence.reshape(2 * chips, rows + extra, width)[:, rows]
    by_device = by_device.astype(f32)
    places = by_device[:, :rows] * 128.0 + by_device[:, rows : 2 * rows]
    angles = freqs[:, None] * places.reshape(1, length)
    cosine = jnp.cos(angles)
    sine = jnp.sin(angles)
    unit_all, qkv, keys, values = project(sequence, head_weights, cosine, sine, extra)
    keys, one_shard, first_other, half_heads_other = lax.optimization_barrier(
        (keys, one_shard, first_other, half_heads_other)
    )
    second_pieces = [second_joined, *along("x", one_shard)]
    first_pieces = [
        lax.all_gather(jnp.stack([first_part, first_other]), "y", axis=0, tiled=True)
    ]
    low_out, out, lse = attend(keys, qkv, chips)
    heads_pair, low_out, *second_pieces = lax.optimization_barrier(
        (jnp.stack([half_heads, half_heads_other]), low_out, *second_pieces)
    )
    mat_qkv = lax.all_gather(heads_pair, "y", axis=0, tiled=True)
    attended = lax.all_to_all(low_out, CHIPS, 0, 0, tiled=True)
    attended = attended.reshape(heads // 2 * HDIM, 2 * rows)
    mixed, mat_attn = attend_out(first_order, attended, first_pieces)
    current = lax.dynamic_slice_in_dim(
        sequence, chip * 2 * (rows + extra), 2 * (rows + extra), 0
    ).reshape(2, rows + extra, width)[:, :rows].reshape(2 * rows, width)
    residual, partial, back, grads = feed(
        first_order, second_order, current, mixed, swap(mixed), gradient, first_pieces,
        second_pieces, axes,
    )
    grads, mat_qkv = lax.optimization_barrier((grads, mat_qkv))
    first_sum = lax.psum_scatter(grads, "y", scatter_dimension=0, tiled=True)

    def move(pieces, sign):
        moved = [pieces[0]]
        for (far, near), piece in list(zip(offsets, pieces))[1:]:
            pairs = [
                (at, (at // 2 + sign * far) % wide * 2 + (at % 2 ^ near)) for at in range(chips)
            ]
            moved.append(lax.ppermute(piece, CHIPS, pairs))
        return moved

    ahead, behind = chips_at(1), chips_at(-1)
    theirs = swap(lax.dynamic_slice_in_dim(partial, (1 - core) * rows, rows, 0))
    layer_out, residual_grad, *pieces = middle_back(
        core_at, ahead, line.reshape(1).astype(jnp.int32), residual, gradient, back, swap(back),
        mat_attn, attended, partial, theirs, axes,
    )
    dout_pieces, attn_pieces = pieces[:chips], pieces[chips:]

    douts = move(dout_pieces, 1)
    attn_arrived = attn_pieces[:1] + [
        lax.ppermute(piece, "y", ring("y", shift))
        for shift, piece in list(enumerate(attn_pieces))[1:]
    ]
    pieces = attend_back(behind, keys, values, qkv, douts, out, lse, cosine, sine)
    rest = lax.optimization_barrier((*pieces, *attn_arrived))
    pieces, attn_arrived = rest[:chips], rest[chips:]
    owner_places = [(far, shift) for far in range(2) for shift in range(lines)]
    owner_order = jnp.stack(
        [(plane ^ far) * lines + (line + shift) % lines for far, shift in owner_places]
    ).astype(jnp.int32)
    head_parts = head_grad(behind, owner_order, unit_all, pieces)

    def total(arrays):
        return sum(array.astype(f32) for array in arrays).astype(bf16)

    first_sum, *head_parts = lax.optimization_barrier((first_sum, *head_parts))
    first_sum = jnp.concatenate([first_sum, total(attn_arrived)], axis=1)
    first_sum, *pieces = lax.optimization_barrier((first_sum, *pieces))
    arrived = lax.all_to_all(first_sum, ("x", "zh", "zl"), 0, 0, tiled=True)
    moved = move(pieces, -1)
    own_hidden, other_hidden = hidden_back(ahead, core_at, first_order, mat_qkv, moved)
    grad_hidden = own_hidden + swap(other_hidden).astype(f32)
    unit_in, scale_in = unit_rows(local.astype(f32))
    own_residual = lax.dynamic_slice_in_dim(residual_grad, core * rows, rows, 0)
    tokens_grad = (own_residual + unit_back(grad_hidden, unit_in, scale_in))[None]

    head_arrived = [head_parts[0]]
    for (far, shift), piece in list(zip(owner_places, head_parts))[1:]:
        pairs = [
            (at, (at // lines ^ far) * lines + (at % lines + shift) % lines) for at in range(owners)
        ]
        head_arrived.append(lax.ppermute(piece, FSDP, pairs))
    head_own = total(head_arrived)[None]
    arrived, head_own = lax.optimization_barrier((arrived, head_own))
    head_arrived = [head_parts[0]]
    for (far, shift), piece in list(zip(owner_places, head_parts))[1:]:
        pairs = [
            (at, (at // lines ^ far) * lines + (at % lines + shift) % lines) for at in range(owners)
        ]
        head_arrived.append(lax.ppermute(piece, FSDP, pairs))
    head_own = total(head_arrived)[None]
    arrived = arrived.reshape(2 * chips, shard_rows // chips, -1)
    second_sum = jnp.sum(arrived.astype(f32), axis=0).astype(bf16)
    all_grads = lax.all_gather(second_sum, CTX, axis=0, tiled=False)

    head_pair = jnp.concatenate([head_own, swap(head_own)], axis=0)
    head_four = jnp.concatenate([head_pair, lax.ppermute(head_pair, "zl", SWAP)], axis=0)
    head_grads = [head_four] + [
        lax.ppermute(head_four, "x", ring("x", shift)) for shift in range(1, wide)
    ]
    head_order = jnp.stack(
        [
            (across - shift) % wide * 4 + (beside ^ near) * 2 + (core ^ other)
            for shift in range(wide)
            for near in range(2)
            for other in range(2)
        ]
    ).astype(jnp.int32)

    rates = (
        width ** (-0.5),
        max(1, 3 * width // length) ** (-0.5),
        width ** (-0.5),
        hidden ** (-0.5),
    )
    columns_of_gains = norm_gains[0].astype(bf16).astype(f32).T
    *new_qkv, gain_first = adam_qkv(
        head_order, head_grads, columns_of_gains[:, :1], weight_qkv[0], first_qkv[0], second_qkv[0], rates[0]
    )
    new_in, new_attn, new_out, new_gains = adam_most(
        all_grads,
        columns_of_gains[:, 1:],
        gain_first,
        (weight_in[0], first_in[0], second_in[0]),
        (weight_attn[0], first_attn[0], second_attn[0]),
        (weight_out[0], first_out[0], second_out[0]),
        (norm_gains[0], first_gains[0], second_gains[0]),
        (rates[2], rates[1], rates[3]),
    )
    updated = (new_qkv, new_attn, new_in, new_out, new_gains)
    return (
        layer_out[None],
        tokens_grad,
        *[updated[member][0][None] for member in range(5)],
        *[updated[member][1][None] for member in range(5)],
        *[updated[member][2][None] for member in range(5)],
    )


def solution(mesh):
    split = Mesh(mesh.devices.reshape(4, 2, 2, 2, 4), ("x", "zl", "c", "zh", "y"))
    by_row = P(None, FSDP, None)
    by_column = P(None, None, FSDP)
    weights = (by_row, by_row, by_row, by_column, by_column)
    by_token = P(FSDP, CTX, None)
    return jax.shard_map(
        shards,
        mesh=split,
        in_specs=(by_token, P(FSDP, CTX), by_token) + weights * 3,
        out_specs=(by_token, by_token) + weights * 3,
        check_vma=False,
    )
```

```python
import functools
import math

import jax
import jax.numpy as jnp
from jax import lax
from jax.experimental import pallas as pl
from jax.experimental.pallas import tpu as pltpu
from jax.sharding import Mesh, PartitionSpec as P

HDIM = 64
STEP = 10
BETA_FIRST = 0.5
BETA_SECOND = 0.5
EPSILON = 1e-08
DECAY = 0.01
NORM_EPS = 1e-05
ROPE_BASE = 160000.0
GAIN_RATE = 0.6
LOG2E = math.log2(math.e)
f32 = jnp.float32
bf16 = jnp.bfloat16

CHIPS = ("x", "zl")
CTX = ("x", "zl", "c")
FSDP = ("zh", "y")
SWAP = [(0, 1), (1, 0)]
VMEM = 60 << 20


def dot(left, right, left_dim=1, right_dim=0):
    return lax.dot_general(
        left, right, (((left_dim,), (right_dim,)), ((), ())), preferred_element_type=f32
    )


def cost(flops, moved):
    return pl.CostEstimate(flops=flops, bytes_accessed=moved, transcendentals=0)


def unit_rows(values):
    average = jnp.mean(values, axis=-1, keepdims=True)
    centered = values - average
    spread = jnp.mean(centered * centered, axis=-1, keepdims=True)
    inverse = lax.rsqrt(spread + NORM_EPS)
    return centered * inverse, inverse


def unit_back(scaled, unit, inverse):
    first_mean = jnp.mean(scaled, axis=-1, keepdims=True)
    second_mean = jnp.mean(scaled * unit, axis=-1, keepdims=True)
    return inverse * (scaled - first_mean - unit * second_mean)


def prepare_kernel(
    place_ref, gains_ref, qkv_ref, attn_ref, in_ref, out_ref,
    first_ref, second_ref, head_ref, heads_ref,
):
    core, chip = place_ref[0], place_ref[1]
    rows = qkv_ref.shape[0]
    width = attn_ref.shape[1]
    hidden = out_ref.shape[0]
    main = hidden // 256 * 128
    few = hidden // 2 - main
    half = width // 2
    low_gains = gains_ref[...].astype(bf16).astype(f32)
    columns = jnp.concatenate([low_gains, jnp.zeros((6, rows), f32)], axis=0).T
    gain_first, gain_second = columns[:, 0:1], columns[:, 1:2]

    def pick(array):
        size = array.shape[1] // 2
        return jnp.where(core == 0, array[:, :size], array[:, size:])

    def scaled(values, gain):
        return (values.astype(bf16).astype(f32) * gain).astype(bf16)

    attn_rows = attn_ref[pl.ds(pl.multiple_of(core * HDIM, HDIM), HDIM)].astype(bf16)
    first_ref[:HDIM, :half] = attn_rows[:, :half]
    first_ref[HDIM:, :half] = attn_rows[:, half:]
    first_ref[:, half : half + main] = scaled(pick(in_ref[:, : 2 * main]), gain_second)
    first_ref[:, half + main :] = scaled(pick(in_ref[:, hidden : hidden + 2 * main]), gain_second)
    out_rows = out_ref[pl.ds(pl.multiple_of(core * main, 128), main)]
    second_ref[:, :main] = out_rows.T.astype(bf16)
    odd_out = out_ref[2 * main :].T
    odd = [
        scaled(pick(in_ref[:, 2 * main : hidden]), gain_second),
        scaled(pick(in_ref[:, hidden + 2 * main :]), gain_second),
        pick(odd_out).astype(bf16),
        jnp.zeros((rows, few), bf16),
    ]
    second_ref[:, main:] = jnp.concatenate(odd, axis=1)
    pieces = []
    for at in range(width // 128):
        for part in range(3):
            start = part * width + at * 128
            pieces.append(scaled(pick(qkv_ref[:, start : start + 128]), gain_first))
    heads_ref[...] = jnp.concatenate(pieces, axis=1)
    own = []
    for part in range(3):
        start = pl.multiple_of(part * width + chip * 128, 128)
        own.append(scaled(pick(qkv_ref[:, pl.ds(start, 128)]), gain_first).astype(f32))
    own.append(jnp.zeros((rows, HDIM), f32))
    head_ref[...] = jnp.concatenate(own, axis=1).T[: 3 * HDIM].astype(bf16)


def prepare(place, gains, qkv, attn, weight_in, weight_out):
    rows, width = attn.shape
    hidden = weight_out.shape[0]
    main = hidden // 256 * 128
    arrays = (gains, qkv, attn, weight_in, weight_out)
    shapes = [
        (rows, width // 2 + 2 * main),
        (rows, main + 4 * (hidden // 2 - main)),
        (3 * HDIM, rows),
        (rows, 3 * width // 2),
    ]

    def whole(shape):
        return pl.BlockSpec(shape, lambda i, place: (0, 0))

    return pl.pallas_call(
        prepare_kernel,
        name="prepare",
        grid_spec=pltpu.PrefetchScalarGridSpec(
            num_scalar_prefetch=1,
            grid=(1,),
            in_specs=[whole(array.shape) for array in arrays],
            out_specs=[whole(shape) for shape in shapes],
        ),
        out_shape=[jax.ShapeDtypeStruct(shape, bf16) for shape in shapes],
        compiler_params=pltpu.CompilerParams(vmem_limit_bytes=VMEM),
        cost_estimate=cost(rows * width * 60, 10 << 20),
    )(place, *arrays)


def project_kernel(
    x_ref, w_ref, cos_ref, sin_ref, unit_ref, qkv_ref, keys_ref, values_ref, w_all, *, extra
):
    half = HDIM // 2
    rows = cos_ref.shape[1]

    @pl.when(pl.program_id(0) == 0)
    def _():
        for part in range(w_ref.shape[0]):
            w_all[part * 128 : (part + 1) * 128] = w_ref[part].astype(f32).T.astype(bf16)

    count = (x_ref.shape[0] - rows) // extra
    each = rows // count
    for at in range(count):
        tokens = x_ref[at * (each + extra) : at * (each + extra) + each].astype(f32)
        unit_ref[at * each : (at + 1) * each] = unit_rows(tokens)[0].astype(bf16)
    unit = unit_ref[...]
    mixed = dot(unit, w_all[...]).T
    cosine = cos_ref[...]
    sine = sin_ref[...]

    def turn(one, two):
        return jnp.concatenate([one * cosine - two * sine, two * cosine + one * sine], axis=0)

    queries = turn(mixed[:half], mixed[half:HDIM])
    keys = turn(mixed[HDIM : HDIM + half], mixed[HDIM + half : 2 * HDIM])
    values = mixed[2 * HDIM :]
    qkv_ref[...] = jnp.concatenate([queries, keys, values], axis=0).astype(bf16)
    key_rows = keys.T.astype(bf16)
    value_rows = values.T.astype(bf16)
    ones = jnp.where(lax.broadcasted_iota(jnp.int32, (rows, HDIM), 1) < 3, 1.0, 0.0).astype(bf16)
    keys_ref[...] = jnp.concatenate([key_rows, key_rows, key_rows, ones], axis=1)
    values_ref[...] = jnp.concatenate([value_rows, ones], axis=1)


def project(tokens, weights, cosine, sine, extra, block=1024):
    width = tokens.shape[1]
    length = cosine.shape[1]
    steps = length // block
    return pl.pallas_call(
        functools.partial(project_kernel, extra=extra),
        name="project",
        grid=(steps,),
        in_specs=[
            pl.BlockSpec((tokens.shape[0] // steps, width), lambda i: (i, 0)),
            pl.BlockSpec(weights.shape, lambda i: (0, 0, 0)),
            pl.BlockSpec((HDIM // 2, block), lambda i: (0, i)),
            pl.BlockSpec((HDIM // 2, block), lambda i: (0, i)),
        ],
        out_specs=[
            pl.BlockSpec((block, width), lambda i: (i, 0)),
            pl.BlockSpec((3 * HDIM, block), lambda i: (0, i)),
            pl.BlockSpec((block, 256), lambda i: (i, 0)),
            pl.BlockSpec((block, 128), lambda i: (i, 0)),
        ],
        out_shape=[
            jax.ShapeDtypeStruct((length, width), bf16),
            jax.ShapeDtypeStruct((3 * HDIM, length), bf16),
            jax.ShapeDtypeStruct((length, 256), bf16),
            jax.ShapeDtypeStruct((length, 128), bf16),
        ],
        scratch_shapes=[pltpu.VMEM((width, 3 * HDIM), bf16)],
        compiler_params=pltpu.CompilerParams(vmem_limit_bytes=VMEM),
        cost_estimate=cost(length * width, 1 << 20),
    )(tokens, weights, cosine, sine)


def scaled_queries(queries):
    scaled = queries.astype(f32) * (LOG2E / math.sqrt(HDIM))
    high = scaled.astype(bf16)
    rest = scaled - high.astype(f32)
    middle = rest.astype(bf16)
    low = (rest - middle.astype(f32)).astype(bf16)
    return high, middle, low


def minus_in_three(values):
    rows = values.shape[1]
    at = lax.broadcasted_iota(jnp.int32, (16, rows), 0)
    high = (-values).astype(bf16).astype(f32)
    rest = -values - high
    middle = rest.astype(bf16).astype(f32)
    low = rest - middle
    stacked = jnp.where(at == 0, high, jnp.where(at == 1, middle, jnp.where(at == 2, low, 0.0)))
    return stacked.astype(bf16)


def attend_kernel(
    keys_ref, q_ref, k_ref, v_ref, low_ref, out_ref, lse_ref, v_ones, longest, *, part
):
    length = keys_ref.shape[0]
    count = length // part

    @pl.when(pl.program_id(0) == 0)
    def _():
        v_ones[:HDIM] = v_ref[...]
        v_ones[HDIM:] = jnp.where(
            lax.broadcasted_iota(jnp.int32, (16, length), 0) < 1, 1.0, 0.0
        ).astype(bf16)
        squares = jnp.sum(k_ref[...].astype(f32) ** 2, axis=0, keepdims=True)
        longest[...] = jnp.broadcast_to(jnp.max(squares, axis=1, keepdims=True), longest.shape)

    queries = jnp.concatenate(scaled_queries(q_ref[...]), axis=0)

    def finish(total, shift):
        summed = total[HDIM : HDIM + 1]
        result = total[:HDIM] / summed
        out_ref[...] = result
        lse_ref[...] = shift + jnp.log2(summed)
        step = low_ref.shape[2]
        for at in range(low_ref.shape[0]):
            low_ref[at] = result[:, at * step : (at + 1) * step].astype(bf16)
        return summed

    squares = jnp.sum((q_ref[...].astype(f32) * (LOG2E / math.sqrt(HDIM))) ** 2, axis=0, keepdims=True)
    shift = jnp.sqrt(squares * longest[0:1, 0:1])
    shifted = jnp.concatenate([queries, minus_in_three(shift)], axis=0)

    def score(at):
        return dot(keys_ref[at * part : (at + 1) * part, : 3 * HDIM + 16], shifted)

    scores = score(0)
    total = None
    for at in range(count):
        following = score(at + 1) if at + 1 < count else None
        soft = jnp.exp2(scores).astype(bf16)
        added = dot(v_ones[:, at * part : (at + 1) * part], soft)
        total = added if total is None else total + added
        scores = following
    summed = finish(total, shift)

    @pl.when(jnp.min(summed) < 2.0**-60)
    def _():
        def exact(at, carry):
            highest, total = carry
            rows = pl.ds(pl.multiple_of(at * part, part), part)
            scores = dot(keys_ref[rows, : 3 * HDIM], queries)
            raised = jnp.maximum(highest, jnp.max(scores, axis=0, keepdims=True))
            soft = jnp.exp2(scores - raised).astype(bf16)
            added = dot(v_ones[:, rows], soft)
            return raised, total * jnp.exp2(highest - raised) + added

        start = (
            jnp.full((1, q_ref.shape[1]), -1e30, f32),
            jnp.zeros((HDIM + 16, q_ref.shape[1]), f32),
        )
        highest, total = lax.fori_loop(0, count, exact, start)
        finish(total, highest)


def attend(keys, qkv, chips, block=1024, part=512):
    length = keys.shape[0]
    return pl.pallas_call(
        functools.partial(attend_kernel, part=part),
        name="attend",
        grid=(length // block,),
        in_specs=[
            pl.BlockSpec(keys.shape, lambda i: (0, 0)),
            pl.BlockSpec((HDIM, block), lambda i: (0, i)),
            pl.BlockSpec((HDIM, length), lambda i: (1, 0)),
            pl.BlockSpec((HDIM, length), lambda i: (2, 0)),
        ],
        out_specs=[
            pl.BlockSpec((block * chips // length, HDIM, length // chips), lambda i: (i, 0, 0)),
            pl.BlockSpec((HDIM, block), lambda i: (0, i)),
            pl.BlockSpec((1, block), lambda i: (0, i)),
        ],
        out_shape=[
            jax.ShapeDtypeStruct((chips, HDIM, length // chips), bf16),
            jax.ShapeDtypeStruct((HDIM, length), f32),
            jax.ShapeDtypeStruct((1, length), f32),
        ],
        scratch_shapes=[pltpu.VMEM((HDIM + 16, length), bf16), pltpu.VMEM((8, 128), f32)],
        compiler_params=pltpu.CompilerParams(vmem_limit_bytes=VMEM),
        cost_estimate=cost(length * HDIM, 1 << 20),
    )(keys, qkv, qkv, qkv)


def attend_back_kernel(
    order_ref,
    keys_ref,
    values_ref,
    q_ref,
    k_ref,
    out_ref,
    lse_ref,
    cos_ref,
    sin_ref,
    *rest,
    part,
):
    count = (len(rest) - 3) // 2
    dout_refs, dp_refs, (sums, dq_all, dout_all) = rest[:count], rest[count:-3], rest[-3:]
    half = HDIM // 2
    here = pl.program_id(0)
    length = keys_ref.shape[0]
    block = q_ref.shape[1]
    count = length // part
    factor = HDIM ** (-0.5)

    def turn_back(grads, cosine, sine):
        low = grads.astype(bf16).astype(f32)
        one, two = low[:half], low[half:]
        return jnp.concatenate([one * cosine + two * sine, two * cosine - one * sine], axis=0)

    @pl.when(here == 0)
    def _():
        sums[...] = jnp.zeros_like(sums)
        for place, dout_ref in enumerate(dout_refs):
            dout_all[place] = dout_ref[...]

    low_queries = q_ref[...]
    queries = jnp.concatenate(
        [*scaled_queries(low_queries), minus_in_three(lse_ref[...])], axis=0
    )
    low_dout = dout_all[here]
    dout = low_dout.astype(f32)
    centre = jnp.sum(dout * out_ref[...], axis=0, keepdims=True)
    douts = jnp.concatenate([low_dout, minus_in_three(centre)], axis=0)
    blank = jnp.zeros((block, HDIM), bf16)
    right = jnp.concatenate(
        [
            jnp.concatenate([low_queries.astype(f32).T.astype(bf16), blank], axis=1),
            jnp.concatenate([blank, dout.T.astype(bf16)], axis=1),
        ],
        axis=0,
    )

    def score(at):
        rows = slice(at * part, (at + 1) * part)
        return (
            dot(keys_ref[rows, : 3 * HDIM + 16], queries),
            dot(values_ref[rows, : HDIM + 16], douts),
        )

    now = score(0)
    grad_queries = None
    for at in range(count):
        following = score(at + 1) if at + 1 < count else None
        rows = slice(at * part, (at + 1) * part)
        soft = jnp.exp2(now[0])
        grads = (soft * now[1]).astype(bf16)
        added = dot(k_ref[:, rows], grads)
        grad_queries = added if grad_queries is None else grad_queries + added
        sums[rows] += dot(jnp.concatenate([grads, soft.astype(bf16)], axis=1), right)
        now = following

    def columns_of(place):
        return pl.ds(pl.multiple_of(order_ref[place] * block, block), block)

    columns = columns_of(here)
    dq_all[here] = turn_back(
        grad_queries * factor, cos_ref[:, columns], sin_ref[:, columns]
    ).astype(bf16)

    @pl.when(here == length // block - 1)
    def _():
        for place, dp_ref in enumerate(dp_refs):
            columns = columns_of(place)
            both = sums[columns].T
            dp_ref[:HDIM] = dq_all[place]
            dp_ref[HDIM : 2 * HDIM] = turn_back(
                both[:HDIM] * factor, cos_ref[:, columns], sin_ref[:, columns]
            ).astype(bf16)
            dp_ref[2 * HDIM :] = both[HDIM:].astype(bf16)


def attend_back(order, keys, values, qkv, douts, out, lse, cosine, sine, part=256):
    length = keys.shape[0]
    chips = len(douts)
    block = douts[0].shape[1]
    scores = length * length

    def whole(array):
        return pl.BlockSpec(array.shape, lambda i, order: (0, 0))

    return pl.pallas_call(
        functools.partial(attend_back_kernel, part=part),
        name="attend_back",
        grid_spec=pltpu.PrefetchScalarGridSpec(
            num_scalar_prefetch=1,
            grid=(chips,),
            in_specs=[
                whole(keys),
                whole(values),
                pl.BlockSpec((HDIM, block), lambda i, order: (0, order[i])),
                pl.BlockSpec((HDIM, length), lambda i, order: (1, 0)),
                pl.BlockSpec((HDIM, block), lambda i, order: (0, order[i])),
                pl.BlockSpec((1, block), lambda i, order: (0, order[i])),
                whole(cosine),
                whole(sine),
                *[whole(piece) for piece in douts],
            ],
            out_specs=[pl.BlockSpec((3 * HDIM, block), lambda i, order: (0, 0))] * chips,
            scratch_shapes=[
                pltpu.VMEM((length, 2 * HDIM), f32),
                pltpu.VMEM((chips, HDIM, block), bf16),
                pltpu.VMEM((chips, HDIM, block), bf16),
            ],
        ),
        out_shape=[jax.ShapeDtypeStruct((3 * HDIM, block), bf16)] * chips,
        compiler_params=pltpu.CompilerParams(vmem_limit_bytes=VMEM),
        cost_estimate=cost(5 * 4 * 2 * scores * HDIM, 8 << 20),
    )(order, keys, values, qkv, qkv, out, lse, cosine, sine, *douts)


def attend_out_kernel(order_ref, attended_ref, *rest):
    piece_refs, (mixed_ref, attn_ref) = rest[:-2], rest[-2:]
    half = attn_ref.shape[1] // 2
    at = 0
    for piece_ref in piece_refs:
        for place in range(piece_ref.shape[0]):
            rows = pl.ds(pl.multiple_of(order_ref[at] * HDIM, HDIM), HDIM)
            attn_ref[rows, :half] = piece_ref[place, :HDIM]
            attn_ref[rows, half:] = piece_ref[place, HDIM:]
            at += 1
    turned = attended_ref[...].astype(f32).T.astype(bf16)
    mixed_ref[...] = dot(turned, attn_ref[...]).astype(bf16)


def attend_out(order, attended, pieces):
    size, tokens = attended.shape
    width = 2 * size

    def whole(*shape):
        return pl.BlockSpec(shape, lambda i, order: (0,) * len(shape))

    return pl.pallas_call(
        attend_out_kernel,
        name="attend_out",
        grid_spec=pltpu.PrefetchScalarGridSpec(
            num_scalar_prefetch=1,
            grid=(1,),
            in_specs=[whole(size, tokens)]
            + [whole(*piece.shape[:2], width // 2) for piece in pieces],
            out_specs=[whole(tokens, width), whole(size, width)],
        ),
        out_shape=[
            jax.ShapeDtypeStruct((tokens, width), bf16),
            jax.ShapeDtypeStruct((size, width), bf16),
        ],
        compiler_params=pltpu.CompilerParams(vmem_limit_bytes=VMEM),
        cost_estimate=cost(2 * 2 * tokens * width * size, 4 << 20),
    )(order, attended, *pieces)


def feed_kernel(
    first_order, second_order, x_ref, ours_ref, theirs_ref, g_ref, *rest, firsts, seconds, axes
):
    weight_refs = []
    start = 0
    for size in (firsts, firsts, seconds, seconds):
        weight_refs.append(rest[start : start + size])
        start += size
    planes, lines, wide, beside = axes

    def put(grads, columns):
        size = grads.shape[0] // (planes * lines * wide)
        low = grads.astype(bf16)
        for plane in range(planes):
            for line in range(lines):
                for far in range(wide):
                    source = ((plane * lines + line) * wide + far) * size
                    target = ((line * wide + far) * planes + plane) * size
                    grads_ref[target : target + size, columns] = low[source : source + size]
    residual_ref, partial_ref, back_ref, grads_ref = rest[-13:-9]
    unit, unit_t, g_t, sum_out, sum_back = rest[-9:-4]
    gate_ref, up_ref, out_ref, rest_ref = rest[-4:]
    here = pl.program_id(0)
    last = pl.num_programs(0) - 1
    width = x_ref.shape[1]
    step = gate_ref.shape[1]

    def join(total, parts, order):
        at = 0
        for part in parts:
            size = part.shape[1]
            for place in range(part.shape[0]):
                total[pl.ds(pl.multiple_of(order[at] * size, size), size)] = part[place]
                at += 1

    def bend(gate, upward):
        cdf = 0.5 + 0.5 * lax.erf(gate * math.sqrt(0.5))
        slope = cdf + gate * jnp.exp(gate * gate * -0.5) * (1.0 / math.sqrt(2.0 * math.pi))
        bent = gate * cdf
        return bent, slope, (bent * upward).astype(bf16)

    @pl.when(here == 0)
    def _():
        residual = (
            x_ref[...].astype(f32) + ours_ref[...].astype(f32) + theirs_ref[...].astype(f32)
        )
        residual_ref[...] = residual
        normed = unit_rows(residual)[0]
        unit[...] = normed.astype(bf16)
        unit_t[...] = normed.T.astype(bf16)
        g_t[...] = g_ref[...].astype(f32).T.astype(bf16)
        join(rest_ref, weight_refs[3], second_order)
        few = rest_ref.shape[1] // 4
        both = dot(unit[...], rest_ref[...])
        grad = dot(g_ref[...], rest_ref[...])[:, 2 * few : 3 * few]
        bent, slope, active = bend(both[:, :few], both[:, few : 2 * few])
        grad_gate = (grad * both[:, few : 2 * few] * slope).astype(bf16)
        grad_up = (grad * bent).astype(bf16)
        blank = jnp.zeros_like(active)
        outs = jnp.concatenate([blank, blank, active, blank], axis=1)
        ins = jnp.concatenate([grad_gate, grad_up, blank, blank], axis=1)
        sum_out[...] = dot(outs, rest_ref[...], 1, 1)
        sum_back[...] = dot(ins, rest_ref[...], 1, 1)
        put(
            dot(unit_t[...], ins) + dot(g_t[...], outs),
            slice(grads_ref.shape[1] - 4 * few, grads_ref.shape[1]),
        )

    join(gate_ref, weight_refs[0], first_order)
    join(up_ref, weight_refs[1], first_order)
    join(out_ref, weight_refs[2], second_order)
    gate = dot(unit[...], gate_ref[...])
    upward = dot(unit[...], up_ref[...])
    grad = dot(g_ref[...], out_ref[...])
    bent, slope, active = bend(gate, upward)
    grad_gate = (grad * upward * slope).astype(bf16)
    grad_up = (grad * bent).astype(bf16)
    sum_out[...] += dot(active, out_ref[...], 1, 1)
    sum_back[...] += dot(grad_gate, gate_ref[...], 1, 1) + dot(grad_up, up_ref[...], 1, 1)
    count = grads_ref.shape[1] // step // 3
    for at, grads in enumerate(
        (dot(unit_t[...], grad_gate), dot(unit_t[...], grad_up), dot(g_t[...], active))
    ):
        place = pl.multiple_of(at * count * step + here * step, 128)
        put(grads, pl.ds(place, step))

    @pl.when(here == last)
    def _():
        partial_ref[...] = sum_out[...].astype(bf16)
        back_ref[...] = sum_back[...].astype(bf16)


def feed(first_order, second_order, x, ours, theirs, g, first, second, axes, step=256):
    tokens, width = x.shape
    start = width // 2 // step
    count = (first[0].shape[2] - width // 2) // step // 2
    rest = second[0].shape[2] - count * step
    columns = 3 * count * step + rest

    def whole(*shape):
        return pl.BlockSpec(shape, lambda i, one, two: (0, 0))

    def piece(arrays, size, at):
        return [
            pl.BlockSpec((*array.shape[:2], size), lambda i, one, two: (0, 0, at(i)))
            for array in arrays
        ]

    pair = jax.ShapeDtypeStruct((tokens, width), bf16)
    return pl.pallas_call(
        functools.partial(feed_kernel, firsts=len(first), seconds=len(second), axes=axes),
        name="feed",
        grid_spec=pltpu.PrefetchScalarGridSpec(
            num_scalar_prefetch=2,
            grid=(count,),
            in_specs=[whole(tokens, width)] * 4
            + piece(first, step, lambda i: start + i)
            + piece(first, step, lambda i: start + count + i)
            + piece(second, step, lambda i: i)
            + piece(second, rest, lambda i: count * step // rest),
            out_specs=[whole(tokens, width)] * 3 + [whole(width, columns)],
            scratch_shapes=[
                pltpu.VMEM((tokens, width), bf16),
                pltpu.VMEM((width, tokens), bf16),
                pltpu.VMEM((width, tokens), bf16),
                pltpu.VMEM((tokens, width), f32),
                pltpu.VMEM((tokens, width), f32),
                pltpu.VMEM((width, step), bf16),
                pltpu.VMEM((width, step), bf16),
                pltpu.VMEM((width, step), bf16),
                pltpu.VMEM((width, rest), bf16),
            ],
        ),
        out_shape=[
            jax.ShapeDtypeStruct((tokens, width), f32),
            pair,
            pair,
            jax.ShapeDtypeStruct((width, columns), bf16),
        ],
        compiler_params=pltpu.CompilerParams(vmem_limit_bytes=VMEM),
        cost_estimate=cost(2 * 9 * 2 * tokens * width * count * step, 24 << 20),
    )(first_order, second_order, x, ours, theirs, g, *first, *first, *second, *second)


def middle_back_kernel(
    core_ref, order_ref, line_ref, residual_ref, g_ref, ours_ref, theirs_ref, attn_ref,
    attended_ref, out_ours_ref, out_theirs_ref, layer_ref, residual_grad_ref, *rest, axes,
):
    planes, lines, wide, beside = axes
    dout_refs, grads_refs, (dout_all, grads_all) = rest[: -2 - lines], rest[-2 - lines : -2], rest[-2:]
    rows = layer_ref.shape[0]
    half = attn_ref.shape[0]
    own = pl.ds(pl.multiple_of(core_ref[0] * rows, rows), rows)
    layer_ref[...] = (
        residual_ref[own, :]
        + out_ours_ref[own, :].astype(f32)
        + out_theirs_ref[...].astype(f32)
    ).astype(bf16)
    unit, inverse = unit_rows(residual_ref[...])
    scaled = ours_ref[...].astype(f32) + theirs_ref[...].astype(f32)
    grad = g_ref[...].astype(f32) + unit_back(scaled, unit, inverse)
    low = grad.astype(bf16)
    residual_grad_ref[...] = grad
    dout_all[...] = dot(attn_ref[...], low, 1, 1).astype(bf16)
    for at, dout_ref in enumerate(dout_refs):
        dout_ref[...] = dout_all[pl.ds(pl.multiple_of(order_ref[at] * HDIM, HDIM), HDIM)]
    grads_all[...] = dot(attended_ref[...], low)
    few = HDIM // wide // beside
    for shift, grads_ref in enumerate(grads_refs):
        line = (line_ref[0] + shift) % lines
        blocks = [
            grads_all[pl.ds(pl.multiple_of((plane * lines + line) * HDIM, HDIM), HDIM)]
            for plane in range(planes)
        ]
        pieces = []
        for far in range(wide):
            for plane in range(planes):
                for near in range(beside):
                    start = (far * beside + near) * few
                    piece = blocks[plane][start : start + few]
                    pieces += [piece[:, :half], piece[:, half:]]
        grads_ref[...] = jnp.concatenate(pieces, axis=0).astype(bf16)


def middle_back(
    core, order, line, residual, g, ours, theirs, attn, attended, out_ours, out_theirs, axes
):
    tokens, width = residual.shape
    rows = tokens // 2
    half = width // 2
    chips = half // HDIM
    lines = axes[1]

    def whole(*shape):
        return pl.BlockSpec(shape, lambda i, core, order, line: (0,) * len(shape))

    return pl.pallas_call(
        functools.partial(middle_back_kernel, axes=axes),
        name="middle_back",
        grid_spec=pltpu.PrefetchScalarGridSpec(
            num_scalar_prefetch=3,
            grid=(1,),
            in_specs=[whole(tokens, width)] * 4
            + [whole(half, width), whole(half, tokens), whole(tokens, width), whole(rows, width)],
            out_specs=[whole(rows, width), whole(tokens, width)]
            + [whole(HDIM, tokens)] * chips
            + [whole(width // lines, half)] * lines,
            scratch_shapes=[pltpu.VMEM((half, tokens), bf16), pltpu.VMEM((half, width), f32)],
        ),
        out_shape=[
            jax.ShapeDtypeStruct((rows, width), bf16),
            jax.ShapeDtypeStruct((tokens, width), f32),
        ]
        + [jax.ShapeDtypeStruct((HDIM, tokens), bf16)] * chips
        + [jax.ShapeDtypeStruct((width // lines, half), bf16)] * lines,
        compiler_params=pltpu.CompilerParams(vmem_limit_bytes=VMEM),
        cost_estimate=cost(2 * 2 * 2 * tokens * width * half, 16 << 20),
    )(core, order, line, residual, g, ours, theirs, attn, attended, out_ours, out_theirs)


def hidden_back_kernel(order_ref, core_ref, shard_ref, w_ref, *rest):
    dp_refs, (own_ref, other_ref, stacked) = rest[:-3], rest[-3:]
    for place, dp_ref in enumerate(dp_refs):
        size = dp_ref.shape[0]
        stacked[pl.ds(pl.multiple_of(order_ref[place] * size, 64), size)] = dp_ref[...]
    rows = own_ref.shape[0]
    zero = core_ref[0] == 0
    size = w_ref.shape[1]
    for at in range(w_ref.shape[0]):
        flat = dot(w_ref[at], stacked[...])
        first = flat[:, :rows].T
        second = flat[:, rows:].T
        columns = pl.ds(pl.multiple_of(shard_ref[at] * size, size), size)
        own_ref[:, columns] = jnp.where(zero, first, second)
        other_ref[:, columns] = jnp.where(zero, second, first).astype(bf16)


def hidden_back(order, core, shard_order, weights, pieces):
    shards, size, columns = weights.shape
    width = shards * size
    rows = pieces[0].shape[1] // 2

    def whole(*shape):
        return pl.BlockSpec(shape, lambda i, order, core, shard: (0,) * len(shape))

    return pl.pallas_call(
        hidden_back_kernel,
        name="hidden_back",
        grid_spec=pltpu.PrefetchScalarGridSpec(
            num_scalar_prefetch=3,
            grid=(1,),
            in_specs=[whole(shards, size, columns)] + [whole(*pieces[0].shape)] * len(pieces),
            out_specs=[whole(rows, width)] * 2,
            scratch_shapes=[pltpu.VMEM((columns, 2 * rows), bf16)],
        ),
        out_shape=[
            jax.ShapeDtypeStruct((rows, width), f32),
            jax.ShapeDtypeStruct((rows, width), bf16),
        ],
        compiler_params=pltpu.CompilerParams(vmem_limit_bytes=VMEM),
        cost_estimate=cost(2 * 2 * 2 * rows * width * columns, 8 << 20),
    )(order, core, shard_order, weights, *pieces)


def head_grad_kernel(order_ref, owner_ref, unit_ref, *rest, owners):
    dp_refs, out_refs, out_all = rest[: -1 - owners], rest[-1 - owners : -1], rest[-1]
    block = dp_refs[0].shape[1]
    total = None
    for place, dp_ref in enumerate(dp_refs):
        rows = pl.ds(pl.multiple_of(order_ref[place] * block, block), block)
        added = dot(dp_ref[...], unit_ref[rows])
        total = added if total is None else total + added
    for at in range(owners):
        out_all[at] = total[:, at * 128 : (at + 1) * 128].astype(bf16)
    for at, out_ref in enumerate(out_refs):
        out_ref[...] = out_all[owner_ref[at]]


def head_grad(order, owner_order, unit_all, pieces):
    length, width = unit_all.shape
    owners = width // 128
    size = pieces[0].shape[0]

    def whole(*shape):
        return pl.BlockSpec(shape, lambda i, order, owner: (0,) * len(shape))

    return pl.pallas_call(
        functools.partial(head_grad_kernel, owners=owners),
        name="head_grad",
        grid_spec=pltpu.PrefetchScalarGridSpec(
            num_scalar_prefetch=2,
            grid=(1,),
            in_specs=[whole(length, width)] + [whole(*pieces[0].shape)] * len(pieces),
            out_specs=[whole(size, 128)] * owners,
            scratch_shapes=[pltpu.VMEM((owners, size, 128), bf16)],
        ),
        out_shape=[jax.ShapeDtypeStruct((size, 128), bf16)] * owners,
        compiler_params=pltpu.CompilerParams(vmem_limit_bytes=VMEM),
        cost_estimate=cost(2 * 2 * length * width * size, 10 << 20),
    )(order, owner_order, unit_all, *pieces)


def adam_in_kernels(weight, gradient, first, second, rate):
    first = BETA_FIRST * first + (1.0 - BETA_FIRST) * gradient
    second = BETA_SECOND * second + (1.0 - BETA_SECOND) * gradient * gradient
    second_hat = second * (1.0 / (1.0 - BETA_SECOND**STEP))
    bottom = second_hat * lax.rsqrt(second_hat) + EPSILON
    guess = pl.reciprocal(bottom, approx=True)
    guess = guess * (2.0 - bottom * guess)
    scale = rate / (1.0 - BETA_FIRST**STEP)
    weight = weight * (1.0 - rate * DECAY) - (scale * first) * guess
    return (weight, first, second)


def adam_into(refs, weight, gradient, first, second, rate):
    for ref, value in zip(refs, adam_in_kernels(weight, gradient, first, second, rate)):
        ref[...] = value


def rounded_in_kernel(values):
    return values.astype(bf16).astype(f32)


def adam_most_kernel(grads_ref, gain_ref, other_gain_ref, *refs, rates):
    (w_in, m_in, v_in), attn, out, gains = refs[:3], refs[3:6], refs[6:9], refs[9:12]
    new_in, new_attn, new_out, new_gains = refs[12:15], refs[15:18], refs[18:21], refs[21:24]
    gain_grad, turned = refs[24:]
    here = pl.program_id(0)
    chips = grads_ref.shape[0] // 2
    width = w_in.shape[1] // 2
    main = width // 256 * 128
    few = width // 2 - main

    @pl.when(here == 0)
    def _():
        for core in range(2):
            columns = jnp.concatenate(
                [grads_ref[2 * chip + core, :, 2 * main : 3 * main] for chip in range(chips)],
                axis=0,
            )
            turned[core * main : (core + 1) * main] = columns.astype(f32).T
            rest = jnp.concatenate(
                [
                    grads_ref[2 * chip + core, :, 3 * main : 3 * main + 128]
                    for chip in range(chips)
                ],
                axis=0,
            )
            start = 2 * main + core * few
            turned[start : start + few] = rest.astype(f32).T[2 * few : 3 * few]

    each = grads_ref.shape[1]
    some = w_in.shape[0] // each
    for at_chip in range(some):
        source = 2 * (here * some + at_chip)
        columns = []
        for at in range(2):
            for core in range(2):
                place = at * main
                columns.append(grads_ref[source + core, :, place : place + main].astype(f32))
            for core in range(2):
                rest = grads_ref[source + core, :, 3 * main : 3 * main + 128].astype(f32)
                columns.append(rest[:, at * few : (at + 1) * few])
        grads = jnp.concatenate(columns, axis=1)
        rows = slice(at_chip * each, (at_chip + 1) * each)
        weight = w_in[rows]
        gain_rows = pl.ds(pl.multiple_of((here * some + at_chip) * each, each), each)
        gain_grad[gain_rows] = jnp.sum(
            grads * rounded_in_kernel(weight), axis=1, keepdims=True
        )
        values = adam_in_kernels(
            weight, grads * gain_ref[rows], m_in[rows], v_in[rows], rates[0]
        )
        for ref, value in zip(new_in, values):
            ref[rows] = value
        rows = slice(at_chip * each // 2, (at_chip + 1) * each // 2)
        for core in range(2):
            piece = grads_ref[source + core, :, 3 * main + 128 :].astype(f32)
            grads = jnp.concatenate([piece[: each // 2], piece[each // 2 :]], axis=1)
            values = adam_in_kernels(
                attn[0][core, rows], grads, attn[1][core, rows], attn[2][core, rows], rates[1]
            )
            for ref, value in zip(new_attn, values):
                ref[core, rows] = value

    size = out[0].shape[0]
    grads = turned[pl.ds(pl.multiple_of(here * size, 8), size)]
    adam_into(new_out, out[0][...], grads, out[1][...], out[2][...], rates[2])

    @pl.when(here == pl.num_programs(0) - 1)
    def _():
        both = jnp.concatenate(
            [other_gain_ref[...], gain_grad[...], jnp.zeros((gain_grad.shape[0], 6), f32)], axis=1
        )
        adam_into(
            new_gains, gains[0][...], both.T[:2], gains[1][...], gains[2][...], GAIN_RATE
        )


def adam_most(
    grads, gain, other_gain, weights_in, weights_attn, weights_out, gains, rates, steps=2
):
    rows, columns = weights_in[0].shape
    width = weights_attn[0].shape[1]
    hidden = weights_out[0].shape[0]
    weights_attn = [array.reshape(2, rows // 2, width) for array in weights_attn]
    block_in = pl.BlockSpec((rows // steps, columns), lambda i: (i, 0))
    block_attn = pl.BlockSpec((2, rows // 2 // steps, width), lambda i: (0, i, 0))
    block_out = pl.BlockSpec((hidden // steps, rows), lambda i: (i, 0))
    column = pl.BlockSpec((rows // steps, 1), lambda i: (i, 0))
    whole_column = pl.BlockSpec((rows, 1), lambda i: (0, 0))
    block_gains = pl.BlockSpec(gains[0].shape, lambda i: (0, 0))
    blocks = [block_in] * 3 + [block_attn] * 3 + [block_out] * 3 + [block_gains] * 3
    arrays = (*weights_in, *weights_attn, *weights_out, *gains)
    results = pl.pallas_call(
        functools.partial(adam_most_kernel, rates=rates),
        name="adam_most",
        grid=(steps,),
        in_specs=[pl.BlockSpec(grads.shape, lambda i: (0, 0, 0)), column, whole_column] + blocks,
        out_specs=blocks,
        out_shape=[jax.ShapeDtypeStruct(array.shape, f32) for array in arrays],
        scratch_shapes=[pltpu.VMEM((rows, 1), f32), pltpu.VMEM((hidden, rows), f32)],
        compiler_params=pltpu.CompilerParams(vmem_limit_bytes=VMEM),
        cost_estimate=cost(rows * columns * 20, rows * columns * 26),
    )(grads, gain, other_gain, *arrays)
    new_attn = [array.reshape(rows, width) for array in results[3:6]]
    return results[:3], new_attn, results[6:9], results[9:]


def adam_qkv_kernel(order_ref, *refs, rate):
    grads_refs, (gain_ref, w_ref, m_ref, v_ref, new_w, new_m, new_v, gain_grad, joined) = (
        refs[:-9], refs[-9:]
    )
    here = pl.program_id(0)
    heads = sum(grads_ref.shape[0] for grads_ref in grads_refs)

    @pl.when(here == 0)
    def _():
        at = 0
        for grads_ref in grads_refs:
            for place in range(grads_ref.shape[0]):
                for part in range(3):
                    row = (part * heads + order_ref[at]) * HDIM
                    joined[pl.ds(pl.multiple_of(row, HDIM), HDIM)] = grads_ref[
                        place, part * HDIM : (part + 1) * HDIM
                    ].astype(f32)
                at += 1

    size = w_ref.shape[1]
    grads = joined[pl.ds(pl.multiple_of(here * size, size), size)].T
    weight = w_ref[...]
    added = jnp.sum(grads * rounded_in_kernel(weight), axis=1, keepdims=True)
    gain_grad[...] = added + jnp.where(here == 0, 0.0, gain_grad[...])
    adam_into(
        (new_w, new_m, new_v), weight, grads * gain_ref[...], m_ref[...], v_ref[...], rate
    )


def adam_qkv(order, grads, gain, weight, first, second, rate, step=1536):
    rows, columns = weight.shape
    block = pl.BlockSpec((rows, step), lambda i, order: (0, i))
    column = pl.BlockSpec((rows, 1), lambda i, order: (0, 0))
    same = jax.ShapeDtypeStruct((rows, columns), f32)
    return pl.pallas_call(
        functools.partial(adam_qkv_kernel, rate=rate),
        name="adam_qkv",
        grid_spec=pltpu.PrefetchScalarGridSpec(
            num_scalar_prefetch=1,
            grid=(columns // step,),
            in_specs=[pl.BlockSpec(piece.shape, lambda i, order: (0, 0, 0)) for piece in grads]
            + [column]
            + [block] * 3,
            out_specs=[block] * 3 + [column],
            scratch_shapes=[pltpu.VMEM((columns, rows), f32)],
        ),
        out_shape=[same] * 3 + [jax.ShapeDtypeStruct((rows, 1), f32)],
        compiler_params=pltpu.CompilerParams(vmem_limit_bytes=VMEM),
        cost_estimate=cost(rows * columns * 20, rows * columns * 26),
    )(order, *grads, gain, weight, first, second)


def ring(axis, shift):
    size = lax.axis_size(axis)
    return [(at, (at + shift) % size) for at in range(size)]


def gather_first_step(planes_first, lines_first):
    swapped = lax.ppermute(planes_first, "zh", SWAP)
    others = [
        lax.ppermute(lines_first, "y", ring("y", shift)) for shift in range(1, lax.axis_size("y"))
    ]
    return jnp.stack([planes_first, swapped]), jnp.stack([lines_first, *others])


def shards(
    tokens,
    positions,
    cotangent,
    weight_qkv,
    weight_attn,
    weight_in,
    weight_out,
    norm_gains,
    first_qkv,
    first_attn,
    first_in,
    first_out,
    first_gains,
    second_qkv,
    second_attn,
    second_in,
    second_out,
    second_gains,
):
    rows, width = tokens.shape[1:]
    shard_rows = weight_qkv.shape[1]
    heads = width // HDIM
    hidden = weight_out.shape[1]
    core = lax.axis_index("c")
    mine = lax.axis_index(CTX)
    chip = lax.axis_index(CHIPS)
    chips = lax.axis_size(CHIPS)
    owners = lax.axis_size(FSDP)
    length = rows * chips * 2
    main = hidden // 256 * 128
    few = hidden // 2 - main
    core_at = core.reshape(1).astype(jnp.int32)
    axes = (lax.axis_size("zh"), lax.axis_size("y"), lax.axis_size("x"), lax.axis_size("zl"))
    offsets = [(far, near) for far in range(lax.axis_size("x")) for near in range(2)]
    across, beside = lax.axis_index("x"), lax.axis_index("zl")
    wide = lax.axis_size("x")

    def chips_at(sign):
        places = [(across + sign * far) % wide * 2 + (beside ^ near) for far, near in offsets]
        return jnp.stack(places).astype(jnp.int32)

    local = tokens[0]
    extra = 16
    high, low = positions[0] // 128, positions[0] % 128
    places_row = jnp.concatenate([high, low, jnp.zeros((width - 2 * rows,), jnp.int32)])
    places_rows = jnp.concatenate(
        [places_row[None], jnp.zeros((extra - 1, width), jnp.int32)], axis=0
    ).astype(bf16)
    sequence = lax.all_gather(
        jnp.concatenate([local, places_rows], axis=0), CTX, axis=0, tiled=True
    )
    first_part, second_part, head_part, half_heads = prepare(
        jnp.stack([core, chip]).astype(jnp.int32),
        norm_gains[0],
        weight_qkv[0],
        weight_attn[0],
        weight_in[0],
        weight_out[0],
    )
    first_joined, second_joined = gather_first_step(first_part, second_part)
    head_weights = lax.all_to_all(
        jnp.broadcast_to(head_part, (owners, *head_part.shape)), FSDP, 0, 0, tiled=True
    )
    first_pieces = [first_joined] + [
        lax.ppermute(first_joined, "y", ring("y", shift))
        for shift in range(1, lax.axis_size("y"))
    ]
    sequence, _, second_joined, half_heads, _ = lax.optimization_barrier(
        (sequence, first_joined, second_joined, half_heads, head_weights)
    )
    half_heads_other = lax.ppermute(half_heads, "zh", SWAP)
    second_pieces = [second_joined, lax.ppermute(second_joined, "zh", SWAP)]
    lines = lax.axis_size("y")
    plane, line = lax.axis_index("zh"), lax.axis_index("y")
    heads_order = jnp.stack(
        [(plane ^ far) * lines + at for at in range(lines) for far in range(2)]
    ).astype(jnp.int32)
    first_order = jnp.stack(
        [(plane ^ far) * lines + (line - shift) % lines for shift in range(lines) for far in range(2)]
    ).astype(jnp.int32)
    second_order = jnp.stack(
        [(plane ^ far) * lines + (line - shift) % lines for far in range(2) for shift in range(lines)]
    ).astype(jnp.int32)

    def in_order(ours, theirs):
        first = jnp.where(core == 0, ours, theirs)
        second = jnp.where(core == 0, theirs, ours)
        return jnp.concatenate([first, second], axis=0)

    def swap(array):
        return lax.ppermute(array, "c", SWAP)

    gradient = in_order(cotangent[0], swap(cotangent[0]))

    freqs = jnp.exp(jnp.arange(HDIM // 2, dtype=f32) * (-2.0 * math.log(ROPE_BASE) / HDIM))
    by_device = sequence.reshape(2 * chips, rows + extra, width)[:, rows]
    by_device = by_device.astype(f32)
    places = by_device[:, :rows] * 128.0 + by_device[:, rows : 2 * rows]
    angles = freqs[:, None] * places.reshape(1, length)
    cosine = jnp.cos(angles)
    sine = jnp.sin(angles)
    unit_all, qkv, keys, values = project(sequence, head_weights, cosine, sine, extra)
    low_out, out, lse = attend(keys, qkv, chips)
    firsts = len(first_pieces)
    low_out, half_heads_other, *arrived = lax.optimization_barrier(
        (low_out, half_heads_other, *first_pieces, *second_pieces)
    )
    first_pieces, second_pieces = arrived[:firsts], arrived[firsts:]
    mat_qkv = lax.all_gather(
        jnp.stack([half_heads, half_heads_other]), "y", axis=0, tiled=True
    )
    attended = lax.all_to_all(low_out, CHIPS, 0, 0, tiled=True)
    attended = attended.reshape(heads // 2 * HDIM, 2 * rows)
    mixed, mat_attn = attend_out(first_order, attended, first_pieces)
    current = lax.dynamic_slice_in_dim(
        sequence, chip * 2 * (rows + extra), 2 * (rows + extra), 0
    ).reshape(2, rows + extra, width)[:, :rows].reshape(2 * rows, width)
    residual, partial, back, grads = feed(
        first_order, second_order, current, mixed, swap(mixed), gradient, first_pieces,
        second_pieces, axes,
    )
    grads, mat_qkv = lax.optimization_barrier((grads, mat_qkv))
    first_sum = lax.psum_scatter(grads, "y", scatter_dimension=0, tiled=True)

    def move(pieces, sign):
        moved = [pieces[0]]
        for (far, near), piece in list(zip(offsets, pieces))[1:]:
            pairs = [
                (at, (at // 2 + sign * far) % wide * 2 + (at % 2 ^ near)) for at in range(chips)
            ]
            moved.append(lax.ppermute(piece, CHIPS, pairs))
        return moved

    ahead, behind = chips_at(1), chips_at(-1)
    theirs = swap(lax.dynamic_slice_in_dim(partial, (1 - core) * rows, rows, 0))
    layer_out, residual_grad, *pieces = middle_back(
        core_at, ahead, line.reshape(1).astype(jnp.int32), residual, gradient, back, swap(back),
        mat_attn, attended, partial, theirs, axes,
    )
    dout_pieces, attn_pieces = pieces[:chips], pieces[chips:]

    douts = move(dout_pieces, 1)
    attn_arrived = attn_pieces[:1] + [
        lax.ppermute(piece, "y", ring("y", shift))
        for shift, piece in list(enumerate(attn_pieces))[1:]
    ]
    pieces = attend_back(behind, keys, values, qkv, douts, out, lse, cosine, sine)
    rest = lax.optimization_barrier((*pieces, *attn_arrived))
    pieces, attn_arrived = rest[:chips], rest[chips:]
    owner_places = [(far, shift) for far in range(2) for shift in range(lines)]
    owner_order = jnp.stack(
        [(plane ^ far) * lines + (line + shift) % lines for far, shift in owner_places]
    ).astype(jnp.int32)
    head_parts = head_grad(behind, owner_order, unit_all, pieces)

    def total(arrays):
        return sum(array.astype(f32) for array in arrays).astype(bf16)

    moved = move(pieces, -1)
    first_sum, *rest = lax.optimization_barrier((first_sum, *moved, *head_parts))
    moved, head_parts = rest[:chips], rest[chips:]
    first_sum = jnp.concatenate([first_sum, total(attn_arrived)], axis=1)
    arrived = lax.all_to_all(first_sum, ("x", "zh", "zl"), 0, 0, tiled=True)
    own_hidden, other_hidden = hidden_back(ahead, core_at, heads_order, mat_qkv, moved)
    arrived, own_hidden, *head_parts = lax.optimization_barrier(
        (arrived, own_hidden, *head_parts)
    )
    grad_hidden = own_hidden + swap(other_hidden).astype(f32)
    unit_in, scale_in = unit_rows(local.astype(f32))
    own_residual = lax.dynamic_slice_in_dim(residual_grad, core * rows, rows, 0)
    tokens_grad = (own_residual + unit_back(grad_hidden, unit_in, scale_in))[None]

    head_arrived = [head_parts[0]]
    for (far, shift), piece in list(zip(owner_places, head_parts))[1:]:
        pairs = [
            (at, (at // lines ^ far) * lines + (at % lines + shift) % lines) for at in range(owners)
        ]
        head_arrived.append(lax.ppermute(piece, FSDP, pairs))
    head_own = total(head_arrived)[None]
    arrived = arrived.reshape(2 * chips, shard_rows // chips, -1)
    second_sum = jnp.sum(arrived.astype(f32), axis=0).astype(bf16)
    all_grads = lax.all_gather(second_sum, CTX, axis=0, tiled=False)

    head_pair = jnp.concatenate([head_own, swap(head_own)], axis=0)
    head_four = jnp.concatenate([head_pair, lax.ppermute(head_pair, "zl", SWAP)], axis=0)
    head_grads = [head_four] + [
        lax.ppermute(head_four, "x", ring("x", shift)) for shift in range(1, wide)
    ]
    head_order = jnp.stack(
        [
            (across - shift) % wide * 4 + (beside ^ near) * 2 + (core ^ other)
            for shift in range(wide)
            for near in range(2)
            for other in range(2)
        ]
    ).astype(jnp.int32)

    rates = (
        width ** (-0.5),
        max(1, 3 * width // length) ** (-0.5),
        width ** (-0.5),
        hidden ** (-0.5),
    )
    columns_of_gains = norm_gains[0].astype(bf16).astype(f32).T
    *new_qkv, gain_first = adam_qkv(
        head_order, head_grads, columns_of_gains[:, :1], weight_qkv[0], first_qkv[0], second_qkv[0], rates[0]
    )
    new_in, new_attn, new_out, new_gains = adam_most(
        all_grads,
        columns_of_gains[:, 1:],
        gain_first,
        (weight_in[0], first_in[0], second_in[0]),
        (weight_attn[0], first_attn[0], second_attn[0]),
        (weight_out[0], first_out[0], second_out[0]),
        (norm_gains[0], first_gains[0], second_gains[0]),
        (rates[2], rates[1], rates[3]),
    )
    updated = (new_qkv, new_attn, new_in, new_out, new_gains)
    return (
        layer_out[None],
        tokens_grad,
        *[updated[member][0][None] for member in range(5)],
        *[updated[member][1][None] for member in range(5)],
        *[updated[member][2][None] for member in range(5)],
    )


def solution(mesh):
    split = Mesh(mesh.devices.reshape(4, 2, 2, 2, 4), ("x", "zl", "c", "zh", "y"))
    by_row = P(None, FSDP, None)
    by_column = P(None, None, FSDP)
    weights = (by_row, by_row, by_row, by_column, by_column)
    by_token = P(FSDP, CTX, None)
    return jax.shard_map(
        shards,
        mesh=split,
        in_specs=(by_token, P(FSDP, CTX), by_token) + weights * 3,
        out_specs=(by_token, by_token) + weights * 3,
        check_vma=False,
    )
```

```python
import functools
import math

import jax
import jax.numpy as jnp
from jax import lax
from jax.experimental import pallas as pl
from jax.experimental.pallas import tpu as pltpu
from jax.sharding import Mesh, PartitionSpec as P

HDIM = 64
STEP = 10
BETA_FIRST = 0.5
BETA_SECOND = 0.5
EPSILON = 1e-08
DECAY = 0.01
NORM_EPS = 1e-05
ROPE_BASE = 160000.0
GAIN_RATE = 0.6
LOG2E = math.log2(math.e)
f32 = jnp.float32
bf16 = jnp.bfloat16

CHIPS = ("x", "zl")
CTX = ("x", "zl", "c")
FSDP = ("zh", "y")
SWAP = [(0, 1), (1, 0)]
VMEM = 60 << 20


def dot(left, right, left_dim=1, right_dim=0):
    return lax.dot_general(
        left, right, (((left_dim,), (right_dim,)), ((), ())), preferred_element_type=f32
    )


def cost(flops, moved):
    return pl.CostEstimate(flops=flops, bytes_accessed=moved, transcendentals=0)


def unit_rows(values):
    average = jnp.mean(values, axis=-1, keepdims=True)
    centered = values - average
    spread = jnp.mean(centered * centered, axis=-1, keepdims=True)
    inverse = lax.rsqrt(spread + NORM_EPS)
    return centered * inverse, inverse


def unit_back(scaled, unit, inverse):
    first_mean = jnp.mean(scaled, axis=-1, keepdims=True)
    second_mean = jnp.mean(scaled * unit, axis=-1, keepdims=True)
    return inverse * (scaled - first_mean - unit * second_mean)


def prepare_kernel(
    place_ref, gains_ref, qkv_ref, attn_ref, in_ref, out_ref,
    first_ref, second_ref, head_ref, heads_ref,
):
    core, chip = place_ref[0], place_ref[1]
    rows = qkv_ref.shape[0]
    width = attn_ref.shape[1]
    hidden = out_ref.shape[0]
    main = hidden // 256 * 128
    few = hidden // 2 - main
    half = width // 2
    low_gains = gains_ref[...].astype(bf16).astype(f32)
    columns = jnp.concatenate([low_gains, jnp.zeros((6, rows), f32)], axis=0).T
    gain_first, gain_second = columns[:, 0:1], columns[:, 1:2]

    def pick(array):
        size = array.shape[1] // 2
        return jnp.where(core == 0, array[:, :size], array[:, size:])

    def scaled(values, gain):
        return (values.astype(bf16).astype(f32) * gain).astype(bf16)

    attn_rows = attn_ref[pl.ds(pl.multiple_of(core * HDIM, HDIM), HDIM)].astype(bf16)
    first_ref[:HDIM, :half] = attn_rows[:, :half]
    first_ref[HDIM:, :half] = attn_rows[:, half:]
    first_ref[:, half : half + main] = scaled(pick(in_ref[:, : 2 * main]), gain_second)
    first_ref[:, half + main :] = scaled(pick(in_ref[:, hidden : hidden + 2 * main]), gain_second)
    out_rows = out_ref[pl.ds(pl.multiple_of(core * main, 128), main)]
    second_ref[:, :main] = out_rows.T.astype(bf16)
    odd_out = out_ref[2 * main :].T
    odd = [
        scaled(pick(in_ref[:, 2 * main : hidden]), gain_second),
        scaled(pick(in_ref[:, hidden + 2 * main :]), gain_second),
        pick(odd_out).astype(bf16),
        jnp.zeros((rows, few), bf16),
    ]
    second_ref[:, main:] = jnp.concatenate(odd, axis=1)
    pieces = []
    for at in range(width // 128):
        for part in range(3):
            start = part * width + at * 128
            pieces.append(scaled(pick(qkv_ref[:, start : start + 128]), gain_first))
    heads_ref[...] = jnp.concatenate(pieces, axis=1)
    own = []
    for part in range(3):
        start = pl.multiple_of(part * width + chip * 128, 128)
        own.append(scaled(pick(qkv_ref[:, pl.ds(start, 128)]), gain_first).astype(f32))
    own.append(jnp.zeros((rows, HDIM), f32))
    head_ref[...] = jnp.concatenate(own, axis=1).T[: 3 * HDIM].astype(bf16)


def prepare(place, gains, qkv, attn, weight_in, weight_out):
    rows, width = attn.shape
    hidden = weight_out.shape[0]
    main = hidden // 256 * 128
    arrays = (gains, qkv, attn, weight_in, weight_out)
    shapes = [
        (rows, width // 2 + 2 * main),
        (rows, main + 4 * (hidden // 2 - main)),
        (3 * HDIM, rows),
        (rows, 3 * width // 2),
    ]

    def whole(shape):
        return pl.BlockSpec(shape, lambda i, place: (0, 0))

    return pl.pallas_call(
        prepare_kernel,
        name="prepare",
        grid_spec=pltpu.PrefetchScalarGridSpec(
            num_scalar_prefetch=1,
            grid=(1,),
            in_specs=[whole(array.shape) for array in arrays],
            out_specs=[whole(shape) for shape in shapes],
        ),
        out_shape=[jax.ShapeDtypeStruct(shape, bf16) for shape in shapes],
        compiler_params=pltpu.CompilerParams(vmem_limit_bytes=VMEM),
        cost_estimate=cost(rows * width * 60, 10 << 20),
    )(place, *arrays)


def project_kernel(
    x_ref, w_ref, cos_ref, sin_ref, unit_ref, qkv_ref, keys_ref, values_ref, w_all, *, extra
):
    half = HDIM // 2
    rows = cos_ref.shape[1]

    @pl.when(pl.program_id(0) == 0)
    def _():
        for part in range(w_ref.shape[0]):
            w_all[part * 128 : (part + 1) * 128] = w_ref[part].astype(f32).T.astype(bf16)

    count = (x_ref.shape[0] - rows) // extra
    each = rows // count
    for at in range(count):
        tokens = x_ref[at * (each + extra) : at * (each + extra) + each].astype(f32)
        unit_ref[at * each : (at + 1) * each] = unit_rows(tokens)[0].astype(bf16)
    unit = unit_ref[...]
    mixed = dot(unit, w_all[...]).T
    cosine = cos_ref[...]
    sine = sin_ref[...]

    def turn(one, two):
        return jnp.concatenate([one * cosine - two * sine, two * cosine + one * sine], axis=0)

    queries = turn(mixed[:half], mixed[half:HDIM])
    keys = turn(mixed[HDIM : HDIM + half], mixed[HDIM + half : 2 * HDIM])
    values = mixed[2 * HDIM :]
    qkv_ref[...] = jnp.concatenate([queries, keys, values], axis=0).astype(bf16)
    key_rows = keys.T.astype(bf16)
    value_rows = values.T.astype(bf16)
    ones = jnp.where(lax.broadcasted_iota(jnp.int32, (rows, HDIM), 1) < 3, 1.0, 0.0).astype(bf16)
    keys_ref[...] = jnp.concatenate([key_rows, key_rows, key_rows, ones], axis=1)
    values_ref[...] = jnp.concatenate([value_rows, ones], axis=1)


def project(tokens, weights, cosine, sine, extra, block=1024):
    width = tokens.shape[1]
    length = cosine.shape[1]
    steps = length // block
    return pl.pallas_call(
        functools.partial(project_kernel, extra=extra),
        name="project",
        grid=(steps,),
        in_specs=[
            pl.BlockSpec((tokens.shape[0] // steps, width), lambda i: (i, 0)),
            pl.BlockSpec(weights.shape, lambda i: (0, 0, 0)),
            pl.BlockSpec((HDIM // 2, block), lambda i: (0, i)),
            pl.BlockSpec((HDIM // 2, block), lambda i: (0, i)),
        ],
        out_specs=[
            pl.BlockSpec((block, width), lambda i: (i, 0)),
            pl.BlockSpec((3 * HDIM, block), lambda i: (0, i)),
            pl.BlockSpec((block, 256), lambda i: (i, 0)),
            pl.BlockSpec((block, 128), lambda i: (i, 0)),
        ],
        out_shape=[
            jax.ShapeDtypeStruct((length, width), bf16),
            jax.ShapeDtypeStruct((3 * HDIM, length), bf16),
            jax.ShapeDtypeStruct((length, 256), bf16),
            jax.ShapeDtypeStruct((length, 128), bf16),
        ],
        scratch_shapes=[pltpu.VMEM((width, 3 * HDIM), bf16)],
        compiler_params=pltpu.CompilerParams(vmem_limit_bytes=VMEM),
        cost_estimate=cost(length * width, 1 << 20),
    )(tokens, weights, cosine, sine)


def scaled_queries(queries):
    scaled = queries.astype(f32) * (LOG2E / math.sqrt(HDIM))
    high = scaled.astype(bf16)
    rest = scaled - high.astype(f32)
    middle = rest.astype(bf16)
    low = (rest - middle.astype(f32)).astype(bf16)
    return high, middle, low


def minus_in_three(values):
    rows = values.shape[1]
    at = lax.broadcasted_iota(jnp.int32, (16, rows), 0)
    high = (-values).astype(bf16).astype(f32)
    rest = -values - high
    middle = rest.astype(bf16).astype(f32)
    low = rest - middle
    stacked = jnp.where(at == 0, high, jnp.where(at == 1, middle, jnp.where(at == 2, low, 0.0)))
    return stacked.astype(bf16)


def attend_kernel(
    keys_ref, q_ref, k_ref, v_ref, low_ref, out_ref, lse_ref, v_ones, longest, *, part
):
    length = keys_ref.shape[0]
    count = length // part

    @pl.when(pl.program_id(0) == 0)
    def _():
        v_ones[:HDIM] = v_ref[...]
        v_ones[HDIM:] = jnp.where(
            lax.broadcasted_iota(jnp.int32, (16, length), 0) < 1, 1.0, 0.0
        ).astype(bf16)
        squares = jnp.sum(k_ref[...].astype(f32) ** 2, axis=0, keepdims=True)
        longest[...] = jnp.broadcast_to(jnp.max(squares, axis=1, keepdims=True), longest.shape)

    queries = jnp.concatenate(scaled_queries(q_ref[...]), axis=0)

    def finish(total, shift):
        summed = total[HDIM : HDIM + 1]
        result = total[:HDIM] / summed
        out_ref[...] = result
        lse_ref[...] = shift + jnp.log2(summed)
        step = low_ref.shape[2]
        for at in range(low_ref.shape[0]):
            low_ref[at] = result[:, at * step : (at + 1) * step].astype(bf16)
        return summed

    squares = jnp.sum((q_ref[...].astype(f32) * (LOG2E / math.sqrt(HDIM))) ** 2, axis=0, keepdims=True)
    shift = jnp.sqrt(squares * longest[0:1, 0:1])
    shifted = jnp.concatenate([queries, minus_in_three(shift)], axis=0)

    def score(at):
        return dot(keys_ref[at * part : (at + 1) * part, : 3 * HDIM + 16], shifted)

    scores = score(0)
    total = None
    for at in range(count):
        following = score(at + 1) if at + 1 < count else None
        soft = jnp.exp2(scores).astype(bf16)
        added = dot(v_ones[:, at * part : (at + 1) * part], soft)
        total = added if total is None else total + added
        scores = following
    summed = finish(total, shift)

    @pl.when(jnp.min(summed) < 2.0**-60)
    def _():
        def exact(at, carry):
            highest, total = carry
            rows = pl.ds(pl.multiple_of(at * part, part), part)
            scores = dot(keys_ref[rows, : 3 * HDIM], queries)
            raised = jnp.maximum(highest, jnp.max(scores, axis=0, keepdims=True))
            soft = jnp.exp2(scores - raised).astype(bf16)
            added = dot(v_ones[:, rows], soft)
            return raised, total * jnp.exp2(highest - raised) + added

        start = (
            jnp.full((1, q_ref.shape[1]), -1e30, f32),
            jnp.zeros((HDIM + 16, q_ref.shape[1]), f32),
        )
        highest, total = lax.fori_loop(0, count, exact, start)
        finish(total, highest)


def attend(keys, qkv, chips, block=1024, part=512):
    length = keys.shape[0]
    return pl.pallas_call(
        functools.partial(attend_kernel, part=part),
        name="attend",
        grid=(length // block,),
        in_specs=[
            pl.BlockSpec(keys.shape, lambda i: (0, 0)),
            pl.BlockSpec((HDIM, block), lambda i: (0, i)),
            pl.BlockSpec((HDIM, length), lambda i: (1, 0)),
            pl.BlockSpec((HDIM, length), lambda i: (2, 0)),
        ],
        out_specs=[
            pl.BlockSpec((block * chips // length, HDIM, length // chips), lambda i: (i, 0, 0)),
            pl.BlockSpec((HDIM, block), lambda i: (0, i)),
            pl.BlockSpec((1, block), lambda i: (0, i)),
        ],
        out_shape=[
            jax.ShapeDtypeStruct((chips, HDIM, length // chips), bf16),
            jax.ShapeDtypeStruct((HDIM, length), f32),
            jax.ShapeDtypeStruct((1, length), f32),
        ],
        scratch_shapes=[pltpu.VMEM((HDIM + 16, length), bf16), pltpu.VMEM((8, 128), f32)],
        compiler_params=pltpu.CompilerParams(vmem_limit_bytes=VMEM),
        cost_estimate=cost(length * HDIM, 1 << 20),
    )(keys, qkv, qkv, qkv)


def attend_back_kernel(
    order_ref,
    keys_ref,
    values_ref,
    q_ref,
    k_ref,
    out_ref,
    lse_ref,
    cos_ref,
    sin_ref,
    *rest,
    part,
):
    count = (len(rest) - 3) // 2
    dout_refs, dp_refs, (sums, dq_all, dout_all) = rest[:count], rest[count:-3], rest[-3:]
    half = HDIM // 2
    here = pl.program_id(0)
    length = keys_ref.shape[0]
    block = q_ref.shape[1]
    count = length // part
    factor = HDIM ** (-0.5)

    def turn_back(grads, cosine, sine):
        low = grads.astype(bf16).astype(f32)
        one, two = low[:half], low[half:]
        return jnp.concatenate([one * cosine + two * sine, two * cosine - one * sine], axis=0)

    @pl.when(here == 0)
    def _():
        sums[...] = jnp.zeros_like(sums)
        for place, dout_ref in enumerate(dout_refs):
            dout_all[place] = dout_ref[...]

    low_queries = q_ref[...]
    queries = jnp.concatenate(
        [*scaled_queries(low_queries), minus_in_three(lse_ref[...])], axis=0
    )
    low_dout = dout_all[here]
    dout = low_dout.astype(f32)
    centre = jnp.sum(dout * out_ref[...], axis=0, keepdims=True)
    douts = jnp.concatenate([low_dout, minus_in_three(centre)], axis=0)
    blank = jnp.zeros((block, HDIM), bf16)
    right = jnp.concatenate(
        [
            jnp.concatenate([low_queries.astype(f32).T.astype(bf16), blank], axis=1),
            jnp.concatenate([blank, dout.T.astype(bf16)], axis=1),
        ],
        axis=0,
    )

    def score(at):
        rows = slice(at * part, (at + 1) * part)
        return (
            dot(keys_ref[rows, : 3 * HDIM + 16], queries),
            dot(values_ref[rows, : HDIM + 16], douts),
        )

    now = score(0)
    grad_queries = None
    for at in range(count):
        following = score(at + 1) if at + 1 < count else None
        rows = slice(at * part, (at + 1) * part)
        soft = jnp.exp2(now[0])
        grads = (soft * now[1]).astype(bf16)
        added = dot(k_ref[:, rows], grads)
        grad_queries = added if grad_queries is None else grad_queries + added
        sums[rows] += dot(jnp.concatenate([grads, soft.astype(bf16)], axis=1), right)
        now = following

    def columns_of(place):
        return pl.ds(pl.multiple_of(order_ref[place] * block, block), block)

    columns = columns_of(here)
    dq_all[here] = turn_back(
        grad_queries * factor, cos_ref[:, columns], sin_ref[:, columns]
    ).astype(bf16)

    @pl.when(here == length // block - 1)
    def _():
        for place, dp_ref in enumerate(dp_refs):
            columns = columns_of(place)
            both = sums[columns].T
            dp_ref[:HDIM] = dq_all[place]
            dp_ref[HDIM : 2 * HDIM] = turn_back(
                both[:HDIM] * factor, cos_ref[:, columns], sin_ref[:, columns]
            ).astype(bf16)
            dp_ref[2 * HDIM :] = both[HDIM:].astype(bf16)


def attend_back(order, keys, values, qkv, douts, out, lse, cosine, sine, part=256):
    length = keys.shape[0]
    chips = len(douts)
    block = douts[0].shape[1]
    scores = length * length

    def whole(array):
        return pl.BlockSpec(array.shape, lambda i, order: (0, 0))

    return pl.pallas_call(
        functools.partial(attend_back_kernel, part=part),
        name="attend_back",
        grid_spec=pltpu.PrefetchScalarGridSpec(
            num_scalar_prefetch=1,
            grid=(chips,),
            in_specs=[
                whole(keys),
                whole(values),
                pl.BlockSpec((HDIM, block), lambda i, order: (0, order[i])),
                pl.BlockSpec((HDIM, length), lambda i, order: (1, 0)),
                pl.BlockSpec((HDIM, block), lambda i, order: (0, order[i])),
                pl.BlockSpec((1, block), lambda i, order: (0, order[i])),
                whole(cosine),
                whole(sine),
                *[whole(piece) for piece in douts],
            ],
            out_specs=[pl.BlockSpec((3 * HDIM, block), lambda i, order: (0, 0))] * chips,
            scratch_shapes=[
                pltpu.VMEM((length, 2 * HDIM), f32),
                pltpu.VMEM((chips, HDIM, block), bf16),
                pltpu.VMEM((chips, HDIM, block), bf16),
            ],
        ),
        out_shape=[jax.ShapeDtypeStruct((3 * HDIM, block), bf16)] * chips,
        compiler_params=pltpu.CompilerParams(vmem_limit_bytes=VMEM),
        cost_estimate=cost(5 * 4 * 2 * scores * HDIM, 8 << 20),
    )(order, keys, values, qkv, qkv, out, lse, cosine, sine, *douts)


def attend_out_kernel(order_ref, attended_ref, *rest):
    piece_refs, (mixed_ref, attn_ref) = rest[:-2], rest[-2:]
    half = attn_ref.shape[1] // 2
    at = 0
    for piece_ref in piece_refs:
        for place in range(piece_ref.shape[0]):
            rows = pl.ds(pl.multiple_of(order_ref[at] * HDIM, HDIM), HDIM)
            attn_ref[rows, :half] = piece_ref[place, :HDIM]
            attn_ref[rows, half:] = piece_ref[place, HDIM:]
            at += 1
    turned = attended_ref[...].astype(f32).T.astype(bf16)
    mixed_ref[...] = dot(turned, attn_ref[...]).astype(bf16)


def attend_out(order, attended, pieces):
    size, tokens = attended.shape
    width = 2 * size

    def whole(*shape):
        return pl.BlockSpec(shape, lambda i, order: (0,) * len(shape))

    return pl.pallas_call(
        attend_out_kernel,
        name="attend_out",
        grid_spec=pltpu.PrefetchScalarGridSpec(
            num_scalar_prefetch=1,
            grid=(1,),
            in_specs=[whole(size, tokens)]
            + [whole(*piece.shape[:2], width // 2) for piece in pieces],
            out_specs=[whole(tokens, width), whole(size, width)],
        ),
        out_shape=[
            jax.ShapeDtypeStruct((tokens, width), bf16),
            jax.ShapeDtypeStruct((size, width), bf16),
        ],
        compiler_params=pltpu.CompilerParams(vmem_limit_bytes=VMEM),
        cost_estimate=cost(2 * 2 * tokens * width * size, 4 << 20),
    )(order, attended, *pieces)


def feed_kernel(
    first_order, second_order, x_ref, ours_ref, theirs_ref, g_ref, *rest, firsts, seconds, axes
):
    weight_refs = []
    start = 0
    for size in (firsts, firsts, seconds, seconds):
        weight_refs.append(rest[start : start + size])
        start += size
    planes, lines, wide, beside = axes

    def put(grads, columns):
        size = grads.shape[0] // (planes * lines * wide)
        low = grads.astype(bf16)
        for plane in range(planes):
            for line in range(lines):
                for far in range(wide):
                    source = ((plane * lines + line) * wide + far) * size
                    target = ((line * wide + far) * planes + plane) * size
                    grads_ref[target : target + size, columns] = low[source : source + size]
    residual_ref, partial_ref, back_ref, grads_ref, out_grads_ref = rest[-14:-9]
    unit, unit_t, g_t, sum_out, sum_back = rest[-9:-4]
    gate_ref, up_ref, out_ref, rest_ref = rest[-4:]
    here = pl.program_id(0)
    last = pl.num_programs(0) - 1
    width = x_ref.shape[1]
    step = gate_ref.shape[1]

    def join(total, parts, order):
        at = 0
        for part in parts:
            size = part.shape[1]
            for place in range(part.shape[0]):
                total[pl.ds(pl.multiple_of(order[at] * size, size), size)] = part[place]
                at += 1

    def bend(gate, upward):
        cdf = 0.5 + 0.5 * lax.erf(gate * math.sqrt(0.5))
        slope = cdf + gate * jnp.exp(gate * gate * -0.5) * (1.0 / math.sqrt(2.0 * math.pi))
        bent = gate * cdf
        return bent, slope, (bent * upward).astype(bf16)

    @pl.when(here == 0)
    def _():
        residual = (
            x_ref[...].astype(f32) + ours_ref[...].astype(f32) + theirs_ref[...].astype(f32)
        )
        residual_ref[...] = residual
        normed = unit_rows(residual)[0]
        unit[...] = normed.astype(bf16)
        unit_t[...] = normed.T.astype(bf16)
        g_t[...] = g_ref[...].astype(f32).T.astype(bf16)
        join(rest_ref, weight_refs[3], second_order)
        few = rest_ref.shape[1] // 4
        both = dot(unit[...], rest_ref[...])
        grad = dot(g_ref[...], rest_ref[...])[:, 2 * few : 3 * few]
        bent, slope, active = bend(both[:, :few], both[:, few : 2 * few])
        grad_gate = (grad * both[:, few : 2 * few] * slope).astype(bf16)
        grad_up = (grad * bent).astype(bf16)
        blank = jnp.zeros_like(active)
        outs = jnp.concatenate([blank, blank, active, blank], axis=1)
        ins = jnp.concatenate([grad_gate, grad_up, blank, blank], axis=1)
        sum_out[...] = dot(outs, rest_ref[...], 1, 1)
        sum_back[...] = dot(ins, rest_ref[...], 1, 1)
        out_grads_ref[:, out_grads_ref.shape[1] - 4 * few :] = (
            dot(unit_t[...], ins) + dot(g_t[...], outs)
        ).astype(bf16)

    join(gate_ref, weight_refs[0], first_order)
    join(up_ref, weight_refs[1], first_order)
    join(out_ref, weight_refs[2], second_order)
    gate = dot(unit[...], gate_ref[...])
    upward = dot(unit[...], up_ref[...])
    grad = dot(g_ref[...], out_ref[...])
    bent, slope, active = bend(gate, upward)
    grad_gate = (grad * upward * slope).astype(bf16)
    grad_up = (grad * bent).astype(bf16)
    sum_out[...] += dot(active, out_ref[...], 1, 1)
    sum_back[...] += dot(grad_gate, gate_ref[...], 1, 1) + dot(grad_up, up_ref[...], 1, 1)
    count = grads_ref.shape[1] // step // 2
    put(dot(unit_t[...], grad_gate), pl.ds(pl.multiple_of(here * step, 128), step))
    put(dot(unit_t[...], grad_up), pl.ds(pl.multiple_of((count + here) * step, 128), step))
    out_grads_ref[:, pl.ds(pl.multiple_of(here * step, 128), step)] = dot(
        g_t[...], active
    ).astype(bf16)

    @pl.when(here == last)
    def _():
        partial_ref[...] = sum_out[...].astype(bf16)
        back_ref[...] = sum_back[...].astype(bf16)


def feed(first_order, second_order, x, ours, theirs, g, first, second, axes, step=256):
    tokens, width = x.shape
    start = width // 2 // step
    count = (first[0].shape[2] - width // 2) // step // 2
    rest = second[0].shape[2] - count * step

    def whole(*shape):
        return pl.BlockSpec(shape, lambda i, one, two: (0, 0))

    def piece(arrays, size, at):
        return [
            pl.BlockSpec((*array.shape[:2], size), lambda i, one, two: (0, 0, at(i)))
            for array in arrays
        ]

    pair = jax.ShapeDtypeStruct((tokens, width), bf16)
    return pl.pallas_call(
        functools.partial(feed_kernel, firsts=len(first), seconds=len(second), axes=axes),
        name="feed",
        grid_spec=pltpu.PrefetchScalarGridSpec(
            num_scalar_prefetch=2,
            grid=(count,),
            in_specs=[whole(tokens, width)] * 4
            + piece(first, step, lambda i: start + i)
            + piece(first, step, lambda i: start + count + i)
            + piece(second, step, lambda i: i)
            + piece(second, rest, lambda i: count * step // rest),
            out_specs=[whole(tokens, width)] * 3
            + [whole(width, 2 * count * step), whole(width, count * step + rest)],
            scratch_shapes=[
                pltpu.VMEM((tokens, width), bf16),
                pltpu.VMEM((width, tokens), bf16),
                pltpu.VMEM((width, tokens), bf16),
                pltpu.VMEM((tokens, width), f32),
                pltpu.VMEM((tokens, width), f32),
                pltpu.VMEM((width, step), bf16),
                pltpu.VMEM((width, step), bf16),
                pltpu.VMEM((width, step), bf16),
                pltpu.VMEM((width, rest), bf16),
            ],
        ),
        out_shape=[
            jax.ShapeDtypeStruct((tokens, width), f32),
            pair,
            pair,
            jax.ShapeDtypeStruct((width, 2 * count * step), bf16),
            jax.ShapeDtypeStruct((width, count * step + rest), bf16),
        ],
        compiler_params=pltpu.CompilerParams(vmem_limit_bytes=VMEM),
        cost_estimate=cost(2 * 9 * 2 * tokens * width * count * step, 24 << 20),
    )(first_order, second_order, x, ours, theirs, g, *first, *first, *second, *second)


def middle_back_kernel(
    core_ref, order_ref, line_ref, residual_ref, g_ref, ours_ref, theirs_ref, attn_ref,
    attended_ref, out_ours_ref, out_theirs_ref, layer_ref, residual_grad_ref, *rest, axes,
):
    planes, lines, wide, beside = axes
    dout_refs, grads_refs, (dout_all, grads_all) = rest[: -2 - lines], rest[-2 - lines : -2], rest[-2:]
    rows = layer_ref.shape[0]
    half = attn_ref.shape[0]
    own = pl.ds(pl.multiple_of(core_ref[0] * rows, rows), rows)
    layer_ref[...] = (
        residual_ref[own, :]
        + out_ours_ref[own, :].astype(f32)
        + out_theirs_ref[...].astype(f32)
    ).astype(bf16)
    unit, inverse = unit_rows(residual_ref[...])
    scaled = ours_ref[...].astype(f32) + theirs_ref[...].astype(f32)
    grad = g_ref[...].astype(f32) + unit_back(scaled, unit, inverse)
    low = grad.astype(bf16)
    residual_grad_ref[...] = grad
    dout_all[...] = dot(attn_ref[...], low, 1, 1).astype(bf16)
    for at, dout_ref in enumerate(dout_refs):
        dout_ref[...] = dout_all[pl.ds(pl.multiple_of(order_ref[at] * HDIM, HDIM), HDIM)]
    grads_all[...] = dot(attended_ref[...], low)
    few = HDIM // wide // beside
    for shift, grads_ref in enumerate(grads_refs):
        line = (line_ref[0] + shift) % lines
        blocks = [
            grads_all[pl.ds(pl.multiple_of((plane * lines + line) * HDIM, HDIM), HDIM)]
            for plane in range(planes)
        ]
        pieces = []
        for far in range(wide):
            for plane in range(planes):
                for near in range(beside):
                    start = (far * beside + near) * few
                    piece = blocks[plane][start : start + few]
                    pieces += [piece[:, :half], piece[:, half:]]
        grads_ref[...] = jnp.concatenate(pieces, axis=0).astype(bf16)


def middle_back(
    core, order, line, residual, g, ours, theirs, attn, attended, out_ours, out_theirs, axes
):
    tokens, width = residual.shape
    rows = tokens // 2
    half = width // 2
    chips = half // HDIM
    lines = axes[1]

    def whole(*shape):
        return pl.BlockSpec(shape, lambda i, core, order, line: (0,) * len(shape))

    return pl.pallas_call(
        functools.partial(middle_back_kernel, axes=axes),
        name="middle_back",
        grid_spec=pltpu.PrefetchScalarGridSpec(
            num_scalar_prefetch=3,
            grid=(1,),
            in_specs=[whole(tokens, width)] * 4
            + [whole(half, width), whole(half, tokens), whole(tokens, width), whole(rows, width)],
            out_specs=[whole(rows, width), whole(tokens, width)]
            + [whole(HDIM, tokens)] * chips
            + [whole(width // lines, half)] * lines,
            scratch_shapes=[pltpu.VMEM((half, tokens), bf16), pltpu.VMEM((half, width), f32)],
        ),
        out_shape=[
            jax.ShapeDtypeStruct((rows, width), bf16),
            jax.ShapeDtypeStruct((tokens, width), f32),
        ]
        + [jax.ShapeDtypeStruct((HDIM, tokens), bf16)] * chips
        + [jax.ShapeDtypeStruct((width // lines, half), bf16)] * lines,
        compiler_params=pltpu.CompilerParams(vmem_limit_bytes=VMEM),
        cost_estimate=cost(2 * 2 * 2 * tokens * width * half, 16 << 20),
    )(core, order, line, residual, g, ours, theirs, attn, attended, out_ours, out_theirs)


def hidden_back_kernel(order_ref, core_ref, shard_ref, w_ref, *rest):
    dp_refs, (own_ref, other_ref, stacked) = rest[:-3], rest[-3:]
    for place, dp_ref in enumerate(dp_refs):
        size = dp_ref.shape[0]
        stacked[pl.ds(pl.multiple_of(order_ref[place] * size, 64), size)] = dp_ref[...]
    rows = own_ref.shape[0]
    zero = core_ref[0] == 0
    size = w_ref.shape[1]
    for at in range(w_ref.shape[0]):
        flat = dot(w_ref[at], stacked[...])
        first = flat[:, :rows].T
        second = flat[:, rows:].T
        columns = pl.ds(pl.multiple_of(shard_ref[at] * size, size), size)
        own_ref[:, columns] = jnp.where(zero, first, second)
        other_ref[:, columns] = jnp.where(zero, second, first).astype(bf16)


def hidden_back(order, core, shard_order, weights, pieces):
    shards, size, columns = weights.shape
    width = shards * size
    rows = pieces[0].shape[1] // 2

    def whole(*shape):
        return pl.BlockSpec(shape, lambda i, order, core, shard: (0,) * len(shape))

    return pl.pallas_call(
        hidden_back_kernel,
        name="hidden_back",
        grid_spec=pltpu.PrefetchScalarGridSpec(
            num_scalar_prefetch=3,
            grid=(1,),
            in_specs=[whole(shards, size, columns)] + [whole(*pieces[0].shape)] * len(pieces),
            out_specs=[whole(rows, width)] * 2,
            scratch_shapes=[pltpu.VMEM((columns, 2 * rows), bf16)],
        ),
        out_shape=[
            jax.ShapeDtypeStruct((rows, width), f32),
            jax.ShapeDtypeStruct((rows, width), bf16),
        ],
        compiler_params=pltpu.CompilerParams(vmem_limit_bytes=VMEM),
        cost_estimate=cost(2 * 2 * 2 * rows * width * columns, 8 << 20),
    )(order, core, shard_order, weights, *pieces)


def head_grad_kernel(order_ref, owner_ref, unit_ref, *rest, owners):
    dp_refs, out_refs, out_all = rest[: -1 - owners], rest[-1 - owners : -1], rest[-1]
    block = dp_refs[0].shape[1]
    total = None
    for place, dp_ref in enumerate(dp_refs):
        rows = pl.ds(pl.multiple_of(order_ref[place] * block, block), block)
        added = dot(dp_ref[...], unit_ref[rows])
        total = added if total is None else total + added
    for at in range(owners):
        out_all[at] = total[:, at * 128 : (at + 1) * 128].astype(bf16)
    for at, out_ref in enumerate(out_refs):
        out_ref[...] = out_all[owner_ref[at]]


def head_grad(order, owner_order, unit_all, pieces):
    length, width = unit_all.shape
    owners = width // 128
    size = pieces[0].shape[0]

    def whole(*shape):
        return pl.BlockSpec(shape, lambda i, order, owner: (0,) * len(shape))

    return pl.pallas_call(
        functools.partial(head_grad_kernel, owners=owners),
        name="head_grad",
        grid_spec=pltpu.PrefetchScalarGridSpec(
            num_scalar_prefetch=2,
            grid=(1,),
            in_specs=[whole(length, width)] + [whole(*pieces[0].shape)] * len(pieces),
            out_specs=[whole(size, 128)] * owners,
            scratch_shapes=[pltpu.VMEM((owners, size, 128), bf16)],
        ),
        out_shape=[jax.ShapeDtypeStruct((size, 128), bf16)] * owners,
        compiler_params=pltpu.CompilerParams(vmem_limit_bytes=VMEM),
        cost_estimate=cost(2 * 2 * length * width * size, 10 << 20),
    )(order, owner_order, unit_all, *pieces)


def adam_in_kernels(weight, gradient, first, second, rate):
    first = BETA_FIRST * first + (1.0 - BETA_FIRST) * gradient
    second = BETA_SECOND * second + (1.0 - BETA_SECOND) * gradient * gradient
    second_hat = second * (1.0 / (1.0 - BETA_SECOND**STEP))
    bottom = second_hat * lax.rsqrt(second_hat) + EPSILON
    guess = pl.reciprocal(bottom, approx=True)
    guess = guess * (2.0 - bottom * guess)
    scale = rate / (1.0 - BETA_FIRST**STEP)
    weight = weight * (1.0 - rate * DECAY) - (scale * first) * guess
    return (weight, first, second)


def adam_into(refs, weight, gradient, first, second, rate):
    for ref, value in zip(refs, adam_in_kernels(weight, gradient, first, second, rate)):
        ref[...] = value


def rounded_in_kernel(values):
    return values.astype(bf16).astype(f32)


def adam_most_kernel(grads_ref, gain_ref, other_gain_ref, *refs, rates):
    (w_in, m_in, v_in), attn, out, gains = refs[:3], refs[3:6], refs[6:9], refs[9:12]
    new_in, new_attn, new_out, new_gains = refs[12:15], refs[15:18], refs[18:21], refs[21:24]
    gain_grad, turned = refs[24:]
    here = pl.program_id(0)
    chips = grads_ref.shape[0] // 2
    width = w_in.shape[1] // 2
    main = width // 256 * 128
    few = width // 2 - main
    out_at = 2 * main + attn[0].shape[2] // 2

    @pl.when(here == 0)
    def _():
        for core in range(2):
            columns = jnp.concatenate(
                [grads_ref[2 * chip + core, :, out_at : out_at + main] for chip in range(chips)],
                axis=0,
            )
            turned[core * main : (core + 1) * main] = columns.astype(f32).T
            rest = jnp.concatenate(
                [
                    grads_ref[2 * chip + core, :, out_at + main :] for chip in range(chips)
                ],
                axis=0,
            )
            start = 2 * main + core * few
            turned[start : start + few] = rest.astype(f32).T[2 * few : 3 * few]

    each = grads_ref.shape[1]
    some = w_in.shape[0] // each
    for at_chip in range(some):
        source = 2 * (here * some + at_chip)
        columns = []
        for at in range(2):
            for core in range(2):
                place = at * main
                columns.append(grads_ref[source + core, :, place : place + main].astype(f32))
            for core in range(2):
                rest = grads_ref[source + core, :, out_at + main :].astype(f32)
                columns.append(rest[:, at * few : (at + 1) * few])
        grads = jnp.concatenate(columns, axis=1)
        rows = slice(at_chip * each, (at_chip + 1) * each)
        weight = w_in[rows]
        gain_rows = pl.ds(pl.multiple_of((here * some + at_chip) * each, each), each)
        gain_grad[gain_rows] = jnp.sum(
            grads * rounded_in_kernel(weight), axis=1, keepdims=True
        )
        values = adam_in_kernels(
            weight, grads * gain_ref[rows], m_in[rows], v_in[rows], rates[0]
        )
        for ref, value in zip(new_in, values):
            ref[rows] = value
        rows = slice(at_chip * each // 2, (at_chip + 1) * each // 2)
        for core in range(2):
            piece = grads_ref[source + core, :, 2 * main : out_at].astype(f32)
            grads = jnp.concatenate([piece[: each // 2], piece[each // 2 :]], axis=1)
            values = adam_in_kernels(
                attn[0][core, rows], grads, attn[1][core, rows], attn[2][core, rows], rates[1]
            )
            for ref, value in zip(new_attn, values):
                ref[core, rows] = value

    size = out[0].shape[0]
    grads = turned[pl.ds(pl.multiple_of(here * size, 8), size)]
    adam_into(new_out, out[0][...], grads, out[1][...], out[2][...], rates[2])

    @pl.when(here == pl.num_programs(0) - 1)
    def _():
        both = jnp.concatenate(
            [other_gain_ref[...], gain_grad[...], jnp.zeros((gain_grad.shape[0], 6), f32)], axis=1
        )
        adam_into(
            new_gains, gains[0][...], both.T[:2], gains[1][...], gains[2][...], GAIN_RATE
        )


def adam_most(
    grads, gain, other_gain, weights_in, weights_attn, weights_out, gains, rates, steps=2
):
    rows, columns = weights_in[0].shape
    width = weights_attn[0].shape[1]
    hidden = weights_out[0].shape[0]
    weights_attn = [array.reshape(2, rows // 2, width) for array in weights_attn]
    block_in = pl.BlockSpec((rows // steps, columns), lambda i: (i, 0))
    block_attn = pl.BlockSpec((2, rows // 2 // steps, width), lambda i: (0, i, 0))
    block_out = pl.BlockSpec((hidden // steps, rows), lambda i: (i, 0))
    column = pl.BlockSpec((rows // steps, 1), lambda i: (i, 0))
    whole_column = pl.BlockSpec((rows, 1), lambda i: (0, 0))
    block_gains = pl.BlockSpec(gains[0].shape, lambda i: (0, 0))
    blocks = [block_in] * 3 + [block_attn] * 3 + [block_out] * 3 + [block_gains] * 3
    arrays = (*weights_in, *weights_attn, *weights_out, *gains)
    results = pl.pallas_call(
        functools.partial(adam_most_kernel, rates=rates),
        name="adam_most",
        grid=(steps,),
        in_specs=[pl.BlockSpec(grads.shape, lambda i: (0, 0, 0)), column, whole_column] + blocks,
        out_specs=blocks,
        out_shape=[jax.ShapeDtypeStruct(array.shape, f32) for array in arrays],
        scratch_shapes=[pltpu.VMEM((rows, 1), f32), pltpu.VMEM((hidden, rows), f32)],
        compiler_params=pltpu.CompilerParams(vmem_limit_bytes=VMEM),
        cost_estimate=cost(rows * columns * 20, rows * columns * 26),
    )(grads, gain, other_gain, *arrays)
    new_attn = [array.reshape(rows, width) for array in results[3:6]]
    return results[:3], new_attn, results[6:9], results[9:]


def adam_qkv_kernel(order_ref, *refs, rate):
    grads_refs, (gain_ref, w_ref, m_ref, v_ref, new_w, new_m, new_v, gain_grad, joined) = (
        refs[:-9], refs[-9:]
    )
    here = pl.program_id(0)
    heads = sum(grads_ref.shape[0] for grads_ref in grads_refs)

    @pl.when(here == 0)
    def _():
        at = 0
        for grads_ref in grads_refs:
            for place in range(grads_ref.shape[0]):
                for part in range(3):
                    row = (part * heads + order_ref[at]) * HDIM
                    joined[pl.ds(pl.multiple_of(row, HDIM), HDIM)] = grads_ref[
                        place, part * HDIM : (part + 1) * HDIM
                    ].astype(f32)
                at += 1

    size = w_ref.shape[1]
    grads = joined[pl.ds(pl.multiple_of(here * size, size), size)].T
    weight = w_ref[...]
    added = jnp.sum(grads * rounded_in_kernel(weight), axis=1, keepdims=True)
    gain_grad[...] = added + jnp.where(here == 0, 0.0, gain_grad[...])
    adam_into(
        (new_w, new_m, new_v), weight, grads * gain_ref[...], m_ref[...], v_ref[...], rate
    )


def adam_qkv(order, grads, gain, weight, first, second, rate, step=1536):
    rows, columns = weight.shape
    block = pl.BlockSpec((rows, step), lambda i, order: (0, i))
    column = pl.BlockSpec((rows, 1), lambda i, order: (0, 0))
    same = jax.ShapeDtypeStruct((rows, columns), f32)
    return pl.pallas_call(
        functools.partial(adam_qkv_kernel, rate=rate),
        name="adam_qkv",
        grid_spec=pltpu.PrefetchScalarGridSpec(
            num_scalar_prefetch=1,
            grid=(columns // step,),
            in_specs=[pl.BlockSpec(piece.shape, lambda i, order: (0, 0, 0)) for piece in grads]
            + [column]
            + [block] * 3,
            out_specs=[block] * 3 + [column],
            scratch_shapes=[pltpu.VMEM((columns, rows), f32)],
        ),
        out_shape=[same] * 3 + [jax.ShapeDtypeStruct((rows, 1), f32)],
        compiler_params=pltpu.CompilerParams(vmem_limit_bytes=VMEM),
        cost_estimate=cost(rows * columns * 20, rows * columns * 26),
    )(order, *grads, gain, weight, first, second)


def ring(axis, shift):
    size = lax.axis_size(axis)
    return [(at, (at + shift) % size) for at in range(size)]


def gather_first_step(planes_first, lines_first):
    swapped = lax.ppermute(planes_first, "zh", SWAP)
    others = [
        lax.ppermute(lines_first, "y", ring("y", shift)) for shift in range(1, lax.axis_size("y"))
    ]
    return jnp.stack([planes_first, swapped]), jnp.stack([lines_first, *others])


def shards(
    tokens,
    positions,
    cotangent,
    weight_qkv,
    weight_attn,
    weight_in,
    weight_out,
    norm_gains,
    first_qkv,
    first_attn,
    first_in,
    first_out,
    first_gains,
    second_qkv,
    second_attn,
    second_in,
    second_out,
    second_gains,
):
    rows, width = tokens.shape[1:]
    shard_rows = weight_qkv.shape[1]
    heads = width // HDIM
    hidden = weight_out.shape[1]
    core = lax.axis_index("c")
    mine = lax.axis_index(CTX)
    chip = lax.axis_index(CHIPS)
    chips = lax.axis_size(CHIPS)
    owners = lax.axis_size(FSDP)
    length = rows * chips * 2
    main = hidden // 256 * 128
    few = hidden // 2 - main
    core_at = core.reshape(1).astype(jnp.int32)
    axes = (lax.axis_size("zh"), lax.axis_size("y"), lax.axis_size("x"), lax.axis_size("zl"))
    offsets = [(far, near) for far in range(lax.axis_size("x")) for near in range(2)]
    across, beside = lax.axis_index("x"), lax.axis_index("zl")
    wide = lax.axis_size("x")

    def chips_at(sign):
        places = [(across + sign * far) % wide * 2 + (beside ^ near) for far, near in offsets]
        return jnp.stack(places).astype(jnp.int32)

    local = tokens[0]
    extra = 16
    high, low = positions[0] // 128, positions[0] % 128
    places_row = jnp.concatenate([high, low, jnp.zeros((width - 2 * rows,), jnp.int32)])
    places_rows = jnp.concatenate(
        [places_row[None], jnp.zeros((extra - 1, width), jnp.int32)], axis=0
    ).astype(bf16)
    sequence = lax.all_gather(
        jnp.concatenate([local, places_rows], axis=0), CTX, axis=0, tiled=True
    )
    first_part, second_part, head_part, half_heads = prepare(
        jnp.stack([core, chip]).astype(jnp.int32),
        norm_gains[0],
        weight_qkv[0],
        weight_attn[0],
        weight_in[0],
        weight_out[0],
    )
    first_joined, second_joined = gather_first_step(first_part, second_part)
    head_weights = lax.all_to_all(
        jnp.broadcast_to(head_part, (owners, *head_part.shape)), FSDP, 0, 0, tiled=True
    )
    first_pieces = [first_joined] + [
        lax.ppermute(first_joined, "y", ring("y", shift))
        for shift in range(1, lax.axis_size("y"))
    ]
    sequence, _, second_joined, half_heads, _ = lax.optimization_barrier(
        (sequence, first_joined, second_joined, half_heads, head_weights)
    )
    half_heads_other = lax.ppermute(half_heads, "zh", SWAP)
    second_pieces = [second_joined, lax.ppermute(second_joined, "zh", SWAP)]
    lines = lax.axis_size("y")
    plane, line = lax.axis_index("zh"), lax.axis_index("y")
    heads_order = jnp.stack(
        [(plane ^ far) * lines + at for at in range(lines) for far in range(2)]
    ).astype(jnp.int32)
    first_order = jnp.stack(
        [(plane ^ far) * lines + (line - shift) % lines for shift in range(lines) for far in range(2)]
    ).astype(jnp.int32)
    second_order = jnp.stack(
        [(plane ^ far) * lines + (line - shift) % lines for far in range(2) for shift in range(lines)]
    ).astype(jnp.int32)

    def in_order(ours, theirs):
        first = jnp.where(core == 0, ours, theirs)
        second = jnp.where(core == 0, theirs, ours)
        return jnp.concatenate([first, second], axis=0)

    def swap(array):
        return lax.ppermute(array, "c", SWAP)

    gradient = in_order(cotangent[0], swap(cotangent[0]))

    freqs = jnp.exp(jnp.arange(HDIM // 2, dtype=f32) * (-2.0 * math.log(ROPE_BASE) / HDIM))
    by_device = sequence.reshape(2 * chips, rows + extra, width)[:, rows]
    by_device = by_device.astype(f32)
    places = by_device[:, :rows] * 128.0 + by_device[:, rows : 2 * rows]
    angles = freqs[:, None] * places.reshape(1, length)
    cosine = jnp.cos(angles)
    sine = jnp.sin(angles)
    unit_all, qkv, keys, values = project(sequence, head_weights, cosine, sine, extra)
    low_out, out, lse = attend(keys, qkv, chips)
    firsts = len(first_pieces)
    low_out, half_heads_other, *arrived = lax.optimization_barrier(
        (low_out, half_heads_other, *first_pieces, *second_pieces)
    )
    first_pieces, second_pieces = arrived[:firsts], arrived[firsts:]
    mat_qkv = lax.all_gather(
        jnp.stack([half_heads, half_heads_other]), "y", axis=0, tiled=True
    )
    attended = lax.all_to_all(low_out, CHIPS, 0, 0, tiled=True)
    attended = attended.reshape(heads // 2 * HDIM, 2 * rows)
    mixed, mat_attn = attend_out(first_order, attended, first_pieces)
    current = lax.dynamic_slice_in_dim(
        sequence, chip * 2 * (rows + extra), 2 * (rows + extra), 0
    ).reshape(2, rows + extra, width)[:, :rows].reshape(2 * rows, width)
    residual, partial, back, grads, out_grads = feed(
        first_order, second_order, current, mixed, swap(mixed), gradient, first_pieces,
        second_pieces, axes,
    )
    grads, mat_qkv = lax.optimization_barrier((grads, mat_qkv))
    first_sum = lax.psum_scatter(grads, "y", scatter_dimension=0, tiled=True)

    def move(pieces, sign):
        moved = [pieces[0]]
        for (far, near), piece in list(zip(offsets, pieces))[1:]:
            pairs = [
                (at, (at // 2 + sign * far) % wide * 2 + (at % 2 ^ near)) for at in range(chips)
            ]
            moved.append(lax.ppermute(piece, CHIPS, pairs))
        return moved

    ahead, behind = chips_at(1), chips_at(-1)
    theirs = swap(lax.dynamic_slice_in_dim(partial, (1 - core) * rows, rows, 0))
    layer_out, residual_grad, *pieces = middle_back(
        core_at, ahead, line.reshape(1).astype(jnp.int32), residual, gradient, back, swap(back),
        mat_attn, attended, partial, theirs, axes,
    )
    dout_pieces, attn_pieces = pieces[:chips], pieces[chips:]

    douts = move(dout_pieces, 1)
    attn_arrived = attn_pieces[:1] + [
        lax.ppermute(piece, "y", ring("y", shift))
        for shift, piece in list(enumerate(attn_pieces))[1:]
    ]
    out_grads, *douts = lax.optimization_barrier((out_grads, *douts))
    out_arrived = lax.all_to_all(out_grads, FSDP + CHIPS, 0, 0, tiled=True)
    pieces = attend_back(behind, keys, values, qkv, douts, out, lse, cosine, sine)
    out_arrived, *rest = lax.optimization_barrier((out_arrived, *pieces, *attn_arrived))
    pieces, attn_arrived = rest[:chips], rest[chips:]
    def total(arrays):
        return sum(array.astype(f32) for array in arrays).astype(bf16)

    first_sum = jnp.concatenate([first_sum, total(attn_arrived)], axis=1)
    first_sum, *pieces = lax.optimization_barrier((first_sum, *pieces))
    moved = move(pieces, -1)
    owner_places = [(far, shift) for far in range(2) for shift in range(lines)]
    owner_order = jnp.stack(
        [(plane ^ far) * lines + (line + shift) % lines for far, shift in owner_places]
    ).astype(jnp.int32)
    head_parts = head_grad(behind, owner_order, unit_all, pieces)

    out_arrived = out_arrived.reshape(owners * chips, shard_rows // chips, -1)
    out_sum = jnp.sum(out_arrived.astype(f32), axis=0).astype(bf16)
    arrived = lax.all_to_all(first_sum, ("x", "zh", "zl"), 0, 0, tiled=True)
    arrived, *rest = lax.optimization_barrier((arrived, *moved, *head_parts))
    moved, head_parts = rest[:chips], rest[chips:]
    own_hidden, other_hidden = hidden_back(ahead, core_at, heads_order, mat_qkv, moved)
    grad_hidden = own_hidden + swap(other_hidden).astype(f32)
    unit_in, scale_in = unit_rows(local.astype(f32))
    own_residual = lax.dynamic_slice_in_dim(residual_grad, core * rows, rows, 0)
    tokens_grad = (own_residual + unit_back(grad_hidden, unit_in, scale_in))[None]

    head_arrived = [head_parts[0]]
    for (far, shift), piece in list(zip(owner_places, head_parts))[1:]:
        pairs = [
            (at, (at // lines ^ far) * lines + (at % lines + shift) % lines) for at in range(owners)
        ]
        head_arrived.append(lax.ppermute(piece, FSDP, pairs))
    head_own = total(head_arrived)[None]
    arrived = arrived.reshape(2 * chips, shard_rows // chips, -1)
    second_sum = jnp.sum(arrived.astype(f32), axis=0).astype(bf16)
    second_sum = jnp.concatenate([second_sum, out_sum], axis=1)
    all_grads = lax.all_gather(second_sum, CTX, axis=0, tiled=False)

    head_pair = jnp.concatenate([head_own, swap(head_own)], axis=0)
    head_four = jnp.concatenate([head_pair, lax.ppermute(head_pair, "zl", SWAP)], axis=0)
    head_grads = [head_four] + [
        lax.ppermute(head_four, "x", ring("x", shift)) for shift in range(1, wide)
    ]
    head_order = jnp.stack(
        [
            (across - shift) % wide * 4 + (beside ^ near) * 2 + (core ^ other)
            for shift in range(wide)
            for near in range(2)
            for other in range(2)
        ]
    ).astype(jnp.int32)

    rates = (
        width ** (-0.5),
        max(1, 3 * width // length) ** (-0.5),
        width ** (-0.5),
        hidden ** (-0.5),
    )
    columns_of_gains = norm_gains[0].astype(bf16).astype(f32).T
    *new_qkv, gain_first = adam_qkv(
        head_order, head_grads, columns_of_gains[:, :1], weight_qkv[0], first_qkv[0], second_qkv[0], rates[0]
    )
    new_in, new_attn, new_out, new_gains = adam_most(
        all_grads,
        columns_of_gains[:, 1:],
        gain_first,
        (weight_in[0], first_in[0], second_in[0]),
        (weight_attn[0], first_attn[0], second_attn[0]),
        (weight_out[0], first_out[0], second_out[0]),
        (norm_gains[0], first_gains[0], second_gains[0]),
        (rates[2], rates[1], rates[3]),
    )
    updated = (new_qkv, new_attn, new_in, new_out, new_gains)
    return (
        layer_out[None],
        tokens_grad,
        *[updated[member][0][None] for member in range(5)],
        *[updated[member][1][None] for member in range(5)],
        *[updated[member][2][None] for member in range(5)],
    )


def solution(mesh):
    split = Mesh(mesh.devices.reshape(4, 2, 2, 2, 4), ("x", "zl", "c", "zh", "y"))
    by_row = P(None, FSDP, None)
    by_column = P(None, None, FSDP)
    weights = (by_row, by_row, by_row, by_column, by_column)
    by_token = P(FSDP, CTX, None)
    return jax.shard_map(
        shards,
        mesh=split,
        in_specs=(by_token, P(FSDP, CTX), by_token) + weights * 3,
        out_specs=(by_token, by_token) + weights * 3,
        check_vma=False,
    )
```

```python
import functools
import math

import jax
import jax.numpy as jnp
from jax import lax
from jax.experimental import pallas as pl
from jax.experimental.pallas import tpu as pltpu
from jax.sharding import Mesh, PartitionSpec as P

HDIM = 64
STEP = 10
BETA_FIRST = 0.5
BETA_SECOND = 0.5
EPSILON = 1e-08
DECAY = 0.01
NORM_EPS = 1e-05
ROPE_BASE = 160000.0
GAIN_RATE = 0.6
LOG2E = math.log2(math.e)
f32 = jnp.float32
bf16 = jnp.bfloat16

CHIPS = ("x", "zl")
CTX = ("x", "zl", "c")
FSDP = ("zh", "y")
SWAP = [(0, 1), (1, 0)]
VMEM = 60 << 20


def dot(left, right, left_dim=1, right_dim=0):
    return lax.dot_general(
        left, right, (((left_dim,), (right_dim,)), ((), ())), preferred_element_type=f32
    )


def cost(flops, moved):
    return pl.CostEstimate(flops=flops, bytes_accessed=moved, transcendentals=0)


def unit_rows(values):
    average = jnp.mean(values, axis=-1, keepdims=True)
    centered = values - average
    spread = jnp.mean(centered * centered, axis=-1, keepdims=True)
    inverse = lax.rsqrt(spread + NORM_EPS)
    return centered * inverse, inverse


def unit_back(scaled, unit, inverse):
    first_mean = jnp.mean(scaled, axis=-1, keepdims=True)
    second_mean = jnp.mean(scaled * unit, axis=-1, keepdims=True)
    return inverse * (scaled - first_mean - unit * second_mean)


def prepare_kernel(
    place_ref, gains_ref, qkv_ref, attn_ref, in_ref, out_ref,
    first_ref, second_ref, head_ref, heads_ref,
):
    core, chip = place_ref[0], place_ref[1]
    rows = qkv_ref.shape[0]
    width = attn_ref.shape[1]
    hidden = out_ref.shape[0]
    main = hidden // 256 * 128
    few = hidden // 2 - main
    half = width // 2
    low_gains = gains_ref[...].astype(bf16).astype(f32)
    columns = jnp.concatenate([low_gains, jnp.zeros((6, rows), f32)], axis=0).T
    gain_first, gain_second = columns[:, 0:1], columns[:, 1:2]

    def pick(array):
        size = array.shape[1] // 2
        return jnp.where(core == 0, array[:, :size], array[:, size:])

    def scaled(values, gain):
        return (values.astype(bf16).astype(f32) * gain).astype(bf16)

    attn_rows = attn_ref[pl.ds(pl.multiple_of(core * HDIM, HDIM), HDIM)].astype(bf16)
    first_ref[:HDIM, :half] = attn_rows[:, :half]
    first_ref[HDIM:, :half] = attn_rows[:, half:]
    first_ref[:, half : half + main] = scaled(pick(in_ref[:, : 2 * main]), gain_second)
    first_ref[:, half + main :] = scaled(pick(in_ref[:, hidden : hidden + 2 * main]), gain_second)
    out_rows = out_ref[pl.ds(pl.multiple_of(core * main, 128), main)]
    second_ref[:, :main] = out_rows.T.astype(bf16)
    odd_out = out_ref[2 * main :].T
    odd = [
        scaled(pick(in_ref[:, 2 * main : hidden]), gain_second),
        scaled(pick(in_ref[:, hidden + 2 * main :]), gain_second),
        pick(odd_out).astype(bf16),
        jnp.zeros((rows, few), bf16),
    ]
    second_ref[:, main:] = jnp.concatenate(odd, axis=1)
    pieces = []
    for at in range(width // 128):
        for part in range(3):
            start = part * width + at * 128
            pieces.append(scaled(pick(qkv_ref[:, start : start + 128]), gain_first))
    heads_ref[...] = jnp.concatenate(pieces, axis=1)
    own = []
    for part in range(3):
        start = pl.multiple_of(part * width + chip * 128, 128)
        own.append(scaled(pick(qkv_ref[:, pl.ds(start, 128)]), gain_first).astype(f32))
    own.append(jnp.zeros((rows, HDIM), f32))
    head_ref[...] = jnp.concatenate(own, axis=1).T[: 3 * HDIM].astype(bf16)


def prepare(place, gains, qkv, attn, weight_in, weight_out):
    rows, width = attn.shape
    hidden = weight_out.shape[0]
    main = hidden // 256 * 128
    arrays = (gains, qkv, attn, weight_in, weight_out)
    shapes = [
        (rows, width // 2 + 2 * main),
        (rows, main + 4 * (hidden // 2 - main)),
        (3 * HDIM, rows),
        (rows, 3 * width // 2),
    ]

    def whole(shape):
        return pl.BlockSpec(shape, lambda i, place: (0, 0))

    return pl.pallas_call(
        prepare_kernel,
        name="prepare",
        grid_spec=pltpu.PrefetchScalarGridSpec(
            num_scalar_prefetch=1,
            grid=(1,),
            in_specs=[whole(array.shape) for array in arrays],
            out_specs=[whole(shape) for shape in shapes],
        ),
        out_shape=[jax.ShapeDtypeStruct(shape, bf16) for shape in shapes],
        compiler_params=pltpu.CompilerParams(vmem_limit_bytes=VMEM),
        cost_estimate=cost(rows * width * 60, 10 << 20),
    )(place, *arrays)


def project_kernel(
    x_ref, w_ref, cos_ref, sin_ref, unit_ref, qkv_ref, keys_ref, values_ref, w_all, *, extra
):
    half = HDIM // 2
    rows = cos_ref.shape[1]

    @pl.when(pl.program_id(0) == 0)
    def _():
        for part in range(w_ref.shape[0]):
            w_all[part * 128 : (part + 1) * 128] = w_ref[part].astype(f32).T.astype(bf16)

    count = (x_ref.shape[0] - rows) // extra
    each = rows // count
    for at in range(count):
        tokens = x_ref[at * (each + extra) : at * (each + extra) + each].astype(f32)
        unit_ref[at * each : (at + 1) * each] = unit_rows(tokens)[0].astype(bf16)
    unit = unit_ref[...]
    mixed = dot(unit, w_all[...]).T
    cosine = cos_ref[...]
    sine = sin_ref[...]

    def turn(one, two):
        return jnp.concatenate([one * cosine - two * sine, two * cosine + one * sine], axis=0)

    queries = turn(mixed[:half], mixed[half:HDIM])
    keys = turn(mixed[HDIM : HDIM + half], mixed[HDIM + half : 2 * HDIM])
    values = mixed[2 * HDIM :]
    qkv_ref[...] = jnp.concatenate([queries, keys, values], axis=0).astype(bf16)
    key_rows = keys.T.astype(bf16)
    value_rows = values.T.astype(bf16)
    ones = jnp.where(lax.broadcasted_iota(jnp.int32, (rows, HDIM), 1) < 3, 1.0, 0.0).astype(bf16)
    keys_ref[...] = jnp.concatenate([key_rows, key_rows, key_rows, ones], axis=1)
    values_ref[...] = jnp.concatenate([value_rows, ones], axis=1)


def project(tokens, weights, cosine, sine, extra, block=1024):
    width = tokens.shape[1]
    length = cosine.shape[1]
    steps = length // block
    return pl.pallas_call(
        functools.partial(project_kernel, extra=extra),
        name="project",
        grid=(steps,),
        in_specs=[
            pl.BlockSpec((tokens.shape[0] // steps, width), lambda i: (i, 0)),
            pl.BlockSpec(weights.shape, lambda i: (0, 0, 0)),
            pl.BlockSpec((HDIM // 2, block), lambda i: (0, i)),
            pl.BlockSpec((HDIM // 2, block), lambda i: (0, i)),
        ],
        out_specs=[
            pl.BlockSpec((block, width), lambda i: (i, 0)),
            pl.BlockSpec((3 * HDIM, block), lambda i: (0, i)),
            pl.BlockSpec((block, 256), lambda i: (i, 0)),
            pl.BlockSpec((block, 128), lambda i: (i, 0)),
        ],
        out_shape=[
            jax.ShapeDtypeStruct((length, width), bf16),
            jax.ShapeDtypeStruct((3 * HDIM, length), bf16),
            jax.ShapeDtypeStruct((length, 256), bf16),
            jax.ShapeDtypeStruct((length, 128), bf16),
        ],
        scratch_shapes=[pltpu.VMEM((width, 3 * HDIM), bf16)],
        compiler_params=pltpu.CompilerParams(vmem_limit_bytes=VMEM),
        cost_estimate=cost(length * width, 1 << 20),
    )(tokens, weights, cosine, sine)


def scaled_queries(queries):
    scaled = queries.astype(f32) * (LOG2E / math.sqrt(HDIM))
    high = scaled.astype(bf16)
    rest = scaled - high.astype(f32)
    middle = rest.astype(bf16)
    low = (rest - middle.astype(f32)).astype(bf16)
    return high, middle, low


def minus_in_three(values):
    rows = values.shape[1]
    at = lax.broadcasted_iota(jnp.int32, (16, rows), 0)
    high = (-values).astype(bf16).astype(f32)
    rest = -values - high
    middle = rest.astype(bf16).astype(f32)
    low = rest - middle
    stacked = jnp.where(at == 0, high, jnp.where(at == 1, middle, jnp.where(at == 2, low, 0.0)))
    return stacked.astype(bf16)


def attend_kernel(
    keys_ref, q_ref, k_ref, v_ref, low_ref, out_ref, lse_ref, v_ones, longest, *, part
):
    length = keys_ref.shape[0]
    count = length // part

    @pl.when(pl.program_id(0) == 0)
    def _():
        v_ones[:HDIM] = v_ref[...]
        v_ones[HDIM:] = jnp.where(
            lax.broadcasted_iota(jnp.int32, (16, length), 0) < 1, 1.0, 0.0
        ).astype(bf16)
        squares = jnp.sum(k_ref[...].astype(f32) ** 2, axis=0, keepdims=True)
        longest[...] = jnp.broadcast_to(jnp.max(squares, axis=1, keepdims=True), longest.shape)

    queries = jnp.concatenate(scaled_queries(q_ref[...]), axis=0)

    def finish(total, shift):
        summed = total[HDIM : HDIM + 1]
        result = total[:HDIM] / summed
        out_ref[...] = result
        lse_ref[...] = shift + jnp.log2(summed)
        step = low_ref.shape[2]
        for at in range(low_ref.shape[0]):
            low_ref[at] = result[:, at * step : (at + 1) * step].astype(bf16)
        return summed

    squares = jnp.sum((q_ref[...].astype(f32) * (LOG2E / math.sqrt(HDIM))) ** 2, axis=0, keepdims=True)
    shift = jnp.sqrt(squares * longest[0:1, 0:1])
    shifted = jnp.concatenate([queries, minus_in_three(shift)], axis=0)

    def score(at):
        return dot(keys_ref[at * part : (at + 1) * part, : 3 * HDIM + 16], shifted)

    scores = score(0)
    total = None
    for at in range(count):
        following = score(at + 1) if at + 1 < count else None
        soft = jnp.exp2(scores).astype(bf16)
        added = dot(v_ones[:, at * part : (at + 1) * part], soft)
        total = added if total is None else total + added
        scores = following
    summed = finish(total, shift)

    @pl.when(jnp.min(summed) < 2.0**-60)
    def _():
        def exact(at, carry):
            highest, total = carry
            rows = pl.ds(pl.multiple_of(at * part, part), part)
            scores = dot(keys_ref[rows, : 3 * HDIM], queries)
            raised = jnp.maximum(highest, jnp.max(scores, axis=0, keepdims=True))
            soft = jnp.exp2(scores - raised).astype(bf16)
            added = dot(v_ones[:, rows], soft)
            return raised, total * jnp.exp2(highest - raised) + added

        start = (
            jnp.full((1, q_ref.shape[1]), -1e30, f32),
            jnp.zeros((HDIM + 16, q_ref.shape[1]), f32),
        )
        highest, total = lax.fori_loop(0, count, exact, start)
        finish(total, highest)


def attend(keys, qkv, chips, block=1024, part=512):
    length = keys.shape[0]
    return pl.pallas_call(
        functools.partial(attend_kernel, part=part),
        name="attend",
        grid=(length // block,),
        in_specs=[
            pl.BlockSpec(keys.shape, lambda i: (0, 0)),
            pl.BlockSpec((HDIM, block), lambda i: (0, i)),
            pl.BlockSpec((HDIM, length), lambda i: (1, 0)),
            pl.BlockSpec((HDIM, length), lambda i: (2, 0)),
        ],
        out_specs=[
            pl.BlockSpec((block * chips // length, HDIM, length // chips), lambda i: (i, 0, 0)),
            pl.BlockSpec((HDIM, block), lambda i: (0, i)),
            pl.BlockSpec((1, block), lambda i: (0, i)),
        ],
        out_shape=[
            jax.ShapeDtypeStruct((chips, HDIM, length // chips), bf16),
            jax.ShapeDtypeStruct((HDIM, length), f32),
            jax.ShapeDtypeStruct((1, length), f32),
        ],
        scratch_shapes=[pltpu.VMEM((HDIM + 16, length), bf16), pltpu.VMEM((8, 128), f32)],
        compiler_params=pltpu.CompilerParams(vmem_limit_bytes=VMEM),
        cost_estimate=cost(length * HDIM, 1 << 20),
    )(keys, qkv, qkv, qkv)


def attend_back_kernel(
    order_ref,
    keys_ref,
    values_ref,
    q_ref,
    k_ref,
    out_ref,
    lse_ref,
    cos_ref,
    sin_ref,
    *rest,
    part,
):
    count = (len(rest) - 3) // 2
    dout_refs, dp_refs, (sums, dq_all, dout_all) = rest[:count], rest[count:-3], rest[-3:]
    half = HDIM // 2
    here = pl.program_id(0)
    length = keys_ref.shape[0]
    block = q_ref.shape[1]
    count = length // part
    factor = HDIM ** (-0.5)

    def turn_back(grads, cosine, sine):
        low = grads.astype(bf16).astype(f32)
        one, two = low[:half], low[half:]
        return jnp.concatenate([one * cosine + two * sine, two * cosine - one * sine], axis=0)

    @pl.when(here == 0)
    def _():
        sums[...] = jnp.zeros_like(sums)
        for place, dout_ref in enumerate(dout_refs):
            dout_all[place] = dout_ref[...]

    low_queries = q_ref[...]
    queries = jnp.concatenate(
        [*scaled_queries(low_queries), minus_in_three(lse_ref[...])], axis=0
    )
    low_dout = dout_all[here]
    dout = low_dout.astype(f32)
    centre = jnp.sum(dout * out_ref[...], axis=0, keepdims=True)
    douts = jnp.concatenate([low_dout, minus_in_three(centre)], axis=0)
    blank = jnp.zeros((block, HDIM), bf16)
    right = jnp.concatenate(
        [
            jnp.concatenate([low_queries.astype(f32).T.astype(bf16), blank], axis=1),
            jnp.concatenate([blank, dout.T.astype(bf16)], axis=1),
        ],
        axis=0,
    )

    def score(at):
        rows = slice(at * part, (at + 1) * part)
        return (
            dot(keys_ref[rows, : 3 * HDIM + 16], queries),
            dot(values_ref[rows, : HDIM + 16], douts),
        )

    now = score(0)
    grad_queries = None
    for at in range(count):
        following = score(at + 1) if at + 1 < count else None
        rows = slice(at * part, (at + 1) * part)
        soft = jnp.exp2(now[0])
        grads = (soft * now[1]).astype(bf16)
        added = dot(k_ref[:, rows], grads)
        grad_queries = added if grad_queries is None else grad_queries + added
        sums[rows] += dot(jnp.concatenate([grads, soft.astype(bf16)], axis=1), right)
        now = following

    def columns_of(place):
        return pl.ds(pl.multiple_of(order_ref[place] * block, block), block)

    columns = columns_of(here)
    dq_all[here] = turn_back(
        grad_queries * factor, cos_ref[:, columns], sin_ref[:, columns]
    ).astype(bf16)

    @pl.when(here == length // block - 1)
    def _():
        for place, dp_ref in enumerate(dp_refs):
            columns = columns_of(place)
            both = sums[columns].T
            dp_ref[:HDIM] = dq_all[place]
            dp_ref[HDIM : 2 * HDIM] = turn_back(
                both[:HDIM] * factor, cos_ref[:, columns], sin_ref[:, columns]
            ).astype(bf16)
            dp_ref[2 * HDIM :] = both[HDIM:].astype(bf16)


def attend_back(order, keys, values, qkv, douts, out, lse, cosine, sine, part=256):
    length = keys.shape[0]
    chips = len(douts)
    block = douts[0].shape[1]
    scores = length * length

    def whole(array):
        return pl.BlockSpec(array.shape, lambda i, order: (0, 0))

    return pl.pallas_call(
        functools.partial(attend_back_kernel, part=part),
        name="attend_back",
        grid_spec=pltpu.PrefetchScalarGridSpec(
            num_scalar_prefetch=1,
            grid=(chips,),
            in_specs=[
                whole(keys),
                whole(values),
                pl.BlockSpec((HDIM, block), lambda i, order: (0, order[i])),
                pl.BlockSpec((HDIM, length), lambda i, order: (1, 0)),
                pl.BlockSpec((HDIM, block), lambda i, order: (0, order[i])),
                pl.BlockSpec((1, block), lambda i, order: (0, order[i])),
                whole(cosine),
                whole(sine),
                *[whole(piece) for piece in douts],
            ],
            out_specs=[pl.BlockSpec((3 * HDIM, block), lambda i, order: (0, 0))] * chips,
            scratch_shapes=[
                pltpu.VMEM((length, 2 * HDIM), f32),
                pltpu.VMEM((chips, HDIM, block), bf16),
                pltpu.VMEM((chips, HDIM, block), bf16),
            ],
        ),
        out_shape=[jax.ShapeDtypeStruct((3 * HDIM, block), bf16)] * chips,
        compiler_params=pltpu.CompilerParams(vmem_limit_bytes=VMEM),
        cost_estimate=cost(5 * 4 * 2 * scores * HDIM, 8 << 20),
    )(order, keys, values, qkv, qkv, out, lse, cosine, sine, *douts)


def attend_out_kernel(order_ref, attended_ref, *rest):
    piece_refs, (mixed_ref, attn_ref) = rest[:-2], rest[-2:]
    half = attn_ref.shape[1] // 2
    at = 0
    for piece_ref in piece_refs:
        for place in range(piece_ref.shape[0]):
            rows = pl.ds(pl.multiple_of(order_ref[at] * HDIM, HDIM), HDIM)
            attn_ref[rows, :half] = piece_ref[place, :HDIM]
            attn_ref[rows, half:] = piece_ref[place, HDIM:]
            at += 1
    turned = attended_ref[...].astype(f32).T.astype(bf16)
    mixed_ref[...] = dot(turned, attn_ref[...]).astype(bf16)


def attend_out(order, attended, pieces):
    size, tokens = attended.shape
    width = 2 * size

    def whole(*shape):
        return pl.BlockSpec(shape, lambda i, order: (0,) * len(shape))

    return pl.pallas_call(
        attend_out_kernel,
        name="attend_out",
        grid_spec=pltpu.PrefetchScalarGridSpec(
            num_scalar_prefetch=1,
            grid=(1,),
            in_specs=[whole(size, tokens)]
            + [whole(*piece.shape[:2], width // 2) for piece in pieces],
            out_specs=[whole(tokens, width), whole(size, width)],
        ),
        out_shape=[
            jax.ShapeDtypeStruct((tokens, width), bf16),
            jax.ShapeDtypeStruct((size, width), bf16),
        ],
        compiler_params=pltpu.CompilerParams(vmem_limit_bytes=VMEM),
        cost_estimate=cost(2 * 2 * tokens * width * size, 4 << 20),
    )(order, attended, *pieces)


def crossed_rows(axes):
    planes, lines, wide, beside = axes
    for plane in range(planes):
        for line in range(lines):
            for far in range(wide):
                for near in range(beside):
                    yield (
                        ((plane * lines + line) * wide + far) * beside + near,
                        ((far * planes + plane) * beside + near) * lines + line,
                    )


def feed_kernel(
    first_order, second_order, x_ref, ours_ref, theirs_ref, g_ref, *rest, firsts, seconds, axes
):
    weight_refs = []
    start = 0
    for size in (firsts, firsts, seconds, seconds):
        weight_refs.append(rest[start : start + size])
        start += size
    planes, lines, wide, beside = axes

    def put(grads, columns):
        size = grads.shape[0] // (planes * lines * wide)
        low = grads.astype(bf16)
        for plane in range(planes):
            for line in range(lines):
                for far in range(wide):
                    source = ((plane * lines + line) * wide + far) * size
                    target = ((line * wide + far) * planes + plane) * size
                    grads_ref[target : target + size, columns] = low[source : source + size]
    residual_ref, partial_ref, back_ref, grads_ref, out_grads_ref = rest[-14:-9]
    unit, unit_t, g_t, sum_out, sum_back = rest[-9:-4]
    gate_ref, up_ref, out_ref, rest_ref = rest[-4:]
    here = pl.program_id(0)
    last = pl.num_programs(0) - 1
    width = x_ref.shape[1]
    step = gate_ref.shape[1]

    def join(total, parts, order):
        at = 0
        for part in parts:
            size = part.shape[1]
            for place in range(part.shape[0]):
                total[pl.ds(pl.multiple_of(order[at] * size, size), size)] = part[place]
                at += 1

    def bend(gate, upward):
        cdf = 0.5 + 0.5 * lax.erf(gate * math.sqrt(0.5))
        slope = cdf + gate * jnp.exp(gate * gate * -0.5) * (1.0 / math.sqrt(2.0 * math.pi))
        bent = gate * cdf
        return bent, slope, (bent * upward).astype(bf16)

    def put_out(grads, columns):
        size = grads.shape[0] // (planes * lines * wide * beside)
        low = grads.astype(bf16)
        for source, target in crossed_rows(axes):
            out_grads_ref[target * size : (target + 1) * size, columns] = low[
                source * size : (source + 1) * size
            ]

    @pl.when(here == 0)
    def _():
        residual = (
            x_ref[...].astype(f32) + ours_ref[...].astype(f32) + theirs_ref[...].astype(f32)
        )
        residual_ref[...] = residual
        normed = unit_rows(residual)[0]
        unit[...] = normed.astype(bf16)
        unit_t[...] = normed.T.astype(bf16)
        g_t[...] = g_ref[...].astype(f32).T.astype(bf16)
        join(rest_ref, weight_refs[3], second_order)
        few = rest_ref.shape[1] // 4
        both = dot(unit[...], rest_ref[...])
        grad = dot(g_ref[...], rest_ref[...])[:, 2 * few : 3 * few]
        bent, slope, active = bend(both[:, :few], both[:, few : 2 * few])
        grad_gate = (grad * both[:, few : 2 * few] * slope).astype(bf16)
        grad_up = (grad * bent).astype(bf16)
        blank = jnp.zeros_like(active)
        outs = jnp.concatenate([blank, blank, active, blank], axis=1)
        ins = jnp.concatenate([grad_gate, grad_up, blank, blank], axis=1)
        sum_out[...] = dot(outs, rest_ref[...], 1, 1)
        sum_back[...] = dot(ins, rest_ref[...], 1, 1)
        put_out(
            dot(unit_t[...], ins) + dot(g_t[...], outs),
            slice(out_grads_ref.shape[1] - 4 * few, out_grads_ref.shape[1]),
        )

    join(gate_ref, weight_refs[0], first_order)
    join(up_ref, weight_refs[1], first_order)
    join(out_ref, weight_refs[2], second_order)
    gate = dot(unit[...], gate_ref[...])
    upward = dot(unit[...], up_ref[...])
    grad = dot(g_ref[...], out_ref[...])
    bent, slope, active = bend(gate, upward)
    grad_gate = (grad * upward * slope).astype(bf16)
    grad_up = (grad * bent).astype(bf16)
    sum_out[...] += dot(active, out_ref[...], 1, 1)
    sum_back[...] += dot(grad_gate, gate_ref[...], 1, 1) + dot(grad_up, up_ref[...], 1, 1)
    count = grads_ref.shape[1] // step // 2
    put(dot(unit_t[...], grad_gate), pl.ds(pl.multiple_of(here * step, 128), step))
    put(dot(unit_t[...], grad_up), pl.ds(pl.multiple_of((count + here) * step, 128), step))
    put_out(
        dot(g_t[...], active), pl.ds(pl.multiple_of(width // 2 + here * step, 128), step)
    )

    @pl.when(here == last)
    def _():
        partial_ref[...] = sum_out[...].astype(bf16)
        back_ref[...] = sum_back[...].astype(bf16)


def feed(first_order, second_order, x, ours, theirs, g, first, second, axes, step=256):
    tokens, width = x.shape
    start = width // 2 // step
    count = (first[0].shape[2] - width // 2) // step // 2
    rest = second[0].shape[2] - count * step

    def whole(*shape):
        return pl.BlockSpec(shape, lambda i, one, two: (0, 0))

    def piece(arrays, size, at):
        return [
            pl.BlockSpec((*array.shape[:2], size), lambda i, one, two: (0, 0, at(i)))
            for array in arrays
        ]

    pair = jax.ShapeDtypeStruct((tokens, width), bf16)
    return pl.pallas_call(
        functools.partial(feed_kernel, firsts=len(first), seconds=len(second), axes=axes),
        name="feed",
        grid_spec=pltpu.PrefetchScalarGridSpec(
            num_scalar_prefetch=2,
            grid=(count,),
            in_specs=[whole(tokens, width)] * 4
            + piece(first, step, lambda i: start + i)
            + piece(first, step, lambda i: start + count + i)
            + piece(second, step, lambda i: i)
            + piece(second, rest, lambda i: count * step // rest),
            out_specs=[whole(tokens, width)] * 3
            + [whole(width, 2 * count * step), whole(width, width // 2 + count * step + rest)],
            scratch_shapes=[
                pltpu.VMEM((tokens, width), bf16),
                pltpu.VMEM((width, tokens), bf16),
                pltpu.VMEM((width, tokens), bf16),
                pltpu.VMEM((tokens, width), f32),
                pltpu.VMEM((tokens, width), f32),
                pltpu.VMEM((width, step), bf16),
                pltpu.VMEM((width, step), bf16),
                pltpu.VMEM((width, step), bf16),
                pltpu.VMEM((width, rest), bf16),
            ],
        ),
        out_shape=[
            jax.ShapeDtypeStruct((tokens, width), f32),
            pair,
            pair,
            jax.ShapeDtypeStruct((width, 2 * count * step), bf16),
            jax.ShapeDtypeStruct((width, width // 2 + count * step + rest), bf16),
        ],
        compiler_params=pltpu.CompilerParams(vmem_limit_bytes=VMEM),
        cost_estimate=cost(2 * 9 * 2 * tokens * width * count * step, 24 << 20),
    )(first_order, second_order, x, ours, theirs, g, *first, *first, *second, *second)


def middle_back_kernel(
    core_ref, order_ref, residual_ref, g_ref, ours_ref, theirs_ref, attn_ref, attended_ref,
    out_ours_ref, out_theirs_ref, grads_in_ref, layer_ref, residual_grad_ref, *rest, axes,
):
    dout_refs, (grads_ref, dout_all) = rest[:-2], rest[-2:]
    rows = layer_ref.shape[0]
    half = attn_ref.shape[0]
    own = pl.ds(pl.multiple_of(core_ref[0] * rows, rows), rows)
    layer_ref[...] = (
        residual_ref[own, :]
        + out_ours_ref[own, :].astype(f32)
        + out_theirs_ref[...].astype(f32)
    ).astype(bf16)
    unit, inverse = unit_rows(residual_ref[...])
    scaled = ours_ref[...].astype(f32) + theirs_ref[...].astype(f32)
    grad = g_ref[...].astype(f32) + unit_back(scaled, unit, inverse)
    low = grad.astype(bf16)
    residual_grad_ref[...] = grad
    dout_all[...] = dot(attn_ref[...], low, 1, 1).astype(bf16)
    for at, dout_ref in enumerate(dout_refs):
        dout_ref[...] = dout_all[pl.ds(pl.multiple_of(order_ref[at] * HDIM, HDIM), HDIM)]
    grads = dot(attended_ref[...], low)
    few = grads.shape[0] // 8
    both = [part.reshape(few, 8, half) for part in (grads[:, :half], grads[:, half:])]
    both = jnp.stack(both, axis=1).reshape(grads_ref.shape).astype(bf16)
    for source, target in crossed_rows(axes):
        grads_ref[target * 16 : (target + 1) * 16] = both[source * 16 : (source + 1) * 16]


def middle_back(
    core, order, residual, g, ours, theirs, attn, attended, out_ours, out_theirs, grads, axes
):
    tokens, width = residual.shape
    rows = tokens // 2
    half = width // 2
    chips = half // HDIM

    def whole(*shape):
        return pl.BlockSpec(shape, lambda i, core, order: (0,) * len(shape))

    return pl.pallas_call(
        functools.partial(middle_back_kernel, axes=axes),
        name="middle_back",
        grid_spec=pltpu.PrefetchScalarGridSpec(
            num_scalar_prefetch=2,
            grid=(1,),
            in_specs=[whole(tokens, width)] * 4
            + [whole(half, width), whole(half, tokens), whole(tokens, width), whole(rows, width)]
            + [pl.BlockSpec(memory_space=pl.ANY)],
            out_specs=[whole(rows, width), whole(tokens, width)]
            + [whole(HDIM, tokens)] * chips
            + [whole(width, half)],
            scratch_shapes=[pltpu.VMEM((half, tokens), bf16)],
        ),
        out_shape=[
            jax.ShapeDtypeStruct((rows, width), bf16),
            jax.ShapeDtypeStruct((tokens, width), f32),
        ]
        + [jax.ShapeDtypeStruct((HDIM, tokens), bf16)] * chips
        + [jax.ShapeDtypeStruct(grads.shape, bf16)],
        input_output_aliases={10: 2 + chips},
        compiler_params=pltpu.CompilerParams(vmem_limit_bytes=VMEM),
        cost_estimate=cost(2 * 2 * 2 * tokens * width * half, 16 << 20),
    )(core, order, residual, g, ours, theirs, attn, attended, out_ours, out_theirs, grads)


def hidden_back_kernel(order_ref, core_ref, shard_ref, w_ref, *rest):
    dp_refs, (own_ref, other_ref, stacked) = rest[:-3], rest[-3:]
    for place, dp_ref in enumerate(dp_refs):
        size = dp_ref.shape[0]
        stacked[pl.ds(pl.multiple_of(order_ref[place] * size, 64), size)] = dp_ref[...]
    rows = own_ref.shape[0]
    zero = core_ref[0] == 0
    size = w_ref.shape[1]
    for at in range(w_ref.shape[0]):
        flat = dot(w_ref[at], stacked[...])
        first = flat[:, :rows].T
        second = flat[:, rows:].T
        columns = pl.ds(pl.multiple_of(shard_ref[at] * size, size), size)
        own_ref[:, columns] = jnp.where(zero, first, second)
        other_ref[:, columns] = jnp.where(zero, second, first).astype(bf16)


def hidden_back(order, core, shard_order, weights, pieces):
    shards, size, columns = weights.shape
    width = shards * size
    rows = pieces[0].shape[1] // 2

    def whole(*shape):
        return pl.BlockSpec(shape, lambda i, order, core, shard: (0,) * len(shape))

    return pl.pallas_call(
        hidden_back_kernel,
        name="hidden_back",
        grid_spec=pltpu.PrefetchScalarGridSpec(
            num_scalar_prefetch=3,
            grid=(1,),
            in_specs=[whole(shards, size, columns)] + [whole(*pieces[0].shape)] * len(pieces),
            out_specs=[whole(rows, width)] * 2,
            scratch_shapes=[pltpu.VMEM((columns, 2 * rows), bf16)],
        ),
        out_shape=[
            jax.ShapeDtypeStruct((rows, width), f32),
            jax.ShapeDtypeStruct((rows, width), bf16),
        ],
        compiler_params=pltpu.CompilerParams(vmem_limit_bytes=VMEM),
        cost_estimate=cost(2 * 2 * 2 * rows * width * columns, 8 << 20),
    )(order, core, shard_order, weights, *pieces)


def head_grad_kernel(order_ref, owner_ref, unit_ref, *rest, owners):
    dp_refs, out_refs, out_all = rest[: -1 - owners], rest[-1 - owners : -1], rest[-1]
    block = dp_refs[0].shape[1]
    total = None
    for place, dp_ref in enumerate(dp_refs):
        rows = pl.ds(pl.multiple_of(order_ref[place] * block, block), block)
        added = dot(dp_ref[...], unit_ref[rows])
        total = added if total is None else total + added
    for at in range(owners):
        out_all[at] = total[:, at * 128 : (at + 1) * 128].astype(bf16)
    for at, out_ref in enumerate(out_refs):
        out_ref[...] = out_all[owner_ref[at]]


def head_grad(order, owner_order, unit_all, pieces):
    length, width = unit_all.shape
    owners = width // 128
    size = pieces[0].shape[0]

    def whole(*shape):
        return pl.BlockSpec(shape, lambda i, order, owner: (0,) * len(shape))

    return pl.pallas_call(
        functools.partial(head_grad_kernel, owners=owners),
        name="head_grad",
        grid_spec=pltpu.PrefetchScalarGridSpec(
            num_scalar_prefetch=2,
            grid=(1,),
            in_specs=[whole(length, width)] + [whole(*pieces[0].shape)] * len(pieces),
            out_specs=[whole(size, 128)] * owners,
            scratch_shapes=[pltpu.VMEM((owners, size, 128), bf16)],
        ),
        out_shape=[jax.ShapeDtypeStruct((size, 128), bf16)] * owners,
        compiler_params=pltpu.CompilerParams(vmem_limit_bytes=VMEM),
        cost_estimate=cost(2 * 2 * length * width * size, 10 << 20),
    )(order, owner_order, unit_all, *pieces)


def adam_in_kernels(weight, gradient, first, second, rate):
    first = BETA_FIRST * first + (1.0 - BETA_FIRST) * gradient
    second = BETA_SECOND * second + (1.0 - BETA_SECOND) * gradient * gradient
    second_hat = second * (1.0 / (1.0 - BETA_SECOND**STEP))
    bottom = second_hat * lax.rsqrt(second_hat) + EPSILON
    guess = pl.reciprocal(bottom, approx=True)
    guess = guess * (2.0 - bottom * guess)
    scale = rate / (1.0 - BETA_FIRST**STEP)
    weight = weight * (1.0 - rate * DECAY) - (scale * first) * guess
    return (weight, first, second)


def adam_into(refs, weight, gradient, first, second, rate):
    for ref, value in zip(refs, adam_in_kernels(weight, gradient, first, second, rate)):
        ref[...] = value


def rounded_in_kernel(values):
    return values.astype(bf16).astype(f32)


def adam_most_kernel(grads_ref, gain_ref, other_gain_ref, *refs, rates):
    (w_in, m_in, v_in), attn, out, gains = refs[:3], refs[3:6], refs[6:9], refs[9:12]
    new_in, new_attn, new_out, new_gains = refs[12:15], refs[15:18], refs[18:21], refs[21:24]
    gain_grad, turned = refs[24:]
    here = pl.program_id(0)
    chips = grads_ref.shape[0] // 2
    width = w_in.shape[1] // 2
    main = width // 256 * 128
    few = width // 2 - main
    out_at = 2 * main + attn[0].shape[2] // 2

    @pl.when(here == 0)
    def _():
        for core in range(2):
            columns = jnp.concatenate(
                [grads_ref[2 * chip + core, :, out_at : out_at + main] for chip in range(chips)],
                axis=0,
            )
            turned[core * main : (core + 1) * main] = columns.astype(f32).T
            rest = jnp.concatenate(
                [
                    grads_ref[2 * chip + core, :, out_at + main :] for chip in range(chips)
                ],
                axis=0,
            )
            start = 2 * main + core * few
            turned[start : start + few] = rest.astype(f32).T[2 * few : 3 * few]

    each = grads_ref.shape[1]
    some = w_in.shape[0] // each
    for at_chip in range(some):
        source = 2 * (here * some + at_chip)
        columns = []
        for at in range(2):
            for core in range(2):
                place = at * main
                columns.append(grads_ref[source + core, :, place : place + main].astype(f32))
            for core in range(2):
                rest = grads_ref[source + core, :, out_at + main :].astype(f32)
                columns.append(rest[:, at * few : (at + 1) * few])
        grads = jnp.concatenate(columns, axis=1)
        rows = slice(at_chip * each, (at_chip + 1) * each)
        weight = w_in[rows]
        gain_rows = pl.ds(pl.multiple_of((here * some + at_chip) * each, each), each)
        gain_grad[gain_rows] = jnp.sum(
            grads * rounded_in_kernel(weight), axis=1, keepdims=True
        )
        values = adam_in_kernels(
            weight, grads * gain_ref[rows], m_in[rows], v_in[rows], rates[0]
        )
        for ref, value in zip(new_in, values):
            ref[rows] = value
        rows = slice(at_chip * each // 2, (at_chip + 1) * each // 2)
        for core in range(2):
            piece = grads_ref[source + core, :, 2 * main : out_at].astype(f32)
            grads = jnp.concatenate([piece[: each // 2], piece[each // 2 :]], axis=1)
            values = adam_in_kernels(
                attn[0][core, rows], grads, attn[1][core, rows], attn[2][core, rows], rates[1]
            )
            for ref, value in zip(new_attn, values):
                ref[core, rows] = value

    size = out[0].shape[0]
    grads = turned[pl.ds(pl.multiple_of(here * size, 8), size)]
    adam_into(new_out, out[0][...], grads, out[1][...], out[2][...], rates[2])

    @pl.when(here == pl.num_programs(0) - 1)
    def _():
        both = jnp.concatenate(
            [other_gain_ref[...], gain_grad[...], jnp.zeros((gain_grad.shape[0], 6), f32)], axis=1
        )
        adam_into(
            new_gains, gains[0][...], both.T[:2], gains[1][...], gains[2][...], GAIN_RATE
        )


def adam_most(
    grads, gain, other_gain, weights_in, weights_attn, weights_out, gains, rates, steps=2
):
    rows, columns = weights_in[0].shape
    width = weights_attn[0].shape[1]
    hidden = weights_out[0].shape[0]
    weights_attn = [array.reshape(2, rows // 2, width) for array in weights_attn]
    block_in = pl.BlockSpec((rows // steps, columns), lambda i: (i, 0))
    block_attn = pl.BlockSpec((2, rows // 2 // steps, width), lambda i: (0, i, 0))
    block_out = pl.BlockSpec((hidden // steps, rows), lambda i: (i, 0))
    column = pl.BlockSpec((rows // steps, 1), lambda i: (i, 0))
    whole_column = pl.BlockSpec((rows, 1), lambda i: (0, 0))
    block_gains = pl.BlockSpec(gains[0].shape, lambda i: (0, 0))
    blocks = [block_in] * 3 + [block_attn] * 3 + [block_out] * 3 + [block_gains] * 3
    arrays = (*weights_in, *weights_attn, *weights_out, *gains)
    results = pl.pallas_call(
        functools.partial(adam_most_kernel, rates=rates),
        name="adam_most",
        grid=(steps,),
        in_specs=[pl.BlockSpec(grads.shape, lambda i: (0, 0, 0)), column, whole_column] + blocks,
        out_specs=blocks,
        out_shape=[jax.ShapeDtypeStruct(array.shape, f32) for array in arrays],
        scratch_shapes=[pltpu.VMEM((rows, 1), f32), pltpu.VMEM((hidden, rows), f32)],
        compiler_params=pltpu.CompilerParams(vmem_limit_bytes=VMEM),
        cost_estimate=cost(rows * columns * 20, rows * columns * 26),
    )(grads, gain, other_gain, *arrays)
    new_attn = [array.reshape(rows, width) for array in results[3:6]]
    return results[:3], new_attn, results[6:9], results[9:]


def adam_qkv_kernel(order_ref, *refs, rate):
    grads_refs, (gain_ref, w_ref, m_ref, v_ref, new_w, new_m, new_v, gain_grad, joined) = (
        refs[:-9], refs[-9:]
    )
    here = pl.program_id(0)
    heads = sum(grads_ref.shape[0] for grads_ref in grads_refs)

    @pl.when(here == 0)
    def _():
        at = 0
        for grads_ref in grads_refs:
            for place in range(grads_ref.shape[0]):
                for part in range(3):
                    row = (part * heads + order_ref[at]) * HDIM
                    joined[pl.ds(pl.multiple_of(row, HDIM), HDIM)] = grads_ref[
                        place, part * HDIM : (part + 1) * HDIM
                    ].astype(f32)
                at += 1

    size = w_ref.shape[1]
    grads = joined[pl.ds(pl.multiple_of(here * size, size), size)].T
    weight = w_ref[...]
    added = jnp.sum(grads * rounded_in_kernel(weight), axis=1, keepdims=True)
    gain_grad[...] = added + jnp.where(here == 0, 0.0, gain_grad[...])
    adam_into(
        (new_w, new_m, new_v), weight, grads * gain_ref[...], m_ref[...], v_ref[...], rate
    )


def adam_qkv(order, grads, gain, weight, first, second, rate, step=1536):
    rows, columns = weight.shape
    block = pl.BlockSpec((rows, step), lambda i, order: (0, i))
    column = pl.BlockSpec((rows, 1), lambda i, order: (0, 0))
    same = jax.ShapeDtypeStruct((rows, columns), f32)
    return pl.pallas_call(
        functools.partial(adam_qkv_kernel, rate=rate),
        name="adam_qkv",
        grid_spec=pltpu.PrefetchScalarGridSpec(
            num_scalar_prefetch=1,
            grid=(columns // step,),
            in_specs=[pl.BlockSpec(piece.shape, lambda i, order: (0, 0, 0)) for piece in grads]
            + [column]
            + [block] * 3,
            out_specs=[block] * 3 + [column],
            scratch_shapes=[pltpu.VMEM((columns, rows), f32)],
        ),
        out_shape=[same] * 3 + [jax.ShapeDtypeStruct((rows, 1), f32)],
        compiler_params=pltpu.CompilerParams(vmem_limit_bytes=VMEM),
        cost_estimate=cost(rows * columns * 20, rows * columns * 26),
    )(order, *grads, gain, weight, first, second)


def ring(axis, shift):
    size = lax.axis_size(axis)
    return [(at, (at + shift) % size) for at in range(size)]


def gather_first_step(planes_first, lines_first):
    swapped = lax.ppermute(planes_first, "zh", SWAP)
    others = [
        lax.ppermute(lines_first, "y", ring("y", shift)) for shift in range(1, lax.axis_size("y"))
    ]
    return jnp.stack([planes_first, swapped]), jnp.stack([lines_first, *others])


def shards(
    tokens,
    positions,
    cotangent,
    weight_qkv,
    weight_attn,
    weight_in,
    weight_out,
    norm_gains,
    first_qkv,
    first_attn,
    first_in,
    first_out,
    first_gains,
    second_qkv,
    second_attn,
    second_in,
    second_out,
    second_gains,
):
    rows, width = tokens.shape[1:]
    shard_rows = weight_qkv.shape[1]
    heads = width // HDIM
    hidden = weight_out.shape[1]
    core = lax.axis_index("c")
    mine = lax.axis_index(CTX)
    chip = lax.axis_index(CHIPS)
    chips = lax.axis_size(CHIPS)
    owners = lax.axis_size(FSDP)
    length = rows * chips * 2
    main = hidden // 256 * 128
    few = hidden // 2 - main
    core_at = core.reshape(1).astype(jnp.int32)
    axes = (lax.axis_size("zh"), lax.axis_size("y"), lax.axis_size("x"), lax.axis_size("zl"))
    offsets = [(far, near) for far in range(lax.axis_size("x")) for near in range(2)]
    across, beside = lax.axis_index("x"), lax.axis_index("zl")
    wide = lax.axis_size("x")

    def chips_at(sign):
        places = [(across + sign * far) % wide * 2 + (beside ^ near) for far, near in offsets]
        return jnp.stack(places).astype(jnp.int32)

    local = tokens[0]
    extra = 16
    high, low = positions[0] // 128, positions[0] % 128
    places_row = jnp.concatenate([high, low, jnp.zeros((width - 2 * rows,), jnp.int32)])
    places_rows = jnp.concatenate(
        [places_row[None], jnp.zeros((extra - 1, width), jnp.int32)], axis=0
    ).astype(bf16)
    sequence = lax.all_gather(
        jnp.concatenate([local, places_rows], axis=0), CTX, axis=0, tiled=True
    )
    first_part, second_part, head_part, half_heads = prepare(
        jnp.stack([core, chip]).astype(jnp.int32),
        norm_gains[0],
        weight_qkv[0],
        weight_attn[0],
        weight_in[0],
        weight_out[0],
    )
    first_joined, second_joined = gather_first_step(first_part, second_part)
    head_weights = lax.all_to_all(
        jnp.broadcast_to(head_part, (owners, *head_part.shape)), FSDP, 0, 0, tiled=True
    )
    first_pieces = [first_joined] + [
        lax.ppermute(first_joined, "y", ring("y", shift))
        for shift in range(1, lax.axis_size("y"))
    ]
    sequence, _, second_joined, half_heads, _ = lax.optimization_barrier(
        (sequence, first_joined, second_joined, half_heads, head_weights)
    )
    half_heads_other = lax.ppermute(half_heads, "zh", SWAP)
    second_pieces = [second_joined, lax.ppermute(second_joined, "zh", SWAP)]
    lines = lax.axis_size("y")
    plane, line = lax.axis_index("zh"), lax.axis_index("y")
    heads_order = jnp.stack(
        [(plane ^ far) * lines + at for at in range(lines) for far in range(2)]
    ).astype(jnp.int32)
    first_order = jnp.stack(
        [(plane ^ far) * lines + (line - shift) % lines for shift in range(lines) for far in range(2)]
    ).astype(jnp.int32)
    second_order = jnp.stack(
        [(plane ^ far) * lines + (line - shift) % lines for far in range(2) for shift in range(lines)]
    ).astype(jnp.int32)

    def in_order(ours, theirs):
        first = jnp.where(core == 0, ours, theirs)
        second = jnp.where(core == 0, theirs, ours)
        return jnp.concatenate([first, second], axis=0)

    def swap(array):
        return lax.ppermute(array, "c", SWAP)

    gradient = in_order(cotangent[0], swap(cotangent[0]))

    freqs = jnp.exp(jnp.arange(HDIM // 2, dtype=f32) * (-2.0 * math.log(ROPE_BASE) / HDIM))
    by_device = sequence.reshape(2 * chips, rows + extra, width)[:, rows]
    by_device = by_device.astype(f32)
    places = by_device[:, :rows] * 128.0 + by_device[:, rows : 2 * rows]
    angles = freqs[:, None] * places.reshape(1, length)
    cosine = jnp.cos(angles)
    sine = jnp.sin(angles)
    unit_all, qkv, keys, values = project(sequence, head_weights, cosine, sine, extra)
    low_out, out, lse = attend(keys, qkv, chips)
    firsts = len(first_pieces)
    low_out, half_heads_other, *arrived = lax.optimization_barrier(
        (low_out, half_heads_other, *first_pieces, *second_pieces)
    )
    first_pieces, second_pieces = arrived[:firsts], arrived[firsts:]
    mat_qkv = lax.all_gather(
        jnp.stack([half_heads, half_heads_other]), "y", axis=0, tiled=True
    )
    attended = lax.all_to_all(low_out, CHIPS, 0, 0, tiled=True)
    attended = attended.reshape(heads // 2 * HDIM, 2 * rows)
    mixed, mat_attn = attend_out(first_order, attended, first_pieces)
    current = lax.dynamic_slice_in_dim(
        sequence, chip * 2 * (rows + extra), 2 * (rows + extra), 0
    ).reshape(2, rows + extra, width)[:, :rows].reshape(2 * rows, width)
    residual, partial, back, grads, out_grads = feed(
        first_order, second_order, current, mixed, swap(mixed), gradient, first_pieces,
        second_pieces, axes,
    )
    grads, mat_qkv = lax.optimization_barrier((grads, mat_qkv))
    first_sum = lax.psum_scatter(grads, "y", scatter_dimension=0, tiled=True)

    def move(pieces, sign):
        moved = [pieces[0]]
        for (far, near), piece in list(zip(offsets, pieces))[1:]:
            pairs = [
                (at, (at // 2 + sign * far) % wide * 2 + (at % 2 ^ near)) for at in range(chips)
            ]
            moved.append(lax.ppermute(piece, CHIPS, pairs))
        return moved

    ahead, behind = chips_at(1), chips_at(-1)
    theirs = swap(lax.dynamic_slice_in_dim(partial, (1 - core) * rows, rows, 0))
    layer_out, residual_grad, *dout_pieces, out_grads = middle_back(
        core_at, ahead, residual, gradient, back, swap(back), mat_attn, attended, partial, theirs,
        out_grads, axes,
    )

    douts = move(dout_pieces, 1)
    out_grads, *douts = lax.optimization_barrier((out_grads, *douts))
    out_arrived = lax.all_to_all(out_grads, ("x", "zh", "zl"), 0, 0, tiled=True)
    pieces = attend_back(behind, keys, values, qkv, douts, out, lse, cosine, sine)
    out_arrived, *pieces = lax.optimization_barrier((out_arrived, *pieces))
    first_sum, *pieces = lax.optimization_barrier((first_sum, *pieces))
    arrived = lax.all_to_all(first_sum, ("x", "zh", "zl"), 0, 0, tiled=True)
    moved = move(pieces, -1)

    def total(arrays):
        return sum(array.astype(f32) for array in arrays).astype(bf16)

    out_arrived = out_arrived.reshape(2 * chips, width // (2 * chips), -1)
    out_sum = jnp.sum(out_arrived.astype(f32), axis=0).astype(bf16)
    out_sum = out_sum.reshape(lines, shard_rows // chips, -1)
    out_parts = [
        lax.dynamic_index_in_dim(out_sum, (line + shift) % lines, 0, keepdims=False)
        for shift in range(lines)
    ]
    out_sum = total(
        out_parts[:1]
        + [
            lax.ppermute(part, "y", ring("y", shift))
            for shift, part in list(enumerate(out_parts))[1:]
        ]
    )

    owner_places = [(far, shift) for far in range(2) for shift in range(lines)]
    owner_order = jnp.stack(
        [(plane ^ far) * lines + (line + shift) % lines for far, shift in owner_places]
    ).astype(jnp.int32)
    head_parts = head_grad(behind, owner_order, unit_all, pieces)
    arrived, out_sum, *rest = lax.optimization_barrier(
        (arrived, out_sum, *moved, *head_parts)
    )
    moved, head_parts = rest[:chips], rest[chips:]
    own_hidden, other_hidden = hidden_back(ahead, core_at, heads_order, mat_qkv, moved)
    grad_hidden = own_hidden + swap(other_hidden).astype(f32)
    unit_in, scale_in = unit_rows(local.astype(f32))
    own_residual = lax.dynamic_slice_in_dim(residual_grad, core * rows, rows, 0)
    tokens_grad = (own_residual + unit_back(grad_hidden, unit_in, scale_in))[None]

    head_arrived = [head_parts[0]]
    for (far, shift), piece in list(zip(owner_places, head_parts))[1:]:
        pairs = [
            (at, (at // lines ^ far) * lines + (at % lines + shift) % lines) for at in range(owners)
        ]
        head_arrived.append(lax.ppermute(piece, FSDP, pairs))
    head_own = total(head_arrived)[None]
    arrived = arrived.reshape(2 * chips, shard_rows // chips, -1)
    second_sum = jnp.sum(arrived.astype(f32), axis=0).astype(bf16)
    second_sum = jnp.concatenate([second_sum, out_sum], axis=1)
    all_grads = lax.all_gather(second_sum, CTX, axis=0, tiled=False)

    head_pair = jnp.concatenate([head_own, swap(head_own)], axis=0)
    head_four = jnp.concatenate([head_pair, lax.ppermute(head_pair, "zl", SWAP)], axis=0)
    head_grads = [head_four] + [
        lax.ppermute(head_four, "x", ring("x", shift)) for shift in range(1, wide)
    ]
    head_order = jnp.stack(
        [
            (across - shift) % wide * 4 + (beside ^ near) * 2 + (core ^ other)
            for shift in range(wide)
            for near in range(2)
            for other in range(2)
        ]
    ).astype(jnp.int32)

    rates = (
        width ** (-0.5),
        max(1, 3 * width // length) ** (-0.5),
        width ** (-0.5),
        hidden ** (-0.5),
    )
    columns_of_gains = norm_gains[0].astype(bf16).astype(f32).T
    *new_qkv, gain_first = adam_qkv(
        head_order, head_grads, columns_of_gains[:, :1], weight_qkv[0], first_qkv[0], second_qkv[0], rates[0]
    )
    new_in, new_attn, new_out, new_gains = adam_most(
        all_grads,
        columns_of_gains[:, 1:],
        gain_first,
        (weight_in[0], first_in[0], second_in[0]),
        (weight_attn[0], first_attn[0], second_attn[0]),
        (weight_out[0], first_out[0], second_out[0]),
        (norm_gains[0], first_gains[0], second_gains[0]),
        (rates[2], rates[1], rates[3]),
    )
    updated = (new_qkv, new_attn, new_in, new_out, new_gains)
    return (
        layer_out[None],
        tokens_grad,
        *[updated[member][0][None] for member in range(5)],
        *[updated[member][1][None] for member in range(5)],
        *[updated[member][2][None] for member in range(5)],
    )


def solution(mesh):
    split = Mesh(mesh.devices.reshape(4, 2, 2, 2, 4), ("x", "zl", "c", "zh", "y"))
    by_row = P(None, FSDP, None)
    by_column = P(None, None, FSDP)
    weights = (by_row, by_row, by_row, by_column, by_column)
    by_token = P(FSDP, CTX, None)
    return jax.shard_map(
        shards,
        mesh=split,
        in_specs=(by_token, P(FSDP, CTX), by_token) + weights * 3,
        out_specs=(by_token, by_token) + weights * 3,
        check_vma=False,
    )
```

```python
import functools
import math

import jax
import jax.numpy as jnp
from jax import lax
from jax.experimental import pallas as pl
from jax.experimental.pallas import tpu as pltpu
from jax.sharding import Mesh, PartitionSpec as P

HDIM = 64
STEP = 10
BETA_FIRST = 0.5
BETA_SECOND = 0.5
EPSILON = 1e-08
DECAY = 0.01
NORM_EPS = 1e-05
ROPE_BASE = 160000.0
GAIN_RATE = 0.6
LOG2E = math.log2(math.e)
f32 = jnp.float32
bf16 = jnp.bfloat16

CHIPS = ("x", "zl")
CTX = ("x", "zl", "c")
FSDP = ("zh", "y")
SWAP = [(0, 1), (1, 0)]
VMEM = 60 << 20


def dot(left, right, left_dim=1, right_dim=0):
    return lax.dot_general(
        left, right, (((left_dim,), (right_dim,)), ((), ())), preferred_element_type=f32
    )


def cost(flops, moved):
    return pl.CostEstimate(flops=flops, bytes_accessed=moved, transcendentals=0)


def unit_rows(values):
    average = jnp.mean(values, axis=-1, keepdims=True)
    centered = values - average
    spread = jnp.mean(centered * centered, axis=-1, keepdims=True)
    inverse = lax.rsqrt(spread + NORM_EPS)
    return centered * inverse, inverse


def unit_back(scaled, unit, inverse):
    first_mean = jnp.mean(scaled, axis=-1, keepdims=True)
    second_mean = jnp.mean(scaled * unit, axis=-1, keepdims=True)
    return inverse * (scaled - first_mean - unit * second_mean)


def prepare_kernel(
    place_ref, gains_ref, qkv_ref, attn_ref, in_ref, out_ref,
    first_ref, second_ref, head_ref, heads_ref,
):
    core, chip = place_ref[0], place_ref[1]
    rows = qkv_ref.shape[0]
    width = attn_ref.shape[1]
    hidden = out_ref.shape[0]
    main = hidden // 256 * 128
    few = hidden // 2 - main
    half = width // 2
    low_gains = gains_ref[...].astype(bf16).astype(f32)
    columns = jnp.concatenate([low_gains, jnp.zeros((6, rows), f32)], axis=0).T
    gain_first, gain_second = columns[:, 0:1], columns[:, 1:2]

    def pick(array):
        size = array.shape[1] // 2
        return jnp.where(core == 0, array[:, :size], array[:, size:])

    def scaled(values, gain):
        return (values.astype(bf16).astype(f32) * gain).astype(bf16)

    attn_rows = attn_ref[pl.ds(pl.multiple_of(core * HDIM, HDIM), HDIM)].astype(bf16)
    first_ref[:HDIM, 2 * main :] = attn_rows[:, :half]
    first_ref[HDIM:, 2 * main :] = attn_rows[:, half:]
    first_ref[:, :main] = scaled(pick(in_ref[:, : 2 * main]), gain_second)
    first_ref[:, main : 2 * main] = scaled(
        pick(in_ref[:, hidden : hidden + 2 * main]), gain_second
    )
    out_rows = out_ref[pl.ds(pl.multiple_of(core * main, 128), main)]
    second_ref[:, :main] = out_rows.T.astype(bf16)
    odd_out = out_ref[2 * main :].T
    odd = [
        scaled(pick(in_ref[:, 2 * main : hidden]), gain_second),
        scaled(pick(in_ref[:, hidden + 2 * main :]), gain_second),
        pick(odd_out).astype(bf16),
        jnp.zeros((rows, few), bf16),
    ]
    second_ref[:, main:] = jnp.concatenate(odd, axis=1)
    pieces = []
    for at in range(width // 128):
        for part in range(3):
            start = part * width + at * 128
            pieces.append(scaled(pick(qkv_ref[:, start : start + 128]), gain_first))
    heads_ref[...] = jnp.concatenate(pieces, axis=1)
    own = []
    for part in range(3):
        start = pl.multiple_of(part * width + chip * 128, 128)
        own.append(scaled(pick(qkv_ref[:, pl.ds(start, 128)]), gain_first).astype(f32))
    own.append(jnp.zeros((rows, HDIM), f32))
    head_ref[...] = jnp.concatenate(own, axis=1).T[: 3 * HDIM].astype(bf16)


def prepare(place, gains, qkv, attn, weight_in, weight_out):
    rows, width = attn.shape
    hidden = weight_out.shape[0]
    main = hidden // 256 * 128
    arrays = (gains, qkv, attn, weight_in, weight_out)
    shapes = [
        (rows, width // 2 + 2 * main),
        (rows, main + 4 * (hidden // 2 - main)),
        (3 * HDIM, rows),
        (rows, 3 * width // 2),
    ]

    def whole(shape):
        return pl.BlockSpec(shape, lambda i, place: (0, 0))

    return pl.pallas_call(
        prepare_kernel,
        name="prepare",
        grid_spec=pltpu.PrefetchScalarGridSpec(
            num_scalar_prefetch=1,
            grid=(1,),
            in_specs=[whole(array.shape) for array in arrays],
            out_specs=[whole(shape) for shape in shapes],
        ),
        out_shape=[jax.ShapeDtypeStruct(shape, bf16) for shape in shapes],
        compiler_params=pltpu.CompilerParams(vmem_limit_bytes=VMEM),
        cost_estimate=cost(rows * width * 60, 10 << 20),
    )(place, *arrays)


def project_kernel(
    x_ref, w_ref, cos_ref, sin_ref, unit_ref, qkv_ref, keys_ref, values_ref, w_all, *, extra
):
    half = HDIM // 2
    rows = cos_ref.shape[1]

    @pl.when(pl.program_id(0) == 0)
    def _():
        for part in range(w_ref.shape[0]):
            w_all[part * 128 : (part + 1) * 128] = w_ref[part].astype(f32).T.astype(bf16)

    count = (x_ref.shape[0] - rows) // extra
    each = rows // count
    for at in range(count):
        tokens = x_ref[at * (each + extra) : at * (each + extra) + each].astype(f32)
        unit_ref[at * each : (at + 1) * each] = unit_rows(tokens)[0].astype(bf16)
    unit = unit_ref[...]
    mixed = dot(unit, w_all[...]).T
    cosine = cos_ref[...]
    sine = sin_ref[...]

    def turn(one, two):
        return jnp.concatenate([one * cosine - two * sine, two * cosine + one * sine], axis=0)

    queries = turn(mixed[:half], mixed[half:HDIM])
    keys = turn(mixed[HDIM : HDIM + half], mixed[HDIM + half : 2 * HDIM])
    values = mixed[2 * HDIM :]
    qkv_ref[...] = jnp.concatenate([queries, keys, values], axis=0).astype(bf16)
    key_rows = keys.T.astype(bf16)
    value_rows = values.T.astype(bf16)
    ones = jnp.where(lax.broadcasted_iota(jnp.int32, (rows, HDIM), 1) < 3, 1.0, 0.0).astype(bf16)
    keys_ref[...] = jnp.concatenate([key_rows, key_rows, key_rows, ones], axis=1)
    values_ref[...] = jnp.concatenate([value_rows, ones], axis=1)


def project(tokens, weights, cosine, sine, extra, block=1024):
    width = tokens.shape[1]
    length = cosine.shape[1]
    steps = length // block
    return pl.pallas_call(
        functools.partial(project_kernel, extra=extra),
        name="project",
        grid=(steps,),
        in_specs=[
            pl.BlockSpec((tokens.shape[0] // steps, width), lambda i: (i, 0)),
            pl.BlockSpec(weights.shape, lambda i: (0, 0, 0)),
            pl.BlockSpec((HDIM // 2, block), lambda i: (0, i)),
            pl.BlockSpec((HDIM // 2, block), lambda i: (0, i)),
        ],
        out_specs=[
            pl.BlockSpec((block, width), lambda i: (i, 0)),
            pl.BlockSpec((3 * HDIM, block), lambda i: (0, i)),
            pl.BlockSpec((block, 256), lambda i: (i, 0)),
            pl.BlockSpec((block, 128), lambda i: (i, 0)),
        ],
        out_shape=[
            jax.ShapeDtypeStruct((length, width), bf16),
            jax.ShapeDtypeStruct((3 * HDIM, length), bf16),
            jax.ShapeDtypeStruct((length, 256), bf16),
            jax.ShapeDtypeStruct((length, 128), bf16),
        ],
        scratch_shapes=[pltpu.VMEM((width, 3 * HDIM), bf16)],
        compiler_params=pltpu.CompilerParams(vmem_limit_bytes=VMEM),
        cost_estimate=cost(length * width, 1 << 20),
    )(tokens, weights, cosine, sine)


def scaled_queries(queries):
    scaled = queries.astype(f32) * (LOG2E / math.sqrt(HDIM))
    high = scaled.astype(bf16)
    rest = scaled - high.astype(f32)
    middle = rest.astype(bf16)
    low = (rest - middle.astype(f32)).astype(bf16)
    return high, middle, low


def minus_in_three(values):
    rows = values.shape[1]
    at = lax.broadcasted_iota(jnp.int32, (16, rows), 0)
    high = (-values).astype(bf16).astype(f32)
    rest = -values - high
    middle = rest.astype(bf16).astype(f32)
    low = rest - middle
    stacked = jnp.where(at == 0, high, jnp.where(at == 1, middle, jnp.where(at == 2, low, 0.0)))
    return stacked.astype(bf16)


def attend_kernel(
    keys_ref, q_ref, k_ref, v_ref, low_ref, out_ref, lse_ref, v_ones, longest, *, part
):
    length = keys_ref.shape[0]
    count = length // part

    @pl.when(pl.program_id(0) == 0)
    def _():
        v_ones[:HDIM] = v_ref[...]
        v_ones[HDIM:] = jnp.where(
            lax.broadcasted_iota(jnp.int32, (16, length), 0) < 1, 1.0, 0.0
        ).astype(bf16)
        squares = jnp.sum(k_ref[...].astype(f32) ** 2, axis=0, keepdims=True)
        longest[...] = jnp.broadcast_to(jnp.max(squares, axis=1, keepdims=True), longest.shape)

    queries = jnp.concatenate(scaled_queries(q_ref[...]), axis=0)

    def finish(total, shift):
        summed = total[HDIM : HDIM + 1]
        result = total[:HDIM] / summed
        out_ref[...] = result
        lse_ref[...] = shift + jnp.log2(summed)
        step = low_ref.shape[2]
        for at in range(low_ref.shape[0]):
            low_ref[at] = result[:, at * step : (at + 1) * step].astype(bf16)
        return summed

    squares = jnp.sum((q_ref[...].astype(f32) * (LOG2E / math.sqrt(HDIM))) ** 2, axis=0, keepdims=True)
    shift = jnp.sqrt(squares * longest[0:1, 0:1])
    shifted = jnp.concatenate([queries, minus_in_three(shift)], axis=0)

    def score(at):
        return dot(keys_ref[at * part : (at + 1) * part, : 3 * HDIM + 16], shifted)

    scores = score(0)
    total = None
    for at in range(count):
        following = score(at + 1) if at + 1 < count else None
        soft = jnp.exp2(scores).astype(bf16)
        added = dot(v_ones[:, at * part : (at + 1) * part], soft)
        total = added if total is None else total + added
        scores = following
    summed = finish(total, shift)

    @pl.when(jnp.min(summed) < 2.0**-60)
    def _():
        def exact(at, carry):
            highest, total = carry
            rows = pl.ds(pl.multiple_of(at * part, part), part)
            scores = dot(keys_ref[rows, : 3 * HDIM], queries)
            raised = jnp.maximum(highest, jnp.max(scores, axis=0, keepdims=True))
            soft = jnp.exp2(scores - raised).astype(bf16)
            added = dot(v_ones[:, rows], soft)
            return raised, total * jnp.exp2(highest - raised) + added

        start = (
            jnp.full((1, q_ref.shape[1]), -1e30, f32),
            jnp.zeros((HDIM + 16, q_ref.shape[1]), f32),
        )
        highest, total = lax.fori_loop(0, count, exact, start)
        finish(total, highest)


def attend(keys, qkv, chips, block=1024, part=512):
    length = keys.shape[0]
    return pl.pallas_call(
        functools.partial(attend_kernel, part=part),
        name="attend",
        grid=(length // block,),
        in_specs=[
            pl.BlockSpec(keys.shape, lambda i: (0, 0)),
            pl.BlockSpec((HDIM, block), lambda i: (0, i)),
            pl.BlockSpec((HDIM, length), lambda i: (1, 0)),
            pl.BlockSpec((HDIM, length), lambda i: (2, 0)),
        ],
        out_specs=[
            pl.BlockSpec((block * chips // length, HDIM, length // chips), lambda i: (i, 0, 0)),
            pl.BlockSpec((HDIM, block), lambda i: (0, i)),
            pl.BlockSpec((1, block), lambda i: (0, i)),
        ],
        out_shape=[
            jax.ShapeDtypeStruct((chips, HDIM, length // chips), bf16),
            jax.ShapeDtypeStruct((HDIM, length), f32),
            jax.ShapeDtypeStruct((1, length), f32),
        ],
        scratch_shapes=[pltpu.VMEM((HDIM + 16, length), bf16), pltpu.VMEM((8, 128), f32)],
        compiler_params=pltpu.CompilerParams(vmem_limit_bytes=VMEM),
        cost_estimate=cost(length * HDIM, 1 << 20),
    )(keys, qkv, qkv, qkv)


def attend_back_kernel(
    order_ref,
    keys_ref,
    values_ref,
    q_ref,
    k_ref,
    out_ref,
    lse_ref,
    cos_ref,
    sin_ref,
    *rest,
    part,
):
    dout_ref, dp_refs, (sums, dq_all) = rest[0], rest[1:-2], rest[-2:]
    half = HDIM // 2
    here = pl.program_id(0)
    length = keys_ref.shape[0]
    block = q_ref.shape[1]
    count = length // part
    factor = HDIM ** (-0.5)

    def turn_back(grads, cosine, sine):
        low = grads.astype(bf16).astype(f32)
        one, two = low[:half], low[half:]
        return jnp.concatenate([one * cosine + two * sine, two * cosine - one * sine], axis=0)

    @pl.when(here == 0)
    def _():
        sums[...] = jnp.zeros_like(sums)

    low_queries = q_ref[...]
    queries = jnp.concatenate(
        [*scaled_queries(low_queries), minus_in_three(lse_ref[...])], axis=0
    )
    low_dout = dout_ref[order_ref[here]]
    dout = low_dout.astype(f32)
    centre = jnp.sum(dout * out_ref[...], axis=0, keepdims=True)
    douts = jnp.concatenate([low_dout, minus_in_three(centre)], axis=0)
    blank = jnp.zeros((block, HDIM), bf16)
    right = jnp.concatenate(
        [
            jnp.concatenate([low_queries.astype(f32).T.astype(bf16), blank], axis=1),
            jnp.concatenate([blank, dout.T.astype(bf16)], axis=1),
        ],
        axis=0,
    )

    def score(at):
        rows = slice(at * part, (at + 1) * part)
        return (
            dot(keys_ref[rows, : 3 * HDIM + 16], queries),
            dot(values_ref[rows, : HDIM + 16], douts),
        )

    now = score(0)
    grad_queries = None
    for at in range(count):
        following = score(at + 1) if at + 1 < count else None
        rows = slice(at * part, (at + 1) * part)
        soft = jnp.exp2(now[0])
        grads = (soft * now[1]).astype(bf16)
        added = dot(k_ref[:, rows], grads)
        grad_queries = added if grad_queries is None else grad_queries + added
        sums[rows] += dot(jnp.concatenate([grads, soft.astype(bf16)], axis=1), right)
        now = following

    def columns_of(place):
        return pl.ds(pl.multiple_of(order_ref[place] * block, block), block)

    columns = columns_of(here)
    dq_all[here] = turn_back(
        grad_queries * factor, cos_ref[:, columns], sin_ref[:, columns]
    ).astype(bf16)

    @pl.when(here == length // block - 1)
    def _():
        for place, dp_ref in enumerate(dp_refs):
            columns = columns_of(place)
            both = sums[columns].T
            dp_ref[:HDIM] = dq_all[place]
            dp_ref[HDIM : 2 * HDIM] = turn_back(
                both[:HDIM] * factor, cos_ref[:, columns], sin_ref[:, columns]
            ).astype(bf16)
            dp_ref[2 * HDIM :] = both[HDIM:].astype(bf16)


def attend_back(order, keys, values, qkv, douts, out, lse, cosine, sine, part=256):
    length = keys.shape[0]
    chips, _, block = douts.shape
    scores = length * length

    def whole(array):
        return pl.BlockSpec(array.shape, lambda i, order: (0, 0))

    return pl.pallas_call(
        functools.partial(attend_back_kernel, part=part),
        name="attend_back",
        grid_spec=pltpu.PrefetchScalarGridSpec(
            num_scalar_prefetch=1,
            grid=(chips,),
            in_specs=[
                whole(keys),
                whole(values),
                pl.BlockSpec((HDIM, block), lambda i, order: (0, order[i])),
                pl.BlockSpec((HDIM, length), lambda i, order: (1, 0)),
                pl.BlockSpec((HDIM, block), lambda i, order: (0, order[i])),
                pl.BlockSpec((1, block), lambda i, order: (0, order[i])),
                whole(cosine),
                whole(sine),
                pl.BlockSpec(douts.shape, lambda i, order: (0, 0, 0)),
            ],
            out_specs=[pl.BlockSpec((3 * HDIM, block), lambda i, order: (0, 0))] * chips,
            scratch_shapes=[
                pltpu.VMEM((length, 2 * HDIM), f32),
                pltpu.VMEM((chips, HDIM, block), bf16),
            ],
        ),
        out_shape=[jax.ShapeDtypeStruct((3 * HDIM, block), bf16)] * chips,
        compiler_params=pltpu.CompilerParams(vmem_limit_bytes=VMEM),
        cost_estimate=cost(5 * 4 * 2 * scores * HDIM, 8 << 20),
    )(order, keys, values, qkv, qkv, out, lse, cosine, sine, douts)


def attend_out_kernel(order_ref, attended_ref, *rest):
    piece_refs, (mixed_ref, attn_ref) = rest[:-2], rest[-2:]
    half = attn_ref.shape[1] // 2
    at = 0
    for piece_ref in piece_refs:
        for place in range(piece_ref.shape[0]):
            rows = pl.ds(pl.multiple_of(order_ref[at] * HDIM, HDIM), HDIM)
            attn_ref[rows, :half] = piece_ref[place, :HDIM]
            attn_ref[rows, half:] = piece_ref[place, HDIM:]
            at += 1
    turned = attended_ref[...].astype(f32).T.astype(bf16)
    mixed_ref[...] = dot(turned, attn_ref[...]).astype(bf16)


def attend_out(order, attended, pieces):
    size, tokens = attended.shape
    width = 2 * size

    def whole(*shape):
        return pl.BlockSpec(shape, lambda i, order: (0,) * len(shape))

    return pl.pallas_call(
        attend_out_kernel,
        name="attend_out",
        grid_spec=pltpu.PrefetchScalarGridSpec(
            num_scalar_prefetch=1,
            grid=(1,),
            in_specs=[whole(size, tokens)]
            + [
                pl.BlockSpec(
                    (*piece.shape[:2], size), lambda i, order: (0, 0, pieces[0].shape[2] // size - 1)
                )
                for piece in pieces
            ],
            out_specs=[whole(tokens, width), whole(size, width)],
        ),
        out_shape=[
            jax.ShapeDtypeStruct((tokens, width), bf16),
            jax.ShapeDtypeStruct((size, width), bf16),
        ],
        compiler_params=pltpu.CompilerParams(vmem_limit_bytes=VMEM),
        cost_estimate=cost(2 * 2 * tokens * width * size, 4 << 20),
    )(order, attended, *pieces)


def crossed_rows(axes):
    planes, lines, wide, beside = axes
    for plane in range(planes):
        for line in range(lines):
            for far in range(wide):
                for near in range(beside):
                    yield (
                        ((plane * lines + line) * wide + far) * beside + near,
                        ((far * planes + plane) * beside + near) * lines + line,
                    )


def feed_kernel(
    first_order, second_order, x_ref, ours_ref, theirs_ref, g_ref, *rest, firsts, seconds, axes
):
    weight_refs = []
    start = 0
    for size in (firsts, firsts, seconds, seconds):
        weight_refs.append(rest[start : start + size])
        start += size
    planes, lines, wide, beside = axes

    def put(grads, columns):
        size = grads.shape[0] // (planes * lines * wide)
        low = grads.astype(bf16)
        for plane in range(planes):
            for line in range(lines):
                for far in range(wide):
                    source = ((plane * lines + line) * wide + far) * size
                    target = ((line * wide + far) * planes + plane) * size
                    grads_ref[target : target + size, columns] = low[source : source + size]
    residual_ref, partial_ref, back_ref, grads_ref, out_grads_ref = rest[-14:-9]
    unit, unit_t, g_t, sum_out, sum_back = rest[-9:-4]
    gate_ref, up_ref, out_ref, rest_ref = rest[-4:]
    here = pl.program_id(0)
    last = pl.num_programs(0) - 1
    width = x_ref.shape[1]
    step = gate_ref.shape[1]

    def join(total, parts, order):
        at = 0
        for part in parts:
            size = part.shape[1]
            for place in range(part.shape[0]):
                total[pl.ds(pl.multiple_of(order[at] * size, size), size)] = part[place]
                at += 1

    def bend(gate, upward):
        cdf = 0.5 + 0.5 * lax.erf(gate * math.sqrt(0.5))
        slope = cdf + gate * jnp.exp(gate * gate * -0.5) * (1.0 / math.sqrt(2.0 * math.pi))
        bent = gate * cdf
        return bent, slope, (bent * upward).astype(bf16)

    def put_out(grads, columns):
        size = grads.shape[0] // (planes * lines * wide * beside)
        low = grads.astype(bf16)
        for source, target in crossed_rows(axes):
            out_grads_ref[target * size : (target + 1) * size, columns] = low[
                source * size : (source + 1) * size
            ]

    @pl.when(here == 0)
    def _():
        residual = (
            x_ref[...].astype(f32) + ours_ref[...].astype(f32) + theirs_ref[...].astype(f32)
        )
        residual_ref[...] = residual
        normed = unit_rows(residual)[0]
        unit[...] = normed.astype(bf16)
        unit_t[...] = normed.T.astype(bf16)
        g_t[...] = g_ref[...].astype(f32).T.astype(bf16)
        join(rest_ref, weight_refs[3], second_order)
        few = rest_ref.shape[1] // 4
        both = dot(unit[...], rest_ref[...])
        grad = dot(g_ref[...], rest_ref[...])[:, 2 * few : 3 * few]
        bent, slope, active = bend(both[:, :few], both[:, few : 2 * few])
        grad_gate = (grad * both[:, few : 2 * few] * slope).astype(bf16)
        grad_up = (grad * bent).astype(bf16)
        blank = jnp.zeros_like(active)
        outs = jnp.concatenate([blank, blank, active, blank], axis=1)
        ins = jnp.concatenate([grad_gate, grad_up, blank, blank], axis=1)
        sum_out[...] = dot(outs, rest_ref[...], 1, 1)
        sum_back[...] = dot(ins, rest_ref[...], 1, 1)
        put_out(
            dot(unit_t[...], ins) + dot(g_t[...], outs),
            slice(out_grads_ref.shape[1] - 4 * few, out_grads_ref.shape[1]),
        )

    join(gate_ref, weight_refs[0], first_order)
    join(up_ref, weight_refs[1], first_order)
    join(out_ref, weight_refs[2], second_order)
    gate = dot(unit[...], gate_ref[...])
    upward = dot(unit[...], up_ref[...])
    grad = dot(g_ref[...], out_ref[...])
    bent, slope, active = bend(gate, upward)
    grad_gate = (grad * upward * slope).astype(bf16)
    grad_up = (grad * bent).astype(bf16)
    sum_out[...] += dot(active, out_ref[...], 1, 1)
    sum_back[...] += dot(grad_gate, gate_ref[...], 1, 1) + dot(grad_up, up_ref[...], 1, 1)
    count = grads_ref.shape[1] // step // 2
    put(dot(unit_t[...], grad_gate), pl.ds(pl.multiple_of(here * step, 128), step))
    put(dot(unit_t[...], grad_up), pl.ds(pl.multiple_of((count + here) * step, 128), step))
    put_out(
        dot(g_t[...], active), pl.ds(pl.multiple_of(width // 2 + here * step, 128), step)
    )

    @pl.when(here == last)
    def _():
        partial_ref[...] = sum_out[...].astype(bf16)
        back_ref[...] = sum_back[...].astype(bf16)


def feed(first_order, second_order, x, ours, theirs, g, first, second, axes, step=1280):
    tokens, width = x.shape
    count = (first[0].shape[2] - width // 2) // step // 2
    rest = second[0].shape[2] - count * step

    def whole(*shape):
        return pl.BlockSpec(shape, lambda i, one, two: (0, 0))

    def piece(arrays, size, at):
        return [
            pl.BlockSpec((*array.shape[:2], size), lambda i, one, two: (0, 0, at(i)))
            for array in arrays
        ]

    pair = jax.ShapeDtypeStruct((tokens, width), bf16)
    return pl.pallas_call(
        functools.partial(feed_kernel, firsts=len(first), seconds=len(second), axes=axes),
        name="feed",
        grid_spec=pltpu.PrefetchScalarGridSpec(
            num_scalar_prefetch=2,
            grid=(count,),
            in_specs=[whole(tokens, width)] * 4
            + piece(first, step, lambda i: i)
            + piece(first, step, lambda i: count + i)
            + piece(second, step, lambda i: i)
            + piece(second, rest, lambda i: count * step // rest),
            out_specs=[whole(tokens, width)] * 3
            + [whole(width, 2 * count * step), whole(width, width // 2 + count * step + rest)],
            scratch_shapes=[
                pltpu.VMEM((tokens, width), bf16),
                pltpu.VMEM((width, tokens), bf16),
                pltpu.VMEM((width, tokens), bf16),
                pltpu.VMEM((tokens, width), f32),
                pltpu.VMEM((tokens, width), f32),
                pltpu.VMEM((width, step), bf16),
                pltpu.VMEM((width, step), bf16),
                pltpu.VMEM((width, step), bf16),
                pltpu.VMEM((width, rest), bf16),
            ],
        ),
        out_shape=[
            jax.ShapeDtypeStruct((tokens, width), f32),
            pair,
            pair,
            jax.ShapeDtypeStruct((width, 2 * count * step), bf16),
            jax.ShapeDtypeStruct((width, width // 2 + count * step + rest), bf16),
        ],
        compiler_params=pltpu.CompilerParams(vmem_limit_bytes=VMEM),
        cost_estimate=cost(2 * 9 * 2 * tokens * width * count * step, 24 << 20),
    )(first_order, second_order, x, ours, theirs, g, *first, *first, *second, *second)


def middle_back_kernel(
    core_ref, residual_ref, g_ref, ours_ref, theirs_ref, attn_ref, attended_ref, out_ours_ref,
    out_theirs_ref, grads_in_ref, layer_ref, residual_grad_ref, *rest, axes,
):
    dout_ref, grads_ref = rest
    rows = layer_ref.shape[0]
    half = attn_ref.shape[0]
    own = pl.ds(pl.multiple_of(core_ref[0] * rows, rows), rows)
    layer_ref[...] = (
        residual_ref[own, :]
        + out_ours_ref[own, :].astype(f32)
        + out_theirs_ref[...].astype(f32)
    ).astype(bf16)
    unit, inverse = unit_rows(residual_ref[...])
    scaled = ours_ref[...].astype(f32) + theirs_ref[...].astype(f32)
    grad = g_ref[...].astype(f32) + unit_back(scaled, unit, inverse)
    low = grad.astype(bf16)
    residual_grad_ref[...] = grad
    dout = dot(attn_ref[...], low, 1, 1).astype(bf16)
    for at in range(dout_ref.shape[0]):
        dout_ref[at] = dout[at * HDIM : (at + 1) * HDIM]
    grads = dot(attended_ref[...], low)
    few = grads.shape[0] // 8
    both = [part.reshape(few, 8, half) for part in (grads[:, :half], grads[:, half:])]
    both = jnp.stack(both, axis=1).reshape(grads_ref.shape).astype(bf16)
    for source, target in crossed_rows(axes):
        grads_ref[target * 16 : (target + 1) * 16] = both[source * 16 : (source + 1) * 16]


def middle_back(
    core, residual, g, ours, theirs, attn, attended, out_ours, out_theirs, grads, axes
):
    tokens, width = residual.shape
    rows = tokens // 2
    half = width // 2
    chips = half // HDIM

    def whole(*shape):
        return pl.BlockSpec(shape, lambda i, core: (0,) * len(shape))

    return pl.pallas_call(
        functools.partial(middle_back_kernel, axes=axes),
        name="middle_back",
        grid_spec=pltpu.PrefetchScalarGridSpec(
            num_scalar_prefetch=1,
            grid=(1,),
            in_specs=[whole(tokens, width)] * 4
            + [whole(half, width), whole(half, tokens), whole(tokens, width), whole(rows, width)]
            + [pl.BlockSpec(memory_space=pl.ANY)],
            out_specs=[whole(rows, width), whole(tokens, width)]
            + [whole(chips, HDIM, tokens), whole(width, half)],
        ),
        out_shape=[
            jax.ShapeDtypeStruct((rows, width), bf16),
            jax.ShapeDtypeStruct((tokens, width), f32),
        ]
        + [jax.ShapeDtypeStruct((chips, HDIM, tokens), bf16)]
        + [jax.ShapeDtypeStruct(grads.shape, bf16)],
        input_output_aliases={9: 3},
        compiler_params=pltpu.CompilerParams(vmem_limit_bytes=VMEM),
        cost_estimate=cost(2 * 2 * 2 * tokens * width * half, 16 << 20),
    )(core, residual, g, ours, theirs, attn, attended, out_ours, out_theirs, grads)


def hidden_back_kernel(order_ref, core_ref, shard_ref, w_ref, *rest):
    dp_refs, (own_ref, other_ref, stacked) = rest[:-3], rest[-3:]
    for place, dp_ref in enumerate(dp_refs):
        size = dp_ref.shape[0]
        stacked[pl.ds(pl.multiple_of(order_ref[place] * size, 64), size)] = dp_ref[...]
    rows = own_ref.shape[0]
    zero = core_ref[0] == 0
    size = w_ref.shape[1]
    for at in range(w_ref.shape[0]):
        flat = dot(w_ref[at], stacked[...])
        first = flat[:, :rows].T
        second = flat[:, rows:].T
        columns = pl.ds(pl.multiple_of(shard_ref[at] * size, size), size)
        own_ref[:, columns] = jnp.where(zero, first, second)
        other_ref[:, columns] = jnp.where(zero, second, first).astype(bf16)


def hidden_back(order, core, shard_order, weights, pieces):
    shards, size, columns = weights.shape
    width = shards * size
    rows = pieces[0].shape[1] // 2

    def whole(*shape):
        return pl.BlockSpec(shape, lambda i, order, core, shard: (0,) * len(shape))

    return pl.pallas_call(
        hidden_back_kernel,
        name="hidden_back",
        grid_spec=pltpu.PrefetchScalarGridSpec(
            num_scalar_prefetch=3,
            grid=(1,),
            in_specs=[whole(shards, size, columns)] + [whole(*pieces[0].shape)] * len(pieces),
            out_specs=[whole(rows, width)] * 2,
            scratch_shapes=[pltpu.VMEM((columns, 2 * rows), bf16)],
        ),
        out_shape=[
            jax.ShapeDtypeStruct((rows, width), f32),
            jax.ShapeDtypeStruct((rows, width), bf16),
        ],
        compiler_params=pltpu.CompilerParams(vmem_limit_bytes=VMEM),
        cost_estimate=cost(2 * 2 * 2 * rows * width * columns, 8 << 20),
    )(order, core, shard_order, weights, *pieces)


def head_grad_kernel(order_ref, unit_ref, *rest):
    dp_refs, out_ref = rest[:-1], rest[-1]
    block = dp_refs[0].shape[1]
    total = None
    for place, dp_ref in enumerate(dp_refs):
        rows = pl.ds(pl.multiple_of(order_ref[place] * block, block), block)
        added = dot(dp_ref[...], unit_ref[rows])
        total = added if total is None else total + added
    for at in range(out_ref.shape[0]):
        out_ref[at] = total[:, at * 128 : (at + 1) * 128].astype(bf16)


def head_grad(order, unit_all, pieces):
    length, width = unit_all.shape
    owners = width // 128
    size = pieces[0].shape[0]

    def whole(*shape):
        return pl.BlockSpec(shape, lambda i, order: (0,) * len(shape))

    return pl.pallas_call(
        head_grad_kernel,
        name="head_grad",
        grid_spec=pltpu.PrefetchScalarGridSpec(
            num_scalar_prefetch=1,
            grid=(1,),
            in_specs=[whole(length, width)] + [whole(*pieces[0].shape)] * len(pieces),
            out_specs=whole(owners, size, 128),
        ),
        out_shape=jax.ShapeDtypeStruct((owners, size, 128), bf16),
        compiler_params=pltpu.CompilerParams(vmem_limit_bytes=VMEM),
        cost_estimate=cost(2 * 2 * length * width * size, 10 << 20),
    )(order, unit_all, *pieces)


def adam_in_kernels(weight, gradient, first, second, rate):
    first = BETA_FIRST * first + (1.0 - BETA_FIRST) * gradient
    second = BETA_SECOND * second + (1.0 - BETA_SECOND) * gradient * gradient
    second_hat = second * (1.0 / (1.0 - BETA_SECOND**STEP))
    bottom = second_hat * lax.rsqrt(second_hat) + EPSILON
    guess = pl.reciprocal(bottom, approx=True)
    guess = guess * (2.0 - bottom * guess)
    scale = rate / (1.0 - BETA_FIRST**STEP)
    weight = weight * (1.0 - rate * DECAY) - (scale * first) * guess
    return (weight, first, second)


def adam_into(refs, weight, gradient, first, second, rate):
    for ref, value in zip(refs, adam_in_kernels(weight, gradient, first, second, rate)):
        ref[...] = value


def rounded_in_kernel(values):
    return values.astype(bf16).astype(f32)


def adam_most_kernel(grads_ref, gain_ref, *refs, rates):
    (w_in, m_in, v_in), attn, out = refs[:3], refs[3:6], refs[6:9]
    new_in, new_attn, new_out, gain_grad, turned = refs[9:12], refs[12:15], refs[15:18], *refs[18:]
    here = pl.program_id(0)
    chips = grads_ref.shape[0] // 2
    width = w_in.shape[1] // 2
    main = width // 256 * 128
    few = width // 2 - main
    out_at = 2 * main + attn[0].shape[2] // 2

    @pl.when(here == 0)
    def _():
        for core in range(2):
            columns = jnp.concatenate(
                [grads_ref[2 * chip + core, :, out_at : out_at + main] for chip in range(chips)],
                axis=0,
            )
            turned[core * main : (core + 1) * main] = columns.astype(f32).T
            rest = jnp.concatenate(
                [
                    grads_ref[2 * chip + core, :, out_at + main :] for chip in range(chips)
                ],
                axis=0,
            )
            start = 2 * main + core * few
            turned[start : start + few] = rest.astype(f32).T[2 * few : 3 * few]

    each = grads_ref.shape[1]
    some = w_in.shape[0] // each
    for at_chip in range(some):
        source = 2 * (here * some + at_chip)
        columns = []
        for at in range(2):
            for core in range(2):
                place = at * main
                columns.append(grads_ref[source + core, :, place : place + main].astype(f32))
            for core in range(2):
                rest = grads_ref[source + core, :, out_at + main :].astype(f32)
                columns.append(rest[:, at * few : (at + 1) * few])
        grads = jnp.concatenate(columns, axis=1)
        rows = slice(at_chip * each, (at_chip + 1) * each)
        weight = w_in[rows]
        gain_grad[rows] = jnp.sum(grads * rounded_in_kernel(weight), axis=1, keepdims=True)
        values = adam_in_kernels(
            weight, grads * gain_ref[rows], m_in[rows], v_in[rows], rates[0]
        )
        for ref, value in zip(new_in, values):
            ref[rows] = value
        rows = slice(at_chip * each // 2, (at_chip + 1) * each // 2)
        for core in range(2):
            piece = grads_ref[source + core, :, 2 * main : out_at].astype(f32)
            grads = jnp.concatenate([piece[: each // 2], piece[each // 2 :]], axis=1)
            values = adam_in_kernels(
                attn[0][core, rows], grads, attn[1][core, rows], attn[2][core, rows], rates[1]
            )
            for ref, value in zip(new_attn, values):
                ref[core, rows] = value

    size = out[0].shape[0]
    grads = turned[pl.ds(pl.multiple_of(here * size, 8), size)]
    adam_into(new_out, out[0][...], grads, out[1][...], out[2][...], rates[2])


def adam_most(
    grads, gain, weights_in, weights_attn, weights_out, rates, steps=2
):
    rows, columns = weights_in[0].shape
    width = weights_attn[0].shape[1]
    hidden = weights_out[0].shape[0]
    weights_attn = [array.reshape(2, rows // 2, width) for array in weights_attn]
    block_in = pl.BlockSpec((rows // steps, columns), lambda i: (i, 0))
    block_attn = pl.BlockSpec((2, rows // 2 // steps, width), lambda i: (0, i, 0))
    block_out = pl.BlockSpec((hidden // steps, rows), lambda i: (i, 0))
    column = pl.BlockSpec((rows // steps, 1), lambda i: (i, 0))
    blocks = [block_in] * 3 + [block_attn] * 3 + [block_out] * 3
    arrays = (*weights_in, *weights_attn, *weights_out)
    results = pl.pallas_call(
        functools.partial(adam_most_kernel, rates=rates),
        name="adam_most",
        grid=(steps,),
        in_specs=[pl.BlockSpec(grads.shape, lambda i: (0, 0, 0)), column] + blocks,
        out_specs=blocks + [column],
        out_shape=[jax.ShapeDtypeStruct(array.shape, f32) for array in arrays]
        + [jax.ShapeDtypeStruct((rows, 1), f32)],
        scratch_shapes=[pltpu.VMEM((hidden, rows), f32)],
        compiler_params=pltpu.CompilerParams(vmem_limit_bytes=VMEM),
        cost_estimate=cost(rows * columns * 20, rows * columns * 26),
    )(grads, gain, *arrays)
    new_attn = [array.reshape(rows, width) for array in results[3:6]]
    return results[:3], new_attn, results[6:9], results[9]


def adam_qkv_kernel(order_ref, *refs, rate):
    grads_refs, (gain_ref, other_ref), gains = refs[:-16], refs[-16:-14], refs[-14:-11]
    (w_ref, m_ref, v_ref), new, new_gains = refs[-11:-8], refs[-8:-5], refs[-5:-2]
    gain_grad, joined = refs[-2:]
    here = pl.program_id(0)
    heads = sum(grads_ref.shape[0] for grads_ref in grads_refs)

    @pl.when(here == 0)
    def _():
        at = 0
        for grads_ref in grads_refs:
            for place in range(grads_ref.shape[0]):
                for part in range(3):
                    row = (part * heads + order_ref[at]) * HDIM
                    joined[pl.ds(pl.multiple_of(row, HDIM), HDIM)] = grads_ref[
                        place, part * HDIM : (part + 1) * HDIM
                    ].astype(f32)
                at += 1

    size = w_ref.shape[1]
    grads = joined[pl.ds(pl.multiple_of(here * size, size), size)].T
    weight = w_ref[...]
    added = jnp.sum(grads * rounded_in_kernel(weight), axis=1, keepdims=True)
    gain_grad[...] = added + jnp.where(here == 0, 0.0, gain_grad[...])
    adam_into(new, weight, grads * gain_ref[...], m_ref[...], v_ref[...], rate)

    @pl.when(here == pl.num_programs(0) - 1)
    def _():
        both = jnp.concatenate(
            [gain_grad[...], other_ref[...], jnp.zeros((gain_grad.shape[0], 6), f32)], axis=1
        )
        adam_into(
            new_gains, gains[0][...], both.T[:2], gains[1][...], gains[2][...], GAIN_RATE
        )


def adam_qkv(order, grads, gain, other_gain, gains, weight, first, second, rate, step=1536):
    rows, columns = weight.shape
    block = pl.BlockSpec((rows, step), lambda i, order: (0, i))
    column = pl.BlockSpec((rows, 1), lambda i, order: (0, 0))
    block_gains = pl.BlockSpec(gains[0].shape, lambda i, order: (0, 0))
    same = jax.ShapeDtypeStruct((rows, columns), f32)
    return pl.pallas_call(
        functools.partial(adam_qkv_kernel, rate=rate),
        name="adam_qkv",
        grid_spec=pltpu.PrefetchScalarGridSpec(
            num_scalar_prefetch=1,
            grid=(columns // step,),
            in_specs=[pl.BlockSpec(piece.shape, lambda i, order: (0, 0, 0)) for piece in grads]
            + [column] * 2
            + [block_gains] * 3
            + [block] * 3,
            out_specs=[block] * 3 + [block_gains] * 3,
            scratch_shapes=[pltpu.VMEM((rows, 1), f32), pltpu.VMEM((columns, rows), f32)],
        ),
        out_shape=[same] * 3 + [jax.ShapeDtypeStruct(gains[0].shape, f32)] * 3,
        compiler_params=pltpu.CompilerParams(vmem_limit_bytes=VMEM),
        cost_estimate=cost(rows * columns * 20, rows * columns * 26),
    )(order, *grads, gain, other_gain, *gains, weight, first, second)


def ring(axis, shift):
    size = lax.axis_size(axis)
    return [(at, (at + shift) % size) for at in range(size)]


def gather_first_step(planes_first, lines_first):
    swapped = lax.ppermute(planes_first, "zh", SWAP)
    others = [
        lax.ppermute(lines_first, "y", ring("y", shift)) for shift in range(1, lax.axis_size("y"))
    ]
    return jnp.stack([planes_first, swapped]), jnp.stack([lines_first, *others])


def shards(
    tokens,
    positions,
    cotangent,
    weight_qkv,
    weight_attn,
    weight_in,
    weight_out,
    norm_gains,
    first_qkv,
    first_attn,
    first_in,
    first_out,
    first_gains,
    second_qkv,
    second_attn,
    second_in,
    second_out,
    second_gains,
):
    rows, width = tokens.shape[1:]
    shard_rows = weight_qkv.shape[1]
    heads = width // HDIM
    hidden = weight_out.shape[1]
    core = lax.axis_index("c")
    mine = lax.axis_index(CTX)
    chip = lax.axis_index(CHIPS)
    chips = lax.axis_size(CHIPS)
    owners = lax.axis_size(FSDP)
    length = rows * chips * 2
    main = hidden // 256 * 128
    few = hidden // 2 - main
    core_at = core.reshape(1).astype(jnp.int32)
    axes = (lax.axis_size("zh"), lax.axis_size("y"), lax.axis_size("x"), lax.axis_size("zl"))
    offsets = [(far, near) for far in range(lax.axis_size("x")) for near in range(2)]
    across, beside = lax.axis_index("x"), lax.axis_index("zl")
    wide = lax.axis_size("x")

    def chips_at(sign):
        places = [(across + sign * far) % wide * 2 + (beside ^ near) for far, near in offsets]
        return jnp.stack(places).astype(jnp.int32)

    local = tokens[0]
    extra = 16
    high, low = positions[0] // 128, positions[0] % 128
    places_row = jnp.concatenate([high, low, jnp.zeros((width - 2 * rows,), jnp.int32)])
    places_rows = jnp.concatenate(
        [places_row[None], jnp.zeros((extra - 1, width), jnp.int32)], axis=0
    ).astype(bf16)
    sequence = lax.all_gather(
        jnp.concatenate([local, places_rows], axis=0), CTX, axis=0, tiled=True
    )
    first_part, second_part, head_part, half_heads = prepare(
        jnp.stack([core, chip]).astype(jnp.int32),
        norm_gains[0],
        weight_qkv[0],
        weight_attn[0],
        weight_in[0],
        weight_out[0],
    )
    first_joined, second_joined = gather_first_step(first_part, second_part)
    head_weights = lax.all_to_all(
        jnp.broadcast_to(head_part, (owners, *head_part.shape)), FSDP, 0, 0, tiled=True
    )
    first_pieces = [first_joined] + [
        lax.ppermute(first_joined, "y", ring("y", shift))
        for shift in range(1, lax.axis_size("y"))
    ]
    sequence, _, second_joined, half_heads, _ = lax.optimization_barrier(
        (sequence, first_joined, second_joined, half_heads, head_weights)
    )
    half_heads_other = lax.ppermute(half_heads, "zh", SWAP)
    second_pieces = [second_joined, lax.ppermute(second_joined, "zh", SWAP)]
    lines = lax.axis_size("y")
    plane, line = lax.axis_index("zh"), lax.axis_index("y")
    heads_order = jnp.stack(
        [(plane ^ far) * lines + at for at in range(lines) for far in range(2)]
    ).astype(jnp.int32)
    first_order = jnp.stack(
        [(plane ^ far) * lines + (line - shift) % lines for shift in range(lines) for far in range(2)]
    ).astype(jnp.int32)
    second_order = jnp.stack(
        [(plane ^ far) * lines + (line - shift) % lines for far in range(2) for shift in range(lines)]
    ).astype(jnp.int32)

    def in_order(ours, theirs):
        first = jnp.where(core == 0, ours, theirs)
        second = jnp.where(core == 0, theirs, ours)
        return jnp.concatenate([first, second], axis=0)

    def swap(array):
        return lax.ppermute(array, "c", SWAP)

    gradient = in_order(cotangent[0], swap(cotangent[0]))

    freqs = jnp.exp(jnp.arange(HDIM // 2, dtype=f32) * (-2.0 * math.log(ROPE_BASE) / HDIM))
    by_device = sequence.reshape(2 * chips, rows + extra, width)[:, rows]
    by_device = by_device.astype(f32)
    places = by_device[:, :rows] * 128.0 + by_device[:, rows : 2 * rows]
    angles = freqs[:, None] * places.reshape(1, length)
    cosine = jnp.cos(angles)
    sine = jnp.sin(angles)
    unit_all, qkv, keys, values = project(sequence, head_weights, cosine, sine, extra)
    low_out, out, lse = attend(keys, qkv, chips)
    firsts = len(first_pieces)
    low_out, half_heads_other, *arrived = lax.optimization_barrier(
        (low_out, half_heads_other, *first_pieces, *second_pieces)
    )
    first_pieces, second_pieces = arrived[:firsts], arrived[firsts:]
    mat_qkv = lax.all_gather(
        jnp.stack([half_heads, half_heads_other]), "y", axis=0, tiled=True
    )
    attended = lax.all_to_all(low_out, CHIPS, 0, 0, tiled=True)
    attended = attended.reshape(heads // 2 * HDIM, 2 * rows)
    mixed, mat_attn = attend_out(first_order, attended, first_pieces)
    current = lax.dynamic_slice_in_dim(
        sequence, chip * 2 * (rows + extra), 2 * (rows + extra), 0
    ).reshape(2, rows + extra, width)[:, :rows].reshape(2 * rows, width)
    residual, partial, back, grads, out_grads = feed(
        first_order, second_order, current, mixed, swap(mixed), gradient, first_pieces,
        second_pieces, axes,
    )
    grads, mat_qkv = lax.optimization_barrier((grads, mat_qkv))
    first_sum = lax.psum_scatter(grads, "y", scatter_dimension=0, tiled=True)

    def move(pieces, sign):
        moved = [pieces[0]]
        for (far, near), piece in list(zip(offsets, pieces))[1:]:
            pairs = [
                (at, (at // 2 + sign * far) % wide * 2 + (at % 2 ^ near)) for at in range(chips)
            ]
            moved.append(lax.ppermute(piece, CHIPS, pairs))
        return moved

    ahead, behind = chips_at(1), chips_at(-1)
    theirs = swap(lax.dynamic_slice_in_dim(partial, (1 - core) * rows, rows, 0))
    layer_out, residual_grad, dout_pair, out_grads = middle_back(
        core_at, residual, gradient, back, swap(back), mat_attn, attended, partial, theirs,
        out_grads, axes,
    )

    douts = lax.all_to_all(dout_pair, CHIPS, 0, 0, tiled=True)
    out_grads, douts = lax.optimization_barrier((out_grads, douts))
    out_arrived = lax.all_to_all(out_grads, ("x", "zh", "zl"), 0, 0, tiled=True)
    pieces = attend_back(behind, keys, values, qkv, douts, out, lse, cosine, sine)
    out_arrived, *pieces = lax.optimization_barrier((out_arrived, *pieces))
    first_sum, *pieces = lax.optimization_barrier((first_sum, *pieces))
    arrived = lax.all_to_all(first_sum, ("x", "zh", "zl"), 0, 0, tiled=True)
    moved = move(pieces, -1)

    def total(arrays):
        return sum(array.astype(f32) for array in arrays).astype(bf16)

    out_arrived = out_arrived.reshape(2 * chips, width // (2 * chips), -1)
    out_sum = jnp.sum(out_arrived.astype(f32), axis=0).astype(bf16)
    out_sum = out_sum.reshape(lines, shard_rows // chips, -1)
    out_parts = [
        lax.dynamic_index_in_dim(out_sum, (line + shift) % lines, 0, keepdims=False)
        for shift in range(lines)
    ]
    out_sum = total(
        out_parts[:1]
        + [
            lax.ppermute(part, "y", ring("y", shift))
            for shift, part in list(enumerate(out_parts))[1:]
        ]
    )

    arrived, out_sum, *moved = lax.optimization_barrier((arrived, out_sum, *moved))
    pieces = lax.optimization_barrier((*pieces, arrived))[:chips]
    head_parts = head_grad(behind, unit_all, pieces)
    own_hidden, other_hidden = hidden_back(ahead, core_at, heads_order, mat_qkv, moved)
    grad_hidden = own_hidden + swap(other_hidden).astype(f32)
    unit_in, scale_in = unit_rows(local.astype(f32))
    own_residual = lax.dynamic_slice_in_dim(residual_grad, core * rows, rows, 0)
    tokens_grad = (own_residual + unit_back(grad_hidden, unit_in, scale_in))[None]

    arrived = arrived.reshape(2 * chips, shard_rows // chips, -1)
    second_sum = jnp.sum(arrived.astype(f32), axis=0).astype(bf16)
    second_sum = jnp.concatenate([second_sum, out_sum], axis=1)
    all_grads = lax.all_gather(second_sum, CTX, axis=0, tiled=False)

    head_sums = lax.all_to_all(head_parts, FSDP, 0, 0, tiled=True)
    head_own = jnp.sum(head_sums.astype(f32), axis=0).astype(bf16)[None]
    head_pair = jnp.concatenate([head_own, swap(head_own)], axis=0)
    head_four = jnp.concatenate([head_pair, lax.ppermute(head_pair, "zl", SWAP)], axis=0)
    head_grads = [head_four] + [
        lax.ppermute(head_four, "x", ring("x", shift)) for shift in range(1, wide)
    ]
    head_order = jnp.stack(
        [
            (across - shift) % wide * 4 + (beside ^ near) * 2 + (core ^ other)
            for shift in range(wide)
            for near in range(2)
            for other in range(2)
        ]
    ).astype(jnp.int32)

    rates = (
        width ** (-0.5),
        max(1, 3 * width // length) ** (-0.5),
        width ** (-0.5),
        hidden ** (-0.5),
    )
    columns_of_gains = norm_gains[0].astype(bf16).astype(f32).T
    new_in, new_attn, new_out, gain_second = adam_most(
        all_grads,
        columns_of_gains[:, 1:],
        (weight_in[0], first_in[0], second_in[0]),
        (weight_attn[0], first_attn[0], second_attn[0]),
        (weight_out[0], first_out[0], second_out[0]),
        (rates[2], rates[1], rates[3]),
    )
    results = adam_qkv(
        head_order,
        head_grads,
        columns_of_gains[:, :1],
        gain_second,
        (norm_gains[0], first_gains[0], second_gains[0]),
        weight_qkv[0],
        first_qkv[0],
        second_qkv[0],
        rates[0],
    )
    new_qkv, new_gains = results[:3], results[3:]
    updated = (new_qkv, new_attn, new_in, new_out, new_gains)
    return (
        layer_out[None],
        tokens_grad,
        *[updated[member][0][None] for member in range(5)],
        *[updated[member][1][None] for member in range(5)],
        *[updated[member][2][None] for member in range(5)],
    )


def solution(mesh):
    split = Mesh(mesh.devices.reshape(4, 2, 2, 2, 4), ("x", "zl", "c", "zh", "y"))
    by_row = P(None, FSDP, None)
    by_column = P(None, None, FSDP)
    weights = (by_row, by_row, by_row, by_column, by_column)
    by_token = P(FSDP, CTX, None)
    return jax.shard_map(
        shards,
        mesh=split,
        in_specs=(by_token, P(FSDP, CTX), by_token) + weights * 3,
        out_specs=(by_token, by_token) + weights * 3,
        check_vma=False,
    )
```

```python
import functools
import math

import jax
import jax.numpy as jnp
from jax import lax
from jax.experimental import pallas as pl
from jax.experimental.pallas import tpu as pltpu
from jax.sharding import Mesh, PartitionSpec as P

HDIM = 64
STEP = 10
BETA_FIRST = 0.5
BETA_SECOND = 0.5
EPSILON = 1e-08
DECAY = 0.01
NORM_EPS = 1e-05
ROPE_BASE = 160000.0
GAIN_RATE = 0.6
LOG2E = math.log2(math.e)
f32 = jnp.float32
bf16 = jnp.bfloat16

CHIPS = ("x", "zl")
CTX = ("x", "zl", "c")
FSDP = ("zh", "y")
SWAP = [(0, 1), (1, 0)]
VMEM = 60 << 20


def dot(left, right, left_dim=1, right_dim=0):
    return lax.dot_general(
        left, right, (((left_dim,), (right_dim,)), ((), ())), preferred_element_type=f32
    )


def cost(flops, moved):
    return pl.CostEstimate(flops=flops, bytes_accessed=moved, transcendentals=0)


def unit_rows(values):
    average = jnp.mean(values, axis=-1, keepdims=True)
    centered = values - average
    spread = jnp.mean(centered * centered, axis=-1, keepdims=True)
    inverse = lax.rsqrt(spread + NORM_EPS)
    return centered * inverse, inverse


def unit_back(scaled, unit, inverse):
    first_mean = jnp.mean(scaled, axis=-1, keepdims=True)
    second_mean = jnp.mean(scaled * unit, axis=-1, keepdims=True)
    return inverse * (scaled - first_mean - unit * second_mean)


def prepare_kernel(
    place_ref, gains_ref, qkv_ref, attn_ref, in_ref, out_ref,
    first_ref, second_ref, head_ref, heads_ref,
):
    core, chip = place_ref[0], place_ref[1]
    rows = qkv_ref.shape[0]
    width = attn_ref.shape[1]
    hidden = out_ref.shape[0]
    main = hidden // 256 * 128
    few = hidden // 2 - main
    half = width // 2
    low_gains = gains_ref[...].astype(bf16).astype(f32)
    columns = jnp.concatenate([low_gains, jnp.zeros((6, rows), f32)], axis=0).T
    gain_first, gain_second = columns[:, 0:1], columns[:, 1:2]

    def pick(array):
        size = array.shape[1] // 2
        return jnp.where(core == 0, array[:, :size], array[:, size:])

    def scaled(values, gain):
        return (values.astype(bf16).astype(f32) * gain).astype(bf16)

    attn_rows = attn_ref[pl.ds(pl.multiple_of(core * HDIM, HDIM), HDIM)].astype(bf16)
    first_ref[:HDIM, 2 * main :] = attn_rows[:, :half]
    first_ref[HDIM:, 2 * main :] = attn_rows[:, half:]
    first_ref[:, :main] = scaled(pick(in_ref[:, : 2 * main]), gain_second)
    first_ref[:, main : 2 * main] = scaled(
        pick(in_ref[:, hidden : hidden + 2 * main]), gain_second
    )
    out_rows = out_ref[pl.ds(pl.multiple_of(core * main, 128), main)]
    second_ref[:, :main] = out_rows.T.astype(bf16)
    odd_out = out_ref[2 * main :].T
    odd = [
        scaled(pick(in_ref[:, 2 * main : hidden]), gain_second),
        scaled(pick(in_ref[:, hidden + 2 * main :]), gain_second),
        pick(odd_out).astype(bf16),
        jnp.zeros((rows, few), bf16),
    ]
    second_ref[:, main:] = jnp.concatenate(odd, axis=1)
    pieces = []
    for at in range(width // 128):
        for part in range(3):
            start = part * width + at * 128
            pieces.append(scaled(pick(qkv_ref[:, start : start + 128]), gain_first))
    heads_ref[...] = jnp.concatenate(pieces, axis=1)
    own = []
    for part in range(3):
        start = pl.multiple_of(part * width + chip * 128, 128)
        own.append(scaled(pick(qkv_ref[:, pl.ds(start, 128)]), gain_first).astype(f32))
    own.append(jnp.zeros((rows, HDIM), f32))
    head_ref[...] = jnp.concatenate(own, axis=1).T[: 3 * HDIM].astype(bf16)


def prepare(place, gains, qkv, attn, weight_in, weight_out):
    rows, width = attn.shape
    hidden = weight_out.shape[0]
    main = hidden // 256 * 128
    arrays = (gains, qkv, attn, weight_in, weight_out)
    shapes = [
        (rows, width // 2 + 2 * main),
        (rows, main + 4 * (hidden // 2 - main)),
        (3 * HDIM, rows),
        (rows, 3 * width // 2),
    ]

    def whole(shape):
        return pl.BlockSpec(shape, lambda i, place: (0, 0))

    return pl.pallas_call(
        prepare_kernel,
        name="prepare",
        grid_spec=pltpu.PrefetchScalarGridSpec(
            num_scalar_prefetch=1,
            grid=(1,),
            in_specs=[whole(array.shape) for array in arrays],
            out_specs=[whole(shape) for shape in shapes],
        ),
        out_shape=[jax.ShapeDtypeStruct(shape, bf16) for shape in shapes],
        compiler_params=pltpu.CompilerParams(vmem_limit_bytes=VMEM),
        cost_estimate=cost(rows * width * 60, 10 << 20),
    )(place, *arrays)


def project_kernel(
    x_ref, w_ref, cos_ref, sin_ref, unit_ref, qkv_ref, keys_ref, values_ref, w_all, *, extra
):
    half = HDIM // 2
    rows = cos_ref.shape[1]

    @pl.when(pl.program_id(0) == 0)
    def _():
        for part in range(w_ref.shape[0]):
            w_all[part * 128 : (part + 1) * 128] = w_ref[part].astype(f32).T.astype(bf16)

    count = (x_ref.shape[0] - rows) // extra
    each = rows // count
    for at in range(count):
        tokens = x_ref[at * (each + extra) : at * (each + extra) + each].astype(f32)
        unit_ref[at * each : (at + 1) * each] = unit_rows(tokens)[0].astype(bf16)
    unit = unit_ref[...]
    mixed = dot(unit, w_all[...]).T
    cosine = cos_ref[...]
    sine = sin_ref[...]

    def turn(one, two):
        return jnp.concatenate([one * cosine - two * sine, two * cosine + one * sine], axis=0)

    queries = turn(mixed[:half], mixed[half:HDIM])
    keys = turn(mixed[HDIM : HDIM + half], mixed[HDIM + half : 2 * HDIM])
    values = mixed[2 * HDIM :]
    qkv_ref[...] = jnp.concatenate([queries, keys, values], axis=0).astype(bf16)
    key_rows = keys.T.astype(bf16)
    value_rows = values.T.astype(bf16)
    ones = jnp.where(lax.broadcasted_iota(jnp.int32, (rows, HDIM), 1) < 3, 1.0, 0.0).astype(bf16)
    keys_ref[...] = jnp.concatenate([key_rows, key_rows, key_rows, ones], axis=1)
    values_ref[...] = jnp.concatenate([value_rows, ones], axis=1)


def project(tokens, weights, cosine, sine, extra, block=1024):
    width = tokens.shape[1]
    length = cosine.shape[1]
    steps = length // block
    return pl.pallas_call(
        functools.partial(project_kernel, extra=extra),
        name="project",
        grid=(steps,),
        in_specs=[
            pl.BlockSpec((tokens.shape[0] // steps, width), lambda i: (i, 0)),
            pl.BlockSpec(weights.shape, lambda i: (0, 0, 0)),
            pl.BlockSpec((HDIM // 2, block), lambda i: (0, i)),
            pl.BlockSpec((HDIM // 2, block), lambda i: (0, i)),
        ],
        out_specs=[
            pl.BlockSpec((block, width), lambda i: (i, 0)),
            pl.BlockSpec((3 * HDIM, block), lambda i: (0, i)),
            pl.BlockSpec((block, 256), lambda i: (i, 0)),
            pl.BlockSpec((block, 128), lambda i: (i, 0)),
        ],
        out_shape=[
            jax.ShapeDtypeStruct((length, width), bf16),
            jax.ShapeDtypeStruct((3 * HDIM, length), bf16),
            jax.ShapeDtypeStruct((length, 256), bf16),
            jax.ShapeDtypeStruct((length, 128), bf16),
        ],
        scratch_shapes=[pltpu.VMEM((width, 3 * HDIM), bf16)],
        compiler_params=pltpu.CompilerParams(vmem_limit_bytes=VMEM),
        cost_estimate=cost(length * width, 1 << 20),
    )(tokens, weights, cosine, sine)


def scaled_queries(queries):
    scaled = queries.astype(f32) * (LOG2E / math.sqrt(HDIM))
    high = scaled.astype(bf16)
    rest = scaled - high.astype(f32)
    middle = rest.astype(bf16)
    low = (rest - middle.astype(f32)).astype(bf16)
    return high, middle, low


def minus_in_three(values):
    rows = values.shape[1]
    at = lax.broadcasted_iota(jnp.int32, (16, rows), 0)
    high = (-values).astype(bf16).astype(f32)
    rest = -values - high
    middle = rest.astype(bf16).astype(f32)
    low = rest - middle
    stacked = jnp.where(at == 0, high, jnp.where(at == 1, middle, jnp.where(at == 2, low, 0.0)))
    return stacked.astype(bf16)


def attend_kernel(
    keys_ref, q_ref, k_ref, v_ref, low_ref, out_ref, lse_ref, v_ones, longest, *, part
):
    length = keys_ref.shape[0]
    count = length // part

    @pl.when(pl.program_id(0) == 0)
    def _():
        v_ones[:HDIM] = v_ref[...]
        v_ones[HDIM:] = jnp.where(
            lax.broadcasted_iota(jnp.int32, (16, length), 0) < 1, 1.0, 0.0
        ).astype(bf16)
        squares = jnp.sum(k_ref[...].astype(f32) ** 2, axis=0, keepdims=True)
        longest[...] = jnp.broadcast_to(jnp.max(squares, axis=1, keepdims=True), longest.shape)

    queries = jnp.concatenate(scaled_queries(q_ref[...]), axis=0)

    def finish(total, shift):
        summed = total[HDIM : HDIM + 1]
        result = total[:HDIM] / summed
        out_ref[...] = result
        lse_ref[...] = shift + jnp.log2(summed)
        step = low_ref.shape[2]
        for at in range(low_ref.shape[0]):
            low_ref[at] = result[:, at * step : (at + 1) * step].astype(bf16)
        return summed

    squares = jnp.sum((q_ref[...].astype(f32) * (LOG2E / math.sqrt(HDIM))) ** 2, axis=0, keepdims=True)
    shift = jnp.sqrt(squares * longest[0:1, 0:1])
    shifted = jnp.concatenate([queries, minus_in_three(shift)], axis=0)

    def score(at):
        return dot(keys_ref[at * part : (at + 1) * part, : 3 * HDIM + 16], shifted)

    scores = score(0)
    total = None
    for at in range(count):
        following = score(at + 1) if at + 1 < count else None
        soft = jnp.exp2(scores).astype(bf16)
        added = dot(v_ones[:, at * part : (at + 1) * part], soft)
        total = added if total is None else total + added
        scores = following
    summed = finish(total, shift)

    @pl.when(jnp.min(summed) < 2.0**-60)
    def _():
        def exact(at, carry):
            highest, total = carry
            rows = pl.ds(pl.multiple_of(at * part, part), part)
            scores = dot(keys_ref[rows, : 3 * HDIM], queries)
            raised = jnp.maximum(highest, jnp.max(scores, axis=0, keepdims=True))
            soft = jnp.exp2(scores - raised).astype(bf16)
            added = dot(v_ones[:, rows], soft)
            return raised, total * jnp.exp2(highest - raised) + added

        start = (
            jnp.full((1, q_ref.shape[1]), -1e30, f32),
            jnp.zeros((HDIM + 16, q_ref.shape[1]), f32),
        )
        highest, total = lax.fori_loop(0, count, exact, start)
        finish(total, highest)


def attend(keys, qkv, chips, block=1024, part=512):
    length = keys.shape[0]
    return pl.pallas_call(
        functools.partial(attend_kernel, part=part),
        name="attend",
        grid=(length // block,),
        in_specs=[
            pl.BlockSpec(keys.shape, lambda i: (0, 0)),
            pl.BlockSpec((HDIM, block), lambda i: (0, i)),
            pl.BlockSpec((HDIM, length), lambda i: (1, 0)),
            pl.BlockSpec((HDIM, length), lambda i: (2, 0)),
        ],
        out_specs=[
            pl.BlockSpec((block * chips // length, HDIM, length // chips), lambda i: (i, 0, 0)),
            pl.BlockSpec((HDIM, block), lambda i: (0, i)),
            pl.BlockSpec((1, block), lambda i: (0, i)),
        ],
        out_shape=[
            jax.ShapeDtypeStruct((chips, HDIM, length // chips), bf16),
            jax.ShapeDtypeStruct((HDIM, length), f32),
            jax.ShapeDtypeStruct((1, length), f32),
        ],
        scratch_shapes=[pltpu.VMEM((HDIM + 16, length), bf16), pltpu.VMEM((8, 128), f32)],
        compiler_params=pltpu.CompilerParams(vmem_limit_bytes=VMEM),
        cost_estimate=cost(length * HDIM, 1 << 20),
    )(keys, qkv, qkv, qkv)


def attend_back_kernel(
    order_ref,
    keys_ref,
    values_ref,
    q_ref,
    k_ref,
    out_ref,
    lse_ref,
    cos_ref,
    sin_ref,
    *rest,
    part,
):
    dout_ref, dp_refs, (sums, dq_all) = rest[0], rest[1:-2], rest[-2:]
    half = HDIM // 2
    here = pl.program_id(0)
    length = keys_ref.shape[0]
    block = q_ref.shape[1]
    count = length // part
    factor = HDIM ** (-0.5)

    def turn_back(grads, cosine, sine):
        low = grads.astype(bf16).astype(f32)
        one, two = low[:half], low[half:]
        return jnp.concatenate([one * cosine + two * sine, two * cosine - one * sine], axis=0)

    @pl.when(here == 0)
    def _():
        sums[...] = jnp.zeros_like(sums)

    low_queries = q_ref[...]
    queries = jnp.concatenate(
        [*scaled_queries(low_queries), minus_in_three(lse_ref[...])], axis=0
    )
    low_dout = dout_ref[order_ref[here]]
    dout = low_dout.astype(f32)
    centre = jnp.sum(dout * out_ref[...], axis=0, keepdims=True)
    douts = jnp.concatenate([low_dout, minus_in_three(centre)], axis=0)
    blank = jnp.zeros((block, HDIM), bf16)
    right = jnp.concatenate(
        [
            jnp.concatenate([low_queries.astype(f32).T.astype(bf16), blank], axis=1),
            jnp.concatenate([blank, dout.T.astype(bf16)], axis=1),
        ],
        axis=0,
    )

    def score(at):
        rows = slice(at * part, (at + 1) * part)
        return (
            dot(keys_ref[rows, : 3 * HDIM + 16], queries),
            dot(values_ref[rows, : HDIM + 16], douts),
        )

    now = score(0)
    grad_queries = None
    for at in range(count):
        following = score(at + 1) if at + 1 < count else None
        rows = slice(at * part, (at + 1) * part)
        soft = jnp.exp2(now[0])
        grads = (soft * now[1]).astype(bf16)
        added = dot(k_ref[:, rows], grads)
        grad_queries = added if grad_queries is None else grad_queries + added
        sums[rows] += dot(jnp.concatenate([grads, soft.astype(bf16)], axis=1), right)
        now = following

    def columns_of(place):
        return pl.ds(pl.multiple_of(order_ref[place] * block, block), block)

    columns = columns_of(here)
    dq_all[here] = turn_back(
        grad_queries * factor, cos_ref[:, columns], sin_ref[:, columns]
    ).astype(bf16)

    @pl.when(here == length // block - 1)
    def _():
        for place, dp_ref in enumerate(dp_refs):
            columns = columns_of(place)
            both = sums[columns].T
            dp_ref[:HDIM] = dq_all[place]
            dp_ref[HDIM : 2 * HDIM] = turn_back(
                both[:HDIM] * factor, cos_ref[:, columns], sin_ref[:, columns]
            ).astype(bf16)
            dp_ref[2 * HDIM :] = both[HDIM:].astype(bf16)


def attend_back(order, keys, values, qkv, douts, out, lse, cosine, sine, part=256):
    length = keys.shape[0]
    chips, _, block = douts.shape
    scores = length * length

    def whole(array):
        return pl.BlockSpec(array.shape, lambda i, order: (0, 0))

    return pl.pallas_call(
        functools.partial(attend_back_kernel, part=part),
        name="attend_back",
        grid_spec=pltpu.PrefetchScalarGridSpec(
            num_scalar_prefetch=1,
            grid=(chips,),
            in_specs=[
                whole(keys),
                whole(values),
                pl.BlockSpec((HDIM, block), lambda i, order: (0, order[i])),
                pl.BlockSpec((HDIM, length), lambda i, order: (1, 0)),
                pl.BlockSpec((HDIM, block), lambda i, order: (0, order[i])),
                pl.BlockSpec((1, block), lambda i, order: (0, order[i])),
                whole(cosine),
                whole(sine),
                pl.BlockSpec(douts.shape, lambda i, order: (0, 0, 0)),
            ],
            out_specs=[pl.BlockSpec((3 * HDIM, block), lambda i, order: (0, 0))] * chips,
            scratch_shapes=[
                pltpu.VMEM((length, 2 * HDIM), f32),
                pltpu.VMEM((chips, HDIM, block), bf16),
            ],
        ),
        out_shape=[jax.ShapeDtypeStruct((3 * HDIM, block), bf16)] * chips,
        compiler_params=pltpu.CompilerParams(vmem_limit_bytes=VMEM),
        cost_estimate=cost(5 * 4 * 2 * scores * HDIM, 8 << 20),
    )(order, keys, values, qkv, qkv, out, lse, cosine, sine, douts)


def attend_out_kernel(order_ref, attended_ref, *rest):
    piece_refs, (mixed_ref, attn_ref) = rest[:-2], rest[-2:]
    half = attn_ref.shape[1] // 2
    at = 0
    for piece_ref in piece_refs:
        for place in range(piece_ref.shape[0]):
            rows = pl.ds(pl.multiple_of(order_ref[at] * HDIM, HDIM), HDIM)
            attn_ref[rows, :half] = piece_ref[place, :HDIM]
            attn_ref[rows, half:] = piece_ref[place, HDIM:]
            at += 1
    turned = attended_ref[...].astype(f32).T.astype(bf16)
    mixed_ref[...] = dot(turned, attn_ref[...]).astype(bf16)


def attend_out(order, attended, pieces):
    size, tokens = attended.shape
    width = 2 * size

    def whole(*shape):
        return pl.BlockSpec(shape, lambda i, order: (0,) * len(shape))

    return pl.pallas_call(
        attend_out_kernel,
        name="attend_out",
        grid_spec=pltpu.PrefetchScalarGridSpec(
            num_scalar_prefetch=1,
            grid=(1,),
            in_specs=[whole(size, tokens)]
            + [
                pl.BlockSpec(
                    (*piece.shape[:2], size), lambda i, order: (0, 0, pieces[0].shape[2] // size - 1)
                )
                for piece in pieces
            ],
            out_specs=[whole(tokens, width), whole(size, width)],
        ),
        out_shape=[
            jax.ShapeDtypeStruct((tokens, width), bf16),
            jax.ShapeDtypeStruct((size, width), bf16),
        ],
        compiler_params=pltpu.CompilerParams(vmem_limit_bytes=VMEM),
        cost_estimate=cost(2 * 2 * tokens * width * size, 4 << 20),
    )(order, attended, *pieces)


def crossed_rows(axes):
    planes, lines, wide, beside = axes
    for plane in range(planes):
        for line in range(lines):
            for far in range(wide):
                for near in range(beside):
                    yield (
                        ((plane * lines + line) * wide + far) * beside + near,
                        ((far * planes + plane) * beside + near) * lines + line,
                    )


def feed_kernel(
    first_order, second_order, x_ref, ours_ref, theirs_ref, g_ref, *rest, firsts, seconds, axes
):
    weight_refs = []
    start = 0
    for size in (firsts, firsts, seconds, seconds):
        weight_refs.append(rest[start : start + size])
        start += size
    planes, lines, wide, beside = axes

    def put(grads, columns):
        size = grads.shape[0] // (planes * lines * wide)
        low = grads.astype(bf16)
        for plane in range(planes):
            for line in range(lines):
                for far in range(wide):
                    source = ((plane * lines + line) * wide + far) * size
                    target = ((line * wide + far) * planes + plane) * size
                    grads_ref[target : target + size, columns] = low[source : source + size]
    residual_ref, partial_ref, back_ref, grads_ref, out_grads_ref = rest[-14:-9]
    unit, unit_t, g_t, sum_out, sum_back = rest[-9:-4]
    gate_ref, up_ref, out_ref, rest_ref = rest[-4:]
    here = pl.program_id(0)
    last = pl.num_programs(0) - 1
    width = x_ref.shape[1]
    step = gate_ref.shape[1]

    def join(total, parts, order):
        at = 0
        for part in parts:
            size = part.shape[1]
            for place in range(part.shape[0]):
                total[pl.ds(pl.multiple_of(order[at] * size, size), size)] = part[place]
                at += 1

    def bend(gate, upward):
        cdf = 0.5 + 0.5 * lax.erf(gate * math.sqrt(0.5))
        slope = cdf + gate * jnp.exp(gate * gate * -0.5) * (1.0 / math.sqrt(2.0 * math.pi))
        bent = gate * cdf
        return bent, slope, (bent * upward).astype(bf16)

    def put_out(grads, columns):
        size = grads.shape[0] // (planes * lines * wide * beside)
        low = grads.astype(bf16)
        for source, target in crossed_rows(axes):
            out_grads_ref[target * size : (target + 1) * size, columns] = low[
                source * size : (source + 1) * size
            ]

    @pl.when(here == 0)
    def _():
        residual = (
            x_ref[...].astype(f32) + ours_ref[...].astype(f32) + theirs_ref[...].astype(f32)
        )
        residual_ref[...] = residual
        normed = unit_rows(residual)[0]
        unit[...] = normed.astype(bf16)
        unit_t[...] = normed.T.astype(bf16)
        g_t[...] = g_ref[...].astype(f32).T.astype(bf16)
        join(rest_ref, weight_refs[3], second_order)
        few = rest_ref.shape[1] // 4
        both = dot(unit[...], rest_ref[...])
        grad = dot(g_ref[...], rest_ref[...])[:, 2 * few : 3 * few]
        bent, slope, active = bend(both[:, :few], both[:, few : 2 * few])
        grad_gate = (grad * both[:, few : 2 * few] * slope).astype(bf16)
        grad_up = (grad * bent).astype(bf16)
        blank = jnp.zeros_like(active)
        outs = jnp.concatenate([blank, blank, active, blank], axis=1)
        ins = jnp.concatenate([grad_gate, grad_up, blank, blank], axis=1)
        sum_out[...] = dot(outs, rest_ref[...], 1, 1)
        sum_back[...] = dot(ins, rest_ref[...], 1, 1)
        put_out(
            dot(unit_t[...], ins) + dot(g_t[...], outs),
            slice(out_grads_ref.shape[1] - 4 * few, out_grads_ref.shape[1]),
        )

    join(gate_ref, weight_refs[0], first_order)
    join(up_ref, weight_refs[1], first_order)
    join(out_ref, weight_refs[2], second_order)
    gate = dot(unit[...], gate_ref[...])
    upward = dot(unit[...], up_ref[...])
    grad = dot(g_ref[...], out_ref[...])
    bent, slope, active = bend(gate, upward)
    grad_gate = (grad * upward * slope).astype(bf16)
    grad_up = (grad * bent).astype(bf16)
    sum_out[...] += dot(active, out_ref[...], 1, 1)
    sum_back[...] += dot(grad_gate, gate_ref[...], 1, 1) + dot(grad_up, up_ref[...], 1, 1)
    count = grads_ref.shape[1] // step // 2
    put(dot(unit_t[...], grad_gate), pl.ds(pl.multiple_of(here * step, 128), step))
    put(dot(unit_t[...], grad_up), pl.ds(pl.multiple_of((count + here) * step, 128), step))
    put_out(
        dot(g_t[...], active), pl.ds(pl.multiple_of(width // 2 + here * step, 128), step)
    )

    @pl.when(here == last)
    def _():
        partial_ref[...] = sum_out[...].astype(bf16)
        back_ref[...] = sum_back[...].astype(bf16)


def feed(first_order, second_order, x, ours, theirs, g, first, second, axes, step=1280):
    tokens, width = x.shape
    count = (first[0].shape[2] - width // 2) // step // 2
    rest = second[0].shape[2] - count * step

    def whole(*shape):
        return pl.BlockSpec(shape, lambda i, one, two: (0, 0))

    def piece(arrays, size, at):
        return [
            pl.BlockSpec((*array.shape[:2], size), lambda i, one, two: (0, 0, at(i)))
            for array in arrays
        ]

    pair = jax.ShapeDtypeStruct((tokens, width), bf16)
    return pl.pallas_call(
        functools.partial(feed_kernel, firsts=len(first), seconds=len(second), axes=axes),
        name="feed",
        grid_spec=pltpu.PrefetchScalarGridSpec(
            num_scalar_prefetch=2,
            grid=(count,),
            in_specs=[whole(tokens, width)] * 4
            + piece(first, step, lambda i: i)
            + piece(first, step, lambda i: count + i)
            + piece(second, step, lambda i: i)
            + piece(second, rest, lambda i: count * step // rest),
            out_specs=[whole(tokens, width)] * 3
            + [whole(width, 2 * count * step), whole(width, width // 2 + count * step + rest)],
            scratch_shapes=[
                pltpu.VMEM((tokens, width), bf16),
                pltpu.VMEM((width, tokens), bf16),
                pltpu.VMEM((width, tokens), bf16),
                pltpu.VMEM((tokens, width), f32),
                pltpu.VMEM((tokens, width), f32),
                pltpu.VMEM((width, step), bf16),
                pltpu.VMEM((width, step), bf16),
                pltpu.VMEM((width, step), bf16),
                pltpu.VMEM((width, rest), bf16),
            ],
        ),
        out_shape=[
            jax.ShapeDtypeStruct((tokens, width), f32),
            pair,
            pair,
            jax.ShapeDtypeStruct((width, 2 * count * step), bf16),
            jax.ShapeDtypeStruct((width, width // 2 + count * step + rest), bf16),
        ],
        compiler_params=pltpu.CompilerParams(vmem_limit_bytes=VMEM),
        cost_estimate=cost(2 * 9 * 2 * tokens * width * count * step, 24 << 20),
    )(first_order, second_order, x, ours, theirs, g, *first, *first, *second, *second)


def middle_back_kernel(
    core_ref, residual_ref, g_ref, ours_ref, theirs_ref, attn_ref, attended_ref, out_ours_ref,
    out_theirs_ref, grads_in_ref, layer_ref, residual_grad_ref, *rest, axes,
):
    dout_ref, grads_ref = rest
    rows = layer_ref.shape[0]
    half = attn_ref.shape[0]
    own = pl.ds(pl.multiple_of(core_ref[0] * rows, rows), rows)
    layer_ref[...] = (
        residual_ref[own, :]
        + out_ours_ref[own, :].astype(f32)
        + out_theirs_ref[...].astype(f32)
    ).astype(bf16)
    unit, inverse = unit_rows(residual_ref[...])
    scaled = ours_ref[...].astype(f32) + theirs_ref[...].astype(f32)
    grad = g_ref[...].astype(f32) + unit_back(scaled, unit, inverse)
    low = grad.astype(bf16)
    residual_grad_ref[...] = grad
    dout = dot(attn_ref[...], low, 1, 1).astype(bf16)
    for at in range(dout_ref.shape[0]):
        dout_ref[at] = dout[at * HDIM : (at + 1) * HDIM]
    grads = dot(attended_ref[...], low)
    few = grads.shape[0] // 8
    both = [part.reshape(few, 8, half) for part in (grads[:, :half], grads[:, half:])]
    both = jnp.stack(both, axis=1).reshape(grads_ref.shape).astype(bf16)
    for source, target in crossed_rows(axes):
        grads_ref[target * 16 : (target + 1) * 16] = both[source * 16 : (source + 1) * 16]


def middle_back(
    core, residual, g, ours, theirs, attn, attended, out_ours, out_theirs, grads, axes
):
    tokens, width = residual.shape
    rows = tokens // 2
    half = width // 2
    chips = half // HDIM

    def whole(*shape):
        return pl.BlockSpec(shape, lambda i, core: (0,) * len(shape))

    return pl.pallas_call(
        functools.partial(middle_back_kernel, axes=axes),
        name="middle_back",
        grid_spec=pltpu.PrefetchScalarGridSpec(
            num_scalar_prefetch=1,
            grid=(1,),
            in_specs=[whole(tokens, width)] * 4
            + [whole(half, width), whole(half, tokens), whole(tokens, width), whole(rows, width)]
            + [pl.BlockSpec(memory_space=pl.ANY)],
            out_specs=[whole(rows, width), whole(tokens, width)]
            + [whole(chips, HDIM, tokens), whole(width, half)],
        ),
        out_shape=[
            jax.ShapeDtypeStruct((rows, width), bf16),
            jax.ShapeDtypeStruct((tokens, width), f32),
        ]
        + [jax.ShapeDtypeStruct((chips, HDIM, tokens), bf16)]
        + [jax.ShapeDtypeStruct(grads.shape, bf16)],
        input_output_aliases={9: 3},
        compiler_params=pltpu.CompilerParams(vmem_limit_bytes=VMEM),
        cost_estimate=cost(2 * 2 * 2 * tokens * width * half, 16 << 20),
    )(core, residual, g, ours, theirs, attn, attended, out_ours, out_theirs, grads)


def hidden_back_kernel(order_ref, core_ref, shard_ref, w_ref, *rest):
    dp_refs, (own_ref, other_ref, stacked) = rest[:-3], rest[-3:]
    for place, dp_ref in enumerate(dp_refs):
        size = dp_ref.shape[0]
        stacked[pl.ds(pl.multiple_of(order_ref[place] * size, 64), size)] = dp_ref[...]
    rows = own_ref.shape[0]
    zero = core_ref[0] == 0
    size = w_ref.shape[1]
    for at in range(w_ref.shape[0]):
        flat = dot(w_ref[at], stacked[...])
        first = flat[:, :rows].T
        second = flat[:, rows:].T
        columns = pl.ds(pl.multiple_of(shard_ref[at] * size, size), size)
        own_ref[:, columns] = jnp.where(zero, first, second)
        other_ref[:, columns] = jnp.where(zero, second, first).astype(bf16)


def hidden_back(order, core, shard_order, weights, pieces):
    shards, size, columns = weights.shape
    width = shards * size
    rows = pieces[0].shape[1] // 2

    def whole(*shape):
        return pl.BlockSpec(shape, lambda i, order, core, shard: (0,) * len(shape))

    return pl.pallas_call(
        hidden_back_kernel,
        name="hidden_back",
        grid_spec=pltpu.PrefetchScalarGridSpec(
            num_scalar_prefetch=3,
            grid=(1,),
            in_specs=[whole(shards, size, columns)] + [whole(*pieces[0].shape)] * len(pieces),
            out_specs=[whole(rows, width)] * 2,
            scratch_shapes=[pltpu.VMEM((columns, 2 * rows), bf16)],
        ),
        out_shape=[
            jax.ShapeDtypeStruct((rows, width), f32),
            jax.ShapeDtypeStruct((rows, width), bf16),
        ],
        compiler_params=pltpu.CompilerParams(vmem_limit_bytes=VMEM),
        cost_estimate=cost(2 * 2 * 2 * rows * width * columns, 8 << 20),
    )(order, core, shard_order, weights, *pieces)


def head_grad_kernel(order_ref, unit_ref, *rest):
    dp_refs, out_ref = rest[:-1], rest[-1]
    block = dp_refs[0].shape[1]
    total = None
    for place, dp_ref in enumerate(dp_refs):
        rows = pl.ds(pl.multiple_of(order_ref[place] * block, block), block)
        added = dot(dp_ref[...], unit_ref[rows])
        total = added if total is None else total + added
    for at in range(out_ref.shape[0]):
        out_ref[at] = total[:, at * 128 : (at + 1) * 128].astype(bf16)


def head_grad(order, unit_all, pieces):
    length, width = unit_all.shape
    owners = width // 128
    size = pieces[0].shape[0]

    def whole(*shape):
        return pl.BlockSpec(shape, lambda i, order: (0,) * len(shape))

    return pl.pallas_call(
        head_grad_kernel,
        name="head_grad",
        grid_spec=pltpu.PrefetchScalarGridSpec(
            num_scalar_prefetch=1,
            grid=(1,),
            in_specs=[whole(length, width)] + [whole(*pieces[0].shape)] * len(pieces),
            out_specs=whole(owners, size, 128),
        ),
        out_shape=jax.ShapeDtypeStruct((owners, size, 128), bf16),
        compiler_params=pltpu.CompilerParams(vmem_limit_bytes=VMEM),
        cost_estimate=cost(2 * 2 * length * width * size, 10 << 20),
    )(order, unit_all, *pieces)


def adam_in_kernels(weight, gradient, first, second, rate):
    first = BETA_FIRST * first + (1.0 - BETA_FIRST) * gradient
    second = BETA_SECOND * second + (1.0 - BETA_SECOND) * gradient * gradient
    second_hat = second * (1.0 / (1.0 - BETA_SECOND**STEP))
    bottom = second_hat * lax.rsqrt(second_hat) + EPSILON
    guess = pl.reciprocal(bottom, approx=True)
    guess = guess * (2.0 - bottom * guess)
    scale = rate / (1.0 - BETA_FIRST**STEP)
    weight = weight * (1.0 - rate * DECAY) - (scale * first) * guess
    return (weight, first, second)


def adam_into(refs, weight, gradient, first, second, rate):
    for ref, value in zip(refs, adam_in_kernels(weight, gradient, first, second, rate)):
        ref[...] = value


def rounded_in_kernel(values):
    return values.astype(bf16).astype(f32)


def adam_most_kernel(grads_ref, gain_ref, *refs, rates):
    (w_in, m_in, v_in), attn, out = refs[:3], refs[3:6], refs[6:9]
    new_in, new_attn, new_out, gain_grad, turned = refs[9:12], refs[12:15], refs[15:18], *refs[18:]
    here = pl.program_id(0)
    chips = grads_ref.shape[0] // 2
    width = w_in.shape[1] // 2
    main = width // 256 * 128
    few = width // 2 - main
    out_at = 2 * main + attn[0].shape[2] // 2

    @pl.when(here == 0)
    def _():
        for core in range(2):
            columns = jnp.concatenate(
                [grads_ref[2 * chip + core, :, out_at : out_at + main] for chip in range(chips)],
                axis=0,
            )
            turned[core * main : (core + 1) * main] = columns.astype(f32).T
            rest = jnp.concatenate(
                [
                    grads_ref[2 * chip + core, :, out_at + main :] for chip in range(chips)
                ],
                axis=0,
            )
            start = 2 * main + core * few
            turned[start : start + few] = rest.astype(f32).T[2 * few : 3 * few]

    each = grads_ref.shape[1]
    some = w_in.shape[0] // each
    for at_chip in range(some):
        source = 2 * (here * some + at_chip)
        columns = []
        for at in range(2):
            for core in range(2):
                place = at * main
                columns.append(grads_ref[source + core, :, place : place + main].astype(f32))
            for core in range(2):
                rest = grads_ref[source + core, :, out_at + main :].astype(f32)
                columns.append(rest[:, at * few : (at + 1) * few])
        grads = jnp.concatenate(columns, axis=1)
        rows = slice(at_chip * each, (at_chip + 1) * each)
        weight = w_in[rows]
        gain_grad[rows] = jnp.sum(grads * rounded_in_kernel(weight), axis=1, keepdims=True)
        values = adam_in_kernels(
            weight, grads * gain_ref[rows], m_in[rows], v_in[rows], rates[0]
        )
        for ref, value in zip(new_in, values):
            ref[rows] = value
        rows = slice(at_chip * each // 2, (at_chip + 1) * each // 2)
        for core in range(2):
            piece = grads_ref[source + core, :, 2 * main : out_at].astype(f32)
            grads = jnp.concatenate([piece[: each // 2], piece[each // 2 :]], axis=1)
            values = adam_in_kernels(
                attn[0][core, rows], grads, attn[1][core, rows], attn[2][core, rows], rates[1]
            )
            for ref, value in zip(new_attn, values):
                ref[core, rows] = value

    size = out[0].shape[0]
    grads = turned[pl.ds(pl.multiple_of(here * size, 8), size)]
    adam_into(new_out, out[0][...], grads, out[1][...], out[2][...], rates[2])


def adam_most(
    grads, gain, weights_in, weights_attn, weights_out, rates, steps=2
):
    rows, columns = weights_in[0].shape
    width = weights_attn[0].shape[1]
    hidden = weights_out[0].shape[0]
    weights_attn = [array.reshape(2, rows // 2, width) for array in weights_attn]
    block_in = pl.BlockSpec((rows // steps, columns), lambda i: (i, 0))
    block_attn = pl.BlockSpec((2, rows // 2 // steps, width), lambda i: (0, i, 0))
    block_out = pl.BlockSpec((hidden // steps, rows), lambda i: (i, 0))
    column = pl.BlockSpec((rows // steps, 1), lambda i: (i, 0))
    blocks = [block_in] * 3 + [block_attn] * 3 + [block_out] * 3
    arrays = (*weights_in, *weights_attn, *weights_out)
    results = pl.pallas_call(
        functools.partial(adam_most_kernel, rates=rates),
        name="adam_most",
        grid=(steps,),
        in_specs=[pl.BlockSpec(grads.shape, lambda i: (0, 0, 0)), column] + blocks,
        out_specs=blocks + [column],
        out_shape=[jax.ShapeDtypeStruct(array.shape, f32) for array in arrays]
        + [jax.ShapeDtypeStruct((rows, 1), f32)],
        scratch_shapes=[pltpu.VMEM((hidden, rows), f32)],
        compiler_params=pltpu.CompilerParams(vmem_limit_bytes=VMEM),
        cost_estimate=cost(rows * columns * 20, rows * columns * 26),
    )(grads, gain, *arrays)
    new_attn = [array.reshape(rows, width) for array in results[3:6]]
    return results[:3], new_attn, results[6:9], results[9]


def adam_qkv_kernel(order_ref, *refs, rate):
    grads_refs, (gain_ref, other_ref), gains = refs[:-16], refs[-16:-14], refs[-14:-11]
    (w_ref, m_ref, v_ref), new, new_gains = refs[-11:-8], refs[-8:-5], refs[-5:-2]
    gain_grad, joined = refs[-2:]
    here = pl.program_id(0)
    heads = sum(grads_ref.shape[0] for grads_ref in grads_refs)

    @pl.when(here == 0)
    def _():
        at = 0
        for grads_ref in grads_refs:
            for place in range(grads_ref.shape[0]):
                for part in range(3):
                    row = (part * heads + order_ref[at]) * HDIM
                    joined[pl.ds(pl.multiple_of(row, HDIM), HDIM)] = grads_ref[
                        place, part * HDIM : (part + 1) * HDIM
                    ].astype(f32)
                at += 1

    size = w_ref.shape[1]
    grads = joined[pl.ds(pl.multiple_of(here * size, size), size)].T
    weight = w_ref[...]
    added = jnp.sum(grads * rounded_in_kernel(weight), axis=1, keepdims=True)
    gain_grad[...] = added + jnp.where(here == 0, 0.0, gain_grad[...])
    adam_into(new, weight, grads * gain_ref[...], m_ref[...], v_ref[...], rate)

    @pl.when(here == pl.num_programs(0) - 1)
    def _():
        both = jnp.concatenate(
            [gain_grad[...], other_ref[...], jnp.zeros((gain_grad.shape[0], 6), f32)], axis=1
        )
        adam_into(
            new_gains, gains[0][...], both.T[:2], gains[1][...], gains[2][...], GAIN_RATE
        )


def adam_qkv(order, grads, gain, other_gain, gains, weight, first, second, rate, step=1536):
    rows, columns = weight.shape
    block = pl.BlockSpec((rows, step), lambda i, order: (0, i))
    column = pl.BlockSpec((rows, 1), lambda i, order: (0, 0))
    block_gains = pl.BlockSpec(gains[0].shape, lambda i, order: (0, 0))
    same = jax.ShapeDtypeStruct((rows, columns), f32)
    return pl.pallas_call(
        functools.partial(adam_qkv_kernel, rate=rate),
        name="adam_qkv",
        grid_spec=pltpu.PrefetchScalarGridSpec(
            num_scalar_prefetch=1,
            grid=(columns // step,),
            in_specs=[pl.BlockSpec(piece.shape, lambda i, order: (0, 0, 0)) for piece in grads]
            + [column] * 2
            + [block_gains] * 3
            + [block] * 3,
            out_specs=[block] * 3 + [block_gains] * 3,
            scratch_shapes=[pltpu.VMEM((rows, 1), f32), pltpu.VMEM((columns, rows), f32)],
        ),
        out_shape=[same] * 3 + [jax.ShapeDtypeStruct(gains[0].shape, f32)] * 3,
        compiler_params=pltpu.CompilerParams(vmem_limit_bytes=VMEM),
        cost_estimate=cost(rows * columns * 20, rows * columns * 26),
    )(order, *grads, gain, other_gain, *gains, weight, first, second)


def ring(axis, shift):
    size = lax.axis_size(axis)
    return [(at, (at + shift) % size) for at in range(size)]


def gather_first_step(planes_first, lines_first):
    swapped = lax.ppermute(planes_first, "zh", SWAP)
    others = [
        lax.ppermute(lines_first, "y", ring("y", shift)) for shift in range(1, lax.axis_size("y"))
    ]
    return jnp.stack([planes_first, swapped]), jnp.stack([lines_first, *others])


def shards(
    tokens,
    positions,
    cotangent,
    weight_qkv,
    weight_attn,
    weight_in,
    weight_out,
    norm_gains,
    first_qkv,
    first_attn,
    first_in,
    first_out,
    first_gains,
    second_qkv,
    second_attn,
    second_in,
    second_out,
    second_gains,
):
    rows, width = tokens.shape[1:]
    shard_rows = weight_qkv.shape[1]
    heads = width // HDIM
    hidden = weight_out.shape[1]
    core = lax.axis_index("c")
    mine = lax.axis_index(CTX)
    chip = lax.axis_index(CHIPS)
    chips = lax.axis_size(CHIPS)
    owners = lax.axis_size(FSDP)
    length = rows * chips * 2
    main = hidden // 256 * 128
    few = hidden // 2 - main
    core_at = core.reshape(1).astype(jnp.int32)
    axes = (lax.axis_size("zh"), lax.axis_size("y"), lax.axis_size("x"), lax.axis_size("zl"))
    offsets = [(far, near) for far in range(lax.axis_size("x")) for near in range(2)]
    across, beside = lax.axis_index("x"), lax.axis_index("zl")
    wide = lax.axis_size("x")

    def chips_at(sign):
        places = [(across + sign * far) % wide * 2 + (beside ^ near) for far, near in offsets]
        return jnp.stack(places).astype(jnp.int32)

    local = tokens[0]
    extra = 16
    high, low = positions[0] // 128, positions[0] % 128
    places_row = jnp.concatenate([high, low, jnp.zeros((width - 2 * rows,), jnp.int32)])
    places_rows = jnp.concatenate(
        [places_row[None], jnp.zeros((extra - 1, width), jnp.int32)], axis=0
    ).astype(bf16)
    sequence = lax.all_gather(
        jnp.concatenate([local, places_rows], axis=0), CTX, axis=0, tiled=True
    )
    first_part, second_part, head_part, half_heads = prepare(
        jnp.stack([core, chip]).astype(jnp.int32),
        norm_gains[0],
        weight_qkv[0],
        weight_attn[0],
        weight_in[0],
        weight_out[0],
    )
    first_joined, second_joined = gather_first_step(first_part, second_part)
    head_weights = lax.all_to_all(
        jnp.broadcast_to(head_part, (owners, *head_part.shape)), FSDP, 0, 0, tiled=True
    )
    first_pieces = [first_joined] + [
        lax.ppermute(first_joined, "y", ring("y", shift))
        for shift in range(1, lax.axis_size("y"))
    ]
    sequence, _, second_joined, half_heads, _ = lax.optimization_barrier(
        (sequence, first_joined, second_joined, half_heads, head_weights)
    )
    half_heads_other = lax.ppermute(half_heads, "zh", SWAP)
    second_pieces = [second_joined, lax.ppermute(second_joined, "zh", SWAP)]
    lines = lax.axis_size("y")
    plane, line = lax.axis_index("zh"), lax.axis_index("y")
    heads_order = jnp.stack(
        [(plane ^ far) * lines + at for at in range(lines) for far in range(2)]
    ).astype(jnp.int32)
    first_order = jnp.stack(
        [(plane ^ far) * lines + (line - shift) % lines for shift in range(lines) for far in range(2)]
    ).astype(jnp.int32)
    second_order = jnp.stack(
        [(plane ^ far) * lines + (line - shift) % lines for far in range(2) for shift in range(lines)]
    ).astype(jnp.int32)

    def in_order(ours, theirs):
        first = jnp.where(core == 0, ours, theirs)
        second = jnp.where(core == 0, theirs, ours)
        return jnp.concatenate([first, second], axis=0)

    def swap(array):
        return lax.ppermute(array, "c", SWAP)

    gradient = in_order(cotangent[0], swap(cotangent[0]))

    freqs = jnp.exp(jnp.arange(HDIM // 2, dtype=f32) * (-2.0 * math.log(ROPE_BASE) / HDIM))
    by_device = sequence.reshape(2 * chips, rows + extra, width)[:, rows]
    by_device = by_device.astype(f32)
    places = by_device[:, :rows] * 128.0 + by_device[:, rows : 2 * rows]
    angles = freqs[:, None] * places.reshape(1, length)
    cosine = jnp.cos(angles)
    sine = jnp.sin(angles)
    unit_all, qkv, keys, values = project(sequence, head_weights, cosine, sine, extra)
    low_out, out, lse = attend(keys, qkv, chips)
    firsts = len(first_pieces)
    low_out, half_heads_other, *arrived = lax.optimization_barrier(
        (low_out, half_heads_other, *first_pieces, *second_pieces)
    )
    first_pieces, second_pieces = arrived[:firsts], arrived[firsts:]
    mat_qkv = lax.all_gather(
        jnp.stack([half_heads, half_heads_other]), "y", axis=0, tiled=True
    )
    attended = lax.all_to_all(low_out, CHIPS, 0, 0, tiled=True)
    attended = attended.reshape(heads // 2 * HDIM, 2 * rows)
    mixed, mat_attn = attend_out(first_order, attended, first_pieces)
    current = lax.dynamic_slice_in_dim(
        sequence, chip * 2 * (rows + extra), 2 * (rows + extra), 0
    ).reshape(2, rows + extra, width)[:, :rows].reshape(2 * rows, width)
    residual, partial, back, grads, out_grads = feed(
        first_order, second_order, current, mixed, swap(mixed), gradient, first_pieces,
        second_pieces, axes,
    )
    grads, mat_qkv = lax.optimization_barrier((grads, mat_qkv))
    first_sum = lax.psum_scatter(grads, "y", scatter_dimension=0, tiled=True)

    def move(pieces, sign):
        moved = [pieces[0]]
        for (far, near), piece in list(zip(offsets, pieces))[1:]:
            pairs = [
                (at, (at // 2 + sign * far) % wide * 2 + (at % 2 ^ near)) for at in range(chips)
            ]
            moved.append(lax.ppermute(piece, CHIPS, pairs))
        return moved

    ahead, behind = chips_at(1), chips_at(-1)
    theirs = swap(lax.dynamic_slice_in_dim(partial, (1 - core) * rows, rows, 0))
    layer_out, residual_grad, dout_pair, out_grads = middle_back(
        core_at, residual, gradient, back, swap(back), mat_attn, attended, partial, theirs,
        out_grads, axes,
    )

    douts = lax.all_to_all(dout_pair, CHIPS, 0, 0, tiled=True)
    out_grads, douts = lax.optimization_barrier((out_grads, douts))
    out_arrived = lax.all_to_all(out_grads, ("x", "zh", "zl"), 0, 0, tiled=True)
    pieces = attend_back(behind, keys, values, qkv, douts, out, lse, cosine, sine)
    moved = move(pieces, -1)
    out_arrived, first_sum, moved[1] = lax.optimization_barrier(
        (out_arrived, first_sum, moved[1])
    )
    arrived = lax.all_to_all(first_sum, ("x", "zh", "zl"), 0, 0, tiled=True)

    def total(arrays):
        return sum(array.astype(f32) for array in arrays).astype(bf16)

    out_arrived = out_arrived.reshape(2 * chips, width // (2 * chips), -1)
    out_sum = jnp.sum(out_arrived.astype(f32), axis=0).astype(bf16)
    out_sum = out_sum.reshape(lines, shard_rows // chips, -1)
    out_parts = [
        lax.dynamic_index_in_dim(out_sum, (line + shift) % lines, 0, keepdims=False)
        for shift in range(lines)
    ]
    out_sum = total(
        out_parts[:1]
        + [
            lax.ppermute(part, "y", ring("y", shift))
            for shift, part in list(enumerate(out_parts))[1:]
        ]
    )

    arrived, out_sum, *moved = lax.optimization_barrier((arrived, out_sum, *moved))
    pieces = lax.optimization_barrier((*pieces, arrived))[:chips]
    head_parts = head_grad(behind, unit_all, pieces)
    own_hidden, other_hidden = hidden_back(ahead, core_at, heads_order, mat_qkv, moved)
    grad_hidden = own_hidden + swap(other_hidden).astype(f32)
    unit_in, scale_in = unit_rows(local.astype(f32))
    own_residual = lax.dynamic_slice_in_dim(residual_grad, core * rows, rows, 0)
    tokens_grad = (own_residual + unit_back(grad_hidden, unit_in, scale_in))[None]

    arrived = arrived.reshape(2 * chips, shard_rows // chips, -1)
    second_sum = jnp.sum(arrived.astype(f32), axis=0).astype(bf16)
    second_sum = jnp.concatenate([second_sum, out_sum], axis=1)
    all_grads = lax.all_gather(second_sum, CTX, axis=0, tiled=False)

    head_sums = lax.all_to_all(head_parts, FSDP, 0, 0, tiled=True)
    head_own = jnp.sum(head_sums.astype(f32), axis=0).astype(bf16)[None]
    head_pair = jnp.concatenate([head_own, swap(head_own)], axis=0)
    head_four = jnp.concatenate([head_pair, lax.ppermute(head_pair, "zl", SWAP)], axis=0)
    head_grads = [head_four] + [
        lax.ppermute(head_four, "x", ring("x", shift)) for shift in range(1, wide)
    ]
    head_order = jnp.stack(
        [
            (across - shift) % wide * 4 + (beside ^ near) * 2 + (core ^ other)
            for shift in range(wide)
            for near in range(2)
            for other in range(2)
        ]
    ).astype(jnp.int32)

    rates = (
        width ** (-0.5),
        max(1, 3 * width // length) ** (-0.5),
        width ** (-0.5),
        hidden ** (-0.5),
    )
    columns_of_gains = norm_gains[0].astype(bf16).astype(f32).T
    new_in, new_attn, new_out, gain_second = adam_most(
        all_grads,
        columns_of_gains[:, 1:],
        (weight_in[0], first_in[0], second_in[0]),
        (weight_attn[0], first_attn[0], second_attn[0]),
        (weight_out[0], first_out[0], second_out[0]),
        (rates[2], rates[1], rates[3]),
    )
    results = adam_qkv(
        head_order,
        head_grads,
        columns_of_gains[:, :1],
        gain_second,
        (norm_gains[0], first_gains[0], second_gains[0]),
        weight_qkv[0],
        first_qkv[0],
        second_qkv[0],
        rates[0],
    )
    new_qkv, new_gains = results[:3], results[3:]
    updated = (new_qkv, new_attn, new_in, new_out, new_gains)
    return (
        layer_out[None],
        tokens_grad,
        *[updated[member][0][None] for member in range(5)],
        *[updated[member][1][None] for member in range(5)],
        *[updated[member][2][None] for member in range(5)],
    )


def solution(mesh):
    split = Mesh(mesh.devices.reshape(4, 2, 2, 2, 4), ("x", "zl", "c", "zh", "y"))
    by_row = P(None, FSDP, None)
    by_column = P(None, None, FSDP)
    weights = (by_row, by_row, by_row, by_column, by_column)
    by_token = P(FSDP, CTX, None)
    return jax.shard_map(
        shards,
        mesh=split,
        in_specs=(by_token, P(FSDP, CTX), by_token) + weights * 3,
        out_specs=(by_token, by_token) + weights * 3,
        check_vma=False,
    )
```
